32 devices in a mesh: dom: 4 (over y, x), orb: 8 (over z, core).
Axes of the slice: x: 2, y: 2, z: 4, core: 2. Of those that a mesh axis runs over, the one named last changes fastest.
Arguments:
- orbitals: float32 [128, 32, 16, 128], P('orb', 'dom'), may hold values from -6 to 6
- potential: float32 [32, 16, 128], P('dom'), may hold values from 0.2 to 17, as said below
- rotation: float32 [128, 128], P('orb'), may hold values from -0.6 to 0.6
- block: int32 [1], replicated, may hold values from 0 to 7
- owner: int32 [1], replicated, may hold values from 0 to 7
Outputs:
- gradient: float32 [16, 32, 16, 128], P(None, 'dom')
- updated: float32 [128, 32, 16, 128], P('orb', 'dom')
The draws below stay inside these ranges and needn't reach their ends.
Inputs may be any that keep to these rules, and one draw needn't show every extreme that they name: A positive local potential.
All inputs are finite; a program needn't handle non-finite values.
Results may differ from the reference program's by a relative error of at most 0.00017.
Values sent between devices are 32-bit elements; how exact they have to be, the bound alone decides.
No kernel may reach another device: no remote copies, remote signals or barrier semaphores. Data moves between devices by JAX's collectives and lax.ppermute only.
A program may use at most 128 MiB of HBM per device.

```python
import jax
import jax.numpy as jnp
from jax import lax

NB = 16
NY = 16
NZ = 128
NX = 32
ORBS = 128
N_ORB = 8


def draw_potential(key, part):
    key = jax.random.fold_in(key, 5)
    ramp_pos = jnp.arange(NX, dtype=jnp.float32)[:, None, None] / NX
    rough = jax.random.uniform(key, (NX, NY, NZ), jnp.float32, 0.5, 1.5)
    values = rough * (1.0 + 5.0 * ramp_pos)
    return values.astype(jnp.float32)


def block_levels(rng, shape, split, low, high):
    factor_of = 1.0
    for position, blocks in split:
        draws = jax.random.uniform(jax.random.fold_in(jax.random.fold_in(rng, 6), position), (blocks,), jnp.float32, low / len(split), high / len(split))
        factor_of = factor_of * jnp.repeat(jnp.exp(draws), shape[position] // blocks).reshape((-1,) + (1,) * (len(shape) - 1 - position))
    return factor_of


def normal_values(rng, shape, deviation, reach, pieces=(), held_as=jnp.bfloat16):
    entries = deviation * jax.random.normal(rng, shape, jnp.float32)
    if pieces:
        entries = entries * block_levels(rng, shape, pieces, -0.22, 0.18)
    return jnp.clip(entries, -reach, reach).astype(held_as)


def setup_inputs(seed: int = 0) -> dict:
    splits = jax.random.split(jax.random.key(seed), 6)
    orbitals = normal_values(splits[0], (ORBS, NX, NY, NZ), 1.0, 6.0, ((0, 8), (1, 4)), jnp.float32)
    potential = draw_potential(jax.random.fold_in(splits[5], 71), 0)
    rotation = normal_values(splits[2], (ORBS, ORBS), 0.1, 0.6, ((0, 8),), jnp.float32)
    block = jax.random.randint(splits[3], (1,), 0, N_ORB).astype(jnp.int32)
    owner = jax.random.randint(splits[4], (1,), 0, N_ORB).astype(jnp.int32)
    return dict(orbitals=orbitals, potential=potential, rotation=rotation, block=block, owner=owner)


CENTER = -5369.0 / 1800.0
SIDES = (12.0 / 7.0, -15.0 / 56.0, 10.0 / 189.0, -1.0 / 112.0, 2.0 / 1925.0, -1.0 / 16632.0)


def kinetic(field):
    summed = 3.0 * CENTER * field
    for offset in range(1, 7):
        weight = SIDES[offset - 1]
        for axis_pos in (1, 2, 3):
            summed = summed + weight * (jnp.roll(field, offset, axis_pos) + jnp.roll(field, -offset, axis_pos))
    return -0.5 * summed


def reference(orbitals, potential, rotation, block, owner):
    nblocks = ORBS // NB
    volume = 1.0 / (NX * NY * NZ)
    start = (block[0] * NB).astype(jnp.int32)
    active = lax.dynamic_slice_in_dim(orbitals, start, NB, 0)
    applied = kinetic(active) + potential[None] * active
    grouped = orbitals.reshape(nblocks, NB, NX, NY, NZ)
    proj = jnp.einsum("jaxyz,cxyz->jac", grouped, applied, precision=lax.Precision.HIGHEST) * volume
    removed = jnp.einsum("jaxyz,jac->cxyz", grouped, proj, precision=lax.Precision.HIGHEST)
    gradient = applied - removed
    panel_start = (owner[0] * NB).astype(jnp.int32)
    panel = lax.dynamic_slice_in_dim(rotation, panel_start, NB, 0)
    coeffs = panel.reshape(NB, nblocks, NB)
    added = jnp.einsum("cxyz,cja->jaxyz", gradient, coeffs, precision=lax.Precision.HIGHEST)
    updated = orbitals + added.reshape(ORBS, NX, NY, NZ)
    return gradient, updated
```

```python
import functools

import jax
import jax.numpy as jnp
import numpy as np
from jax import lax
from jax.experimental import pallas as pl
from jax.experimental.pallas import tpu as pltpu
from jax.sharding import PartitionSpec as P

CENTER = -5369.0 / 1800.0
SIDES = (12.0 / 7.0, -15.0 / 56.0, 10.0 / 189.0, -1.0 / 112.0, 2.0 / 1925.0, -1.0 / 16632.0)
WIDTH = 6
VMEM = pl.BlockSpec(memory_space=pltpu.VMEM)
SMEM = pl.BlockSpec(memory_space=pltpu.SMEM)
HIGHEST = lax.Precision.HIGHEST


def params():
    return pltpu.CompilerParams(vmem_limit_bytes=32 * 1024 * 1024)


def plane_weights(planes, rows_y):
    cells = planes * rows_y
    table = np.zeros((3 * cells, cells), np.float64)
    for x in range(planes):
        for y in range(rows_y):
            out = x * rows_y + y
            table[cells + out, out] += 3.0 * CENTER
            for k, weight in enumerate(SIDES, 1):
                for step in (k, -k):
                    table[cells + x * rows_y + (y + step) % rows_y, out] += weight
                    table[cells + (x + step) * rows_y + y, out] += weight
    return (-0.5 * table).astype(np.float32)


def pack_kernel(x_ref, v_ref, t_ref, vt_ref, turned):
    slab = vt_ref.shape[0]
    count, _, rows_z = x_ref.shape
    for a in range(count):
        t_ref[pl.ds(a, rows_z, stride=count), :] = x_ref[a].T
    turned[...] = v_ref[...].T
    rank = lax.axis_index("orb")
    vt_ref[...] = turned[pl.ds(pl.multiple_of(rank * slab, slab), slab), :]


def pick_kernel(block_ref, x_ref, act_ref, low_ref, high_ref):
    slab = act_ref.shape[0]
    act_ref[...] = x_ref[0]
    low_ref[...] = x_ref[0, :WIDTH]
    high_ref[...] = x_ref[0, slab - WIDTH :]


def project_kernel(volume, x_ref, act_ref, zb_ref, za_ref, xb_ref, xa_ref, vt_ref, w_ref, a_ref, p_ref):
    slab, nb, cells = act_ref.shape
    blocks = x_ref.shape[0]
    act = act_ref[...]
    wide = jnp.concatenate([xb_ref[...], act, xa_ref[...]], axis=2).reshape(slab * nb, 3 * cells)
    applied = jnp.dot(wide, w_ref[...], precision=HIGHEST, preferred_element_type=jnp.float32)
    applied = applied.reshape(slab, nb, cells) + vt_ref[...][:, None, :] * act
    tall = jnp.concatenate([zb_ref[...], act, za_ref[...]], axis=0)
    for k, weight in enumerate(SIDES, 1):
        upper = tall[WIDTH + k : WIDTH + k + slab]
        lower = tall[WIDTH - k : WIDTH - k + slab]
        applied = applied + (-0.5 * weight) * (upper + lower)
    a_ref[...] = applied
    total = jnp.zeros((nb, blocks * nb), jnp.float32)
    for z in range(slab):
        orbs = x_ref[:, z].reshape(blocks * nb, cells)
        total = total + lax.dot_general(
            applied[z], orbs, (((1,), (1,)), ((), ())), precision=HIGHEST, preferred_element_type=jnp.float32
        )
    p_ref[...] = total * volume


def remove_kernel(x_ref, a_ref, p_ref, g_ref):
    slab, nb, cells = a_ref.shape
    blocks = x_ref.shape[0]
    proj = p_ref[...]
    for z in range(slab):
        orbs = x_ref[:, z].reshape(blocks * nb, cells)
        g_ref[z] = a_ref[z] - jnp.dot(proj, orbs, precision=HIGHEST, preferred_element_type=jnp.float32)


def update_kernel(panel_ref, g_ref, x_ref, grad_ref, out_ref):
    nb, cells, rows_z = x_ref.shape
    start = lax.axis_index("orb") * nb
    for c in range(nb):
        grad_ref[c] = g_ref[pl.ds(c, rows_z, stride=nb), :].T
    rows = 32
    for a in range(nb):
        @pl.loop(0, cells // rows)
        def _(i, a=a):
            at = pl.ds(pl.multiple_of(i * rows, rows), rows)
            total = x_ref[a, at]
            for c in range(nb):
                total = total + panel_ref[c, start + a] * grad_ref[c, at]
            out_ref[a, at] = total


def per_device(orbitals, potential, rotation, block, owner):
    nb, planes, rows_y, rows_z = orbitals.shape
    blocks, doms = lax.axis_size("orb"), lax.axis_size("dom")
    cells = planes * rows_y
    slab = rows_z // blocks
    volume = 1.0 / (cells * doms * rows_z)
    f32 = jnp.float32
    shape = lambda *dims: jax.ShapeDtypeStruct(dims, f32)

    flat = orbitals.reshape(nb, cells, rows_z)
    turned, v_slab = pl.pallas_call(
        pack_kernel,
        out_shape=(shape(rows_z * nb, cells), shape(slab, cells)),
        in_specs=[VMEM, VMEM],
        out_specs=(VMEM, VMEM),
        scratch_shapes=[pltpu.VMEM((rows_z, cells), f32)],
        compiler_params=params(),
        name="pack",
    )(flat, potential.reshape(cells, rows_z))

    spread = lax.all_to_all(turned.reshape(blocks, slab, nb, cells), "orb", 0, 0)

    piece = pl.BlockSpec((slab, nb, cells), lambda i, b: (0, 0, 0))
    edge = pl.BlockSpec((WIDTH, nb, cells), lambda i, b: (0, 0, 0))
    active, low, high = pl.pallas_call(
        pick_kernel,
        out_shape=(shape(slab, nb, cells), shape(WIDTH, nb, cells), shape(WIDTH, nb, cells)),
        grid_spec=pltpu.PrefetchScalarGridSpec(
            num_scalar_prefetch=1,
            grid=(1,),
            in_specs=[pl.BlockSpec((1, slab, nb, cells), lambda i, b: (b[0], 0, 0, 0))],
            out_specs=(piece, edge, edge),
        ),
        compiler_params=params(),
        name="pick",
    )(block, spread)

    up = lambda count: [(i, (i + 1) % count) for i in range(count)]
    down = lambda count: [(i, (i - 1) % count) for i in range(count)]
    x_before = lax.ppermute(active, "dom", up(doms))
    x_after = lax.ppermute(active, "dom", down(doms))
    z_before = lax.ppermute(high, "orb", up(blocks))
    z_after = lax.ppermute(low, "orb", down(blocks))

    weights = jnp.asarray(plane_weights(planes, rows_y))
    applied, part = pl.pallas_call(
        functools.partial(project_kernel, volume),
        out_shape=(shape(slab, nb, cells), shape(nb, blocks * nb)),
        in_specs=[VMEM] * 8,
        out_specs=(VMEM, VMEM),
        compiler_params=params(),
        name="project",
    )(spread, active, z_before, z_after, x_before, x_after, v_slab, weights)

    mine = (lax.axis_index("orb") == owner[0]) & (lax.axis_index("dom") == 0)
    sent = jnp.concatenate([part, jnp.where(mine, rotation, 0.0)], axis=0)
    summed = lax.psum(sent, ("dom", "orb"))
    proj, panel = summed[:nb], summed[nb:]

    own = pl.pallas_call(
        remove_kernel,
        out_shape=shape(slab, nb, cells),
        in_specs=[VMEM] * 3,
        out_specs=VMEM,
        compiler_params=params(),
        name="remove",
    )(spread, applied, proj)

    whole = lax.all_gather(own, "orb", axis=0, tiled=True)

    gradient, updated = pl.pallas_call(
        update_kernel,
        out_shape=(shape(nb, cells, rows_z), shape(nb, cells, rows_z)),
        in_specs=[SMEM, VMEM, VMEM],
        out_specs=(VMEM, VMEM),
        compiler_params=params(),
        name="update",
    )(panel, whole.reshape(rows_z * nb, cells), flat)
    return gradient.reshape(orbitals.shape), updated.reshape(orbitals.shape)


def solution(mesh):
    in_specs = (P("orb", "dom", None, None), P("dom", None, None), P("orb", None), P(), P())
    out_specs = (P(None, "dom", None, None), P("orb", "dom", None, None))
    return jax.shard_map(
        per_device, mesh=mesh, in_specs=in_specs, out_specs=out_specs, check_vma=False
    )
```

```python
import functools

import jax
import jax.numpy as jnp
import numpy as np
from jax import lax
from jax.experimental import pallas as pl
from jax.experimental.pallas import tpu as pltpu
from jax.sharding import PartitionSpec as P

CENTER = -5369.0 / 1800.0
SIDES = (12.0 / 7.0, -15.0 / 56.0, 10.0 / 189.0, -1.0 / 112.0, 2.0 / 1925.0, -1.0 / 16632.0)
WIDTH = 6
VMEM = pl.BlockSpec(memory_space=pltpu.VMEM)
SMEM = pl.BlockSpec(memory_space=pltpu.SMEM)
HIGHEST = lax.Precision.HIGHEST


def params():
    return pltpu.CompilerParams(vmem_limit_bytes=32 * 1024 * 1024)


def plane_weights(planes, rows_y):
    cells = planes * rows_y
    table = np.zeros((3 * cells, cells), np.float64)
    for x in range(planes):
        for y in range(rows_y):
            out = x * rows_y + y
            table[cells + out, out] += 3.0 * CENTER
            for k, weight in enumerate(SIDES, 1):
                for step in (k, -k):
                    table[cells + x * rows_y + (y + step) % rows_y, out] += weight
                    table[cells + (x + step) * rows_y + y, out] += weight
    return (-0.5 * table).astype(np.float32)


def pack_kernel(blocks, x_ref, v_ref, *refs):
    t_refs, vt_ref, turned, v_turned = refs[:blocks], refs[blocks], refs[blocks + 1], refs[blocks + 2]
    slab = vt_ref.shape[0]
    count, _, rows_z = x_ref.shape
    for a in range(count):
        turned[pl.ds(a, rows_z, stride=count), :] = x_ref[a].T
    v_turned[...] = v_ref[...].T
    rank = lax.axis_index("orb")
    vt_ref[...] = v_turned[pl.ds(pl.multiple_of(rank * slab, slab), slab), :]
    rows = slab * count
    for k in range(blocks):
        start = pl.multiple_of((rank ^ k) * rows, rows)
        t_refs[k][...] = turned[pl.ds(start, rows), :].reshape(t_refs[k].shape)


def pick_kernel(blocks, block_ref, *refs):
    x_refs, (act_ref, low_ref, high_ref) = refs[:blocks], refs[blocks:]
    slab = act_ref.shape[0]
    wanted = lax.axis_index("orb") ^ block_ref[0]
    for k in range(blocks):
        @pl.when(wanted == k)
        def _(k=k):
            act_ref[...] = x_refs[k][...]
            low_ref[...] = x_refs[k][:WIDTH]
            high_ref[...] = x_refs[k][slab - WIDTH :]


def reorder(value, nb):
    wide = value.shape[1]
    row = lax.broadcasted_iota(jnp.int32, (wide, wide), 0)
    col = lax.broadcasted_iota(jnp.int32, (wide, wide), 1)
    swap = jnp.where(row == (col ^ (lax.axis_index("orb") * nb)), 1.0, 0.0)
    return jnp.dot(value, swap, precision=HIGHEST, preferred_element_type=jnp.float32)


def project_kernel(blocks, volume, *refs):
    x_refs = refs[:blocks]
    act_ref, zb_ref, za_ref, xb_ref, xa_ref, vt_ref, w_ref, a_ref, p_ref = refs[blocks:]
    slab, nb, cells = act_ref.shape
    act = act_ref[...]
    wide = jnp.concatenate([xb_ref[...], act, xa_ref[...]], axis=2).reshape(slab * nb, 3 * cells)
    applied = jnp.dot(wide, w_ref[...], precision=HIGHEST, preferred_element_type=jnp.float32)
    applied = applied.reshape(slab, nb, cells) + vt_ref[...][:, None, :] * act
    tall = jnp.concatenate([zb_ref[...], act, za_ref[...]], axis=0)
    for k, weight in enumerate(SIDES, 1):
        upper = tall[WIDTH + k : WIDTH + k + slab]
        lower = tall[WIDTH - k : WIDTH - k + slab]
        applied = applied + (-0.5 * weight) * (upper + lower)
    a_ref[...] = applied
    total = jnp.zeros((nb, blocks * nb), jnp.float32)
    for z in range(slab):
        orbs = jnp.concatenate([x[z] for x in x_refs], axis=0)
        total = total + lax.dot_general(
            applied[z], orbs, (((1,), (1,)), ((), ())), precision=HIGHEST, preferred_element_type=jnp.float32
        )
    p_ref[...] = reorder(total * volume, nb)


def remove_kernel(blocks, *refs):
    x_refs, (a_ref, p_ref, g_ref) = refs[:blocks], refs[blocks:]
    slab, nb, _ = a_ref.shape
    proj = reorder(p_ref[...], nb)
    for z in range(slab):
        orbs = jnp.concatenate([x[z] for x in x_refs], axis=0)
        g_ref[z] = a_ref[z] - jnp.dot(proj, orbs, precision=HIGHEST, preferred_element_type=jnp.float32)


def update_kernel(blocks, panel_ref, x_ref, *refs):
    g_refs, (grad_ref, out_ref, whole) = refs[:blocks], refs[blocks:]
    nb, cells, rows_z = x_ref.shape
    rank = lax.axis_index("orb")
    share = rows_z // blocks * nb
    for k in range(blocks):
        at = pl.ds(pl.multiple_of((rank ^ k) * share, share), share)
        whole[at, :] = g_refs[k][...].reshape(share, cells)
    for c in range(nb):
        grad_ref[c] = whole[pl.ds(c, rows_z, stride=nb), :].T
    rows = 32
    for a in range(nb):
        @pl.loop(0, cells // rows)
        def _(i, a=a):
            at = pl.ds(pl.multiple_of(i * rows, rows), rows)
            total = x_ref[a, at]
            for c in range(nb):
                total = total + panel_ref[c, rank * nb + a] * grad_ref[c, at]
            out_ref[a, at] = total


def swap(value, axis, k):
    count = lax.axis_size(axis)
    return lax.ppermute(value, axis, [(i, i ^ k) for i in range(count)])


def total_over_all(value):
    doms, blocks = lax.axis_size("dom"), lax.axis_size("orb")
    for axis, steps in (("dom", range(1, doms)), ("orb", range(2, blocks, 2)), ("orb", (1,))):
        value = sum([swap(value, axis, k) for k in steps], value)
    return value


def per_device(orbitals, potential, rotation, block, owner):
    nb, planes, rows_y, rows_z = orbitals.shape
    blocks, doms = lax.axis_size("orb"), lax.axis_size("dom")
    cells = planes * rows_y
    slab = rows_z // blocks
    volume = 1.0 / (cells * doms * rows_z)
    f32 = jnp.float32
    shape = lambda *dims: jax.ShapeDtypeStruct(dims, f32)
    piece, edge = shape(slab, nb, cells), shape(WIDTH, nb, cells)

    flat = orbitals.reshape(nb, cells, rows_z)
    *pieces, v_slab = pl.pallas_call(
        functools.partial(pack_kernel, blocks),
        out_shape=[piece] * blocks + [shape(slab, cells)],
        in_specs=[VMEM, VMEM],
        out_specs=[VMEM] * (blocks + 1),
        scratch_shapes=[pltpu.VMEM((rows_z * nb, cells), f32), pltpu.VMEM((rows_z, cells), f32)],
        compiler_params=params(),
        name="pack",
    )(flat, potential.reshape(cells, rows_z))

    spread = [pieces[0]] + [None] * (blocks - 1)
    for k in sorted(range(1, blocks), key=lambda k: (-(k >= blocks // 2), k)):
        spread[k] = swap(pieces[k], "orb", k)

    active, low, high = pl.pallas_call(
        functools.partial(pick_kernel, blocks),
        out_shape=(piece, edge, edge),
        in_specs=[SMEM] + [VMEM] * blocks,
        out_specs=(VMEM, VMEM, VMEM),
        compiler_params=params(),
        name="pick",
    )(block, *spread)

    up = lambda count: [(i, (i + 1) % count) for i in range(count)]
    down = lambda count: [(i, (i - 1) % count) for i in range(count)]
    x_before = lax.ppermute(active, "dom", up(doms))
    x_after = lax.ppermute(active, "dom", down(doms))
    z_before = lax.ppermute(high, "orb", up(blocks))
    z_after = lax.ppermute(low, "orb", down(blocks))

    weights = jnp.asarray(plane_weights(planes, rows_y))
    applied, part = pl.pallas_call(
        functools.partial(project_kernel, blocks, volume),
        out_shape=(piece, shape(nb, blocks * nb)),
        in_specs=[VMEM] * (blocks + 7),
        out_specs=(VMEM, VMEM),
        compiler_params=params(),
        name="project",
    )(*spread, active, z_before, z_after, x_before, x_after, v_slab, weights)

    mine = (lax.axis_index("orb") == owner[0]) & (lax.axis_index("dom") == 0)
    summed = total_over_all(jnp.concatenate([part, jnp.where(mine, rotation, 0.0)], axis=0))
    proj, panel = summed[:nb], summed[nb:]

    own = pl.pallas_call(
        functools.partial(remove_kernel, blocks),
        out_shape=piece,
        in_specs=[VMEM] * (blocks + 2),
        out_specs=VMEM,
        compiler_params=params(),
        name="remove",
    )(*spread, applied, proj)

    gathered = [own] + [None] * (blocks - 1)
    for k in range(2, blocks, 2):
        gathered[k] = swap(own, "orb", k)
    for k in range(0, blocks, 2):
        gathered[k + 1] = swap(gathered[k], "orb", 1)

    gradient, updated = pl.pallas_call(
        functools.partial(update_kernel, blocks),
        out_shape=(shape(nb, cells, rows_z), shape(nb, cells, rows_z)),
        in_specs=[SMEM, VMEM] + [VMEM] * blocks,
        out_specs=(VMEM, VMEM),
        scratch_shapes=[pltpu.VMEM((rows_z * nb, cells), f32)],
        compiler_params=params(),
        name="update",
    )(panel, flat, *gathered)
    return gradient.reshape(orbitals.shape), updated.reshape(orbitals.shape)


def solution(mesh):
    in_specs = (P("orb", "dom", None, None), P("dom", None, None), P("orb", None), P(), P())
    out_specs = (P(None, "dom", None, None), P("orb", "dom", None, None))
    return jax.shard_map(
        per_device, mesh=mesh, in_specs=in_specs, out_specs=out_specs, check_vma=False
    )
```

```python
import functools

import jax
import jax.numpy as jnp
import numpy as np
from jax import lax
from jax.experimental import pallas as pl
from jax.experimental.pallas import tpu as pltpu
from jax.sharding import PartitionSpec as P

CENTER = -5369.0 / 1800.0
SIDES = (12.0 / 7.0, -15.0 / 56.0, 10.0 / 189.0, -1.0 / 112.0, 2.0 / 1925.0, -1.0 / 16632.0)
WIDTH = 6
CHUNKS = 4
BF16 = jnp.bfloat16
VMEM = pl.BlockSpec(memory_space=pltpu.VMEM)
HBM = pl.BlockSpec(memory_space=pltpu.HBM)
SMEM = pl.BlockSpec(memory_space=pltpu.SMEM)
HIGHEST = lax.Precision.HIGHEST


def params():
    return pltpu.CompilerParams(vmem_limit_bytes=32 * 1024 * 1024)


def plane_weights(planes, rows_y):
    cells = planes * rows_y
    table = np.zeros((3 * cells, cells), np.float64)
    for x in range(planes):
        for y in range(rows_y):
            out = x * rows_y + y
            for k, weight in enumerate(SIDES, 1):
                for step in (k, -k):
                    table[cells + x * rows_y + (y + step) % rows_y, out] += weight
                    table[cells + (x + step) * rows_y + y, out] += weight
    table = -0.5 * table
    high = table.astype(BF16)
    return high, (table - high.astype(np.float64)).astype(BF16)


def split(value):
    high = value.astype(BF16)
    return high, (value - high.astype(jnp.float32)).astype(BF16)


def dot3(left, right, contract):
    dot = lambda x, y: lax.dot_general(x, y, (contract, ((), ())), preferred_element_type=jnp.float32)
    return dot(left[0], right[0]) + (dot(left[0], right[1]) + dot(left[1], right[0]))


def pack_kernel(blocks, x_hbm, *refs):
    t_refs, (x_ref, turned, sems) = refs[:blocks], refs[blocks:]
    count, _, rows_z = x_ref.shape
    chunks = sems.shape[0]
    per = count // chunks
    copies = [
        pltpu.make_async_copy(x_hbm.at[pl.ds(i * per, per)], x_ref.at[pl.ds(i * per, per)], sems.at[i])
        for i in range(chunks)
    ]
    for copy in copies:
        copy.start()
    for i, copy in enumerate(copies):
        copy.wait()
        for a in range(i * per, (i + 1) * per):
            turned[pl.ds(a, rows_z, stride=count), :] = x_ref[a].T
    rank = lax.axis_index("orb")
    rows = rows_z // blocks * count
    for k in range(blocks):
        start = pl.multiple_of((rank ^ k) * rows, rows)
        t_refs[k][...] = turned[pl.ds(start, rows), :].reshape(t_refs[k].shape)


def pick_kernel(blocks, block_ref, *refs):
    x_refs, (act_ref, low_ref, high_ref) = refs[:blocks], refs[blocks:]
    slab = act_ref.shape[0]
    wanted = lax.axis_index("orb") ^ block_ref[0]
    for k in range(blocks):
        @pl.when(wanted == k)
        def _(k=k):
            act_ref[...] = x_refs[k][...]
            low_ref[...] = x_refs[k][:WIDTH]
            high_ref[...] = x_refs[k][slab - WIDTH :]


def split_kernel(blocks, *refs):
    x_refs, (high_ref, low_ref) = refs[:blocks], refs[blocks:]
    slab, nb, cells = x_refs[0].shape
    for k in range(blocks):
        for z in range(slab):
            high, low = split(x_refs[k][z])
            high_ref[k * nb : (k + 1) * nb, z * cells : (z + 1) * cells] = high
            low_ref[k * nb : (k + 1) * nb, z * cells : (z + 1) * cells] = low


def reorder(value, nb):
    wide = value.shape[1]
    row = lax.broadcasted_iota(jnp.int32, (wide, wide), 0)
    col = lax.broadcasted_iota(jnp.int32, (wide, wide), 1)
    exchange = jnp.where(row == (col ^ (lax.axis_index("orb") * nb)), 1.0, 0.0)
    return jnp.dot(value, exchange, precision=HIGHEST, preferred_element_type=jnp.float32)


def project_kernel(
    blocks, volume, xh_ref, xl_ref, act_ref, zb_ref, za_ref, xb_ref, xa_ref, v_ref, wh_ref, wl_ref, a_ref, p_ref, turned
):
    slab, nb, cells = act_ref.shape
    turned[...] = v_ref[...].T
    mine = pl.ds(pl.multiple_of(lax.axis_index("orb") * slab, slab), slab)
    act = act_ref[...]
    wide = jnp.concatenate([xb_ref[...], act, xa_ref[...]], axis=2).reshape(slab * nb, 3 * cells)
    applied = dot3(split(wide), (wh_ref[...], wl_ref[...]), ((1,), (0,))).reshape(slab, nb, cells)
    applied = applied + (turned[mine, :][:, None, :] - 1.5 * CENTER) * act
    tall = jnp.concatenate([zb_ref[...], act, za_ref[...]], axis=0)
    for k, weight in enumerate(SIDES, 1):
        upper = tall[WIDTH + k : WIDTH + k + slab]
        lower = tall[WIDTH - k : WIDTH - k + slab]
        applied = applied + (-0.5 * weight) * (upper + lower)
    a_ref[...] = applied
    flat = jnp.concatenate([applied[z] for z in range(slab)], axis=1)
    total = dot3(split(flat), (xh_ref[...], xl_ref[...]), ((1,), (1,)))
    p_ref[...] = reorder(total * volume, nb)


def remove_kernel(xh_ref, xl_ref, a_ref, p_ref, g_ref):
    slab, nb, cells = a_ref.shape
    proj = split(reorder(p_ref[...], nb))
    removed = dot3(proj, (xh_ref[...], xl_ref[...]), ((1,), (0,)))
    for z in range(slab):
        g_ref[z] = a_ref[z] - removed[:, z * cells : (z + 1) * cells]


def update_kernel(blocks, panel_ref, x_ref, *refs):
    g_refs, (grad_hbm, out_hbm, whole, grad, out, sems) = refs[:blocks], refs[blocks:]
    nb, cells, rows_z = x_ref.shape
    rank = lax.axis_index("orb")
    share = rows_z // blocks * nb
    for k in range(blocks):
        at = pl.ds(pl.multiple_of((rank ^ k) * share, share), share)
        whole[at, :] = g_refs[k][...].reshape(share, cells)
    chunks = sems.shape[1]
    per = nb // chunks
    rows = 32
    copies = []
    for i in range(chunks):
        for c in range(i * per, (i + 1) * per):
            grad[c] = whole[pl.ds(c, rows_z, stride=nb), :].T
        part = pl.ds(i * per, per)
        copies.append(pltpu.make_async_copy(grad.at[part], grad_hbm.at[part], sems.at[0, i]))
        copies[-1].start()
    for i in range(chunks):
        group = range(i * per, (i + 1) * per)

        @pl.loop(0, cells // rows)
        def _(step, group=group):
            at = pl.ds(pl.multiple_of(step * rows, rows), rows)
            totals = [x_ref[a, at] for a in group]
            for c in range(nb):
                value = grad[c, at]
                totals = [total + panel_ref[c, rank * nb + a] * value for a, total in zip(group, totals)]
            for a, total in zip(group, totals):
                out[a, at] = total

        part = pl.ds(i * per, per)
        copies.append(pltpu.make_async_copy(out.at[part], out_hbm.at[part], sems.at[1, i]))
        copies[-1].start()
    for copy in copies:
        copy.wait()


def swap(value, axis, k):
    count = lax.axis_size(axis)
    return lax.ppermute(value, axis, [(i, i ^ k) for i in range(count)])


def total_over_all(value):
    for axis in ("orb", "dom"):
        for bit in range((lax.axis_size(axis) - 1).bit_length()):
            value = value + swap(value, axis, 1 << bit)
    return value


def per_device(orbitals, potential, rotation, block, owner):
    nb, planes, rows_y, rows_z = orbitals.shape
    blocks, doms = lax.axis_size("orb"), lax.axis_size("dom")
    cells = planes * rows_y
    slab = rows_z // blocks
    volume = 1.0 / (cells * doms * rows_z)
    f32 = jnp.float32
    shape = lambda *dims: jax.ShapeDtypeStruct(dims, f32)
    piece, edge = shape(slab, nb, cells), shape(WIDTH, nb, cells)

    flat = orbitals.reshape(nb, cells, rows_z)
    pieces = pl.pallas_call(
        functools.partial(pack_kernel, blocks),
        out_shape=[piece] * blocks,
        in_specs=[HBM],
        out_specs=[VMEM] * blocks,
        scratch_shapes=[
            pltpu.VMEM((nb, cells, rows_z), f32),
            pltpu.VMEM((rows_z * nb, cells), f32),
            pltpu.SemaphoreType.DMA((CHUNKS,)),
        ],
        compiler_params=params(),
        name="pack",
    )(flat)

    spread = [pieces[0]] + [None] * (blocks - 1)
    for k in sorted(range(1, blocks), key=lambda k: (-(k >= blocks // 2), k)):
        spread[k] = swap(pieces[k], "orb", k)

    active, low, high = pl.pallas_call(
        functools.partial(pick_kernel, blocks),
        out_shape=(piece, edge, edge),
        in_specs=[SMEM] + [VMEM] * blocks,
        out_specs=(VMEM, VMEM, VMEM),
        compiler_params=params(),
        name="pick",
    )(block, *spread)

    up = lambda count: [(i, (i + 1) % count) for i in range(count)]
    down = lambda count: [(i, (i - 1) % count) for i in range(count)]
    x_before = lax.ppermute(active, "dom", up(doms))
    x_after = lax.ppermute(active, "dom", down(doms))
    z_before = lax.ppermute(high, "orb", up(blocks))
    z_after = lax.ppermute(low, "orb", down(blocks))

    halves = jax.ShapeDtypeStruct((blocks * nb, slab * cells), BF16)
    parts = pl.pallas_call(
        functools.partial(split_kernel, blocks),
        out_shape=(halves, halves),
        in_specs=[VMEM] * blocks,
        out_specs=(VMEM, VMEM),
        compiler_params=params(),
        cost_estimate=pl.CostEstimate(flops=3 * blocks * nb * slab * cells, bytes_accessed=0, transcendentals=0),
        name="split",
    )(*spread)

    weights = [jnp.asarray(w) for w in plane_weights(planes, rows_y)]
    applied, part = pl.pallas_call(
        functools.partial(project_kernel, blocks, volume),
        out_shape=(piece, shape(nb, blocks * nb)),
        in_specs=[VMEM] * 10,
        out_specs=(VMEM, VMEM),
        scratch_shapes=[pltpu.VMEM((rows_z, cells), f32)],
        compiler_params=params(),
        name="project",
    )(*parts, active, z_before, z_after, x_before, x_after, potential.reshape(cells, rows_z), *weights)

    mine = (lax.axis_index("orb") == owner[0]) & (lax.axis_index("dom") == 0)
    summed = total_over_all(jnp.concatenate([part, jnp.where(mine, rotation, 0.0)], axis=0))
    proj, panel = summed[:nb], summed[nb:]

    own = pl.pallas_call(
        remove_kernel,
        out_shape=piece,
        in_specs=[VMEM] * 4,
        out_specs=VMEM,
        compiler_params=params(),
        name="remove",
    )(*parts, applied, proj)

    gathered = [own] + [None] * (blocks - 1)
    for k in range(2, blocks, 2):
        gathered[k] = swap(own, "orb", k)
    for k in range(0, blocks, 2):
        gathered[k + 1] = swap(gathered[k], "orb", 1)

    gradient, updated = pl.pallas_call(
        functools.partial(update_kernel, blocks),
        out_shape=(shape(nb, cells, rows_z), shape(nb, cells, rows_z)),
        in_specs=[SMEM, VMEM] + [VMEM] * blocks,
        out_specs=(HBM, HBM),
        scratch_shapes=[
            pltpu.VMEM((rows_z * nb, cells), f32),
            pltpu.VMEM((nb, cells, rows_z), f32),
            pltpu.VMEM((nb, cells, rows_z), f32),
            pltpu.SemaphoreType.DMA((2, CHUNKS)),
        ],
        compiler_params=params(),
        name="update",
    )(panel, flat, *gathered)
    return gradient.reshape(orbitals.shape), updated.reshape(orbitals.shape)


def solution(mesh):
    in_specs = (P("orb", "dom", None, None), P("dom", None, None), P("orb", None), P(), P())
    out_specs = (P(None, "dom", None, None), P("orb", "dom", None, None))
    return jax.shard_map(
        per_device, mesh=mesh, in_specs=in_specs, out_specs=out_specs, check_vma=False
    )
```

```python
import functools

import jax
import jax.numpy as jnp
import numpy as np
from jax import lax
from jax.experimental import pallas as pl
from jax.experimental.pallas import tpu as pltpu
from jax.sharding import PartitionSpec as P

CENTER = -5369.0 / 1800.0
SIDES = (12.0 / 7.0, -15.0 / 56.0, 10.0 / 189.0, -1.0 / 112.0, 2.0 / 1925.0, -1.0 / 16632.0)
WIDTH = 6
CHUNKS = 4
BF16 = jnp.bfloat16
VMEM = pl.BlockSpec(memory_space=pltpu.VMEM)
HBM = pl.BlockSpec(memory_space=pltpu.HBM)
SMEM = pl.BlockSpec(memory_space=pltpu.SMEM)
HIGHEST = lax.Precision.HIGHEST


def params():
    return pltpu.CompilerParams(vmem_limit_bytes=32 * 1024 * 1024)


def plane_weights(planes, rows_y):
    cells = planes * rows_y
    table = np.zeros((3 * cells, cells), np.float64)
    skipped = (planes - WIDTH) * rows_y
    for x in range(planes):
        for y in range(rows_y):
            out = x * rows_y + y
            for k, weight in enumerate(SIDES, 1):
                for step in (k, -k):
                    table[cells + x * rows_y + (y + step) % rows_y, out] += weight
                    row = cells + (x + step) * rows_y + y
                    table[row - skipped if row < cells else row, out] += weight
    table = -0.5 * table
    high = table.astype(BF16)
    return high, (table - high.astype(np.float64)).astype(BF16)


def split(value):
    high = value.astype(BF16)
    return high, (value - high.astype(jnp.float32)).astype(BF16)


def dot3(left, right, contract):
    dot = lambda x, y: lax.dot_general(x, y, (contract, ((), ())), preferred_element_type=jnp.float32)
    return dot(left[0], right[0]) + (dot(left[0], right[1]) + dot(left[1], right[0]))


def pack_kernel(blocks, wanted, x_hbm, *refs):
    t_refs, (x_ref, turned, sems) = refs[: len(wanted)], refs[len(wanted) :]
    count, _, rows_z = x_ref.shape
    chunks = sems.shape[0]
    per = count // chunks
    copies = [
        pltpu.make_async_copy(x_hbm.at[pl.ds(i * per, per)], x_ref.at[pl.ds(i * per, per)], sems.at[i])
        for i in range(chunks)
    ]
    for copy in copies:
        copy.start()
    for i, copy in enumerate(copies):
        copy.wait()
        for a in range(i * per, (i + 1) * per):
            turned[pl.ds(a, rows_z, stride=count), :] = x_ref[a].T
    rank = lax.axis_index("orb")
    rows = rows_z // blocks * count
    for m, t_ref in zip(wanted, t_refs):
        for core in range(2):
            start = pl.multiple_of((rank ^ (2 * m + core)) * rows, rows)
            t_ref[core] = turned[pl.ds(start, rows), :].reshape(t_ref.shape[1:])


def by_block(refs):
    half = len(refs) // 2
    return [refs[half + k // 2] if k % 2 else refs[k // 2].at[0] for k in range(2 * half)]


def squeeze(value):
    rows, wide = value.shape
    quarter, free = rows // 4, wide // 4
    lane = lax.broadcasted_iota(jnp.int32, (quarter, wide), 1)
    rest = value[3 * quarter :]
    parts = []
    for j in range(3):
        moved = pltpu.roll(rest, (3 - j) * free, 1)
        parts.append(jnp.where(lane < 3 * free, value[j * quarter : (j + 1) * quarter], moved))
    return jnp.concatenate(parts, axis=0)


def expand(value):
    rows, wide = value.shape
    quarter, free = rows // 3, wide // 4
    lane = lax.broadcasted_iota(jnp.int32, (quarter, wide), 1)
    rest = value[:quarter]
    for j in range(3):
        moved = pltpu.roll(value[j * quarter : (j + 1) * quarter], (j + 1) * free, 1)
        rest = jnp.where((lane >= j * free) & (lane < (j + 1) * free), moved, rest)
    return jnp.concatenate([value, rest], axis=0)


def pick_kernel(blocks, block_ref, *refs):
    x_refs, (act_ref, low_ref, high_ref, first_ref, last_ref) = by_block(refs[:blocks]), refs[blocks:]
    slab, nb, cells = act_ref.shape
    wanted = lax.axis_index("orb") ^ block_ref[0]
    for k in range(blocks):
        @pl.when(wanted == k)
        def _(k=k):
            act_ref[...] = x_refs[k][...]
    low_ref[...] = act_ref[:WIDTH]
    high_ref[...] = act_ref[slab - WIDTH :]
    flat = act_ref[...].reshape(slab * nb, cells)
    first_ref[...] = squeeze(flat)
    last_ref[...] = squeeze(pltpu.roll(flat, 3 * (cells // 4), 1))


def split_kernel(blocks, *refs):
    x_refs, (high_ref, low_ref) = by_block(refs[:blocks]), refs[blocks:]
    slab, nb, cells = x_refs[0].shape
    for k in range(blocks):
        for z in range(slab):
            high, low = split(x_refs[k][z])
            high_ref[k * nb : (k + 1) * nb, z * cells : (z + 1) * cells] = high
            low_ref[k * nb : (k + 1) * nb, z * cells : (z + 1) * cells] = low


def reorder(value, nb):
    wide = value.shape[1]
    row = lax.broadcasted_iota(jnp.int32, (wide, wide), 0)
    col = lax.broadcasted_iota(jnp.int32, (wide, wide), 1)
    exchange = jnp.where(row == (col ^ (lax.axis_index("orb") * nb)), 1.0, 0.0)
    return jnp.dot(value, exchange, precision=HIGHEST, preferred_element_type=jnp.float32)


def project_kernel(
    blocks, volume, xh_ref, xl_ref, act_ref, zb_ref, za_ref, xb_ref, xa_ref, v_ref, wh_ref, wl_ref, a_ref, p_ref, turned
):
    slab, nb, cells = act_ref.shape
    turned[...] = v_ref[...].T
    mine = pl.ds(pl.multiple_of(lax.axis_index("orb") * slab, slab), slab)
    act = act_ref[...]
    wide = jnp.concatenate([expand(xb_ref[...]), act.reshape(slab * nb, cells), expand(xa_ref[...])], axis=1)
    applied = dot3(split(wide), (wh_ref[...], wl_ref[...]), ((1,), (0,))).reshape(slab, nb, cells)
    applied = applied + (turned[mine, :][:, None, :] - 1.5 * CENTER) * act
    tall = jnp.concatenate([zb_ref[...], act, za_ref[...]], axis=0)
    for k, weight in enumerate(SIDES, 1):
        upper = tall[WIDTH + k : WIDTH + k + slab]
        lower = tall[WIDTH - k : WIDTH - k + slab]
        applied = applied + (-0.5 * weight) * (upper + lower)
    a_ref[...] = applied
    flat = jnp.concatenate([applied[z] for z in range(slab)], axis=1)
    total = dot3(split(flat), (xh_ref[...], xl_ref[...]), ((1,), (1,)))
    p_ref[...] = reorder(total * volume, nb)


def remove_kernel(xh_ref, xl_ref, a_ref, p_ref, g_ref):
    slab, nb, cells = a_ref.shape
    proj = split(reorder(p_ref[...], nb))
    removed = dot3(proj, (xh_ref[...], xl_ref[...]), ((1,), (0,)))
    for z in range(slab):
        g_ref[z] = a_ref[z] - removed[:, z * cells : (z + 1) * cells]


def update_kernel(blocks, panel_ref, x_ref, *refs):
    g_refs, (grad_hbm, out_hbm, whole, grad, out, sems) = refs[:blocks], refs[blocks:]
    nb, cells, rows_z = x_ref.shape
    rank = lax.axis_index("orb")
    share = rows_z // blocks * nb
    for k in range(blocks):
        at = pl.ds(pl.multiple_of((rank ^ k) * share, share), share)
        whole[at, :] = g_refs[k][...].reshape(share, cells)
    chunks = sems.shape[1]
    per = nb // chunks
    rows = 32
    copies = []
    for i in range(chunks):
        for c in range(i * per, (i + 1) * per):
            grad[c] = whole[pl.ds(c, rows_z, stride=nb), :].T
        part = pl.ds(i * per, per)
        copies.append(pltpu.make_async_copy(grad.at[part], grad_hbm.at[part], sems.at[0, i]))
        copies[-1].start()
    for i in range(chunks):
        group = range(i * per, (i + 1) * per)

        @pl.loop(0, cells // rows)
        def _(step, group=group):
            at = pl.ds(pl.multiple_of(step * rows, rows), rows)
            totals = [x_ref[a, at] for a in group]
            for c in range(nb):
                value = grad[c, at]
                totals = [total + panel_ref[c, rank * nb + a] * value for a, total in zip(group, totals)]
            for a, total in zip(group, totals):
                out[a, at] = total

        part = pl.ds(i * per, per)
        copies.append(pltpu.make_async_copy(out.at[part], out_hbm.at[part], sems.at[1, i]))
        copies[-1].start()
    for copy in copies:
        copy.wait()


def swap(value, axis, k):
    count = lax.axis_size(axis)
    return lax.ppermute(value, axis, [(i, i ^ k) for i in range(count)])


def total_over_all(value):
    doms, blocks = lax.axis_size("dom"), lax.axis_size("orb")
    for axis, steps in (("dom", range(1, doms)), ("orb", range(2, blocks, 2)), ("orb", (1,))):
        value = sum([swap(value, axis, k) for k in steps], value)
    return value


def per_device(orbitals, potential, rotation, block, owner):
    nb, planes, rows_y, rows_z = orbitals.shape
    blocks, doms = lax.axis_size("orb"), lax.axis_size("dom")
    cells = planes * rows_y
    slab = rows_z // blocks
    volume = 1.0 / (cells * doms * rows_z)
    f32 = jnp.float32
    shape = lambda *dims: jax.ShapeDtypeStruct(dims, f32)
    piece, edge = shape(slab, nb, cells), shape(WIDTH, nb, cells)

    flat = orbitals.reshape(nb, cells, rows_z)
    chips = blocks // 2
    arrived = [None] * chips
    for wanted in (range(chips // 2, chips), range(chips // 2)):
        packed = pl.pallas_call(
            functools.partial(pack_kernel, blocks, wanted),
            out_shape=[shape(2, slab, nb, cells)] * len(wanted),
            in_specs=[HBM],
            out_specs=[VMEM] * len(wanted),
            scratch_shapes=[
                pltpu.VMEM((nb, cells, rows_z), f32),
                pltpu.VMEM((rows_z * nb, cells), f32),
                pltpu.SemaphoreType.DMA((CHUNKS,)),
            ],
            compiler_params=params(),
            cost_estimate=pl.CostEstimate(flops=0, bytes_accessed=8 * nb * cells * rows_z, transcendentals=0),
            name="pack",
        )(flat)
        for m, value in zip(wanted, packed):
            arrived[m] = swap(value, "orb", 2 * m) if m else value
    spread = arrived + [swap(value[1], "orb", 1) for value in arrived]

    side = shape(3 * slab * nb // 4, cells)
    active, low, high, first, last = pl.pallas_call(
        functools.partial(pick_kernel, blocks),
        out_shape=(piece, edge, edge, side, side),
        in_specs=[SMEM] + [VMEM] * blocks,
        out_specs=[VMEM] * 5,
        compiler_params=params(),
        name="pick",
    )(block, *spread)

    up = lambda count: [(i, (i + 1) % count) for i in range(count)]
    down = lambda count: [(i, (i - 1) % count) for i in range(count)]
    x_before = lax.ppermute(last, "dom", up(doms))
    x_after = lax.ppermute(first, "dom", down(doms))
    z_before = lax.ppermute(high, "orb", up(blocks))
    z_after = lax.ppermute(low, "orb", down(blocks))

    halves = jax.ShapeDtypeStruct((blocks * nb, slab * cells), BF16)
    parts = pl.pallas_call(
        functools.partial(split_kernel, blocks),
        out_shape=(halves, halves),
        in_specs=[VMEM] * blocks,
        out_specs=(VMEM, VMEM),
        compiler_params=params(),
        cost_estimate=pl.CostEstimate(flops=3 * blocks * nb * slab * cells, bytes_accessed=0, transcendentals=0),
        name="split",
    )(*spread)

    weights = [jnp.asarray(w) for w in plane_weights(planes, rows_y)]
    applied, part = pl.pallas_call(
        functools.partial(project_kernel, blocks, volume),
        out_shape=(piece, shape(nb, blocks * nb)),
        in_specs=[VMEM] * 10,
        out_specs=(VMEM, VMEM),
        scratch_shapes=[pltpu.VMEM((rows_z, cells), f32)],
        compiler_params=params(),
        name="project",
    )(*parts, active, z_before, z_after, x_before, x_after, potential.reshape(cells, rows_z), *weights)

    mine = (lax.axis_index("orb") == owner[0]) & (lax.axis_index("dom") == 0)
    summed = total_over_all(jnp.concatenate([part, jnp.where(mine, rotation, 0.0)], axis=0))
    proj, panel = summed[:nb], summed[nb:]

    own = pl.pallas_call(
        remove_kernel,
        out_shape=piece,
        in_specs=[VMEM] * 4,
        out_specs=VMEM,
        compiler_params=params(),
        name="remove",
    )(*parts, applied, proj)

    gathered = [own] + [None] * (blocks - 1)
    for k in range(2, blocks, 2):
        gathered[k] = swap(own, "orb", k)
    for k in range(0, blocks, 2):
        gathered[k + 1] = swap(gathered[k], "orb", 1)

    gradient, updated = pl.pallas_call(
        functools.partial(update_kernel, blocks),
        out_shape=(shape(nb, cells, rows_z), shape(nb, cells, rows_z)),
        in_specs=[SMEM, VMEM] + [VMEM] * blocks,
        out_specs=(HBM, HBM),
        scratch_shapes=[
            pltpu.VMEM((rows_z * nb, cells), f32),
            pltpu.VMEM((nb, cells, rows_z), f32),
            pltpu.VMEM((nb, cells, rows_z), f32),
            pltpu.SemaphoreType.DMA((2, CHUNKS)),
        ],
        compiler_params=params(),
        name="update",
    )(panel, flat, *gathered)
    return gradient.reshape(orbitals.shape), updated.reshape(orbitals.shape)


def solution(mesh):
    in_specs = (P("orb", "dom", None, None), P("dom", None, None), P("orb", None), P(), P())
    out_specs = (P(None, "dom", None, None), P("orb", "dom", None, None))
    return jax.shard_map(
        per_device, mesh=mesh, in_specs=in_specs, out_specs=out_specs, check_vma=False
    )
```

```python
import functools

import jax
import jax.numpy as jnp
import numpy as np
from jax import lax
from jax.experimental import pallas as pl
from jax.experimental.pallas import tpu as pltpu
from jax.sharding import PartitionSpec as P

CENTER = -5369.0 / 1800.0
SIDES = (12.0 / 7.0, -15.0 / 56.0, 10.0 / 189.0, -1.0 / 112.0, 2.0 / 1925.0, -1.0 / 16632.0)
WIDTH = 6
CHUNKS = 4
BF16 = jnp.bfloat16
VMEM = pl.BlockSpec(memory_space=pltpu.VMEM)
HBM = pl.BlockSpec(memory_space=pltpu.HBM)
SMEM = pl.BlockSpec(memory_space=pltpu.SMEM)
HIGHEST = lax.Precision.HIGHEST


def params():
    return pltpu.CompilerParams(vmem_limit_bytes=32 * 1024 * 1024)


def plane_weights(planes, rows_y):
    cells = planes * rows_y
    table = np.zeros((3 * cells, cells), np.float64)
    skipped = (planes - WIDTH) * rows_y
    for x in range(planes):
        for y in range(rows_y):
            out = x * rows_y + y
            for k, weight in enumerate(SIDES, 1):
                for step in (k, -k):
                    table[cells + x * rows_y + (y + step) % rows_y, out] += weight
                    row = cells + (x + step) * rows_y + y
                    table[row - skipped if row < cells else row, out] += weight
    table = -0.5 * table
    high = table.astype(BF16)
    return high, (table - high.astype(np.float64)).astype(BF16)


def split(value):
    high = value.astype(BF16)
    return high, (value - high.astype(jnp.float32)).astype(BF16)


def dot3(left, right, contract):
    dot = lambda x, y: lax.dot_general(x, y, (contract, ((), ())), preferred_element_type=jnp.float32)
    return dot(left[0], right[0]) + (dot(left[0], right[1]) + dot(left[1], right[0]))


def pack_kernel(blocks, wanted, x_hbm, *refs):
    t_refs, (x_ref, turned, sems) = refs[: len(wanted)], refs[len(wanted) :]
    count, _, rows_z = x_ref.shape
    chunks = sems.shape[0]
    per = count // chunks
    copies = [
        pltpu.make_async_copy(x_hbm.at[pl.ds(i * per, per)], x_ref.at[pl.ds(i * per, per)], sems.at[i])
        for i in range(chunks)
    ]
    for copy in copies:
        copy.start()
    for i, copy in enumerate(copies):
        copy.wait()
        for a in range(i * per, (i + 1) * per):
            turned[pl.ds(a, rows_z, stride=count), :] = x_ref[a].T
    rank = lax.axis_index("orb")
    rows = rows_z // blocks * count
    for m, t_ref in zip(wanted, t_refs):
        for core in range(2):
            start = pl.multiple_of((rank ^ (2 * m + core)) * rows, rows)
            t_ref[core] = turned[pl.ds(start, rows), :].reshape(t_ref.shape[1:])


def by_block(refs):
    half = len(refs) // 2
    return [refs[half + k // 2] if k % 2 else refs[k // 2].at[0] for k in range(2 * half)]


def squeeze(value):
    rows, wide = value.shape
    quarter, free = rows // 4, wide // 4
    lane = lax.broadcasted_iota(jnp.int32, (quarter, wide), 1)
    rest = value[3 * quarter :]
    parts = []
    for j in range(3):
        moved = pltpu.roll(rest, (3 - j) * free, 1)
        parts.append(jnp.where(lane < 3 * free, value[j * quarter : (j + 1) * quarter], moved))
    return jnp.concatenate(parts, axis=0)


def expand(value):
    rows, wide = value.shape
    quarter, free = rows // 3, wide // 4
    lane = lax.broadcasted_iota(jnp.int32, (quarter, wide), 1)
    rest = value[:quarter]
    for j in range(3):
        moved = pltpu.roll(value[j * quarter : (j + 1) * quarter], (j + 1) * free, 1)
        rest = jnp.where((lane >= j * free) & (lane < (j + 1) * free), moved, rest)
    return jnp.concatenate([value, rest], axis=0)


def pick_kernel(blocks, block_ref, *refs):
    x_refs, (act_ref, low_ref, high_ref, first_ref, last_ref) = by_block(refs[:blocks]), refs[blocks:]
    slab, nb, cells = act_ref.shape
    wanted = lax.axis_index("orb") ^ block_ref[0]
    for k in range(blocks):
        @pl.when(wanted == k)
        def _(k=k):
            act_ref[...] = x_refs[k][...]
    low_ref[...] = act_ref[:WIDTH]
    high_ref[...] = act_ref[slab - WIDTH :]
    flat = act_ref[...].reshape(slab * nb, cells)
    first_ref[...] = squeeze(flat)
    last_ref[...] = squeeze(pltpu.roll(flat, 3 * (cells // 4), 1))


def split_kernel(blocks, *refs):
    x_refs, (high_ref, low_ref) = by_block(refs[:blocks]), refs[blocks:]
    slab, nb, cells = x_refs[0].shape
    for k in range(blocks):
        for z in range(slab):
            high, low = split(x_refs[k][z])
            high_ref[k * nb : (k + 1) * nb, z * cells : (z + 1) * cells] = high
            low_ref[k * nb : (k + 1) * nb, z * cells : (z + 1) * cells] = low


def reorder(value, nb):
    wide = value.shape[1]
    row = lax.broadcasted_iota(jnp.int32, (wide, wide), 0)
    col = lax.broadcasted_iota(jnp.int32, (wide, wide), 1)
    exchange = jnp.where(row == (col ^ (lax.axis_index("orb") * nb)), 1.0, 0.0)
    return jnp.dot(value, exchange, precision=HIGHEST, preferred_element_type=jnp.float32)


def project_kernel(
    blocks, volume, xh_ref, xl_ref, act_ref, zb_ref, za_ref, xb_ref, xa_ref, v_ref, wh_ref, wl_ref, a_ref, p_ref, turned
):
    slab, nb, cells = act_ref.shape
    turned[...] = v_ref[...].T
    mine = pl.ds(pl.multiple_of(lax.axis_index("orb") * slab, slab), slab)
    act = act_ref[...]
    wide = jnp.concatenate([expand(xb_ref[...]), act.reshape(slab * nb, cells), expand(xa_ref[...])], axis=1)
    applied = dot3(split(wide), (wh_ref[...], wl_ref[...]), ((1,), (0,))).reshape(slab, nb, cells)
    applied = applied + (turned[mine, :][:, None, :] - 1.5 * CENTER) * act
    tall = jnp.concatenate([zb_ref[...], act, za_ref[...]], axis=0)
    for k, weight in enumerate(SIDES, 1):
        upper = tall[WIDTH + k : WIDTH + k + slab]
        lower = tall[WIDTH - k : WIDTH - k + slab]
        applied = applied + (-0.5 * weight) * (upper + lower)
    a_ref[...] = applied
    flat = jnp.concatenate([applied[z] for z in range(slab)], axis=1)
    total = dot3(split(flat), (xh_ref[...], xl_ref[...]), ((1,), (1,)))
    p_ref[...] = reorder(total * volume, nb)


def remove_kernel(xh_ref, xl_ref, a_ref, p_ref, g_ref):
    slab, nb, cells = a_ref.shape
    proj = split(reorder(p_ref[...], nb))
    removed = dot3(proj, (xh_ref[...], xl_ref[...]), ((1,), (0,)))
    for z in range(slab):
        g_ref[z] = a_ref[z] - removed[:, z * cells : (z + 1) * cells]


def update_kernel(blocks, panel_ref, x_ref, *refs):
    g_refs, (grad_hbm, out_hbm, whole, grad, out, sems) = refs[:blocks], refs[blocks:]
    nb, cells, rows_z = x_ref.shape
    rank = lax.axis_index("orb")
    share = rows_z // blocks * nb
    for k in range(blocks):
        at = pl.ds(pl.multiple_of((rank ^ k) * share, share), share)
        whole[at, :] = g_refs[k][...].reshape(share, cells)
    chunks = sems.shape[1]
    per = nb // chunks
    rows = 32
    copies = []
    for i in range(chunks):
        for c in range(i * per, (i + 1) * per):
            grad[c] = whole[pl.ds(c, rows_z, stride=nb), :].T
        part = pl.ds(i * per, per)
        copies.append(pltpu.make_async_copy(grad.at[part], grad_hbm.at[part], sems.at[0, i]))
        copies[-1].start()
    for i in range(chunks):
        group = range(i * per, (i + 1) * per)

        @pl.loop(0, cells // rows)
        def _(step, group=group):
            at = pl.ds(pl.multiple_of(step * rows, rows), rows)
            totals = [x_ref[a, at] for a in group]
            for c in range(nb):
                value = grad[c, at]
                totals = [total + panel_ref[c, rank * nb + a] * value for a, total in zip(group, totals)]
            for a, total in zip(group, totals):
                out[a, at] = total

        part = pl.ds(i * per, per)
        copies.append(pltpu.make_async_copy(out.at[part], out_hbm.at[part], sems.at[1, i]))
        copies[-1].start()
    for copy in copies:
        copy.wait()


def swap(value, axis, k):
    count = lax.axis_size(axis)
    return lax.ppermute(value, axis, [(i, i ^ k) for i in range(count)])


def total_over_all(value):
    doms, blocks = lax.axis_size("dom"), lax.axis_size("orb")
    every = [(d, o) for d in range(doms) for o in range(1, blocks, 2)]
    index = lambda d, o: d * blocks + o
    move = lambda value, pairs: lax.ppermute(value, ("dom", "orb"), pairs)
    value = value + swap(value, "orb", 1)
    value = sum([move(value, [(index(d, o), index(d ^ k, o)) for d, o in every]) for k in range(1, doms)], value)
    value = sum([move(value, [(index(d, o), index(d, o ^ k)) for d, o in every]) for k in range(2, blocks, 2)], value)
    other = move(value, [(index(d, o), index(d, o ^ 1)) for d, o in every])
    return jnp.where(lax.axis_index("orb") % 2 == 1, value, other)


def per_device(orbitals, potential, rotation, block, owner):
    nb, planes, rows_y, rows_z = orbitals.shape
    blocks, doms = lax.axis_size("orb"), lax.axis_size("dom")
    cells = planes * rows_y
    slab = rows_z // blocks
    volume = 1.0 / (cells * doms * rows_z)
    f32 = jnp.float32
    shape = lambda *dims: jax.ShapeDtypeStruct(dims, f32)
    piece, edge = shape(slab, nb, cells), shape(WIDTH, nb, cells)

    flat = orbitals.reshape(nb, cells, rows_z)
    held = pltpu.with_memory_space_constraint(flat, pltpu.HBM)
    chips = blocks // 2
    arrived = [None] * chips
    for wanted in (range(chips // 2, chips), range(chips // 2)):
        packed = pl.pallas_call(
            functools.partial(pack_kernel, blocks, wanted),
            out_shape=[shape(2, slab, nb, cells)] * len(wanted),
            in_specs=[HBM],
            out_specs=[VMEM] * len(wanted),
            scratch_shapes=[
                pltpu.VMEM((nb, cells, rows_z), f32),
                pltpu.VMEM((rows_z * nb, cells), f32),
                pltpu.SemaphoreType.DMA((CHUNKS,)),
            ],
            compiler_params=params(),
            cost_estimate=pl.CostEstimate(flops=0, bytes_accessed=8 * nb * cells * rows_z, transcendentals=0),
            name="pack",
        )(held)
        for m, value in zip(wanted, packed):
            arrived[m] = swap(value, "orb", 2 * m) if m else value
    spread = arrived + [swap(value[1], "orb", 1) for value in arrived]

    side = shape(3 * slab * nb // 4, cells)
    active, low, high, first, last = pl.pallas_call(
        functools.partial(pick_kernel, blocks),
        out_shape=(piece, edge, edge, side, side),
        in_specs=[SMEM] + [VMEM] * blocks,
        out_specs=[VMEM] * 5,
        compiler_params=params(),
        name="pick",
    )(block, *spread)

    up = lambda count: [(i, (i + 1) % count) for i in range(count)]
    down = lambda count: [(i, (i - 1) % count) for i in range(count)]
    x_before = lax.ppermute(last, "dom", up(doms))
    x_after = lax.ppermute(first, "dom", down(doms))
    z_before = lax.ppermute(high, "orb", up(blocks))
    z_after = lax.ppermute(low, "orb", down(blocks))

    halves = jax.ShapeDtypeStruct((blocks * nb, slab * cells), BF16)
    parts = pl.pallas_call(
        functools.partial(split_kernel, blocks),
        out_shape=(halves, halves),
        in_specs=[VMEM] * blocks,
        out_specs=(VMEM, VMEM),
        compiler_params=params(),
        cost_estimate=pl.CostEstimate(flops=3 * blocks * nb * slab * cells, bytes_accessed=0, transcendentals=0),
        name="split",
    )(*spread)

    weights = [jnp.asarray(w) for w in plane_weights(planes, rows_y)]
    applied, part = pl.pallas_call(
        functools.partial(project_kernel, blocks, volume),
        out_shape=(piece, shape(nb, blocks * nb)),
        in_specs=[VMEM] * 10,
        out_specs=(VMEM, VMEM),
        scratch_shapes=[pltpu.VMEM((rows_z, cells), f32)],
        compiler_params=params(),
        name="project",
    )(*parts, active, z_before, z_after, x_before, x_after, potential.reshape(cells, rows_z), *weights)

    mine = (lax.axis_index("orb") == owner[0]) & (lax.axis_index("dom") == 0)
    summed = total_over_all(jnp.concatenate([part, jnp.where(mine, rotation, 0.0)], axis=0))
    proj, panel = summed[:nb], summed[nb:]

    own = pl.pallas_call(
        remove_kernel,
        out_shape=piece,
        in_specs=[VMEM] * 4,
        out_specs=VMEM,
        compiler_params=params(),
        name="remove",
    )(*parts, applied, proj)

    gathered = [own] + [None] * (blocks - 1)
    for k in range(2, blocks, 2):
        gathered[k] = swap(own, "orb", k)
    for k in range(0, blocks, 2):
        gathered[k + 1] = swap(gathered[k], "orb", 1)

    gradient, updated = pl.pallas_call(
        functools.partial(update_kernel, blocks),
        out_shape=(shape(nb, cells, rows_z), shape(nb, cells, rows_z)),
        in_specs=[SMEM, VMEM] + [VMEM] * blocks,
        out_specs=(HBM, HBM),
        scratch_shapes=[
            pltpu.VMEM((rows_z * nb, cells), f32),
            pltpu.VMEM((nb, cells, rows_z), f32),
            pltpu.VMEM((nb, cells, rows_z), f32),
            pltpu.SemaphoreType.DMA((2, CHUNKS)),
        ],
        compiler_params=params(),
        name="update",
    )(panel, flat, *gathered)
    return gradient.reshape(orbitals.shape), updated.reshape(orbitals.shape)


def solution(mesh):
    in_specs = (P("orb", "dom", None, None), P("dom", None, None), P("orb", None), P(), P())
    out_specs = (P(None, "dom", None, None), P("orb", "dom", None, None))
    return jax.shard_map(
        per_device, mesh=mesh, in_specs=in_specs, out_specs=out_specs, check_vma=False
    )
```

```python
import functools

import jax
import jax.numpy as jnp
import numpy as np
from jax import lax
from jax.experimental import pallas as pl
from jax.experimental.pallas import tpu as pltpu
from jax.sharding import PartitionSpec as P

CENTER = -5369.0 / 1800.0
SIDES = (12.0 / 7.0, -15.0 / 56.0, 10.0 / 189.0, -1.0 / 112.0, 2.0 / 1925.0, -1.0 / 16632.0)
WIDTH = 6
CHUNKS = 16
BF16 = jnp.bfloat16
VMEM = pl.BlockSpec(memory_space=pltpu.VMEM)
HBM = pl.BlockSpec(memory_space=pltpu.HBM)
SMEM = pl.BlockSpec(memory_space=pltpu.SMEM)
HIGHEST = lax.Precision.HIGHEST


def params():
    return pltpu.CompilerParams(vmem_limit_bytes=32 * 1024 * 1024)


def plane_weights(planes, rows_y):
    cells = planes * rows_y
    table = np.zeros((3 * cells, cells), np.float64)
    skipped = (planes - WIDTH) * rows_y
    for x in range(planes):
        for y in range(rows_y):
            out = x * rows_y + y
            for k, weight in enumerate(SIDES, 1):
                for step in (k, -k):
                    table[cells + x * rows_y + (y + step) % rows_y, out] += weight
                    row = cells + (x + step) * rows_y + y
                    table[row - skipped if row < cells else row, out] += weight
    table = -0.5 * table
    high = table.astype(BF16)
    return high, (table - high.astype(np.float64)).astype(BF16)


def split(value):
    high = value.astype(BF16)
    return high, (value - high.astype(jnp.float32)).astype(BF16)


def dot3(left, right, contract):
    dot = lambda x, y: lax.dot_general(x, y, (contract, ((), ())), preferred_element_type=jnp.float32)
    return dot(left[0], right[0]) + (dot(left[0], right[1]) + dot(left[1], right[0]))


def pack_kernel(blocks, wanted, scalars, *refs):
    x_hbm, refs = refs[scalars], refs[scalars + 1 :]
    t_refs, (x_ref, turned, sems) = refs[: len(wanted)], refs[len(wanted) :]
    count, _, rows_z = x_ref.shape
    chunks = sems.shape[0]
    per = count // chunks
    copies = [
        pltpu.make_async_copy(x_hbm.at[pl.ds(i * per, per)], x_ref.at[pl.ds(i * per, per)], sems.at[i])
        for i in range(chunks)
    ]
    for copy in copies:
        copy.start()
    for i, copy in enumerate(copies):
        copy.wait()
        for a in range(i * per, (i + 1) * per):
            turned[pl.ds(a, rows_z, stride=count), :] = x_ref[a].T
    rank = lax.axis_index("orb")
    rows = rows_z // blocks * count
    for m, t_ref in zip(wanted, t_refs):
        for core in range(2):
            start = pl.multiple_of((rank ^ (2 * m + core)) * rows, rows)
            t_ref[core] = turned[pl.ds(start, rows), :].reshape(t_ref.shape[1:])


def by_block(refs):
    half = len(refs) // 2
    return [refs[half + k // 2] if k % 2 else refs[k // 2].at[0] for k in range(2 * half)]


def squeeze(value):
    rows, wide = value.shape
    quarter, free = rows // 4, wide // 4
    lane = lax.broadcasted_iota(jnp.int32, (quarter, wide), 1)
    rest = value[3 * quarter :]
    parts = []
    for j in range(3):
        moved = pltpu.roll(rest, (3 - j) * free, 1)
        parts.append(jnp.where(lane < 3 * free, value[j * quarter : (j + 1) * quarter], moved))
    return jnp.concatenate(parts, axis=0)


def expand(value):
    rows, wide = value.shape
    quarter, free = rows // 3, wide // 4
    lane = lax.broadcasted_iota(jnp.int32, (quarter, wide), 1)
    rest = value[:quarter]
    for j in range(3):
        moved = pltpu.roll(value[j * quarter : (j + 1) * quarter], (j + 1) * free, 1)
        rest = jnp.where((lane >= j * free) & (lane < (j + 1) * free), moved, rest)
    return jnp.concatenate([value, rest], axis=0)


def pick_kernel(blocks, block_ref, *refs):
    x_refs, (act_ref, near_ref, far_ref, first_ref, last_ref) = by_block(refs[:blocks]), refs[blocks:]
    slab, nb, cells = act_ref.shape
    rank = lax.axis_index("orb")
    for k in range(blocks):
        @pl.when((rank ^ block_ref[0]) == k)
        def _(k=k):
            act_ref[...] = x_refs[k][...]
    odd = rank % 2
    near_ref[...] = act_ref[pl.ds((1 - odd) * (slab - WIDTH), WIDTH)]
    far_ref[...] = act_ref[pl.ds(odd * (slab - WIDTH), WIDTH)]
    flat = act_ref[...].reshape(slab * nb, cells)
    first_ref[...] = squeeze(flat)
    last_ref[...] = squeeze(pltpu.roll(flat, 3 * (cells // 4), 1))


def split_kernel(blocks, *refs):
    x_refs, (high_ref, low_ref) = by_block(refs[:blocks]), refs[blocks:]
    slab, nb, cells = x_refs[0].shape
    for k in range(blocks):
        for z in range(slab):
            high, low = split(x_refs[k][z])
            high_ref[k * nb : (k + 1) * nb, z * cells : (z + 1) * cells] = high
            low_ref[k * nb : (k + 1) * nb, z * cells : (z + 1) * cells] = low


def reorder(value, nb):
    wide = value.shape[1]
    row = lax.broadcasted_iota(jnp.int32, (wide, wide), 0)
    col = lax.broadcasted_iota(jnp.int32, (wide, wide), 1)
    exchange = jnp.where(row == (col ^ (lax.axis_index("orb") * nb)), 1.0, 0.0)
    return jnp.dot(value, exchange, precision=HIGHEST, preferred_element_type=jnp.float32)


def project_kernel(
    blocks, volume, owner_ref, rot_ref, xh_ref, xl_ref, act_ref, near_ref, far_ref, xb_ref, xa_ref, v_ref, wh_ref, wl_ref,
    a_ref, p_ref, turned, tall,
):
    slab, nb, cells = act_ref.shape
    turned[...] = v_ref[...].T
    rank = lax.axis_index("orb")
    mine = pl.ds(pl.multiple_of(rank * slab, slab), slab)
    act = act_ref[...]
    wide = jnp.concatenate([expand(xb_ref[...]), act.reshape(slab * nb, cells), expand(xa_ref[...])], axis=1)
    applied = dot3(split(wide), (wh_ref[...], wl_ref[...]), ((1,), (0,))).reshape(slab, nb, cells)
    applied = applied + (turned[mine, :][:, None, :] - 1.5 * CENTER) * act
    odd = rank % 2
    tall[pl.ds((1 - odd) * (slab + WIDTH), WIDTH)] = near_ref[...]
    tall[pl.ds(odd * (slab + WIDTH), WIDTH)] = far_ref[...]
    tall[WIDTH : WIDTH + slab] = act
    for k, weight in enumerate(SIDES, 1):
        upper = tall[WIDTH + k : WIDTH + k + slab]
        lower = tall[WIDTH - k : WIDTH - k + slab]
        applied = applied + (-0.5 * weight) * (upper + lower)
    a_ref[...] = applied
    flat = jnp.concatenate([applied[z] for z in range(slab)], axis=1)
    total = dot3(split(flat), (xh_ref[...], xl_ref[...]), ((1,), (1,)))
    p_ref[:nb] = reorder(total * volume, nb)
    sender = (rank == owner_ref[0]) & (lax.axis_index("dom") == 0)
    p_ref[nb:] = jnp.where(sender, rot_ref[...], 0.0)


def remove_kernel(xh_ref, xl_ref, a_ref, p_ref, g_ref):
    slab, nb, cells = a_ref.shape
    proj = split(reorder(p_ref[...], nb))
    removed = dot3(proj, (xh_ref[...], xl_ref[...]), ((1,), (0,)))
    for z in range(slab):
        g_ref[z] = a_ref[z] - removed[:, z * cells : (z + 1) * cells]


def update_kernel(blocks, panel_ref, x_ref, *refs):
    g_refs, (grad_hbm, out_hbm, whole, grad, out, sems) = refs[:blocks], refs[blocks:]
    nb, cells, rows_z = x_ref.shape
    rank = lax.axis_index("orb")
    share = rows_z // blocks * nb
    for k in range(blocks):
        at = pl.ds(pl.multiple_of((rank ^ k) * share, share), share)
        whole[at, :] = g_refs[k][...].reshape(share, cells)
    chunks = sems.shape[1]
    per = nb // chunks
    rows = 32
    copies = []
    for i in range(chunks):
        for c in range(i * per, (i + 1) * per):
            grad[c] = whole[pl.ds(c, rows_z, stride=nb), :].T
        part = pl.ds(i * per, per)
        copies.append(pltpu.make_async_copy(grad.at[part], grad_hbm.at[part], sems.at[0, i]))
        copies[-1].start()
    for i in range(chunks):
        group = range(i * per, (i + 1) * per)

        @pl.loop(0, cells // rows)
        def _(step, group=group):
            at = pl.ds(pl.multiple_of(step * rows, rows), rows)
            totals = [x_ref[a, at] for a in group]
            for c in range(nb):
                value = grad[c, at]
                totals = [total + panel_ref[c, rank * nb + a] * value for a, total in zip(group, totals)]
            for a, total in zip(group, totals):
                out[a, at] = total

        part = pl.ds(i * per, per)
        copies.append(pltpu.make_async_copy(out.at[part], out_hbm.at[part], sems.at[1, i]))
        copies[-1].start()
    for copy in copies:
        copy.wait()


def swap(value, axis, k):
    count = lax.axis_size(axis)
    return lax.ppermute(value, axis, [(i, i ^ k) for i in range(count)])


def total_over_all(value):
    doms, blocks = lax.axis_size("dom"), lax.axis_size("orb")
    every = [(d, o) for d in range(doms) for o in range(blocks)]

    def move(dom_step, orb_step):
        pairs = [(d, o, d ^ dom_step, o ^ orb_step) if o % 2 else (d, o, d, o) for d, o in every]
        return lax.ppermute(value, ("dom", "orb"), [(d * blocks + o, e * blocks + p) for d, o, e, p in pairs])

    value = value + swap(value, "orb", 1)
    value = sum([move(k, 0) for k in range(1, doms)], value)
    value = sum([move(0, k) for k in range(2, blocks, 2)], value)
    return jnp.where(lax.axis_index("orb") % 2 == 1, value, swap(value, "orb", 1))


def per_device(orbitals, potential, rotation, block, owner):
    nb, planes, rows_y, rows_z = orbitals.shape
    blocks, doms = lax.axis_size("orb"), lax.axis_size("dom")
    cells = planes * rows_y
    slab = rows_z // blocks
    volume = 1.0 / (cells * doms * rows_z)
    f32 = jnp.float32
    shape = lambda *dims: jax.ShapeDtypeStruct(dims, f32)
    piece, edge = shape(slab, nb, cells), shape(WIDTH, nb, cells)

    flat = orbitals.reshape(nb, cells, rows_z)
    held = pltpu.with_memory_space_constraint(flat, pltpu.HBM)
    chips = blocks // 2
    arrived = [None] * chips
    for wanted, scalars in ((range(chips // 2, chips), ()), (range(chips // 2), (block, owner))):
        packed = pl.pallas_call(
            functools.partial(pack_kernel, blocks, wanted, len(scalars)),
            out_shape=[shape(2, slab, nb, cells)] * len(wanted),
            in_specs=[SMEM] * len(scalars) + [HBM],
            out_specs=[VMEM] * len(wanted),
            scratch_shapes=[
                pltpu.VMEM((nb, cells, rows_z), f32),
                pltpu.VMEM((rows_z * nb, cells), f32),
                pltpu.SemaphoreType.DMA((CHUNKS,)),
            ],
            compiler_params=params(),
            cost_estimate=pl.CostEstimate(flops=0, bytes_accessed=8 * nb * cells * rows_z, transcendentals=0),
            name="pack",
        )(*scalars, held)
        for m, value in zip(wanted, packed):
            arrived[m] = swap(value, "orb", 2 * m) if m else value
    spread = arrived + [swap(value[1], "orb", 1) for value in arrived]

    side = shape(3 * slab * nb // 4, cells)
    active, near, far, first, last = pl.pallas_call(
        functools.partial(pick_kernel, blocks),
        out_shape=(piece, edge, edge, side, side),
        in_specs=[SMEM] + [VMEM] * blocks,
        out_specs=[VMEM] * 5,
        compiler_params=params(),
        name="pick",
    )(block, *spread)

    up = lambda count: [(i, (i + 1) % count) for i in range(count)]
    down = lambda count: [(i, (i - 1) % count) for i in range(count)]
    x_before = lax.ppermute(last, "dom", up(doms))
    x_after = lax.ppermute(first, "dom", down(doms))
    z_near = swap(near, "orb", 1)
    z_far = lax.ppermute(far, "orb", [(o, (o + 2 * (o % 2) - 1) % blocks) for o in range(blocks)])

    halves = jax.ShapeDtypeStruct((blocks * nb, slab * cells), BF16)
    parts = pl.pallas_call(
        functools.partial(split_kernel, blocks),
        out_shape=(halves, halves),
        in_specs=[VMEM] * blocks,
        out_specs=(VMEM, VMEM),
        compiler_params=params(),
        cost_estimate=pl.CostEstimate(flops=3 * blocks * nb * slab * cells, bytes_accessed=0, transcendentals=0),
        name="split",
    )(*spread)

    weights = [jnp.asarray(w) for w in plane_weights(planes, rows_y)]
    applied, part = pl.pallas_call(
        functools.partial(project_kernel, blocks, volume),
        out_shape=(piece, shape(2 * nb, blocks * nb)),
        in_specs=[SMEM] + [VMEM] * 11,
        out_specs=(VMEM, VMEM),
        scratch_shapes=[pltpu.VMEM((rows_z, cells), f32), pltpu.VMEM((slab + 2 * WIDTH, nb, cells), f32)],
        compiler_params=params(),
        name="project",
    )(owner, rotation, *parts, active, z_near, z_far, x_before, x_after, potential.reshape(cells, rows_z), *weights)

    summed = total_over_all(part)
    proj, panel = summed[:nb], summed[nb:]

    own = pl.pallas_call(
        remove_kernel,
        out_shape=piece,
        in_specs=[VMEM] * 4,
        out_specs=VMEM,
        compiler_params=params(),
        name="remove",
    )(*parts, applied, proj)

    gathered = [own] + [None] * (blocks - 1)
    for k in range(2, blocks, 2):
        gathered[k] = swap(own, "orb", k)
    for k in range(0, blocks, 2):
        gathered[k + 1] = swap(gathered[k], "orb", 1)

    gradient, updated = pl.pallas_call(
        functools.partial(update_kernel, blocks),
        out_shape=(shape(nb, cells, rows_z), shape(nb, cells, rows_z)),
        in_specs=[SMEM, VMEM] + [VMEM] * blocks,
        out_specs=(HBM, HBM),
        scratch_shapes=[
            pltpu.VMEM((rows_z * nb, cells), f32),
            pltpu.VMEM((nb, cells, rows_z), f32),
            pltpu.VMEM((nb, cells, rows_z), f32),
            pltpu.SemaphoreType.DMA((2, CHUNKS)),
        ],
        compiler_params=params(),
        name="update",
    )(panel, flat, *gathered)
    return gradient.reshape(orbitals.shape), updated.reshape(orbitals.shape)


def solution(mesh):
    in_specs = (P("orb", "dom", None, None), P("dom", None, None), P("orb", None), P(), P())
    out_specs = (P(None, "dom", None, None), P("orb", "dom", None, None))
    return jax.shard_map(
        per_device, mesh=mesh, in_specs=in_specs, out_specs=out_specs, check_vma=False
    )
```

```python
import functools

import jax
import jax.numpy as jnp
import numpy as np
from jax import lax
from jax.experimental import pallas as pl
from jax.experimental.pallas import tpu as pltpu
from jax.sharding import PartitionSpec as P

CENTER = -5369.0 / 1800.0
SIDES = (12.0 / 7.0, -15.0 / 56.0, 10.0 / 189.0, -1.0 / 112.0, 2.0 / 1925.0, -1.0 / 16632.0)
WIDTH = 6
CHUNKS = 4
BF16 = jnp.bfloat16
VMEM = pl.BlockSpec(memory_space=pltpu.VMEM)
HBM = pl.BlockSpec(memory_space=pltpu.HBM)
SMEM = pl.BlockSpec(memory_space=pltpu.SMEM)
HIGHEST = lax.Precision.HIGHEST


def params():
    return pltpu.CompilerParams(vmem_limit_bytes=32 * 1024 * 1024)


def plane_weights(planes, rows_y):
    cells = planes * rows_y
    table = np.zeros((3 * cells, cells), np.float64)
    skipped = (planes - WIDTH) * rows_y
    for x in range(planes):
        for y in range(rows_y):
            out = x * rows_y + y
            for k, weight in enumerate(SIDES, 1):
                for step in (k, -k):
                    table[cells + x * rows_y + (y + step) % rows_y, out] += weight
                    row = cells + (x + step) * rows_y + y
                    table[row - skipped if row < cells else row, out] += weight
    table = -0.5 * table
    high = table.astype(BF16)
    return high, (table - high.astype(np.float64)).astype(BF16)


def split(value):
    high = value.astype(BF16)
    return high, (value - high.astype(jnp.float32)).astype(BF16)


def dot3(left, right, contract):
    dot = lambda x, y: lax.dot_general(x, y, (contract, ((), ())), preferred_element_type=jnp.float32)
    return dot(left[0], right[0]) + (dot(left[0], right[1]) + dot(left[1], right[0]))


def pack_kernel(blocks, wanted, extra, *refs):
    if extra:
        rot_ref = refs[extra - 1]
    x_hbm, refs = refs[extra], refs[extra + 1 :]
    t_refs, (*copies_ref, x_ref, turned, sems) = refs[: len(wanted)], refs[len(wanted) :]
    count, _, rows_z = x_ref.shape
    chunks = sems.shape[0]
    per = count // chunks
    copies = [
        pltpu.make_async_copy(x_hbm.at[pl.ds(i * per, per)], x_ref.at[pl.ds(i * per, per)], sems.at[i])
        for i in range(chunks)
    ]
    for copy in copies:
        copy.start()
    for i, copy in enumerate(copies):
        copy.wait()
        for a in range(i * per, (i + 1) * per):
            turned[pl.ds(a, rows_z, stride=count), :] = x_ref[a].T
    rank = lax.axis_index("orb")
    rows = rows_z // blocks * count
    for m, t_ref in zip(wanted, t_refs):
        for core in range(2):
            start = pl.multiple_of((rank ^ (2 * m + core)) * rows, rows)
            t_ref[core] = turned[pl.ds(start, rows), :].reshape(t_ref.shape[1:])
    if extra:
        for j in range(blocks):
            copies_ref[0][j] = rot_ref[...]


def by_block(refs):
    half = len(refs) // 2
    return [refs[half + k // 2] if k % 2 else refs[k // 2].at[0] for k in range(2 * half)]


def squeeze(value):
    rows, wide = value.shape
    quarter, free = rows // 4, wide // 4
    lane = lax.broadcasted_iota(jnp.int32, (quarter, wide), 1)
    rest = value[3 * quarter :]
    parts = []
    for j in range(3):
        moved = pltpu.roll(rest, (3 - j) * free, 1)
        parts.append(jnp.where(lane < 3 * free, value[j * quarter : (j + 1) * quarter], moved))
    return jnp.concatenate(parts, axis=0)


def expand(value):
    rows, wide = value.shape
    quarter, free = rows // 3, wide // 4
    lane = lax.broadcasted_iota(jnp.int32, (quarter, wide), 1)
    rest = value[:quarter]
    for j in range(3):
        moved = pltpu.roll(value[j * quarter : (j + 1) * quarter], (j + 1) * free, 1)
        rest = jnp.where((lane >= j * free) & (lane < (j + 1) * free), moved, rest)
    return jnp.concatenate([value, rest], axis=0)


def pick_kernel(blocks, block_ref, *refs):
    x_refs, (act_ref, near_ref, far_ref, first_ref, last_ref) = by_block(refs[:blocks]), refs[blocks:]
    slab, nb, cells = act_ref.shape
    rank = lax.axis_index("orb")
    for k in range(blocks):
        @pl.when((rank ^ block_ref[0]) == k)
        def _(k=k):
            act_ref[...] = x_refs[k][...]
    odd = rank % 2
    near_ref[...] = act_ref[pl.ds((1 - odd) * (slab - WIDTH), WIDTH)]
    far_ref[...] = act_ref[pl.ds(odd * (slab - WIDTH), WIDTH)]
    flat = act_ref[...].reshape(slab * nb, cells)
    first_ref[...] = squeeze(flat)
    last_ref[...] = squeeze(pltpu.roll(flat, 3 * (cells // 4), 1))


def choose_kernel(owner_ref, panels_ref, home_ref, panel_ref, other_ref):
    panel_ref[...] = panels_ref[owner_ref[0]]
    other_ref[...] = home_ref[1]


def split_kernel(blocks, *refs):
    x_refs, (high_ref, low_ref) = by_block(refs[:blocks]), refs[blocks:]
    slab, nb, cells = x_refs[0].shape
    for k in range(blocks):
        for z in range(slab):
            high, low = split(x_refs[k][z])
            high_ref[k * nb : (k + 1) * nb, z * cells : (z + 1) * cells] = high
            low_ref[k * nb : (k + 1) * nb, z * cells : (z + 1) * cells] = low


def reorder(value, nb):
    wide = value.shape[1]
    row = lax.broadcasted_iota(jnp.int32, (wide, wide), 0)
    col = lax.broadcasted_iota(jnp.int32, (wide, wide), 1)
    exchange = jnp.where(row == (col ^ (lax.axis_index("orb") * nb)), 1.0, 0.0)
    return jnp.dot(value, exchange, precision=HIGHEST, preferred_element_type=jnp.float32)


def project_kernel(
    volume, xh_ref, xl_ref, act_ref, near_ref, far_ref, xb_ref, xa_ref, v_ref, wh_ref, wl_ref,
    a_ref, p_ref, turned, tall,
):
    slab, nb, cells = act_ref.shape
    turned[...] = v_ref[...].T
    rank = lax.axis_index("orb")
    mine = pl.ds(pl.multiple_of(rank * slab, slab), slab)
    act = act_ref[...]
    wide = jnp.concatenate([expand(xb_ref[...]), act.reshape(slab * nb, cells), expand(xa_ref[...])], axis=1)
    applied = dot3(split(wide), (wh_ref[...], wl_ref[...]), ((1,), (0,))).reshape(slab, nb, cells)
    applied = applied + (turned[mine, :][:, None, :] - 1.5 * CENTER) * act
    odd = rank % 2
    tall[pl.ds((1 - odd) * (slab + WIDTH), WIDTH)] = near_ref[...]
    tall[pl.ds(odd * (slab + WIDTH), WIDTH)] = far_ref[...]
    tall[WIDTH : WIDTH + slab] = act
    for k, weight in enumerate(SIDES, 1):
        upper = tall[WIDTH + k : WIDTH + k + slab]
        lower = tall[WIDTH - k : WIDTH - k + slab]
        applied = applied + (-0.5 * weight) * (upper + lower)
    a_ref[...] = applied
    flat = jnp.concatenate([applied[z] for z in range(slab)], axis=1)
    total = dot3(split(flat), (xh_ref[...], xl_ref[...]), ((1,), (1,)))
    total = reorder(total * volume, nb)
    for d in range(p_ref.shape[0]):
        p_ref[d] = total


def remove_kernel(xh_ref, xl_ref, a_ref, p_ref, g_ref):
    slab, nb, cells = a_ref.shape
    proj = split(reorder(sum(p_ref[j] for j in range(p_ref.shape[0])), nb))
    removed = dot3(proj, (xh_ref[...], xl_ref[...]), ((1,), (0,)))
    for z in range(slab):
        g_ref[z] = a_ref[z] - removed[:, z * cells : (z + 1) * cells]


def update_kernel(blocks, panel_ref, x_ref, *refs):
    g_refs, (grad_hbm, out_hbm, whole, grad, out, sems) = refs[:blocks], refs[blocks:]
    nb, cells, rows_z = x_ref.shape
    rank = lax.axis_index("orb")
    share = rows_z // blocks * nb
    for k in range(blocks):
        at = pl.ds(pl.multiple_of((rank ^ k) * share, share), share)
        whole[at, :] = g_refs[k][...].reshape(share, cells)
    chunks = sems.shape[1]
    per = nb // chunks
    rows = 32
    copies = []
    for i in range(chunks):
        for c in range(i * per, (i + 1) * per):
            grad[c] = whole[pl.ds(c, rows_z, stride=nb), :].T
        part = pl.ds(i * per, per)
        copies.append(pltpu.make_async_copy(grad.at[part], grad_hbm.at[part], sems.at[0, i]))
        copies[-1].start()
    for i in range(chunks):
        group = range(i * per, (i + 1) * per)

        @pl.loop(0, cells // rows)
        def _(step, group=group):
            at = pl.ds(pl.multiple_of(step * rows, rows), rows)
            totals = [x_ref[a, at] for a in group]
            for c in range(nb):
                value = grad[c, at]
                totals = [total + panel_ref[c, rank * nb + a] * value for a, total in zip(group, totals)]
            for a, total in zip(group, totals):
                out[a, at] = total

        part = pl.ds(i * per, per)
        copies.append(pltpu.make_async_copy(out.at[part], out_hbm.at[part], sems.at[1, i]))
        copies[-1].start()
    for copy in copies:
        copy.wait()


def swap(value, axis, k):
    count = lax.axis_size(axis)
    return lax.ppermute(value, axis, [(i, i ^ k) for i in range(count)])


def share(value, axis):
    return lax.all_to_all(value, axis, 0, 0)


def per_device(orbitals, potential, rotation, block, owner):
    nb, planes, rows_y, rows_z = orbitals.shape
    blocks, doms = lax.axis_size("orb"), lax.axis_size("dom")
    cells = planes * rows_y
    slab = rows_z // blocks
    volume = 1.0 / (cells * doms * rows_z)
    f32 = jnp.float32
    shape = lambda *dims: jax.ShapeDtypeStruct(dims, f32)
    piece, edge = shape(slab, nb, cells), shape(WIDTH, nb, cells)

    flat = orbitals.reshape(nb, cells, rows_z)
    held = pltpu.with_memory_space_constraint(flat, pltpu.HBM)
    chips = blocks // 2
    arrived = [None] * chips
    repeated = [shape(blocks, nb, blocks * nb)]
    for wanted, extra in ((range(chips // 2, chips), ()), (range(chips // 2), (block, owner, rotation))):
        packed = pl.pallas_call(
            functools.partial(pack_kernel, blocks, wanted, len(extra)),
            out_shape=[shape(2, slab, nb, cells)] * len(wanted) + (repeated if extra else []),
            in_specs=([SMEM, SMEM, VMEM] if extra else []) + [HBM],
            out_specs=[VMEM] * (len(wanted) + bool(extra)),
            scratch_shapes=[
                pltpu.VMEM((nb, cells, rows_z), f32),
                pltpu.VMEM((rows_z * nb, cells), f32),
                pltpu.SemaphoreType.DMA((CHUNKS,)),
            ],
            compiler_params=params(),
            cost_estimate=pl.CostEstimate(flops=0, bytes_accessed=8 * nb * cells * rows_z, transcendentals=0),
            name="pack",
        )(*extra, held)
        for m, value in zip(wanted, packed):
            arrived[m] = swap(value, "orb", 2 * m) if m else value
    panel, other = pl.pallas_call(
        choose_kernel,
        out_shape=(shape(nb, blocks * nb), piece),
        in_specs=[SMEM, VMEM, VMEM],
        out_specs=(VMEM, VMEM),
        compiler_params=params(),
        name="choose",
    )(owner, share(packed[-1], "orb"), arrived[0])
    spread = arrived + [swap(value, "orb", 1) for value in [other] + [value[1] for value in arrived[1:]]]

    side = shape(3 * slab * nb // 4, cells)
    active, near, far, first, last = pl.pallas_call(
        functools.partial(pick_kernel, blocks),
        out_shape=(piece, edge, edge, side, side),
        in_specs=[SMEM] + [VMEM] * blocks,
        out_specs=[VMEM] * 5,
        compiler_params=params(),
        name="pick",
    )(block, *spread)

    up = lambda count: [(i, (i + 1) % count) for i in range(count)]
    down = lambda count: [(i, (i - 1) % count) for i in range(count)]
    x_before = lax.ppermute(last, "dom", up(doms))
    x_after = lax.ppermute(first, "dom", down(doms))
    z_near = swap(near, "orb", 1)
    z_far = lax.ppermute(far, "orb", [(o, (o + 2 * (o % 2) - 1) % blocks) for o in range(blocks)])

    halves = jax.ShapeDtypeStruct((blocks * nb, slab * cells), BF16)
    parts = pl.pallas_call(
        functools.partial(split_kernel, blocks),
        out_shape=(halves, halves),
        in_specs=[VMEM] * blocks,
        out_specs=(VMEM, VMEM),
        compiler_params=params(),
        cost_estimate=pl.CostEstimate(flops=3 * blocks * nb * slab * cells, bytes_accessed=0, transcendentals=0),
        name="split",
    )(*spread)

    weights = [jnp.asarray(w) for w in plane_weights(planes, rows_y)]
    applied, part = pl.pallas_call(
        functools.partial(project_kernel, volume),
        out_shape=(piece, shape(doms, nb, blocks * nb)),
        in_specs=[VMEM] * 10,
        out_specs=(VMEM, VMEM),
        scratch_shapes=[pltpu.VMEM((rows_z, cells), f32), pltpu.VMEM((slab + 2 * WIDTH, nb, cells), f32)],
        compiler_params=params(),
        name="project",
    )(*parts, active, z_near, z_far, x_before, x_after, potential.reshape(cells, rows_z), *weights)

    proj = share(jnp.broadcast_to(sum(share(part, "dom")), (blocks, nb, blocks * nb)), "orb")

    own = pl.pallas_call(
        remove_kernel,
        out_shape=piece,
        in_specs=[VMEM] * 4,
        out_specs=VMEM,
        compiler_params=params(),
        name="remove",
    )(*parts, applied, proj)

    gathered = [own] + [None] * (blocks - 1)
    for k in range(2, blocks, 2):
        gathered[k] = swap(own, "orb", k)
    for k in range(0, blocks, 2):
        gathered[k + 1] = swap(gathered[k], "orb", 1)

    gradient, updated = pl.pallas_call(
        functools.partial(update_kernel, blocks),
        out_shape=(shape(nb, cells, rows_z), shape(nb, cells, rows_z)),
        in_specs=[SMEM, VMEM] + [VMEM] * blocks,
        out_specs=(HBM, HBM),
        scratch_shapes=[
            pltpu.VMEM((rows_z * nb, cells), f32),
            pltpu.VMEM((nb, cells, rows_z), f32),
            pltpu.VMEM((nb, cells, rows_z), f32),
            pltpu.SemaphoreType.DMA((2, CHUNKS)),
        ],
        compiler_params=params(),
        name="update",
    )(panel, flat, *gathered)
    return gradient.reshape(orbitals.shape), updated.reshape(orbitals.shape)


def solution(mesh):
    in_specs = (P("orb", "dom", None, None), P("dom", None, None), P("orb", None), P(), P())
    out_specs = (P(None, "dom", None, None), P("orb", "dom", None, None))
    return jax.shard_map(
        per_device, mesh=mesh, in_specs=in_specs, out_specs=out_specs, check_vma=False
    )
```

```python
import functools

import jax
import jax.numpy as jnp
import numpy as np
from jax import lax
from jax.experimental import pallas as pl
from jax.experimental.pallas import tpu as pltpu
from jax.sharding import PartitionSpec as P

CENTER = -5369.0 / 1800.0
SIDES = (12.0 / 7.0, -15.0 / 56.0, 10.0 / 189.0, -1.0 / 112.0, 2.0 / 1925.0, -1.0 / 16632.0)
WIDTH = 6
CHUNKS = 4
BF16 = jnp.bfloat16
VMEM = pl.BlockSpec(memory_space=pltpu.VMEM)
HBM = pl.BlockSpec(memory_space=pltpu.HBM)
SMEM = pl.BlockSpec(memory_space=pltpu.SMEM)
HIGHEST = lax.Precision.HIGHEST


def params():
    return pltpu.CompilerParams(vmem_limit_bytes=32 * 1024 * 1024)


def plane_weights(planes, rows_y):
    cells = planes * rows_y
    table = np.zeros((3 * cells, cells), np.float64)
    skipped = (planes - WIDTH) * rows_y
    for x in range(planes):
        for y in range(rows_y):
            out = x * rows_y + y
            for k, weight in enumerate(SIDES, 1):
                for step in (k, -k):
                    table[cells + x * rows_y + (y + step) % rows_y, out] += weight
                    row = cells + (x + step) * rows_y + y
                    table[row - skipped if row < cells else row, out] += weight
    table = -0.5 * table
    high = table.astype(BF16)
    return high, (table - high.astype(np.float64)).astype(BF16)


def split(value):
    high = value.astype(BF16)
    return high, (value - high.astype(jnp.float32)).astype(BF16)


def dot3(left, right, contract):
    dot = lambda x, y: lax.dot_general(x, y, (contract, ((), ())), preferred_element_type=jnp.float32)
    return dot(left[0], right[0]) + (dot(left[0], right[1]) + dot(left[1], right[0]))


def cut(turned, wanted, t_refs):
    rows = t_refs[0].shape[1] * t_refs[0].shape[2]
    rank = lax.axis_index("orb")
    for m, t_ref in zip(wanted, t_refs):
        for core in range(2):
            start = pl.multiple_of((rank ^ (2 * m + core)) * rows, rows)
            t_ref[core] = turned[pl.ds(start, rows), :].reshape(t_ref.shape[1:])


def far_kernel(wanted, x_hbm, *refs):
    t_refs, (turned, x_ref, sems) = refs[: len(wanted)], refs[len(wanted) :]
    count, _, rows_z = x_ref.shape
    chunks = sems.shape[0]
    per = count // chunks
    copies = [
        pltpu.make_async_copy(x_hbm.at[pl.ds(i * per, per)], x_ref.at[pl.ds(i * per, per)], sems.at[i])
        for i in range(chunks)
    ]
    for copy in copies:
        copy.start()
    for i, copy in enumerate(copies):
        copy.wait()
        for a in range(i * per, (i + 1) * per):
            turned[pl.ds(a, rows_z, stride=count), :] = x_ref[a].T
    cut(turned, wanted, t_refs)


def near_kernel(wanted, block_ref, owner_ref, turned, *t_refs):
    cut(turned, wanted, t_refs)


def by_block(refs):
    half = len(refs) // 2
    return [refs[half + k // 2] if k % 2 else refs[k // 2].at[0] for k in range(2 * half)]


def squeeze(value):
    rows, wide = value.shape
    quarter, free = rows // 4, wide // 4
    lane = lax.broadcasted_iota(jnp.int32, (quarter, wide), 1)
    rest = value[3 * quarter :]
    parts = []
    for j in range(3):
        moved = pltpu.roll(rest, (3 - j) * free, 1)
        parts.append(jnp.where(lane < 3 * free, value[j * quarter : (j + 1) * quarter], moved))
    return jnp.concatenate(parts, axis=0)


def expand(value):
    rows, wide = value.shape
    quarter, free = rows // 3, wide // 4
    lane = lax.broadcasted_iota(jnp.int32, (quarter, wide), 1)
    rest = value[:quarter]
    for j in range(3):
        moved = pltpu.roll(value[j * quarter : (j + 1) * quarter], (j + 1) * free, 1)
        rest = jnp.where((lane >= j * free) & (lane < (j + 1) * free), moved, rest)
    return jnp.concatenate([value, rest], axis=0)


def pick_kernel(blocks, block_ref, *refs):
    x_refs, (act_ref, near_ref, far_ref, first_ref, last_ref) = by_block(refs[:blocks]), refs[blocks:]
    slab, nb, cells = act_ref.shape
    rank = lax.axis_index("orb")
    for k in range(blocks):
        @pl.when((rank ^ block_ref[0]) == k)
        def _(k=k):
            act_ref[...] = x_refs[k][...]
    odd = rank % 2
    near_ref[...] = act_ref[pl.ds((1 - odd) * (slab - WIDTH), WIDTH)]
    far_ref[...] = act_ref[pl.ds(odd * (slab - WIDTH), WIDTH)]
    flat = act_ref[...].reshape(slab * nb, cells)
    first_ref[...] = squeeze(flat)
    last_ref[...] = squeeze(pltpu.roll(flat, 3 * (cells // 4), 1))


def split_kernel(blocks, *refs):
    x_refs, (high_ref, low_ref) = by_block(refs[:blocks]), refs[blocks:]
    slab, nb, cells = x_refs[0].shape
    for k in range(blocks):
        for z in range(slab):
            high, low = split(x_refs[k][z])
            high_ref[k * nb : (k + 1) * nb, z * cells : (z + 1) * cells] = high
            low_ref[k * nb : (k + 1) * nb, z * cells : (z + 1) * cells] = low


def reorder(value, nb):
    wide = value.shape[1]
    row = lax.broadcasted_iota(jnp.int32, (wide, wide), 0)
    col = lax.broadcasted_iota(jnp.int32, (wide, wide), 1)
    exchange = jnp.where(row == (col ^ (lax.axis_index("orb") * nb)), 1.0, 0.0)
    return jnp.dot(value, exchange, precision=HIGHEST, preferred_element_type=jnp.float32)


def project_kernel(
    volume, owner_ref, rot_ref, xh_ref, xl_ref, act_ref, near_ref, far_ref, xb_ref, xa_ref, v_ref, wh_ref, wl_ref,
    a_ref, p_ref, turned, tall,
):
    slab, nb, cells = act_ref.shape
    turned[...] = v_ref[...].T
    rank = lax.axis_index("orb")
    mine = pl.ds(pl.multiple_of(rank * slab, slab), slab)
    act = act_ref[...]
    wide = jnp.concatenate([expand(xb_ref[...]), act.reshape(slab * nb, cells), expand(xa_ref[...])], axis=1)
    applied = dot3(split(wide), (wh_ref[...], wl_ref[...]), ((1,), (0,))).reshape(slab, nb, cells)
    applied = applied + (turned[mine, :][:, None, :] - 1.5 * CENTER) * act
    odd = rank % 2
    tall[pl.ds((1 - odd) * (slab + WIDTH), WIDTH)] = near_ref[...]
    tall[pl.ds(odd * (slab + WIDTH), WIDTH)] = far_ref[...]
    tall[WIDTH : WIDTH + slab] = act
    for k, weight in enumerate(SIDES, 1):
        upper = tall[WIDTH + k : WIDTH + k + slab]
        lower = tall[WIDTH - k : WIDTH - k + slab]
        applied = applied + (-0.5 * weight) * (upper + lower)
    a_ref[...] = applied
    flat = jnp.concatenate([applied[z] for z in range(slab)], axis=1)
    total = dot3(split(flat), (xh_ref[...], xl_ref[...]), ((1,), (1,)))
    p_ref[:nb] = reorder(total * volume, nb)
    sender = (rank == owner_ref[0]) & (lax.axis_index("dom") == 0)
    p_ref[nb:] = jnp.where(sender, rot_ref[...], 0.0)


def remove_kernel(xh_ref, xl_ref, a_ref, p_ref, g_ref):
    slab, nb, cells = a_ref.shape
    proj = split(reorder(p_ref[...], nb))
    removed = dot3(proj, (xh_ref[...], xl_ref[...]), ((1,), (0,)))
    for z in range(slab):
        g_ref[z] = a_ref[z] - removed[:, z * cells : (z + 1) * cells]


def update_kernel(blocks, panel_ref, x_ref, *refs):
    g_refs, (grad_hbm, out_hbm, whole, grad, out, sems) = refs[:blocks], refs[blocks:]
    nb, cells, rows_z = x_ref.shape
    rank = lax.axis_index("orb")
    share = rows_z // blocks * nb
    for k in range(blocks):
        at = pl.ds(pl.multiple_of((rank ^ k) * share, share), share)
        whole[at, :] = g_refs[k][...].reshape(share, cells)
    chunks = sems.shape[1]
    per = nb // chunks
    rows = 32
    copies = []
    for i in range(chunks):
        for c in range(i * per, (i + 1) * per):
            grad[c] = whole[pl.ds(c, rows_z, stride=nb), :].T
        part = pl.ds(i * per, per)
        copies.append(pltpu.make_async_copy(grad.at[part], grad_hbm.at[part], sems.at[0, i]))
        copies[-1].start()
    for i in range(chunks):
        group = range(i * per, (i + 1) * per)

        @pl.loop(0, cells // rows)
        def _(step, group=group):
            at = pl.ds(pl.multiple_of(step * rows, rows), rows)
            totals = [x_ref[a, at] for a in group]
            for c in range(nb):
                value = grad[c, at]
                totals = [total + panel_ref[c, rank * nb + a] * value for a, total in zip(group, totals)]
            for a, total in zip(group, totals):
                out[a, at] = total

        part = pl.ds(i * per, per)
        copies.append(pltpu.make_async_copy(out.at[part], out_hbm.at[part], sems.at[1, i]))
        copies[-1].start()
    for copy in copies:
        copy.wait()


def swap(value, axis, k):
    count = lax.axis_size(axis)
    return lax.ppermute(value, axis, [(i, i ^ k) for i in range(count)])


def total_over_all(value):
    doms, blocks = lax.axis_size("dom"), lax.axis_size("orb")
    for axis, steps in (("orb", (1,)), ("dom", range(1, doms)), ("orb", range(2, blocks, 2))):
        value = sum([swap(value, axis, k) for k in steps], value)
    return value


def per_device(orbitals, potential, rotation, block, owner):
    nb, planes, rows_y, rows_z = orbitals.shape
    blocks, doms = lax.axis_size("orb"), lax.axis_size("dom")
    cells = planes * rows_y
    slab = rows_z // blocks
    volume = 1.0 / (cells * doms * rows_z)
    f32 = jnp.float32
    shape = lambda *dims: jax.ShapeDtypeStruct(dims, f32)
    piece, edge = shape(slab, nb, cells), shape(WIDTH, nb, cells)

    flat = orbitals.reshape(nb, cells, rows_z)
    held = pltpu.with_memory_space_constraint(flat, pltpu.HBM)
    chips = blocks // 2
    pair = shape(2, slab, nb, cells)
    ahead, behind = range(chips // 2, chips), range(chips // 2)
    *packed, turned = pl.pallas_call(
        functools.partial(far_kernel, ahead),
        out_shape=[pair] * len(ahead) + [shape(rows_z * nb, cells)],
        in_specs=[HBM],
        out_specs=[VMEM] * (len(ahead) + 1),
        scratch_shapes=[pltpu.VMEM((nb, cells, rows_z), f32), pltpu.SemaphoreType.DMA((CHUNKS,))],
        compiler_params=params(),
        cost_estimate=pl.CostEstimate(flops=0, bytes_accessed=8 * nb * cells * rows_z, transcendentals=0),
        name="far",
    )(held)
    crossing = [swap(value, "orb", 2 * m) for m, value in zip(ahead, packed)]
    home, *packed = pl.pallas_call(
        functools.partial(near_kernel, behind),
        out_shape=[pair] * len(behind),
        in_specs=[SMEM, SMEM, VMEM],
        out_specs=[VMEM] * len(behind),
        compiler_params=params(),
        cost_estimate=pl.CostEstimate(flops=0, bytes_accessed=8 * nb * cells * rows_z, transcendentals=0),
        name="near",
    )(block, owner, turned)
    arrived = [home] + [swap(value, "orb", 2 * m) for m, value in zip(behind[1:], packed)] + crossing
    spread = arrived + [swap(value[1], "orb", 1) for value in arrived]

    side = shape(3 * slab * nb // 4, cells)
    active, near, far, first, last = pl.pallas_call(
        functools.partial(pick_kernel, blocks),
        out_shape=(piece, edge, edge, side, side),
        in_specs=[SMEM] + [VMEM] * blocks,
        out_specs=[VMEM] * 5,
        compiler_params=params(),
        name="pick",
    )(block, *spread)

    up = lambda count: [(i, (i + 1) % count) for i in range(count)]
    down = lambda count: [(i, (i - 1) % count) for i in range(count)]
    x_before = lax.ppermute(last, "dom", up(doms))
    x_after = lax.ppermute(first, "dom", down(doms))
    z_near = swap(near, "orb", 1)
    z_far = lax.ppermute(far, "orb", [(o, (o + 2 * (o % 2) - 1) % blocks) for o in range(blocks)])

    halves = jax.ShapeDtypeStruct((blocks * nb, slab * cells), BF16)
    parts = pl.pallas_call(
        functools.partial(split_kernel, blocks),
        out_shape=(halves, halves),
        in_specs=[VMEM] * blocks,
        out_specs=(VMEM, VMEM),
        compiler_params=params(),
        cost_estimate=pl.CostEstimate(flops=3 * blocks * nb * slab * cells, bytes_accessed=0, transcendentals=0),
        name="split",
    )(*spread)

    weights = [jnp.asarray(w) for w in plane_weights(planes, rows_y)]
    applied, part = pl.pallas_call(
        functools.partial(project_kernel, volume),
        out_shape=(piece, shape(2 * nb, blocks * nb)),
        in_specs=[SMEM] + [VMEM] * 11,
        out_specs=(VMEM, VMEM),
        scratch_shapes=[pltpu.VMEM((rows_z, cells), f32), pltpu.VMEM((slab + 2 * WIDTH, nb, cells), f32)],
        compiler_params=params(),
        name="project",
    )(owner, rotation, *parts, active, z_near, z_far, x_before, x_after, potential.reshape(cells, rows_z), *weights)

    summed = total_over_all(part)
    proj, panel = summed[:nb], summed[nb:]

    own = pl.pallas_call(
        remove_kernel,
        out_shape=piece,
        in_specs=[VMEM] * 4,
        out_specs=VMEM,
        compiler_params=params(),
        name="remove",
    )(*parts, applied, proj)

    gathered = [own] + [None] * (blocks - 1)
    for k in range(2, blocks, 2):
        gathered[k] = swap(own, "orb", k)
    for k in range(0, blocks, 2):
        gathered[k + 1] = swap(gathered[k], "orb", 1)

    gradient, updated = pl.pallas_call(
        functools.partial(update_kernel, blocks),
        out_shape=(shape(nb, cells, rows_z), shape(nb, cells, rows_z)),
        in_specs=[SMEM, VMEM] + [VMEM] * blocks,
        out_specs=(HBM, HBM),
        scratch_shapes=[
            pltpu.VMEM((rows_z * nb, cells), f32),
            pltpu.VMEM((nb, cells, rows_z), f32),
            pltpu.VMEM((nb, cells, rows_z), f32),
            pltpu.SemaphoreType.DMA((2, CHUNKS)),
        ],
        compiler_params=params(),
        name="update",
    )(panel, flat, *gathered)
    return gradient.reshape(orbitals.shape), updated.reshape(orbitals.shape)


def solution(mesh):
    in_specs = (P("orb", "dom", None, None), P("dom", None, None), P("orb", None), P(), P())
    out_specs = (P(None, "dom", None, None), P("orb", "dom", None, None))
    return jax.shard_map(
        per_device, mesh=mesh, in_specs=in_specs, out_specs=out_specs, check_vma=False
    )
```

```python
import functools

import jax
import jax.numpy as jnp
import numpy as np
from jax import lax
from jax.experimental import pallas as pl
from jax.experimental.pallas import tpu as pltpu
from jax.sharding import PartitionSpec as P

CENTER = -5369.0 / 1800.0
SIDES = (12.0 / 7.0, -15.0 / 56.0, 10.0 / 189.0, -1.0 / 112.0, 2.0 / 1925.0, -1.0 / 16632.0)
WIDTH = 6
CHUNKS = 4
BF16 = jnp.bfloat16
VMEM = pl.BlockSpec(memory_space=pltpu.VMEM)
HBM = pl.BlockSpec(memory_space=pltpu.HBM)
SMEM = pl.BlockSpec(memory_space=pltpu.SMEM)


def params():
    return pltpu.CompilerParams(vmem_limit_bytes=32 * 1024 * 1024)


def plane_weights(planes, rows_y):
    cells = planes * rows_y
    table = np.zeros((3 * cells, cells), np.float64)
    skipped = (planes - WIDTH) * rows_y
    for x in range(planes):
        for y in range(rows_y):
            out = x * rows_y + y
            for k, weight in enumerate(SIDES, 1):
                for step in (k, -k):
                    table[cells + x * rows_y + (y + step) % rows_y, out] += weight
                    row = cells + (x + step) * rows_y + y
                    table[row - skipped if row < cells else row, out] += weight
    table = -0.5 * table
    high = table.astype(BF16)
    return high, (table - high.astype(np.float64)).astype(BF16)


def split(value):
    high = value.astype(BF16)
    return high, (value - high.astype(jnp.float32)).astype(BF16)


def dot3(left, right, contract):
    dot = lambda x, y: lax.dot_general(x, y, (contract, ((), ())), preferred_element_type=jnp.float32)
    return dot(left[0], right[0]) + (dot(left[0], right[1]) + dot(left[1], right[0]))


def pack_kernel(blocks, x_hbm, *refs):
    *t_refs, turned, x_ref, sems = refs
    count, _, rows_z = x_ref.shape
    chunks = sems.shape[0]
    per = count // chunks
    copies = [
        pltpu.make_async_copy(x_hbm.at[pl.ds(i * per, per)], x_ref.at[pl.ds(i * per, per)], sems.at[i])
        for i in range(chunks)
    ]
    for copy in copies:
        copy.start()
    for i, copy in enumerate(copies):
        copy.wait()
        for a in range(i * per, (i + 1) * per):
            turned[pl.ds(a, rows_z, stride=count), :] = x_ref[a].T
    rows = rows_z // blocks * count
    rank = lax.axis_index("orb")
    for m, t_ref in enumerate(t_refs):
        for core in range(2):
            start = pl.multiple_of((rank ^ (2 * m + core)) * rows, rows)
            t_ref[core] = turned[pl.ds(start, rows), :].reshape(t_ref.shape[1:])


def hand_kernel(block_ref, owner_ref, pair_ref, other_ref):
    other_ref[...] = pair_ref[1]


def by_block(refs):
    half = len(refs) // 2
    return [refs[half + k // 2] if k % 2 else refs[k // 2].at[0] for k in range(2 * half)]


def squeeze(value):
    rows, wide = value.shape
    quarter, free = rows // 4, wide // 4
    lane = lax.broadcasted_iota(jnp.int32, (quarter, wide), 1)
    rest = value[3 * quarter :]
    parts = []
    for j in range(3):
        moved = pltpu.roll(rest, (3 - j) * free, 1)
        parts.append(jnp.where(lane < 3 * free, value[j * quarter : (j + 1) * quarter], moved))
    return jnp.concatenate(parts, axis=0)


def expand(value):
    rows, wide = value.shape
    quarter, free = rows // 3, wide // 4
    lane = lax.broadcasted_iota(jnp.int32, (quarter, wide), 1)
    rest = value[:quarter]
    for j in range(3):
        moved = pltpu.roll(value[j * quarter : (j + 1) * quarter], (j + 1) * free, 1)
        rest = jnp.where((lane >= j * free) & (lane < (j + 1) * free), moved, rest)
    return jnp.concatenate([value, rest], axis=0)


def pick_kernel(block_ref, *refs):
    x_refs, (act_ref, near_ref, far_ref, first_ref, last_ref) = by_block(refs[:-5]), refs[-5:]
    slab, nb, cells = act_ref.shape
    rank = lax.axis_index("orb")
    for k, x_ref in enumerate(x_refs):
        @pl.when((rank ^ block_ref[0]) == k)
        def _(x_ref=x_ref):
            act_ref[...] = x_ref[...]
    odd = rank % 2
    near_ref[...] = act_ref[pl.ds((1 - odd) * (slab - WIDTH), WIDTH)]
    far_ref[...] = act_ref[pl.ds(odd * (slab - WIDTH), WIDTH)]
    flat = act_ref[...].reshape(slab * nb, cells)
    first_ref[...] = squeeze(flat)
    last_ref[...] = squeeze(pltpu.roll(flat, 3 * (cells // 4), 1))


def split_kernel(*refs):
    x_refs, (high_ref, low_ref) = by_block(refs[:-2]), refs[-2:]
    slab, nb, cells = x_refs[0].shape
    rank = lax.axis_index("orb")
    for k, x_ref in enumerate(x_refs):
        rows = pl.ds(pl.multiple_of((rank ^ k) * nb, nb), nb)
        for z in range(slab):
            high, low = split(x_ref[z])
            high_ref[rows, z * cells : (z + 1) * cells] = high
            low_ref[rows, z * cells : (z + 1) * cells] = low


def project_kernel(
    volume, owner_ref, rot_ref, xh_ref, xl_ref, act_ref, near_ref, far_ref, xb_ref, xa_ref, v_ref, wh_ref, wl_ref,
    a_ref, p_ref, turned, tall,
):
    slab, nb, cells = act_ref.shape
    turned[...] = v_ref[...].T
    rank = lax.axis_index("orb")
    mine = pl.ds(pl.multiple_of(rank * slab, slab), slab)
    act = act_ref[...]
    wide = jnp.concatenate([expand(xb_ref[...]), act.reshape(slab * nb, cells), expand(xa_ref[...])], axis=1)
    applied = dot3(split(wide), (wh_ref[...], wl_ref[...]), ((1,), (0,))).reshape(slab, nb, cells)
    applied = applied + (turned[mine, :][:, None, :] - 1.5 * CENTER) * act
    odd = rank % 2
    tall[pl.ds((1 - odd) * (slab + WIDTH), WIDTH)] = near_ref[...]
    tall[pl.ds(odd * (slab + WIDTH), WIDTH)] = far_ref[...]
    tall[WIDTH : WIDTH + slab] = act
    for k, weight in enumerate(SIDES, 1):
        upper = tall[WIDTH + k : WIDTH + k + slab]
        lower = tall[WIDTH - k : WIDTH - k + slab]
        applied = applied + (-0.5 * weight) * (upper + lower)
    a_ref[...] = applied
    flat = jnp.concatenate([applied[z] for z in range(slab)], axis=1)
    total = dot3(split(flat), (xh_ref[...], xl_ref[...]), ((1,), (1,)))
    p_ref[:nb] = total * volume
    sender = (rank == owner_ref[0]) & (lax.axis_index("dom") == 0)
    p_ref[nb:] = jnp.where(sender, rot_ref[...], 0.0)


def remove_kernel(xh_ref, xl_ref, a_ref, p_ref, g_ref):
    slab, nb, cells = a_ref.shape
    removed = dot3(split(p_ref[...]), (xh_ref[...], xl_ref[...]), ((1,), (0,)))
    for z in range(slab):
        g_ref[z] = a_ref[z] - removed[:, z * cells : (z + 1) * cells]


def update_kernel(blocks, panel_ref, x_ref, *refs):
    g_refs, (grad_hbm, out_hbm, whole, grad, out, sems) = refs[:blocks], refs[blocks:]
    nb, cells, rows_z = x_ref.shape
    rank = lax.axis_index("orb")
    share = rows_z // blocks * nb
    for k in range(blocks):
        at = pl.ds(pl.multiple_of((rank ^ k) * share, share), share)
        whole[at, :] = g_refs[k][...].reshape(share, cells)
    chunks = sems.shape[1]
    per = nb // chunks
    rows = 64
    copies = []
    for i in range(chunks):
        for c in range(i * per, (i + 1) * per):
            grad[c] = whole[pl.ds(c, rows_z, stride=nb), :].T
        part = pl.ds(i * per, per)
        copies.append(pltpu.make_async_copy(grad.at[part], grad_hbm.at[part], sems.at[0, i]))
        copies[-1].start()
    for i in range(chunks):
        group = range(i * per, (i + 1) * per)

        @pl.loop(0, cells // rows)
        def _(step, group=group):
            at = pl.ds(pl.multiple_of(step * rows, rows), rows)
            totals = [x_ref[a, at] for a in group]
            for c in range(nb):
                value = grad[c, at]
                totals = [total + panel_ref[c, rank * nb + a] * value for a, total in zip(group, totals)]
            for a, total in zip(group, totals):
                out[a, at] = total

        part = pl.ds(i * per, per)
        copies.append(pltpu.make_async_copy(out.at[part], out_hbm.at[part], sems.at[1, i]))
        copies[-1].start()
    for copy in copies:
        copy.wait()


def swap(value, axis, k):
    count = lax.axis_size(axis)
    return lax.ppermute(value, axis, [(i, i ^ k) for i in range(count)])


def total_over_all(value):
    doms, blocks = lax.axis_size("dom"), lax.axis_size("orb")
    for axis, steps in (("orb", (1,)), ("dom", range(1, doms)), ("orb", range(2, blocks, 2))):
        value = sum([swap(value, axis, k) for k in steps], value)
    return value


def per_device(orbitals, potential, rotation, block, owner):
    nb, planes, rows_y, rows_z = orbitals.shape
    blocks, doms = lax.axis_size("orb"), lax.axis_size("dom")
    cells = planes * rows_y
    slab = rows_z // blocks
    volume = 1.0 / (cells * doms * rows_z)
    f32 = jnp.float32
    shape = lambda *dims: jax.ShapeDtypeStruct(dims, f32)
    piece, edge = shape(slab, nb, cells), shape(WIDTH, nb, cells)

    flat = orbitals.reshape(nb, cells, rows_z)
    held = pltpu.with_memory_space_constraint(flat, pltpu.HBM)
    chips = blocks // 2
    pieces = pl.pallas_call(
        functools.partial(pack_kernel, blocks),
        out_shape=[shape(2, slab, nb, cells)] * chips,
        in_specs=[HBM],
        out_specs=[VMEM] * chips,
        scratch_shapes=[
            pltpu.VMEM((rows_z * nb, cells), f32),
            pltpu.VMEM((nb, cells, rows_z), f32),
            pltpu.SemaphoreType.DMA((CHUNKS,)),
        ],
        compiler_params=params(),
        name="pack",
    )(held)
    pairs = [swap(value, "orb", 2 * m) if m else value for m, value in enumerate(pieces)]
    nearest = pl.pallas_call(
        hand_kernel,
        out_shape=piece,
        in_specs=[SMEM, SMEM, VMEM],
        out_specs=VMEM,
        compiler_params=params(),
        name="hand",
    )(block, owner, pairs[1])
    others = [nearest if m == 1 else value[1] for m, value in enumerate(pairs)]
    spread = pairs + [swap(value, "orb", 1) for value in others]

    side = shape(3 * slab * nb // 4, cells)
    active, near, far, first, last = pl.pallas_call(
        pick_kernel,
        out_shape=(piece, edge, edge, side, side),
        in_specs=[SMEM] + [VMEM] * len(spread),
        out_specs=[VMEM] * 5,
        compiler_params=params(),
        name="pick",
    )(block, *spread)

    up = lambda count: [(i, (i + 1) % count) for i in range(count)]
    down = lambda count: [(i, (i - 1) % count) for i in range(count)]
    x_before = lax.ppermute(last, "dom", up(doms))
    x_after = lax.ppermute(first, "dom", down(doms))
    z_near = swap(near, "orb", 1)
    z_far = lax.ppermute(far, "orb", [(o, (o + 2 * (o % 2) - 1) % blocks) for o in range(blocks)])

    halves = jax.ShapeDtypeStruct((blocks * nb, slab * cells), BF16)
    parts = pl.pallas_call(
        split_kernel,
        out_shape=(halves, halves),
        in_specs=[VMEM] * len(spread),
        out_specs=(VMEM, VMEM),
        compiler_params=params(),
        cost_estimate=pl.CostEstimate(flops=3 * blocks * nb * slab * cells, bytes_accessed=0, transcendentals=0),
        name="split",
    )(*spread)

    weights = [jnp.asarray(w) for w in plane_weights(planes, rows_y)]
    applied, part = pl.pallas_call(
        functools.partial(project_kernel, volume),
        out_shape=(piece, shape(2 * nb, blocks * nb)),
        in_specs=[SMEM] + [VMEM] * 11,
        out_specs=(VMEM, VMEM),
        scratch_shapes=[pltpu.VMEM((rows_z, cells), f32), pltpu.VMEM((slab + 2 * WIDTH, nb, cells), f32)],
        compiler_params=params(),
        name="project",
    )(owner, rotation, *parts, active, z_near, z_far, x_before, x_after, potential.reshape(cells, rows_z), *weights)

    summed = total_over_all(part)
    proj, panel = summed[:nb], summed[nb:]

    own = pl.pallas_call(
        remove_kernel,
        out_shape=piece,
        in_specs=[VMEM] * 4,
        out_specs=VMEM,
        compiler_params=params(),
        name="remove",
    )(*parts, applied, proj)

    gathered = [own] + [None] * (blocks - 1)
    for k in range(2, blocks, 2):
        gathered[k] = swap(own, "orb", k)
    for k in range(0, blocks, 2):
        gathered[k + 1] = swap(gathered[k], "orb", 1)

    gradient, updated = pl.pallas_call(
        functools.partial(update_kernel, blocks),
        out_shape=(shape(nb, cells, rows_z), shape(nb, cells, rows_z)),
        in_specs=[SMEM, VMEM] + [VMEM] * blocks,
        out_specs=(HBM, HBM),
        scratch_shapes=[
            pltpu.VMEM((rows_z * nb, cells), f32),
            pltpu.VMEM((nb, cells, rows_z), f32),
            pltpu.VMEM((nb, cells, rows_z), f32),
            pltpu.SemaphoreType.DMA((2, CHUNKS)),
        ],
        compiler_params=params(),
        name="update",
    )(panel, flat, *gathered)
    return gradient.reshape(orbitals.shape), updated.reshape(orbitals.shape)


def solution(mesh):
    in_specs = (P("orb", "dom", None, None), P("dom", None, None), P("orb", None), P(), P())
    out_specs = (P(None, "dom", None, None), P("orb", "dom", None, None))
    return jax.shard_map(
        per_device, mesh=mesh, in_specs=in_specs, out_specs=out_specs, check_vma=False
    )
```

```python
import functools

import jax
import jax.numpy as jnp
import numpy as np
from jax import lax
from jax.experimental import pallas as pl
from jax.experimental.pallas import tpu as pltpu
from jax.sharding import PartitionSpec as P

CENTER = -5369.0 / 1800.0
SIDES = (12.0 / 7.0, -15.0 / 56.0, 10.0 / 189.0, -1.0 / 112.0, 2.0 / 1925.0, -1.0 / 16632.0)
WIDTH = 6
CHUNKS = 4
BF16 = jnp.bfloat16
VMEM = pl.BlockSpec(memory_space=pltpu.VMEM)
HBM = pl.BlockSpec(memory_space=pltpu.HBM)
SMEM = pl.BlockSpec(memory_space=pltpu.SMEM)


def params():
    return pltpu.CompilerParams(vmem_limit_bytes=32 * 1024 * 1024)


def plane_weights(planes, rows_y):
    cells = planes * rows_y
    table = np.zeros((3 * cells, cells), np.float64)
    skipped = (planes - WIDTH) * rows_y
    for x in range(planes):
        for y in range(rows_y):
            out = x * rows_y + y
            for k, weight in enumerate(SIDES, 1):
                for step in (k, -k):
                    table[cells + x * rows_y + (y + step) % rows_y, out] += weight
                    row = cells + (x + step) * rows_y + y
                    table[row - skipped if row < cells else row, out] += weight
    table = -0.5 * table
    high = table.astype(BF16)
    return high, (table - high.astype(np.float64)).astype(BF16)


def split(value):
    high = value.astype(BF16)
    return high, (value - high.astype(jnp.float32)).astype(BF16)


def dot3(left, right, contract):
    dot = lambda x, y: lax.dot_general(x, y, (contract, ((), ())), preferred_element_type=jnp.float32)
    return dot(left[0], right[0]) + (dot(left[0], right[1]) + dot(left[1], right[0]))


def slab_of(rank, blocks):
    chip = rank // 2
    place = chip // 2 + (chip % 2) * (blocks // 2 - 1 - 2 * (chip // 2))
    return 2 * place + rank % 2


def pack_kernel(blocks, x_hbm, *refs):
    *t_refs, turned, x_ref, sems = refs
    count, _, rows_z = x_ref.shape
    chunks = sems.shape[0]
    per = count // chunks
    copies = [
        pltpu.make_async_copy(x_hbm.at[pl.ds(i * per, per)], x_ref.at[pl.ds(i * per, per)], sems.at[i])
        for i in range(chunks)
    ]
    for i, copy in enumerate(copies):
        copy.start(priority=i % 2)
    for i, copy in enumerate(copies):
        copy.wait()
        for a in range(i * per, (i + 1) * per):
            turned[pl.ds(a, rows_z, stride=count), :] = x_ref[a].T
    rows = rows_z // blocks * count
    rank = lax.axis_index("orb")
    for m, t_ref in enumerate(t_refs):
        for core in range(2):
            start = pl.multiple_of(slab_of(rank ^ (2 * m + core), blocks) * rows, rows)
            t_ref[core] = turned[pl.ds(start, rows), :].reshape(t_ref.shape[1:])


def hand_kernel(block_ref, owner_ref, pair_ref, other_ref):
    other_ref[...] = pair_ref[1]


def by_block(refs):
    half = len(refs) // 2
    return [refs[half + k // 2] if k % 2 else refs[k // 2].at[0] for k in range(2 * half)]


def squeeze(value):
    rows, wide = value.shape
    quarter, free = rows // 4, wide // 4
    lane = lax.broadcasted_iota(jnp.int32, (quarter, wide), 1)
    rest = value[3 * quarter :]
    parts = []
    for j in range(3):
        moved = pltpu.roll(rest, (3 - j) * free, 1)
        parts.append(jnp.where(lane < 3 * free, value[j * quarter : (j + 1) * quarter], moved))
    return jnp.concatenate(parts, axis=0)


def expand(value):
    rows, wide = value.shape
    quarter, free = rows // 3, wide // 4
    lane = lax.broadcasted_iota(jnp.int32, (quarter, wide), 1)
    rest = value[:quarter]
    for j in range(3):
        moved = pltpu.roll(value[j * quarter : (j + 1) * quarter], (j + 1) * free, 1)
        rest = jnp.where((lane >= j * free) & (lane < (j + 1) * free), moved, rest)
    return jnp.concatenate([value, rest], axis=0)


def pick_kernel(block_ref, *refs):
    x_refs, (act_ref, near_ref, far_ref, first_ref, last_ref) = by_block(refs[:-5]), refs[-5:]
    slab, nb, cells = act_ref.shape
    rank = lax.axis_index("orb")
    for k, x_ref in enumerate(x_refs):
        @pl.when((rank ^ block_ref[0]) == k)
        def _(x_ref=x_ref):
            act_ref[...] = x_ref[...]
    odd = rank % 2
    near_ref[...] = act_ref[pl.ds((1 - odd) * (slab - WIDTH), WIDTH)]
    far_ref[...] = act_ref[pl.ds(odd * (slab - WIDTH), WIDTH)]
    flat = act_ref[...].reshape(slab * nb, cells)
    first_ref[...] = squeeze(flat)
    last_ref[...] = squeeze(pltpu.roll(flat, 3 * (cells // 4), 1))


def split_kernel(*refs):
    x_refs, (high_ref, low_ref) = by_block(refs[:-2]), refs[-2:]
    slab, nb, cells = x_refs[0].shape
    rank = lax.axis_index("orb")
    for k, x_ref in enumerate(x_refs):
        rows = pl.ds(pl.multiple_of((rank ^ k) * nb, nb), nb)
        for z in range(slab):
            high, low = split(x_ref[z])
            high_ref[rows, z * cells : (z + 1) * cells] = high
            low_ref[rows, z * cells : (z + 1) * cells] = low


def project_kernel(
    blocks, volume, owner_ref, rot_ref, xh_ref, xl_ref, act_ref, near_ref, far_ref, xb_ref, xa_ref, v_ref, wh_ref, wl_ref,
    a_ref, p_ref, turned, tall,
):
    slab, nb, cells = act_ref.shape
    turned[...] = v_ref[...].T
    rank = lax.axis_index("orb")
    mine = pl.ds(pl.multiple_of(slab_of(rank, blocks) * slab, slab), slab)
    act = act_ref[...]
    wide = jnp.concatenate([expand(xb_ref[...]), act.reshape(slab * nb, cells), expand(xa_ref[...])], axis=1)
    applied = dot3(split(wide), (wh_ref[...], wl_ref[...]), ((1,), (0,))).reshape(slab, nb, cells)
    applied = applied + (turned[mine, :][:, None, :] - 1.5 * CENTER) * act
    odd = rank % 2
    tall[pl.ds((1 - odd) * (slab + WIDTH), WIDTH)] = near_ref[...]
    tall[pl.ds(odd * (slab + WIDTH), WIDTH)] = far_ref[...]
    tall[WIDTH : WIDTH + slab] = act
    for k, weight in enumerate(SIDES, 1):
        upper = tall[WIDTH + k : WIDTH + k + slab]
        lower = tall[WIDTH - k : WIDTH - k + slab]
        applied = applied + (-0.5 * weight) * (upper + lower)
    a_ref[...] = applied
    flat = jnp.concatenate([applied[z] for z in range(slab)], axis=1)
    total = dot3(split(flat), (xh_ref[...], xl_ref[...]), ((1,), (1,)))
    p_ref[:nb] = total * volume
    sender = (rank == owner_ref[0]) & (lax.axis_index("dom") == 0)
    p_ref[nb:] = jnp.where(sender, rot_ref[...], 0.0)


def remove_kernel(xh_ref, xl_ref, a_ref, p_ref, g_ref):
    slab, nb, cells = a_ref.shape
    removed = dot3(split(p_ref[...]), (xh_ref[...], xl_ref[...]), ((1,), (0,)))
    for z in range(slab):
        g_ref[z] = a_ref[z] - removed[:, z * cells : (z + 1) * cells]


def update_kernel(blocks, panel_ref, x_ref, *refs):
    g_refs, (grad_hbm, out_hbm, whole, grad, out, sems) = refs[:blocks], refs[blocks:]
    nb, cells, rows_z = x_ref.shape
    rank = lax.axis_index("orb")
    share = rows_z // blocks * nb
    for k in range(blocks):
        at = pl.ds(pl.multiple_of(slab_of(rank ^ k, blocks) * share, share), share)
        whole[at, :] = g_refs[k][...].reshape(share, cells)
    chunks = sems.shape[1]
    per = nb // chunks
    rows = 64
    copies = []
    for i in range(chunks):
        for c in range(i * per, (i + 1) * per):
            grad[c] = whole[pl.ds(c, rows_z, stride=nb), :].T
        part = pl.ds(i * per, per)
        copies.append(pltpu.make_async_copy(grad.at[part], grad_hbm.at[part], sems.at[0, i]))
        copies[-1].start(priority=i % 2)
    for i in range(chunks):
        group = range(i * per, (i + 1) * per)

        @pl.loop(0, cells // rows)
        def _(step, group=group):
            at = pl.ds(pl.multiple_of(step * rows, rows), rows)
            totals = [x_ref[a, at] for a in group]
            for c in range(nb):
                value = grad[c, at]
                totals = [total + panel_ref[c, rank * nb + a] * value for a, total in zip(group, totals)]
            for a, total in zip(group, totals):
                out[a, at] = total

        part = pl.ds(i * per, per)
        copies.append(pltpu.make_async_copy(out.at[part], out_hbm.at[part], sems.at[1, i]))
        copies[-1].start(priority=i % 2)
    for copy in copies:
        copy.wait()


def swap(value, axis, k):
    count = lax.axis_size(axis)
    return lax.ppermute(value, axis, [(i, i ^ k) for i in range(count)])


def total_over_all(value):
    value = value + swap(value, "orb", 1)
    value = sum([swap(value, "dom", k) for k in range(1, lax.axis_size("dom"))], value)
    for bit in range(1, (lax.axis_size("orb") - 1).bit_length()):
        value = value + swap(value, "orb", 1 << bit)
    return value


def per_device(orbitals, potential, rotation, block, owner):
    nb, planes, rows_y, rows_z = orbitals.shape
    blocks, doms = lax.axis_size("orb"), lax.axis_size("dom")
    cells = planes * rows_y
    slab = rows_z // blocks
    volume = 1.0 / (cells * doms * rows_z)
    f32 = jnp.float32
    shape = lambda *dims: jax.ShapeDtypeStruct(dims, f32)
    piece, edge = shape(slab, nb, cells), shape(WIDTH, nb, cells)

    flat = orbitals.reshape(nb, cells, rows_z)
    held = pltpu.with_memory_space_constraint(flat, pltpu.HBM)
    chips = blocks // 2
    pieces = pl.pallas_call(
        functools.partial(pack_kernel, blocks),
        out_shape=[shape(2, slab, nb, cells)] * chips,
        in_specs=[HBM],
        out_specs=[VMEM] * chips,
        scratch_shapes=[
            pltpu.VMEM((rows_z * nb, cells), f32),
            pltpu.VMEM((nb, cells, rows_z), f32),
            pltpu.SemaphoreType.DMA((CHUNKS,)),
        ],
        compiler_params=params(),
        name="pack",
    )(held)
    pairs = [swap(value, "orb", 2 * m) if m else value for m, value in enumerate(pieces)]
    nearest = pl.pallas_call(
        hand_kernel,
        out_shape=piece,
        in_specs=[SMEM, SMEM, VMEM],
        out_specs=VMEM,
        compiler_params=params(),
        name="hand",
    )(block, owner, pairs[1])
    others = [nearest if m == 1 else value[1] for m, value in enumerate(pairs)]
    spread = pairs + [swap(value, "orb", 1) for value in others]

    side = shape(3 * slab * nb // 4, cells)
    active, near, far, first, last = pl.pallas_call(
        pick_kernel,
        out_shape=(piece, edge, edge, side, side),
        in_specs=[SMEM] + [VMEM] * len(spread),
        out_specs=[VMEM] * 5,
        compiler_params=params(),
        name="pick",
    )(block, *spread)

    up = lambda count: [(i, (i + 1) % count) for i in range(count)]
    down = lambda count: [(i, (i - 1) % count) for i in range(count)]
    x_before = lax.ppermute(last, "dom", up(doms))
    x_after = lax.ppermute(first, "dom", down(doms))
    z_near = swap(near, "orb", 1)
    holder = {slab_of(o, blocks): o for o in range(blocks)}
    z_far = lax.ppermute(far, "orb", [(holder[q], holder[(q + 2 * (q % 2) - 1) % blocks]) for q in range(blocks)])

    halves = jax.ShapeDtypeStruct((blocks * nb, slab * cells), BF16)
    parts = pl.pallas_call(
        split_kernel,
        out_shape=(halves, halves),
        in_specs=[VMEM] * len(spread),
        out_specs=(VMEM, VMEM),
        compiler_params=params(),
        cost_estimate=pl.CostEstimate(flops=3 * blocks * nb * slab * cells, bytes_accessed=0, transcendentals=0),
        name="split",
    )(*spread)

    weights = [jnp.asarray(w) for w in plane_weights(planes, rows_y)]
    applied, part = pl.pallas_call(
        functools.partial(project_kernel, blocks, volume),
        out_shape=(piece, shape(2 * nb, blocks * nb)),
        in_specs=[SMEM] + [VMEM] * 11,
        out_specs=(VMEM, VMEM),
        scratch_shapes=[pltpu.VMEM((rows_z, cells), f32), pltpu.VMEM((slab + 2 * WIDTH, nb, cells), f32)],
        compiler_params=params(),
        name="project",
    )(owner, rotation, *parts, active, z_near, z_far, x_before, x_after, potential.reshape(cells, rows_z), *weights)

    summed = total_over_all(part)
    proj, panel = summed[:nb], summed[nb:]

    own = pl.pallas_call(
        remove_kernel,
        out_shape=piece,
        in_specs=[VMEM] * 4,
        out_specs=VMEM,
        compiler_params=params(),
        name="remove",
    )(*parts, applied, proj)

    gathered = [own] + [None] * (blocks - 1)
    for k in range(2, blocks, 2):
        gathered[k] = swap(own, "orb", k)
    for k in range(0, blocks, 2):
        gathered[k + 1] = swap(gathered[k], "orb", 1)

    gradient, updated = pl.pallas_call(
        functools.partial(update_kernel, blocks),
        out_shape=(shape(nb, cells, rows_z), shape(nb, cells, rows_z)),
        in_specs=[SMEM, VMEM] + [VMEM] * blocks,
        out_specs=(HBM, HBM),
        scratch_shapes=[
            pltpu.VMEM((rows_z * nb, cells), f32),
            pltpu.VMEM((nb, cells, rows_z), f32),
            pltpu.VMEM((nb, cells, rows_z), f32),
            pltpu.SemaphoreType.DMA((2, CHUNKS)),
        ],
        compiler_params=params(),
        name="update",
    )(panel, flat, *gathered)
    return gradient.reshape(orbitals.shape), updated.reshape(orbitals.shape)


def solution(mesh):
    in_specs = (P("orb", "dom", None, None), P("dom", None, None), P("orb", None), P(), P())
    out_specs = (P(None, "dom", None, None), P("orb", "dom", None, None))
    return jax.shard_map(
        per_device, mesh=mesh, in_specs=in_specs, out_specs=out_specs, check_vma=False
    )
```

```python
import functools

import jax
import jax.numpy as jnp
import numpy as np
from jax import lax
from jax.experimental import pallas as pl
from jax.experimental.pallas import tpu as pltpu
from jax.sharding import PartitionSpec as P

CENTER = -5369.0 / 1800.0
SIDES = (12.0 / 7.0, -15.0 / 56.0, 10.0 / 189.0, -1.0 / 112.0, 2.0 / 1925.0, -1.0 / 16632.0)
WIDTH = 6
CHUNKS = 4
BF16 = jnp.bfloat16
VMEM = pl.BlockSpec(memory_space=pltpu.VMEM)
HBM = pl.BlockSpec(memory_space=pltpu.HBM)
SMEM = pl.BlockSpec(memory_space=pltpu.SMEM)


def params():
    return pltpu.CompilerParams(vmem_limit_bytes=32 * 1024 * 1024)


def plane_weights(planes, rows_y):
    cells = planes * rows_y
    table = np.zeros((3 * cells, cells), np.float64)
    skipped = (planes - WIDTH) * rows_y
    for x in range(planes):
        for y in range(rows_y):
            out = x * rows_y + y
            for k, weight in enumerate(SIDES, 1):
                for step in (k, -k):
                    table[cells + x * rows_y + (y + step) % rows_y, out] += weight
                    row = cells + (x + step) * rows_y + y
                    table[row - skipped if row < cells else row, out] += weight
    table = -0.5 * table
    high = table.astype(BF16)
    return high, (table - high.astype(np.float64)).astype(BF16)


def split(value):
    high = value.astype(BF16)
    return high, (value - high.astype(jnp.float32)).astype(BF16)


def dot3(left, right, contract):
    dot = lambda x, y: lax.dot_general(x, y, (contract, ((), ())), preferred_element_type=jnp.float32)
    return dot(left[0], right[0]) + (dot(left[0], right[1]) + dot(left[1], right[0]))


def pack_kernel(blocks, x_hbm, *refs):
    *t_refs, turned, x_ref, sems = refs
    count, _, rows_z = x_ref.shape
    chunks = sems.shape[0]
    per = count // chunks
    copies = [
        pltpu.make_async_copy(x_hbm.at[pl.ds(i * per, per)], x_ref.at[pl.ds(i * per, per)], sems.at[i])
        for i in range(chunks)
    ]
    for copy in copies:
        copy.start()
    for i, copy in enumerate(copies):
        copy.wait()
        for a in range(i * per, (i + 1) * per):
            turned[pl.ds(a, rows_z, stride=count), :] = x_ref[a].T
    rows = rows_z // blocks * count
    rank = lax.axis_index("orb")
    for m, t_ref in enumerate(t_refs):
        for core in range(2):
            start = pl.multiple_of((rank ^ (2 * m + core)) * rows, rows)
            t_ref[core] = turned[pl.ds(start, rows), :].reshape(t_ref.shape[1:])


def hand_kernel(block_ref, owner_ref, pair_ref, other_ref):
    other_ref[...] = pair_ref[1]


def by_block(refs):
    half = len(refs) // 2
    return [refs[half + k // 2] if k % 2 else refs[k // 2].at[0] for k in range(2 * half)]


def squeeze(value):
    rows, wide = value.shape
    quarter, free = rows // 4, wide // 4
    lane = lax.broadcasted_iota(jnp.int32, (quarter, wide), 1)
    rest = value[3 * quarter :]
    parts = []
    for j in range(3):
        moved = pltpu.roll(rest, (3 - j) * free, 1)
        parts.append(jnp.where(lane < 3 * free, value[j * quarter : (j + 1) * quarter], moved))
    return jnp.concatenate(parts, axis=0)


def expand(value):
    rows, wide = value.shape
    quarter, free = rows // 3, wide // 4
    lane = lax.broadcasted_iota(jnp.int32, (quarter, wide), 1)
    rest = value[:quarter]
    for j in range(3):
        moved = pltpu.roll(value[j * quarter : (j + 1) * quarter], (j + 1) * free, 1)
        rest = jnp.where((lane >= j * free) & (lane < (j + 1) * free), moved, rest)
    return jnp.concatenate([value, rest], axis=0)


def pick_kernel(block_ref, *refs):
    x_refs, (act_ref, near_ref, far_ref, first_ref, last_ref) = by_block(refs[:-5]), refs[-5:]
    slab, nb, cells = act_ref.shape
    rank = lax.axis_index("orb")
    for k, x_ref in enumerate(x_refs):
        @pl.when((rank ^ block_ref[0]) == k)
        def _(x_ref=x_ref):
            act_ref[...] = x_ref[...]
    odd = rank % 2
    near_ref[...] = act_ref[pl.ds((1 - odd) * (slab - WIDTH), WIDTH)]
    far_ref[...] = act_ref[pl.ds(odd * (slab - WIDTH), WIDTH)]
    flat = act_ref[...].reshape(slab * nb, cells)
    first_ref[...] = squeeze(flat)
    last_ref[...] = squeeze(pltpu.roll(flat, 3 * (cells // 4), 1))


def split_kernel(*refs):
    x_refs, (high_ref, low_ref) = by_block(refs[:-2]), refs[-2:]
    slab, nb, cells = x_refs[0].shape
    rank = lax.axis_index("orb")
    for k, x_ref in enumerate(x_refs):
        rows = pl.ds(pl.multiple_of((rank ^ k) * nb, nb), nb)
        for z in range(slab):
            high, low = split(x_ref[z])
            high_ref[rows, z * cells : (z + 1) * cells] = high
            low_ref[rows, z * cells : (z + 1) * cells] = low


def project_kernel(
    volume, owner_ref, rot_ref, xh_ref, xl_ref, act_ref, near_ref, far_ref, xb_ref, xa_ref, v_ref, wh_ref, wl_ref,
    a_ref, p_ref, turned, tall,
):
    slab, nb, cells = act_ref.shape
    turned[...] = v_ref[...].T
    rank = lax.axis_index("orb")
    mine = pl.ds(pl.multiple_of(rank * slab, slab), slab)
    act = act_ref[...]
    wide = jnp.concatenate([expand(xb_ref[...]), act.reshape(slab * nb, cells), expand(xa_ref[...])], axis=1)
    applied = dot3(split(wide), (wh_ref[...], wl_ref[...]), ((1,), (0,))).reshape(slab, nb, cells)
    applied = applied + (turned[mine, :][:, None, :] - 1.5 * CENTER) * act
    odd = rank % 2
    tall[pl.ds((1 - odd) * (slab + WIDTH), WIDTH)] = near_ref[...]
    tall[pl.ds(odd * (slab + WIDTH), WIDTH)] = far_ref[...]
    tall[WIDTH : WIDTH + slab] = act
    for k, weight in enumerate(SIDES, 1):
        upper = tall[WIDTH + k : WIDTH + k + slab]
        lower = tall[WIDTH - k : WIDTH - k + slab]
        applied = applied + (-0.5 * weight) * (upper + lower)
    a_ref[...] = applied
    flat = jnp.concatenate([applied[z] for z in range(slab)], axis=1)
    total = dot3(split(flat), (xh_ref[...], xl_ref[...]), ((1,), (1,)))
    p_ref[:nb] = total * volume
    sender = (rank == owner_ref[0]) & (lax.axis_index("dom") == 0)
    p_ref[nb:] = jnp.where(sender, rot_ref[...], 0.0)


def remove_kernel(xh_ref, xl_ref, a_ref, p_ref, g_ref):
    slab, nb, cells = a_ref.shape
    removed = dot3(split(p_ref[...]), (xh_ref[...], xl_ref[...]), ((1,), (0,)))
    for z in range(slab):
        g_ref[z] = a_ref[z] - removed[:, z * cells : (z + 1) * cells]


def update_kernel(blocks, panel_ref, x_ref, *refs):
    g_refs, (grad_hbm, out_hbm, whole, grad, out, sems) = refs[:blocks], refs[blocks:]
    nb, cells, rows_z = x_ref.shape
    rank = lax.axis_index("orb")
    share = rows_z // blocks * nb
    for k in range(blocks):
        at = pl.ds(pl.multiple_of((rank ^ k) * share, share), share)
        whole[at, :] = g_refs[k][...].reshape(share, cells)
    chunks = sems.shape[1]
    per = nb // chunks
    rows = 64
    copies = []
    for i in range(chunks):
        for c in range(i * per, (i + 1) * per):
            grad[c] = whole[pl.ds(c, rows_z, stride=nb), :].T
        part = pl.ds(i * per, per)
        copies.append(pltpu.make_async_copy(grad.at[part], grad_hbm.at[part], sems.at[0, i]))
        copies[-1].start()
    for i in range(chunks):
        group = range(i * per, (i + 1) * per)

        @pl.loop(0, cells // rows)
        def _(step, group=group):
            at = pl.ds(pl.multiple_of(step * rows, rows), rows)
            totals = [x_ref[a, at] for a in group]
            for c in range(nb):
                value = grad[c, at]
                totals = [total + panel_ref[c, rank * nb + a] * value for a, total in zip(group, totals)]
            for a, total in zip(group, totals):
                out[a, at] = total

        part = pl.ds(i * per, per)
        copies.append(pltpu.make_async_copy(out.at[part], out_hbm.at[part], sems.at[1, i]))
        copies[-1].start()
    for copy in copies:
        copy.wait()


def swap(value, axis, k):
    count = lax.axis_size(axis)
    return lax.ppermute(value, axis, [(i, i ^ k) for i in range(count)])


def total_over_all(value):
    doms, blocks = lax.axis_size("dom"), lax.axis_size("orb")
    for axis, steps in (("orb", (1,)), ("dom", range(1, doms)), ("orb", range(2, blocks, 2))):
        value = sum([swap(value, axis, k) for k in steps], value)
    return value


def per_device(orbitals, potential, rotation, block, owner):
    nb, planes, rows_y, rows_z = orbitals.shape
    blocks, doms = lax.axis_size("orb"), lax.axis_size("dom")
    cells = planes * rows_y
    slab = rows_z // blocks
    volume = 1.0 / (cells * doms * rows_z)
    f32 = jnp.float32
    shape = lambda *dims: jax.ShapeDtypeStruct(dims, f32)
    piece, edge = shape(slab, nb, cells), shape(WIDTH, nb, cells)

    flat = orbitals.reshape(nb, cells, rows_z)
    held = pltpu.with_memory_space_constraint(flat, pltpu.HBM)
    chips = blocks // 2
    pieces = pl.pallas_call(
        functools.partial(pack_kernel, blocks),
        out_shape=[shape(2, slab, nb, cells)] * chips,
        in_specs=[HBM],
        out_specs=[VMEM] * chips,
        scratch_shapes=[
            pltpu.VMEM((rows_z * nb, cells), f32),
            pltpu.VMEM((nb, cells, rows_z), f32),
            pltpu.SemaphoreType.DMA((CHUNKS,)),
        ],
        compiler_params=params(),
        name="pack",
    )(held)
    pairs = [swap(value, "orb", 2 * m) if m else value for m, value in enumerate(pieces)]
    nearest = pl.pallas_call(
        hand_kernel,
        out_shape=piece,
        in_specs=[SMEM, SMEM, VMEM],
        out_specs=VMEM,
        compiler_params=params(),
        name="hand",
    )(block, owner, pairs[1])
    others = [nearest if m == 1 else value[1] for m, value in enumerate(pairs)]
    spread = pairs + [swap(value, "orb", 1) for value in others]

    side = shape(3 * slab * nb // 4, cells)
    active, near, far, first, last = pl.pallas_call(
        pick_kernel,
        out_shape=(piece, edge, edge, side, side),
        in_specs=[SMEM] + [VMEM] * len(spread),
        out_specs=[VMEM] * 5,
        compiler_params=params(),
        name="pick",
    )(block, *spread)

    up = lambda count: [(i, (i + 1) % count) for i in range(count)]
    down = lambda count: [(i, (i - 1) % count) for i in range(count)]
    x_before = lax.ppermute(last, "dom", up(doms))
    x_after = lax.ppermute(first, "dom", down(doms))
    z_near = swap(near, "orb", 1)
    z_far = lax.ppermute(far, "orb", [(o, (o + 2 * (o % 2) - 1) % blocks) for o in range(blocks)])

    halves = jax.ShapeDtypeStruct((blocks * nb, slab * cells), BF16)
    parts = pl.pallas_call(
        split_kernel,
        out_shape=(halves, halves),
        in_specs=[VMEM] * len(spread),
        out_specs=(VMEM, VMEM),
        compiler_params=params(),
        cost_estimate=pl.CostEstimate(flops=3 * blocks * nb * slab * cells, bytes_accessed=0, transcendentals=0),
        name="split",
    )(*spread)

    weights = [jnp.asarray(w) for w in plane_weights(planes, rows_y)]
    applied, part = pl.pallas_call(
        functools.partial(project_kernel, volume),
        out_shape=(piece, shape(2 * nb, blocks * nb)),
        in_specs=[SMEM] + [VMEM] * 11,
        out_specs=(VMEM, VMEM),
        scratch_shapes=[pltpu.VMEM((rows_z, cells), f32), pltpu.VMEM((slab + 2 * WIDTH, nb, cells), f32)],
        compiler_params=params(),
        name="project",
    )(owner, rotation, *parts, active, z_near, z_far, x_before, x_after, potential.reshape(cells, rows_z), *weights)

    summed = total_over_all(part)
    proj, panel = summed[:nb], summed[nb:]

    own = pl.pallas_call(
        remove_kernel,
        out_shape=piece,
        in_specs=[VMEM] * 4,
        out_specs=VMEM,
        compiler_params=params(),
        name="remove",
    )(*parts, applied, proj)

    gathered = [own] + [None] * (blocks - 1)
    for k in range(2, blocks, 2):
        top = 1 << (k.bit_length() - 1)
        gathered[k] = swap(own, "orb", k) if k == top else swap(gathered[top], "orb", k - top)
    for k in range(0, blocks, 2):
        gathered[k + 1] = swap(gathered[k], "orb", 1)

    gradient, updated = pl.pallas_call(
        functools.partial(update_kernel, blocks),
        out_shape=(shape(nb, cells, rows_z), shape(nb, cells, rows_z)),
        in_specs=[SMEM, VMEM] + [VMEM] * blocks,
        out_specs=(HBM, HBM),
        scratch_shapes=[
            pltpu.VMEM((rows_z * nb, cells), f32),
            pltpu.VMEM((nb, cells, rows_z), f32),
            pltpu.VMEM((nb, cells, rows_z), f32),
            pltpu.SemaphoreType.DMA((2, CHUNKS)),
        ],
        compiler_params=params(),
        name="update",
    )(panel, flat, *gathered)
    return gradient.reshape(orbitals.shape), updated.reshape(orbitals.shape)


def solution(mesh):
    in_specs = (P("orb", "dom", None, None), P("dom", None, None), P("orb", None), P(), P())
    out_specs = (P(None, "dom", None, None), P("orb", "dom", None, None))
    return jax.shard_map(
        per_device, mesh=mesh, in_specs=in_specs, out_specs=out_specs, check_vma=False
    )
```

```python
import functools

import jax
import jax.numpy as jnp
import numpy as np
from jax import lax
from jax.experimental import pallas as pl
from jax.experimental.pallas import tpu as pltpu
from jax.sharding import PartitionSpec as P

CENTER = -5369.0 / 1800.0
SIDES = (12.0 / 7.0, -15.0 / 56.0, 10.0 / 189.0, -1.0 / 112.0, 2.0 / 1925.0, -1.0 / 16632.0)
WIDTH = 6
CHUNKS = 4
BF16 = jnp.bfloat16
VMEM = pl.BlockSpec(memory_space=pltpu.VMEM)
HBM = pl.BlockSpec(memory_space=pltpu.HBM)
SMEM = pl.BlockSpec(memory_space=pltpu.SMEM)


def params():
    return pltpu.CompilerParams(vmem_limit_bytes=32 * 1024 * 1024)


def plane_weights(planes, rows_y):
    cells = planes * rows_y
    table = np.zeros((3 * cells, cells), np.float64)
    skipped = (planes - WIDTH) * rows_y
    for x in range(planes):
        for y in range(rows_y):
            out = x * rows_y + y
            for k, weight in enumerate(SIDES, 1):
                for step in (k, -k):
                    table[cells + x * rows_y + (y + step) % rows_y, out] += weight
                    row = cells + (x + step) * rows_y + y
                    table[row - skipped if row < cells else row, out] += weight
    table = -0.5 * table
    high = table.astype(BF16)
    return high, (table - high.astype(np.float64)).astype(BF16)


def split(value):
    high = value.astype(BF16)
    return high, (value - high.astype(jnp.float32)).astype(BF16)


def dot3(left, right, contract):
    dot = lambda x, y: lax.dot_general(x, y, (contract, ((), ())), preferred_element_type=jnp.float32)
    return dot(left[0], right[0]) + (dot(left[0], right[1]) + dot(left[1], right[0]))


def pack_kernel(blocks, x_hbm, *refs):
    *t_refs, turned, x_ref, sems = refs
    count, _, rows_z = x_ref.shape
    chunks = sems.shape[0]
    per = count // chunks
    copies = [
        pltpu.make_async_copy(x_hbm.at[pl.ds(i * per, per)], x_ref.at[pl.ds(i * per, per)], sems.at[i])
        for i in range(chunks)
    ]
    for copy in copies:
        copy.start()
    for i, copy in enumerate(copies):
        copy.wait()
        for a in range(i * per, (i + 1) * per):
            turned[pl.ds(a, rows_z, stride=count), :] = x_ref[a].T
    rows = rows_z // blocks * count
    rank = lax.axis_index("orb")
    for m, t_ref in enumerate(t_refs):
        for core in range(2):
            start = pl.multiple_of((rank ^ (2 * m + core)) * rows, rows)
            t_ref[core] = turned[pl.ds(start, rows), :].reshape(t_ref.shape[1:])


def hand_kernel(block_ref, owner_ref, pair_ref, other_ref):
    other_ref[...] = pair_ref[1]


def by_block(refs):
    half = len(refs) // 2 - 1
    return [refs[half + k // 2] if k % 2 else refs[k // 2].at[0] for k in range(2 * half)] + list(refs[2 * half :])


def squeeze(value):
    rows, wide = value.shape
    quarter, free = rows // 4, wide // 4
    lane = lax.broadcasted_iota(jnp.int32, (quarter, wide), 1)
    rest = value[3 * quarter :]
    parts = []
    for j in range(3):
        moved = pltpu.roll(rest, (3 - j) * free, 1)
        parts.append(jnp.where(lane < 3 * free, value[j * quarter : (j + 1) * quarter], moved))
    return jnp.concatenate(parts, axis=0)


def expand(value):
    rows, wide = value.shape
    quarter, free = rows // 3, wide // 4
    lane = lax.broadcasted_iota(jnp.int32, (quarter, wide), 1)
    rest = value[:quarter]
    for j in range(3):
        moved = pltpu.roll(value[j * quarter : (j + 1) * quarter], (j + 1) * free, 1)
        rest = jnp.where((lane >= j * free) & (lane < (j + 1) * free), moved, rest)
    return jnp.concatenate([value, rest], axis=0)


def pick_kernel(block_ref, *refs):
    x_refs, (act_ref, near_ref, far_ref, first_ref, last_ref) = by_block(refs[:-5]), refs[-5:]
    slab, nb, cells = act_ref.shape
    rank = lax.axis_index("orb")
    for k, x_ref in enumerate(x_refs):
        @pl.when((rank ^ block_ref[0]) == k)
        def _(x_ref=x_ref):
            act_ref[...] = x_ref[...]
    odd = rank % 2
    near_ref[...] = act_ref[pl.ds((1 - odd) * (slab - WIDTH), WIDTH)]
    far_ref[...] = act_ref[pl.ds(odd * (slab - WIDTH), WIDTH)]
    flat = act_ref[...].reshape(slab * nb, cells)
    first_ref[...] = squeeze(flat)
    last_ref[...] = squeeze(pltpu.roll(flat, 3 * (cells // 4), 1))


def split_kernel(blocks, act_ref, v_ref, wh_ref, wl_ref, *refs):
    x_refs, (high_ref, low_ref, inner_ref, turned) = by_block(refs[:-4]), refs[-4:]
    slab, nb, cells = act_ref.shape
    rank = lax.axis_index("orb")
    for k, x_ref in enumerate(x_refs):
        rows = pl.ds(pl.multiple_of((rank ^ k) * nb, nb), nb)
        for z in range(slab):
            high, low = split(x_ref[z])
            high_ref[rows, z * cells : (z + 1) * cells] = high
            low_ref[rows, z * cells : (z + 1) * cells] = low
    turned[...] = v_ref[...].T
    mine = pl.ds(pl.multiple_of(rank * slab, slab), slab)
    act = act_ref[...]
    middle = slice(cells, 2 * cells)
    inner = dot3(split(act.reshape(slab * nb, cells)), (wh_ref[middle], wl_ref[middle]), ((1,), (0,)))
    inner = inner.reshape(slab, nb, cells) + (turned[mine, :][:, None, :] - 1.5 * CENTER) * act
    edge = jnp.zeros((WIDTH, nb, cells), jnp.float32)
    tall = jnp.concatenate([edge, act, edge], axis=0)
    for k, weight in enumerate(SIDES, 1):
        upper = tall[WIDTH + k : WIDTH + k + slab]
        lower = tall[WIDTH - k : WIDTH - k + slab]
        inner = inner + (-0.5 * weight) * (upper + lower)
    inner_ref[...] = inner


def project_kernel(
    volume, owner_ref, rot_ref, xh_ref, xl_ref, inner_ref, near_ref, far_ref, xb_ref, xa_ref, wh_ref, wl_ref,
    a_ref, p_ref, around,
):
    slab, nb, cells = inner_ref.shape
    rank = lax.axis_index("orb")
    odd = rank % 2
    around[1 - odd] = near_ref[...]
    around[odd] = far_ref[...]
    before, after = slice(0, cells), slice(2 * cells, 3 * cells)
    applied = dot3(split(expand(xb_ref[...])), (wh_ref[before], wl_ref[before]), ((1,), (0,)))
    applied = applied + dot3(split(expand(xa_ref[...])), (wh_ref[after], wl_ref[after]), ((1,), (0,)))
    a_ref[...] = inner_ref[...] + applied.reshape(slab, nb, cells)
    for z in range(WIDTH):
        below, above = a_ref[z], a_ref[slab - 1 - z]
        for k in range(z + 1, WIDTH + 1):
            below = below + (-0.5 * SIDES[k - 1]) * around[0, WIDTH + z - k]
            above = above + (-0.5 * SIDES[k - 1]) * around[1, k - 1 - z]
        a_ref[z] = below
        a_ref[slab - 1 - z] = above
    flat = jnp.concatenate([a_ref[z] for z in range(slab)], axis=1)
    total = dot3(split(flat), (xh_ref[...], xl_ref[...]), ((1,), (1,)))
    p_ref[:nb] = total * volume
    sender = (rank == owner_ref[0]) & (lax.axis_index("dom") == 0)
    p_ref[nb:] = jnp.where(sender, rot_ref[...], 0.0)


def remove_kernel(xh_ref, xl_ref, a_ref, p_ref, g_ref):
    slab, nb, cells = a_ref.shape
    removed = dot3(split(p_ref[...]), (xh_ref[...], xl_ref[...]), ((1,), (0,)))
    for z in range(slab):
        g_ref[z] = a_ref[z] - removed[:, z * cells : (z + 1) * cells]


def update_kernel(blocks, panel_ref, x_ref, *refs):
    g_refs, (grad_hbm, out_hbm, whole, grad, out, sems) = refs[:blocks], refs[blocks:]
    nb, cells, rows_z = x_ref.shape
    rank = lax.axis_index("orb")
    share = rows_z // blocks * nb
    for k in range(blocks):
        at = pl.ds(pl.multiple_of((rank ^ k) * share, share), share)
        whole[at, :] = g_refs[k][...].reshape(share, cells)
    chunks = sems.shape[1]
    per = nb // chunks
    rows = 64
    copies = []
    for i in range(chunks):
        for c in range(i * per, (i + 1) * per):
            grad[c] = whole[pl.ds(c, rows_z, stride=nb), :].T
        part = pl.ds(i * per, per)
        copies.append(pltpu.make_async_copy(grad.at[part], grad_hbm.at[part], sems.at[0, i]))
        copies[-1].start()
    for i in range(chunks):
        group = range(i * per, (i + 1) * per)

        @pl.loop(0, cells // rows)
        def _(step, group=group):
            at = pl.ds(pl.multiple_of(step * rows, rows), rows)
            totals = [x_ref[a, at] for a in group]
            for c in range(nb):
                value = grad[c, at]
                totals = [total + panel_ref[c, rank * nb + a] * value for a, total in zip(group, totals)]
            for a, total in zip(group, totals):
                out[a, at] = total

        part = pl.ds(i * per, per)
        copies.append(pltpu.make_async_copy(out.at[part], out_hbm.at[part], sems.at[1, i]))
        copies[-1].start()
    for copy in copies:
        copy.wait()


def swap(value, axis, k):
    count = lax.axis_size(axis)
    return lax.ppermute(value, axis, [(i, i ^ k) for i in range(count)])


def total_over_all(value):
    doms, blocks = lax.axis_size("dom"), lax.axis_size("orb")
    for axis, steps in (("orb", (1,)), ("dom", range(1, doms)), ("orb", range(2, blocks, 2))):
        value = sum([swap(value, axis, k) for k in steps], value)
    return value


def per_device(orbitals, potential, rotation, block, owner):
    nb, planes, rows_y, rows_z = orbitals.shape
    blocks, doms = lax.axis_size("orb"), lax.axis_size("dom")
    cells = planes * rows_y
    slab = rows_z // blocks
    volume = 1.0 / (cells * doms * rows_z)
    f32 = jnp.float32
    shape = lambda *dims: jax.ShapeDtypeStruct(dims, f32)
    piece, edge = shape(slab, nb, cells), shape(WIDTH, nb, cells)

    flat = orbitals.reshape(nb, cells, rows_z)
    held = pltpu.with_memory_space_constraint(flat, pltpu.HBM)
    chips = blocks // 2
    pieces = pl.pallas_call(
        functools.partial(pack_kernel, blocks),
        out_shape=[shape(2, slab, nb, cells)] * chips,
        in_specs=[HBM],
        out_specs=[VMEM] * chips,
        scratch_shapes=[
            pltpu.VMEM((rows_z * nb, cells), f32),
            pltpu.VMEM((nb, cells, rows_z), f32),
            pltpu.SemaphoreType.DMA((CHUNKS,)),
        ],
        compiler_params=params(),
        name="pack",
    )(held)
    last = 2 * (chips - 1)
    pairs = [swap(value, "orb", 2 * m) if m else value for m, value in enumerate(pieces[:-1])]
    direct = [swap(pieces[-1][core], "orb", last + core) for core in range(2)]
    nearest = pl.pallas_call(
        hand_kernel,
        out_shape=piece,
        in_specs=[SMEM, SMEM, VMEM],
        out_specs=VMEM,
        compiler_params=params(),
        name="hand",
    )(block, owner, pairs[1])
    others = [nearest if m == 1 else value[1] for m, value in enumerate(pairs)]
    spread = pairs + [swap(value, "orb", 1) for value in others] + direct

    side = shape(3 * slab * nb // 4, cells)
    active, near, far, first, last = pl.pallas_call(
        pick_kernel,
        out_shape=(piece, edge, edge, side, side),
        in_specs=[SMEM] + [VMEM] * len(spread),
        out_specs=[VMEM] * 5,
        compiler_params=params(),
        name="pick",
    )(block, *spread)

    up = lambda count: [(i, (i + 1) % count) for i in range(count)]
    down = lambda count: [(i, (i - 1) % count) for i in range(count)]
    x_before = lax.ppermute(last, "dom", up(doms))
    x_after = lax.ppermute(first, "dom", down(doms))
    z_near = swap(near, "orb", 1)
    z_far = lax.ppermute(far, "orb", [(o, (o + 2 * (o % 2) - 1) % blocks) for o in range(blocks)])

    halves = jax.ShapeDtypeStruct((blocks * nb, slab * cells), BF16)
    weights = [jnp.asarray(w) for w in plane_weights(planes, rows_y)]
    *parts, inner = pl.pallas_call(
        functools.partial(split_kernel, blocks),
        out_shape=(halves, halves, piece),
        in_specs=[VMEM] * (len(spread) + 4),
        out_specs=(VMEM, VMEM, VMEM),
        scratch_shapes=[pltpu.VMEM((rows_z, cells), f32)],
        compiler_params=params(),
        cost_estimate=pl.CostEstimate(flops=3 * blocks * nb * slab * cells, bytes_accessed=0, transcendentals=0),
        name="split",
    )(active, potential.reshape(cells, rows_z), *weights, *spread)

    applied, part = pl.pallas_call(
        functools.partial(project_kernel, volume),
        out_shape=(piece, shape(2 * nb, blocks * nb)),
        in_specs=[SMEM] + [VMEM] * 10,
        out_specs=(VMEM, VMEM),
        scratch_shapes=[pltpu.VMEM((2, WIDTH, nb, cells), f32)],
        compiler_params=params(),
        name="project",
    )(owner, rotation, *parts, inner, z_near, z_far, x_before, x_after, *weights)

    summed = total_over_all(part)
    proj, panel = summed[:nb], summed[nb:]

    own = pl.pallas_call(
        remove_kernel,
        out_shape=piece,
        in_specs=[VMEM] * 4,
        out_specs=VMEM,
        compiler_params=params(),
        name="remove",
    )(*parts, applied, proj)

    gathered = [own] + [None] * (blocks - 1)
    for k in range(2, blocks, 2):
        gathered[k] = swap(own, "orb", k)
    for k in range(0, blocks, 2):
        gathered[k + 1] = swap(gathered[k], "orb", 1)

    gradient, updated = pl.pallas_call(
        functools.partial(update_kernel, blocks),
        out_shape=(shape(nb, cells, rows_z), shape(nb, cells, rows_z)),
        in_specs=[SMEM, VMEM] + [VMEM] * blocks,
        out_specs=(HBM, HBM),
        scratch_shapes=[
            pltpu.VMEM((rows_z * nb, cells), f32),
            pltpu.VMEM((nb, cells, rows_z), f32),
            pltpu.VMEM((nb, cells, rows_z), f32),
            pltpu.SemaphoreType.DMA((2, CHUNKS)),
        ],
        compiler_params=params(),
        name="update",
    )(panel, flat, *gathered)
    return gradient.reshape(orbitals.shape), updated.reshape(orbitals.shape)


def solution(mesh):
    in_specs = (P("orb", "dom", None, None), P("dom", None, None), P("orb", None), P(), P())
    out_specs = (P(None, "dom", None, None), P("orb", "dom", None, None))
    return jax.shard_map(
        per_device, mesh=mesh, in_specs=in_specs, out_specs=out_specs, check_vma=False
    )
```

```python
import functools

import jax
import jax.numpy as jnp
import numpy as np
from jax import lax
from jax.experimental import pallas as pl
from jax.experimental.pallas import tpu as pltpu
from jax.sharding import PartitionSpec as P

CENTER = -5369.0 / 1800.0
SIDES = (12.0 / 7.0, -15.0 / 56.0, 10.0 / 189.0, -1.0 / 112.0, 2.0 / 1925.0, -1.0 / 16632.0)
WIDTH = 6
CHUNKS = 4
MIX = 8
BF16 = jnp.bfloat16
VMEM = pl.BlockSpec(memory_space=pltpu.VMEM)
HBM = pl.BlockSpec(memory_space=pltpu.HBM)
SMEM = pl.BlockSpec(memory_space=pltpu.SMEM)


def params():
    return pltpu.CompilerParams(vmem_limit_bytes=32 * 1024 * 1024)


def plane_weights(planes, rows_y):
    cells = planes * rows_y
    table = np.zeros((3 * cells, cells), np.float64)
    skipped = (planes - WIDTH) * rows_y
    for x in range(planes):
        for y in range(rows_y):
            out = x * rows_y + y
            for k, weight in enumerate(SIDES, 1):
                for step in (k, -k):
                    table[cells + x * rows_y + (y + step) % rows_y, out] += weight
                    row = cells + (x + step) * rows_y + y
                    table[row - skipped if row < cells else row, out] += weight
    table = -0.5 * table
    high = table.astype(BF16)
    return high, (table - high.astype(np.float64)).astype(BF16)


def split(value):
    high = value.astype(BF16)
    return high, (value - high.astype(jnp.float32)).astype(BF16)


def dot3(left, right, contract):
    dot = lambda x, y: lax.dot_general(x, y, (contract, ((), ())), preferred_element_type=jnp.float32)
    return dot(left[0], right[0]) + (dot(left[0], right[1]) + dot(left[1], right[0]))


def pack_kernel(blocks, x_hbm, *refs):
    *t_refs, turned, x_ref, sems = refs
    count, _, rows_z = x_ref.shape
    chunks = sems.shape[0]
    per = count // chunks
    copies = [
        pltpu.make_async_copy(x_hbm.at[pl.ds(i * per, per)], x_ref.at[pl.ds(i * per, per)], sems.at[i])
        for i in range(chunks)
    ]
    for copy in copies:
        copy.start()
    for i, copy in enumerate(copies):
        copy.wait()
        for a in range(i * per, (i + 1) * per):
            turned[pl.ds(a, rows_z, stride=count), :] = x_ref[a].T
    rows = rows_z // blocks * count
    rank = lax.axis_index("orb")
    for m, t_ref in enumerate(t_refs):
        for core in range(2):
            start = pl.multiple_of((rank ^ (2 * m + core)) * rows, rows)
            t_ref[core] = turned[pl.ds(start, rows), :].reshape(t_ref.shape[1:])


def hand_kernel(block_ref, owner_ref, pair_ref, other_ref):
    other_ref[...] = pair_ref[1]


def by_block(refs):
    half = len(refs) // 2 - 1
    return [refs[half + k // 2] if k % 2 else refs[k // 2].at[0] for k in range(2 * half)] + list(refs[2 * half :])


def squeeze(value):
    rows, wide = value.shape
    quarter, free = rows // 4, wide // 4
    lane = lax.broadcasted_iota(jnp.int32, (quarter, wide), 1)
    rest = value[3 * quarter :]
    parts = []
    for j in range(3):
        moved = pltpu.roll(rest, (3 - j) * free, 1)
        parts.append(jnp.where(lane < 3 * free, value[j * quarter : (j + 1) * quarter], moved))
    return jnp.concatenate(parts, axis=0)


def expand(value):
    rows, wide = value.shape
    quarter, free = rows // 3, wide // 4
    lane = lax.broadcasted_iota(jnp.int32, (quarter, wide), 1)
    rest = value[:quarter]
    for j in range(3):
        moved = pltpu.roll(value[j * quarter : (j + 1) * quarter], (j + 1) * free, 1)
        rest = jnp.where((lane >= j * free) & (lane < (j + 1) * free), moved, rest)
    return jnp.concatenate([value, rest], axis=0)


def pick_kernel(block_ref, *refs):
    x_refs, (act_ref, near_ref, far_ref, first_ref, last_ref) = by_block(refs[:-5]), refs[-5:]
    slab, nb, cells = act_ref.shape
    rank = lax.axis_index("orb")
    for k, x_ref in enumerate(x_refs):
        @pl.when((rank ^ block_ref[0]) == k)
        def _(x_ref=x_ref):
            act_ref[...] = x_ref[...]
    odd = rank % 2
    near_ref[...] = act_ref[pl.ds((1 - odd) * (slab - WIDTH), WIDTH)]
    far_ref[...] = act_ref[pl.ds(odd * (slab - WIDTH), WIDTH)]
    flat = act_ref[...].reshape(slab * nb, cells)
    first_ref[...] = squeeze(flat)
    last_ref[...] = squeeze(pltpu.roll(flat, 3 * (cells // 4), 1))


def split_kernel(blocks, act_ref, v_ref, wh_ref, wl_ref, *refs):
    x_refs, (high_ref, low_ref, inner_ref, turned) = by_block(refs[:-4]), refs[-4:]
    slab, nb, cells = act_ref.shape
    rank = lax.axis_index("orb")
    for k, x_ref in enumerate(x_refs):
        rows = pl.ds(pl.multiple_of((rank ^ k) * nb, nb), nb)
        for z in range(slab):
            high, low = split(x_ref[z])
            high_ref[rows, z * cells : (z + 1) * cells] = high
            low_ref[rows, z * cells : (z + 1) * cells] = low
    turned[...] = v_ref[...].T
    mine = pl.ds(pl.multiple_of(rank * slab, slab), slab)
    act = act_ref[...]
    middle = slice(cells, 2 * cells)
    inner = dot3(split(act.reshape(slab * nb, cells)), (wh_ref[middle], wl_ref[middle]), ((1,), (0,)))
    inner = inner.reshape(slab, nb, cells) + (turned[mine, :][:, None, :] - 1.5 * CENTER) * act
    edge = jnp.zeros((WIDTH, nb, cells), jnp.float32)
    tall = jnp.concatenate([edge, act, edge], axis=0)
    for k, weight in enumerate(SIDES, 1):
        upper = tall[WIDTH + k : WIDTH + k + slab]
        lower = tall[WIDTH - k : WIDTH - k + slab]
        inner = inner + (-0.5 * weight) * (upper + lower)
    inner_ref[...] = inner


def project_kernel(
    volume, owner_ref, rot_ref, xh_ref, xl_ref, inner_ref, near_ref, far_ref, xb_ref, xa_ref, wh_ref, wl_ref,
    a_ref, p_ref, around,
):
    slab, nb, cells = inner_ref.shape
    rank = lax.axis_index("orb")
    odd = rank % 2
    around[1 - odd] = near_ref[...]
    around[odd] = far_ref[...]
    before, after = slice(0, cells), slice(2 * cells, 3 * cells)
    applied = dot3(split(expand(xb_ref[...])), (wh_ref[before], wl_ref[before]), ((1,), (0,)))
    applied = applied + dot3(split(expand(xa_ref[...])), (wh_ref[after], wl_ref[after]), ((1,), (0,)))
    a_ref[...] = inner_ref[...] + applied.reshape(slab, nb, cells)
    for z in range(WIDTH):
        below, above = a_ref[z], a_ref[slab - 1 - z]
        for k in range(z + 1, WIDTH + 1):
            below = below + (-0.5 * SIDES[k - 1]) * around[0, WIDTH + z - k]
            above = above + (-0.5 * SIDES[k - 1]) * around[1, k - 1 - z]
        a_ref[z] = below
        a_ref[slab - 1 - z] = above
    flat = jnp.concatenate([a_ref[z] for z in range(slab)], axis=1)
    total = dot3(split(flat), (xh_ref[...], xl_ref[...]), ((1,), (1,)))
    p_ref[:nb] = total * volume
    sender = (rank == owner_ref[0]) & (lax.axis_index("dom") == 0)
    p_ref[nb:] = jnp.where(sender, rot_ref[...], 0.0)


def remove_kernel(xh_ref, xl_ref, a_ref, p_ref, g_ref):
    slab, nb, cells = a_ref.shape
    removed = dot3(split(p_ref[...]), (xh_ref[...], xl_ref[...]), ((1,), (0,)))
    for z in range(slab):
        g_ref[z] = a_ref[z] - removed[:, z * cells : (z + 1) * cells]


def mixing_kernel(panel_ref, high_ref, low_ref):
    nb, size = panel_ref.shape[0], high_ref.shape[0]
    wide = panel_ref.shape[1]
    row, col = (lax.broadcasted_iota(jnp.int32, (size, wide), axis) for axis in (0, 1))
    mine = jnp.where(col == lax.axis_index("orb") * nb + row % nb, 1.0, 0.0).astype(BF16)
    orbital, col = (lax.broadcasted_iota(jnp.int32, (nb, size), axis) for axis in (0, 1))
    repeat = jnp.where(orbital == col % nb, 1.0, 0.0).astype(BF16)
    row, col = (lax.broadcasted_iota(jnp.int32, (size, size), axis) for axis in (0, 1))
    same = row // nb == col // nb
    dot = lambda x, y, axes: lax.dot_general(x, y, (axes, ((), ())), preferred_element_type=jnp.float32)
    for part, ref in zip(split(panel_ref[...]), (high_ref, low_ref)):
        block = dot(mine, part, ((1,), (1,))).astype(BF16)
        ref[...] = jnp.where(same, dot(block, repeat, ((1,), (0,))), 0.0).astype(BF16)


def update_kernel(blocks, wh_ref, wl_ref, x_ref, *refs):
    g_refs, (grad_hbm, out_hbm, whole, grad, mixed, added, out, sems) = refs[:blocks], refs[blocks:]
    nb, cells, rows_z = x_ref.shape
    rank = lax.axis_index("orb")
    share = rows_z // blocks * nb
    for k in range(blocks):
        at = pl.ds(pl.multiple_of((rank ^ k) * share, share), share)
        whole[at, :] = g_refs[k][...].reshape(share, cells)
    per = nb // CHUNKS
    copies = []
    for i in range(CHUNKS):
        for c in range(i * per, (i + 1) * per):
            plane = whole[pl.ds(c, rows_z, stride=nb), :].T
            grad[c] = plane
            mixed[pl.ds(c, cells, stride=nb), :] = plane
        part = pl.ds(i * per, per)
        copies.append(pltpu.make_async_copy(grad.at[part], grad_hbm.at[part], sems.at[0, i]))
        copies[-1].start()
    size = wh_ref.shape[0]
    mix = (wh_ref[...], wl_ref[...])
    rows = cells // CHUNKS
    tall = rows * nb
    for i in range(CHUNKS):
        parts = split(mixed[i * tall : (i + 1) * tall])
        sides = [jnp.concatenate([p[j : j + size] for j in range(0, tall, size)], axis=1) for p in parts]
        result = dot3(mix, sides, ((1,), (0,)))
        for j in range(tall // size):
            added[i * tall + j * size : i * tall + (j + 1) * size] = result[:, j * rows_z : (j + 1) * rows_z]
        some = pl.ds(i * rows, rows)
        for a in range(nb):
            out[a, some] = x_ref[a, some] + added[pl.ds(i * tall + a, rows, stride=nb), :]
        copies.append(pltpu.make_async_copy(out.at[:, some], out_hbm.at[:, some], sems.at[1, i]))
        copies[-1].start()
    for copy in copies:
        copy.wait()


def swap(value, axis, k):
    count = lax.axis_size(axis)
    return lax.ppermute(value, axis, [(i, i ^ k) for i in range(count)])


def total_over_all(value):
    doms, blocks = lax.axis_size("dom"), lax.axis_size("orb")
    for axis, steps in (("orb", (1,)), ("dom", range(1, doms)), ("orb", range(2, blocks, 2))):
        value = sum([swap(value, axis, k) for k in steps], value)
    return value


def per_device(orbitals, potential, rotation, block, owner):
    nb, planes, rows_y, rows_z = orbitals.shape
    blocks, doms = lax.axis_size("orb"), lax.axis_size("dom")
    cells = planes * rows_y
    slab = rows_z // blocks
    volume = 1.0 / (cells * doms * rows_z)
    f32 = jnp.float32
    shape = lambda *dims: jax.ShapeDtypeStruct(dims, f32)
    piece, edge = shape(slab, nb, cells), shape(WIDTH, nb, cells)

    flat = orbitals.reshape(nb, cells, rows_z)
    held = pltpu.with_memory_space_constraint(flat, pltpu.HBM)
    chips = blocks // 2
    pieces = pl.pallas_call(
        functools.partial(pack_kernel, blocks),
        out_shape=[shape(2, slab, nb, cells)] * chips,
        in_specs=[HBM],
        out_specs=[VMEM] * chips,
        scratch_shapes=[
            pltpu.VMEM((rows_z * nb, cells), f32),
            pltpu.VMEM((nb, cells, rows_z), f32),
            pltpu.SemaphoreType.DMA((CHUNKS,)),
        ],
        compiler_params=params(),
        name="pack",
    )(held)
    last = 2 * (chips - 1)
    pairs = [swap(value, "orb", 2 * m) if m else value for m, value in enumerate(pieces[:-1])]
    direct = [swap(pieces[-1][core], "orb", last + core) for core in range(2)]
    nearest = pl.pallas_call(
        hand_kernel,
        out_shape=piece,
        in_specs=[SMEM, SMEM, VMEM],
        out_specs=VMEM,
        compiler_params=params(),
        name="hand",
    )(block, owner, pairs[1])
    others = [nearest if m == 1 else value[1] for m, value in enumerate(pairs)]
    spread = pairs + [swap(value, "orb", 1) for value in others] + direct

    side = shape(3 * slab * nb // 4, cells)
    active, near, far, first, last = pl.pallas_call(
        pick_kernel,
        out_shape=(piece, edge, edge, side, side),
        in_specs=[SMEM] + [VMEM] * len(spread),
        out_specs=[VMEM] * 5,
        compiler_params=params(),
        name="pick",
    )(block, *spread)

    up = lambda count: [(i, (i + 1) % count) for i in range(count)]
    down = lambda count: [(i, (i - 1) % count) for i in range(count)]
    x_before = lax.ppermute(last, "dom", up(doms))
    x_after = lax.ppermute(first, "dom", down(doms))
    z_near = swap(near, "orb", 1)
    z_far = lax.ppermute(far, "orb", [(o, (o + 2 * (o % 2) - 1) % blocks) for o in range(blocks)])

    halves = jax.ShapeDtypeStruct((blocks * nb, slab * cells), BF16)
    weights = [jnp.asarray(w) for w in plane_weights(planes, rows_y)]
    *parts, inner = pl.pallas_call(
        functools.partial(split_kernel, blocks),
        out_shape=(halves, halves, piece),
        in_specs=[VMEM] * (len(spread) + 4),
        out_specs=(VMEM, VMEM, VMEM),
        scratch_shapes=[pltpu.VMEM((rows_z, cells), f32)],
        compiler_params=params(),
        cost_estimate=pl.CostEstimate(flops=3 * blocks * nb * slab * cells, bytes_accessed=0, transcendentals=0),
        name="split",
    )(active, potential.reshape(cells, rows_z), *weights, *spread)

    applied, part = pl.pallas_call(
        functools.partial(project_kernel, volume),
        out_shape=(piece, shape(2 * nb, blocks * nb)),
        in_specs=[SMEM] + [VMEM] * 10,
        out_specs=(VMEM, VMEM),
        scratch_shapes=[pltpu.VMEM((2, WIDTH, nb, cells), f32)],
        compiler_params=params(),
        name="project",
    )(owner, rotation, *parts, inner, z_near, z_far, x_before, x_after, *weights)

    summed = total_over_all(part)
    proj, panel = summed[:nb], summed[nb:]

    own = pl.pallas_call(
        remove_kernel,
        out_shape=piece,
        in_specs=[VMEM] * 4,
        out_specs=VMEM,
        compiler_params=params(),
        name="remove",
    )(*parts, applied, proj)

    gathered = [own] + [None] * (blocks - 1)
    for k in range(2, blocks, 2):
        gathered[k] = swap(own, "orb", k)
    for k in range(0, blocks, 2):
        gathered[k + 1] = swap(gathered[k], "orb", 1)

    square = jax.ShapeDtypeStruct((MIX * nb, MIX * nb), BF16)
    mixing = pl.pallas_call(
        mixing_kernel,
        out_shape=(square, square),
        in_specs=[VMEM],
        out_specs=(VMEM, VMEM),
        compiler_params=params(),
        name="mixing",
    )(panel)

    gradient, updated = pl.pallas_call(
        functools.partial(update_kernel, blocks),
        out_shape=(shape(nb, cells, rows_z), shape(nb, cells, rows_z)),
        in_specs=[VMEM] * (3 + blocks),
        out_specs=(HBM, HBM),
        scratch_shapes=[
            pltpu.VMEM((rows_z * nb, cells), f32),
            pltpu.VMEM((nb, cells, rows_z), f32),
            pltpu.VMEM((cells * nb, rows_z), f32),
            pltpu.VMEM((cells * nb, rows_z), f32),
            pltpu.VMEM((nb, cells, rows_z), f32),
            pltpu.SemaphoreType.DMA((2, CHUNKS)),
        ],
        compiler_params=params(),
        name="update",
    )(*mixing, flat, *gathered)
    return gradient.reshape(orbitals.shape), updated.reshape(orbitals.shape)


def solution(mesh):
    in_specs = (P("orb", "dom", None, None), P("dom", None, None), P("orb", None), P(), P())
    out_specs = (P(None, "dom", None, None), P("orb", "dom", None, None))
    return jax.shard_map(
        per_device, mesh=mesh, in_specs=in_specs, out_specs=out_specs, check_vma=False
    )
```

```python
import functools

import jax
import jax.numpy as jnp
import numpy as np
from jax import lax
from jax.experimental import pallas as pl
from jax.experimental.pallas import tpu as pltpu
from jax.sharding import PartitionSpec as P

CENTER = -5369.0 / 1800.0
SIDES = (12.0 / 7.0, -15.0 / 56.0, 10.0 / 189.0, -1.0 / 112.0, 2.0 / 1925.0, -1.0 / 16632.0)
WIDTH = 6
CHUNKS = 4
MIX = 8
BF16 = jnp.bfloat16
VMEM = pl.BlockSpec(memory_space=pltpu.VMEM)
HBM = pl.BlockSpec(memory_space=pltpu.HBM)
SMEM = pl.BlockSpec(memory_space=pltpu.SMEM)


def params():
    return pltpu.CompilerParams(vmem_limit_bytes=32 * 1024 * 1024)


def plane_weights(planes, rows_y):
    cells = planes * rows_y
    table = np.zeros((3 * cells, cells), np.float64)
    skipped = (planes - WIDTH) * rows_y
    for x in range(planes):
        for y in range(rows_y):
            out = x * rows_y + y
            for k, weight in enumerate(SIDES, 1):
                for step in (k, -k):
                    table[cells + x * rows_y + (y + step) % rows_y, out] += weight
                    row = cells + (x + step) * rows_y + y
                    table[row - skipped if row < cells else row, out] += weight
    table = -0.5 * table
    high = table.astype(BF16)
    return high, (table - high.astype(np.float64)).astype(BF16)


def split(value):
    high = value.astype(BF16)
    return high, (value - high.astype(jnp.float32)).astype(BF16)


def dot3(left, right, contract):
    dot = lambda x, y: lax.dot_general(x, y, (contract, ((), ())), preferred_element_type=jnp.float32)
    return dot(left[0], right[0]) + (dot(left[0], right[1]) + dot(left[1], right[0]))


def pack_kernel(blocks, x_hbm, *refs):
    *t_refs, turned, x_ref, sems = refs
    count, _, rows_z = x_ref.shape
    chunks = sems.shape[0]
    per = count // chunks
    copies = [
        pltpu.make_async_copy(x_hbm.at[pl.ds(i * per, per)], x_ref.at[pl.ds(i * per, per)], sems.at[i])
        for i in range(chunks)
    ]
    for copy in copies:
        copy.start()
    for i, copy in enumerate(copies):
        copy.wait()
        for a in range(i * per, (i + 1) * per):
            turned[pl.ds(a, rows_z, stride=count), :] = x_ref[a].T
    rows = rows_z // blocks * count
    rank = lax.axis_index("orb")
    for m, t_ref in enumerate(t_refs):
        for core in range(2):
            start = pl.multiple_of((rank ^ (2 * m + core)) * rows, rows)
            t_ref[core] = turned[pl.ds(start, rows), :].reshape(t_ref.shape[1:])


def hand_kernel(block_ref, owner_ref, pair_ref, other_ref):
    other_ref[...] = pair_ref[1]


def by_block(refs):
    refs = refs[::-1]
    half = len(refs) // 2 - 1
    return [refs[half + k // 2] if k % 2 else refs[k // 2].at[0] for k in range(2 * half)] + list(refs[2 * half :])


def squeeze(value):
    rows, wide = value.shape
    quarter, free = rows // 4, wide // 4
    lane = lax.broadcasted_iota(jnp.int32, (quarter, wide), 1)
    rest = value[3 * quarter :]
    parts = []
    for j in range(3):
        moved = pltpu.roll(rest, (3 - j) * free, 1)
        parts.append(jnp.where(lane < 3 * free, value[j * quarter : (j + 1) * quarter], moved))
    return jnp.concatenate(parts, axis=0)


def expand(value):
    rows, wide = value.shape
    quarter, free = rows // 3, wide // 4
    lane = lax.broadcasted_iota(jnp.int32, (quarter, wide), 1)
    rest = value[:quarter]
    for j in range(3):
        moved = pltpu.roll(value[j * quarter : (j + 1) * quarter], (j + 1) * free, 1)
        rest = jnp.where((lane >= j * free) & (lane < (j + 1) * free), moved, rest)
    return jnp.concatenate([value, rest], axis=0)


def pick_kernel(block_ref, *refs):
    x_refs, (act_ref, near_ref, far_ref, first_ref, last_ref) = by_block(refs[:-5]), refs[-5:]
    slab, nb, cells = act_ref.shape
    rank = lax.axis_index("orb")
    for k, x_ref in enumerate(x_refs):
        @pl.when((rank ^ block_ref[0]) == k)
        def _(x_ref=x_ref):
            act_ref[...] = x_ref[...]
    odd = rank % 2
    near_ref[...] = act_ref[pl.ds((1 - odd) * (slab - WIDTH), WIDTH)]
    far_ref[...] = act_ref[pl.ds(odd * (slab - WIDTH), WIDTH)]
    flat = act_ref[...].reshape(slab * nb, cells)
    first_ref[...] = squeeze(flat)
    last_ref[...] = squeeze(pltpu.roll(flat, 3 * (cells // 4), 1))


def split_kernel(blocks, act_ref, v_ref, wh_ref, wl_ref, *refs):
    x_refs, (high_ref, low_ref, inner_ref, turned) = by_block(refs[:-4]), refs[-4:]
    slab, nb, cells = act_ref.shape
    rank = lax.axis_index("orb")
    for k, x_ref in enumerate(x_refs):
        rows = pl.ds(pl.multiple_of((rank ^ k) * nb, nb), nb)
        for z in range(slab):
            high, low = split(x_ref[z])
            high_ref[rows, z * cells : (z + 1) * cells] = high
            low_ref[rows, z * cells : (z + 1) * cells] = low
    turned[...] = v_ref[...].T
    mine = pl.ds(pl.multiple_of(rank * slab, slab), slab)
    act = act_ref[...]
    middle = slice(cells, 2 * cells)
    inner = dot3(split(act.reshape(slab * nb, cells)), (wh_ref[middle], wl_ref[middle]), ((1,), (0,)))
    inner = inner.reshape(slab, nb, cells) + (turned[mine, :][:, None, :] - 1.5 * CENTER) * act
    edge = jnp.zeros((WIDTH, nb, cells), jnp.float32)
    tall = jnp.concatenate([edge, act, edge], axis=0)
    for k, weight in enumerate(SIDES, 1):
        upper = tall[WIDTH + k : WIDTH + k + slab]
        lower = tall[WIDTH - k : WIDTH - k + slab]
        inner = inner + (-0.5 * weight) * (upper + lower)
    inner_ref[...] = inner


def project_kernel(
    volume, owner_ref, rot_ref, xh_ref, xl_ref, inner_ref, near_ref, far_ref, xb_ref, xa_ref, wh_ref, wl_ref,
    a_ref, p_ref, around,
):
    slab, nb, cells = inner_ref.shape
    rank = lax.axis_index("orb")
    odd = rank % 2
    around[1 - odd] = near_ref[...]
    around[odd] = far_ref[...]
    before, after = slice(0, cells), slice(2 * cells, 3 * cells)
    applied = dot3(split(expand(xb_ref[...])), (wh_ref[before], wl_ref[before]), ((1,), (0,)))
    applied = applied + dot3(split(expand(xa_ref[...])), (wh_ref[after], wl_ref[after]), ((1,), (0,)))
    a_ref[...] = inner_ref[...] + applied.reshape(slab, nb, cells)
    for z in range(WIDTH):
        below, above = a_ref[z], a_ref[slab - 1 - z]
        for k in range(z + 1, WIDTH + 1):
            below = below + (-0.5 * SIDES[k - 1]) * around[0, WIDTH + z - k]
            above = above + (-0.5 * SIDES[k - 1]) * around[1, k - 1 - z]
        a_ref[z] = below
        a_ref[slab - 1 - z] = above
    flat = jnp.concatenate([a_ref[z] for z in range(slab)], axis=1)
    total = dot3(split(flat), (xh_ref[...], xl_ref[...]), ((1,), (1,)))
    p_ref[:nb] = total * volume
    sender = (rank == owner_ref[0]) & (lax.axis_index("dom") == 0)
    p_ref[nb:] = jnp.where(sender, rot_ref[...], 0.0)


def remove_kernel(xh_ref, xl_ref, a_ref, p_ref, g_ref):
    slab, nb, cells = a_ref.shape
    removed = dot3(split(p_ref[...]), (xh_ref[...], xl_ref[...]), ((1,), (0,)))
    for z in range(slab):
        g_ref[z] = a_ref[z] - removed[:, z * cells : (z + 1) * cells]


def mixing_kernel(panel_ref, high_ref, low_ref):
    nb, size = panel_ref.shape[0], high_ref.shape[0]
    wide = panel_ref.shape[1]
    row, col = (lax.broadcasted_iota(jnp.int32, (size, wide), axis) for axis in (0, 1))
    mine = jnp.where(col == lax.axis_index("orb") * nb + row % nb, 1.0, 0.0).astype(BF16)
    orbital, col = (lax.broadcasted_iota(jnp.int32, (nb, size), axis) for axis in (0, 1))
    repeat = jnp.where(orbital == col % nb, 1.0, 0.0).astype(BF16)
    row, col = (lax.broadcasted_iota(jnp.int32, (size, size), axis) for axis in (0, 1))
    same = row // nb == col // nb
    dot = lambda x, y, axes: lax.dot_general(x, y, (axes, ((), ())), preferred_element_type=jnp.float32)
    for part, ref in zip(split(panel_ref[...]), (high_ref, low_ref)):
        block = dot(mine, part, ((1,), (1,))).astype(BF16)
        ref[...] = jnp.where(same, dot(block, repeat, ((1,), (0,))), 0.0).astype(BF16)


def update_kernel(blocks, wh_ref, wl_ref, x_ref, *refs):
    g_refs, (grad_hbm, out_hbm, whole, grad, mixed, added, out, sems) = refs[:blocks], refs[blocks:]
    nb, cells, rows_z = x_ref.shape
    rank = lax.axis_index("orb")
    share = rows_z // blocks * nb
    for k in range(blocks):
        at = pl.ds(pl.multiple_of((rank ^ k) * share, share), share)
        whole[at, :] = g_refs[-k][...].reshape(share, cells)
    per = nb // CHUNKS
    copies = []
    for i in range(CHUNKS):
        for c in range(i * per, (i + 1) * per):
            plane = whole[pl.ds(c, rows_z, stride=nb), :].T
            grad[c] = plane
            mixed[pl.ds(c, cells, stride=nb), :] = plane
        part = pl.ds(i * per, per)
        copies.append(pltpu.make_async_copy(grad.at[part], grad_hbm.at[part], sems.at[0, i]))
        copies[-1].start()
    size = wh_ref.shape[0]
    mix = (wh_ref[...], wl_ref[...])
    rows = cells // CHUNKS
    tall = rows * nb
    for i in range(CHUNKS):
        parts = split(mixed[i * tall : (i + 1) * tall])
        sides = [jnp.concatenate([p[j : j + size] for j in range(0, tall, size)], axis=1) for p in parts]
        result = dot3(mix, sides, ((1,), (0,)))
        for j in range(tall // size):
            added[i * tall + j * size : i * tall + (j + 1) * size] = result[:, j * rows_z : (j + 1) * rows_z]
        some = pl.ds(i * rows, rows)
        for a in range(nb):
            out[a, some] = x_ref[a, some] + added[pl.ds(i * tall + a, rows, stride=nb), :]
        copies.append(pltpu.make_async_copy(out.at[:, some], out_hbm.at[:, some], sems.at[1, i]))
        copies[-1].start()
    for copy in copies:
        copy.wait()


def swap(value, axis, k):
    count = lax.axis_size(axis)
    return lax.ppermute(value, axis, [(i, i ^ k) for i in range(count)])


def total_over_all(value):
    doms, blocks = lax.axis_size("dom"), lax.axis_size("orb")
    for axis, steps in (("orb", (1,)), ("dom", range(1, doms)), ("orb", range(2, blocks, 2))):
        value = sum([swap(value, axis, k) for k in steps], value)
    return value


def per_device(orbitals, potential, rotation, block, owner):
    nb, planes, rows_y, rows_z = orbitals.shape
    blocks, doms = lax.axis_size("orb"), lax.axis_size("dom")
    cells = planes * rows_y
    slab = rows_z // blocks
    volume = 1.0 / (cells * doms * rows_z)
    f32 = jnp.float32
    shape = lambda *dims: jax.ShapeDtypeStruct(dims, f32)
    piece, edge = shape(slab, nb, cells), shape(WIDTH, nb, cells)

    flat = orbitals.reshape(nb, cells, rows_z)
    held = pltpu.with_memory_space_constraint(flat, pltpu.HBM)
    chips = blocks // 2
    pieces = pl.pallas_call(
        functools.partial(pack_kernel, blocks),
        out_shape=[shape(2, slab, nb, cells)] * chips,
        in_specs=[HBM],
        out_specs=[VMEM] * chips,
        scratch_shapes=[
            pltpu.VMEM((rows_z * nb, cells), f32),
            pltpu.VMEM((nb, cells, rows_z), f32),
            pltpu.SemaphoreType.DMA((CHUNKS,)),
        ],
        compiler_params=params(),
        name="pack",
    )(held)
    last = 2 * (chips - 1)
    pairs = [swap(value, "orb", 2 * m) if m else value for m, value in enumerate(pieces[:-1])]
    direct = [swap(pieces[-1][core], "orb", last + core) for core in range(2)]
    nearest = pl.pallas_call(
        hand_kernel,
        out_shape=piece,
        in_specs=[SMEM, SMEM, VMEM],
        out_specs=VMEM,
        compiler_params=params(),
        name="hand",
    )(block, owner, pairs[1])
    others = [nearest if m == 1 else value[1] for m, value in enumerate(pairs)]
    spread = (pairs + [swap(value, "orb", 1) for value in others] + direct)[::-1]

    side = shape(3 * slab * nb // 4, cells)
    active, near, far, first, last = pl.pallas_call(
        pick_kernel,
        out_shape=(piece, edge, edge, side, side),
        in_specs=[SMEM] + [VMEM] * len(spread),
        out_specs=[VMEM] * 5,
        compiler_params=params(),
        name="pick",
    )(block, *spread)

    up = lambda count: [(i, (i + 1) % count) for i in range(count)]
    down = lambda count: [(i, (i - 1) % count) for i in range(count)]
    x_before = lax.ppermute(last, "dom", up(doms))
    x_after = lax.ppermute(first, "dom", down(doms))
    z_near = swap(near, "orb", 1)
    z_far = lax.ppermute(far, "orb", [(o, (o + 2 * (o % 2) - 1) % blocks) for o in range(blocks)])

    halves = jax.ShapeDtypeStruct((blocks * nb, slab * cells), BF16)
    weights = [jnp.asarray(w) for w in plane_weights(planes, rows_y)]
    *parts, inner = pl.pallas_call(
        functools.partial(split_kernel, blocks),
        out_shape=(halves, halves, piece),
        in_specs=[VMEM] * (len(spread) + 4),
        out_specs=(VMEM, VMEM, VMEM),
        scratch_shapes=[pltpu.VMEM((rows_z, cells), f32)],
        compiler_params=params(),
        cost_estimate=pl.CostEstimate(flops=3 * blocks * nb * slab * cells, bytes_accessed=0, transcendentals=0),
        name="split",
    )(active, potential.reshape(cells, rows_z), *weights, *spread)

    applied, part = pl.pallas_call(
        functools.partial(project_kernel, volume),
        out_shape=(piece, shape(2 * nb, blocks * nb)),
        in_specs=[SMEM] + [VMEM] * 10,
        out_specs=(VMEM, VMEM),
        scratch_shapes=[pltpu.VMEM((2, WIDTH, nb, cells), f32)],
        compiler_params=params(),
        name="project",
    )(owner, rotation, *parts, inner, z_near, z_far, x_before, x_after, *weights)

    summed = total_over_all(part)
    proj, panel = summed[:nb], summed[nb:]

    own = pl.pallas_call(
        remove_kernel,
        out_shape=piece,
        in_specs=[VMEM] * 4,
        out_specs=VMEM,
        compiler_params=params(),
        name="remove",
    )(*parts, applied, proj)

    gathered = [own] + [None] * (blocks - 1)
    for k in range(2, blocks, 2):
        gathered[k] = swap(own, "orb", k)
    for k in range(0, blocks, 2):
        gathered[k + 1] = swap(gathered[k], "orb", 1)

    square = jax.ShapeDtypeStruct((MIX * nb, MIX * nb), BF16)
    mixing = pl.pallas_call(
        mixing_kernel,
        out_shape=(square, square),
        in_specs=[VMEM],
        out_specs=(VMEM, VMEM),
        compiler_params=params(),
        name="mixing",
    )(panel)

    gradient, updated = pl.pallas_call(
        functools.partial(update_kernel, blocks),
        out_shape=(shape(nb, cells, rows_z), shape(nb, cells, rows_z)),
        in_specs=[VMEM] * (3 + blocks),
        out_specs=(HBM, HBM),
        scratch_shapes=[
            pltpu.VMEM((rows_z * nb, cells), f32),
            pltpu.VMEM((nb, cells, rows_z), f32),
            pltpu.VMEM((cells * nb, rows_z), f32),
            pltpu.VMEM((cells * nb, rows_z), f32),
            pltpu.VMEM((nb, cells, rows_z), f32),
            pltpu.SemaphoreType.DMA((2, CHUNKS)),
        ],
        compiler_params=params(),
        name="update",
    )(*mixing, flat, gathered[0], *gathered[:0:-1])
    return gradient.reshape(orbitals.shape), updated.reshape(orbitals.shape)


def solution(mesh):
    in_specs = (P("orb", "dom", None, None), P("dom", None, None), P("orb", None), P(), P())
    out_specs = (P(None, "dom", None, None), P("orb", "dom", None, None))
    return jax.shard_map(
        per_device, mesh=mesh, in_specs=in_specs, out_specs=out_specs, check_vma=False
    )
```

```python
import functools

import jax
import jax.numpy as jnp
import numpy as np
from jax import lax
from jax.experimental import pallas as pl
from jax.experimental.pallas import tpu as pltpu
from jax.sharding import PartitionSpec as P

CENTER = -5369.0 / 1800.0
SIDES = (12.0 / 7.0, -15.0 / 56.0, 10.0 / 189.0, -1.0 / 112.0, 2.0 / 1925.0, -1.0 / 16632.0)
WIDTH = 6
CHUNKS = 4
MIX = 8
BF16 = jnp.bfloat16
VMEM = pl.BlockSpec(memory_space=pltpu.VMEM)
HBM = pl.BlockSpec(memory_space=pltpu.HBM)
SMEM = pl.BlockSpec(memory_space=pltpu.SMEM)


def params():
    return pltpu.CompilerParams(vmem_limit_bytes=32 * 1024 * 1024)


def plane_weights(planes, rows_y):
    cells = planes * rows_y
    table = np.zeros((3 * cells, cells), np.float64)
    skipped = (planes - WIDTH) * rows_y
    for x in range(planes):
        for y in range(rows_y):
            out = x * rows_y + y
            for k, weight in enumerate(SIDES, 1):
                for step in (k, -k):
                    table[cells + x * rows_y + (y + step) % rows_y, out] += weight
                    row = cells + (x + step) * rows_y + y
                    table[row - skipped if row < cells else row, out] += weight
    table = -0.5 * table
    high = table.astype(BF16)
    return high, (table - high.astype(np.float64)).astype(BF16)


def split(value):
    high = value.astype(BF16)
    return high, (value - high.astype(jnp.float32)).astype(BF16)


def dot3(left, right, contract):
    dot = lambda x, y: lax.dot_general(x, y, (contract, ((), ())), preferred_element_type=jnp.float32)
    return dot(left[0], right[0]) + (dot(left[0], right[1]) + dot(left[1], right[0]))


def pack_kernel(blocks, x_hbm, *refs):
    *t_refs, turned, x_ref, sems = refs
    count, _, rows_z = x_ref.shape
    chunks = sems.shape[0]
    per = count // chunks
    copies = [
        pltpu.make_async_copy(x_hbm.at[pl.ds(i * per, per)], x_ref.at[pl.ds(i * per, per)], sems.at[i])
        for i in range(chunks)
    ]
    for copy in copies:
        copy.start()
    for i, copy in enumerate(copies):
        copy.wait()
        for a in range(i * per, (i + 1) * per):
            turned[pl.ds(a, rows_z, stride=count), :] = x_ref[a].T
    rows = rows_z // blocks * count
    rank = lax.axis_index("orb")
    for m, t_ref in enumerate(t_refs):
        for core in range(2):
            start = pl.multiple_of((rank ^ (2 * m + core)) * rows, rows)
            t_ref[core] = turned[pl.ds(start, rows), :].reshape(t_ref.shape[1:])


def hand_kernel(block_ref, owner_ref, pair_ref, other_ref):
    other_ref[...] = pair_ref[1]


def by_block(refs):
    refs = refs[::-1]
    half = len(refs) // 2 - 1
    return [refs[half + k // 2] if k % 2 else refs[k // 2].at[0] for k in range(2 * half)] + list(refs[2 * half :])


def squeeze(value):
    rows, wide = value.shape
    quarter, free = rows // 4, wide // 4
    lane = lax.broadcasted_iota(jnp.int32, (quarter, wide), 1)
    rest = value[3 * quarter :]
    parts = []
    for j in range(3):
        moved = pltpu.roll(rest, (3 - j) * free, 1)
        parts.append(jnp.where(lane < 3 * free, value[j * quarter : (j + 1) * quarter], moved))
    return jnp.concatenate(parts, axis=0)


def expand(value):
    rows, wide = value.shape
    quarter, free = rows // 3, wide // 4
    lane = lax.broadcasted_iota(jnp.int32, (quarter, wide), 1)
    rest = value[:quarter]
    for j in range(3):
        moved = pltpu.roll(value[j * quarter : (j + 1) * quarter], (j + 1) * free, 1)
        rest = jnp.where((lane >= j * free) & (lane < (j + 1) * free), moved, rest)
    return jnp.concatenate([value, rest], axis=0)


def pick_kernel(block_ref, *refs):
    x_refs, (act_ref, near_ref, far_ref, first_ref, last_ref) = by_block(refs[:-5]), refs[-5:]
    slab, nb, cells = act_ref.shape
    rank = lax.axis_index("orb")
    for k, x_ref in enumerate(x_refs):
        @pl.when((rank ^ block_ref[0]) == k)
        def _(x_ref=x_ref):
            act_ref[...] = x_ref[...]
    odd = rank % 2
    near_ref[...] = act_ref[pl.ds((1 - odd) * (slab - WIDTH), WIDTH)]
    far_ref[...] = act_ref[pl.ds(odd * (slab - WIDTH), WIDTH)]
    flat = act_ref[...].reshape(slab * nb, cells)
    first_ref[...] = squeeze(flat)
    last_ref[...] = squeeze(pltpu.roll(flat, 3 * (cells // 4), 1))


def split_kernel(blocks, act_ref, v_ref, wh_ref, wl_ref, *refs):
    x_refs, (high_ref, low_ref, inner_ref, turned) = by_block(refs[:-4]), refs[-4:]
    slab, nb, cells = act_ref.shape
    rank = lax.axis_index("orb")
    for k, x_ref in enumerate(x_refs):
        rows = pl.ds(pl.multiple_of((rank ^ k) * nb, nb), nb)
        for z in range(slab):
            high, low = split(x_ref[z])
            high_ref[rows, z * cells : (z + 1) * cells] = high
            low_ref[rows, z * cells : (z + 1) * cells] = low
    turned[...] = v_ref[...].T
    mine = pl.ds(pl.multiple_of(rank * slab, slab), slab)
    act = act_ref[...]
    middle = slice(cells, 2 * cells)
    inner = dot3(split(act.reshape(slab * nb, cells)), (wh_ref[middle], wl_ref[middle]), ((1,), (0,)))
    inner = inner.reshape(slab, nb, cells) + (turned[mine, :][:, None, :] - 1.5 * CENTER) * act
    edge = jnp.zeros((WIDTH, nb, cells), jnp.float32)
    tall = jnp.concatenate([edge, act, edge], axis=0)
    for k, weight in enumerate(SIDES, 1):
        upper = tall[WIDTH + k : WIDTH + k + slab]
        lower = tall[WIDTH - k : WIDTH - k + slab]
        inner = inner + (-0.5 * weight) * (upper + lower)
    inner_ref[...] = inner


def project_kernel(
    volume, owner_ref, rot_ref, xh_ref, xl_ref, inner_ref, near_ref, far_ref, xb_ref, xa_ref, wh_ref, wl_ref,
    a_ref, p_ref, around,
):
    slab, nb, cells = inner_ref.shape
    rank = lax.axis_index("orb")
    odd = rank % 2
    around[1 - odd] = near_ref[...]
    around[odd] = far_ref[...]
    before, after = slice(0, cells), slice(2 * cells, 3 * cells)
    applied = dot3(split(expand(xb_ref[...])), (wh_ref[before], wl_ref[before]), ((1,), (0,)))
    applied = applied + dot3(split(expand(xa_ref[...])), (wh_ref[after], wl_ref[after]), ((1,), (0,)))
    a_ref[...] = inner_ref[...] + applied.reshape(slab, nb, cells)
    for z in range(WIDTH):
        below, above = a_ref[z], a_ref[slab - 1 - z]
        for k in range(z + 1, WIDTH + 1):
            below = below + (-0.5 * SIDES[k - 1]) * around[0, WIDTH + z - k]
            above = above + (-0.5 * SIDES[k - 1]) * around[1, k - 1 - z]
        a_ref[z] = below
        a_ref[slab - 1 - z] = above
    flat = jnp.concatenate([a_ref[z] for z in range(slab)], axis=1)
    total = dot3(split(flat), (xh_ref[...], xl_ref[...]), ((1,), (1,)))
    p_ref[:nb] = total * volume
    p_ref[nb:] = jnp.where(rank == owner_ref[0], rot_ref[...], 0.0)


def remove_kernel(xh_ref, xl_ref, a_ref, p_ref, g_ref):
    slab, nb, cells = a_ref.shape
    removed = dot3(split(p_ref[...]), (xh_ref[...], xl_ref[...]), ((1,), (0,)))
    for z in range(slab):
        g_ref[z] = a_ref[z] - removed[:, z * cells : (z + 1) * cells]


def mixing_kernel(panel_ref, high_ref, low_ref):
    nb, size = panel_ref.shape[0], high_ref.shape[0]
    wide = panel_ref.shape[1]
    row, col = (lax.broadcasted_iota(jnp.int32, (size, wide), axis) for axis in (0, 1))
    mine = jnp.where(col == lax.axis_index("orb") * nb + row % nb, 1.0, 0.0).astype(BF16)
    orbital, col = (lax.broadcasted_iota(jnp.int32, (nb, size), axis) for axis in (0, 1))
    repeat = jnp.where(orbital == col % nb, 1.0, 0.0).astype(BF16)
    row, col = (lax.broadcasted_iota(jnp.int32, (size, size), axis) for axis in (0, 1))
    same = row // nb == col // nb
    dot = lambda x, y, axes: lax.dot_general(x, y, (axes, ((), ())), preferred_element_type=jnp.float32)
    for part, ref in zip(split(panel_ref[...]), (high_ref, low_ref)):
        block = dot(mine, part, ((1,), (1,))).astype(BF16)
        ref[...] = jnp.where(same, dot(block, repeat, ((1,), (0,))), 0.0).astype(BF16)


def update_kernel(blocks, wh_ref, wl_ref, x_ref, *refs):
    g_refs, (grad_hbm, out_hbm, whole, grad, mixed, added, out, sems) = refs[:blocks], refs[blocks:]
    nb, cells, rows_z = x_ref.shape
    rank = lax.axis_index("orb")
    share = rows_z // blocks * nb
    for k in range(blocks):
        at = pl.ds(pl.multiple_of((rank ^ k) * share, share), share)
        whole[at, :] = g_refs[k][...].reshape(share, cells)
    per = nb // CHUNKS
    copies = []
    for i in range(CHUNKS):
        for c in range(i * per, (i + 1) * per):
            plane = whole[pl.ds(c, rows_z, stride=nb), :].T
            grad[c] = plane
            mixed[pl.ds(c, cells, stride=nb), :] = plane
        part = pl.ds(i * per, per)
        copies.append(pltpu.make_async_copy(grad.at[part], grad_hbm.at[part], sems.at[0, i]))
        copies[-1].start()
    size = wh_ref.shape[0]
    mix = (wh_ref[...], wl_ref[...])
    rows = cells // CHUNKS
    tall = rows * nb
    for i in range(CHUNKS):
        parts = split(mixed[i * tall : (i + 1) * tall])
        sides = [jnp.concatenate([p[j : j + size] for j in range(0, tall, size)], axis=1) for p in parts]
        result = dot3(mix, sides, ((1,), (0,)))
        for j in range(tall // size):
            added[i * tall + j * size : i * tall + (j + 1) * size] = result[:, j * rows_z : (j + 1) * rows_z]
        some = pl.ds(i * rows, rows)
        for a in range(nb):
            out[a, some] = x_ref[a, some] + added[pl.ds(i * tall + a, rows, stride=nb), :]
        copies.append(pltpu.make_async_copy(out.at[:, some], out_hbm.at[:, some], sems.at[1, i]))
        copies[-1].start()
    for copy in copies:
        copy.wait()


def swap(value, axis, k):
    count = lax.axis_size(axis)
    return lax.ppermute(value, axis, [(i, i ^ k) for i in range(count)])


def total_over_all(value, nb):
    value = value + swap(value, "orb", 1)
    first = sum([swap(value[:nb], "dom", k) for k in range(1, lax.axis_size("dom"))], value[:nb])
    value = jnp.concatenate([first, value[nb:]], axis=0)
    return sum([swap(value, "orb", k) for k in range(2, lax.axis_size("orb"), 2)], value)


def per_device(orbitals, potential, rotation, block, owner):
    nb, planes, rows_y, rows_z = orbitals.shape
    blocks, doms = lax.axis_size("orb"), lax.axis_size("dom")
    cells = planes * rows_y
    slab = rows_z // blocks
    volume = 1.0 / (cells * doms * rows_z)
    f32 = jnp.float32
    shape = lambda *dims: jax.ShapeDtypeStruct(dims, f32)
    piece, edge = shape(slab, nb, cells), shape(WIDTH, nb, cells)

    flat = orbitals.reshape(nb, cells, rows_z)
    held = pltpu.with_memory_space_constraint(flat, pltpu.HBM)
    chips = blocks // 2
    pieces = pl.pallas_call(
        functools.partial(pack_kernel, blocks),
        out_shape=[shape(2, slab, nb, cells)] * chips,
        in_specs=[HBM],
        out_specs=[VMEM] * chips,
        scratch_shapes=[
            pltpu.VMEM((rows_z * nb, cells), f32),
            pltpu.VMEM((nb, cells, rows_z), f32),
            pltpu.SemaphoreType.DMA((CHUNKS,)),
        ],
        compiler_params=params(),
        name="pack",
    )(held)
    last = 2 * (chips - 1)
    pairs = [swap(value, "orb", 2 * m) if m else value for m, value in enumerate(pieces[:-1])]
    direct = [swap(pieces[-1][core], "orb", last + core) for core in range(2)]
    nearest = pl.pallas_call(
        hand_kernel,
        out_shape=piece,
        in_specs=[SMEM, SMEM, VMEM],
        out_specs=VMEM,
        compiler_params=params(),
        name="hand",
    )(block, owner, pairs[1])
    others = [nearest if m == 1 else value[1] for m, value in enumerate(pairs)]
    spread = (pairs + [swap(value, "orb", 1) for value in others] + direct)[::-1]

    side = shape(3 * slab * nb // 4, cells)
    active, near, far, first, last = pl.pallas_call(
        pick_kernel,
        out_shape=(piece, edge, edge, side, side),
        in_specs=[SMEM] + [VMEM] * len(spread),
        out_specs=[VMEM] * 5,
        compiler_params=params(),
        name="pick",
    )(block, *spread)

    up = lambda count: [(i, (i + 1) % count) for i in range(count)]
    down = lambda count: [(i, (i - 1) % count) for i in range(count)]
    x_before = lax.ppermute(last, "dom", up(doms))
    x_after = lax.ppermute(first, "dom", down(doms))
    z_near = swap(near, "orb", 1)
    z_far = lax.ppermute(far, "orb", [(o, (o + 2 * (o % 2) - 1) % blocks) for o in range(blocks)])

    halves = jax.ShapeDtypeStruct((blocks * nb, slab * cells), BF16)
    weights = [jnp.asarray(w) for w in plane_weights(planes, rows_y)]
    *parts, inner = pl.pallas_call(
        functools.partial(split_kernel, blocks),
        out_shape=(halves, halves, piece),
        in_specs=[VMEM] * (len(spread) + 4),
        out_specs=(VMEM, VMEM, VMEM),
        scratch_shapes=[pltpu.VMEM((rows_z, cells), f32)],
        compiler_params=params(),
        cost_estimate=pl.CostEstimate(flops=3 * blocks * nb * slab * cells, bytes_accessed=0, transcendentals=0),
        name="split",
    )(active, potential.reshape(cells, rows_z), *weights, *spread)

    applied, part = pl.pallas_call(
        functools.partial(project_kernel, volume),
        out_shape=(piece, shape(2 * nb, blocks * nb)),
        in_specs=[SMEM] + [VMEM] * 10,
        out_specs=(VMEM, VMEM),
        scratch_shapes=[pltpu.VMEM((2, WIDTH, nb, cells), f32)],
        compiler_params=params(),
        name="project",
    )(owner, rotation, *parts, inner, z_near, z_far, x_before, x_after, *weights)

    summed = total_over_all(part, nb)
    proj, panel = summed[:nb], summed[nb:]

    own = pl.pallas_call(
        remove_kernel,
        out_shape=piece,
        in_specs=[VMEM] * 4,
        out_specs=VMEM,
        compiler_params=params(),
        name="remove",
    )(*parts, applied, proj)

    gathered = [own] + [None] * (blocks - 1)
    for k in range(2, blocks, 2):
        gathered[k] = swap(own, "orb", k)
    for k in range(0, blocks, 2):
        gathered[k + 1] = swap(gathered[k], "orb", 1)

    square = jax.ShapeDtypeStruct((MIX * nb, MIX * nb), BF16)
    mixing = pl.pallas_call(
        mixing_kernel,
        out_shape=(square, square),
        in_specs=[VMEM],
        out_specs=(VMEM, VMEM),
        compiler_params=params(),
        name="mixing",
    )(panel)

    gradient, updated = pl.pallas_call(
        functools.partial(update_kernel, blocks),
        out_shape=(shape(nb, cells, rows_z), shape(nb, cells, rows_z)),
        in_specs=[VMEM] * (3 + blocks),
        out_specs=(HBM, HBM),
        scratch_shapes=[
            pltpu.VMEM((rows_z * nb, cells), f32),
            pltpu.VMEM((nb, cells, rows_z), f32),
            pltpu.VMEM((cells * nb, rows_z), f32),
            pltpu.VMEM((cells * nb, rows_z), f32),
            pltpu.VMEM((nb, cells, rows_z), f32),
            pltpu.SemaphoreType.DMA((2, CHUNKS)),
        ],
        compiler_params=params(),
        name="update",
    )(*mixing, flat, *gathered)
    return gradient.reshape(orbitals.shape), updated.reshape(orbitals.shape)


def solution(mesh):
    in_specs = (P("orb", "dom", None, None), P("dom", None, None), P("orb", None), P(), P())
    out_specs = (P(None, "dom", None, None), P("orb", "dom", None, None))
    return jax.shard_map(
        per_device, mesh=mesh, in_specs=in_specs, out_specs=out_specs, check_vma=False
    )
```

```python
import functools

import jax
import jax.numpy as jnp
import numpy as np
from jax import lax
from jax.experimental import pallas as pl
from jax.experimental.pallas import tpu as pltpu
from jax.sharding import PartitionSpec as P

CENTER = -5369.0 / 1800.0
SIDES = (12.0 / 7.0, -15.0 / 56.0, 10.0 / 189.0, -1.0 / 112.0, 2.0 / 1925.0, -1.0 / 16632.0)
WIDTH = 6
CHUNKS = 4
MIX = 8
BF16 = jnp.bfloat16
VMEM = pl.BlockSpec(memory_space=pltpu.VMEM)
HBM = pl.BlockSpec(memory_space=pltpu.HBM)
SMEM = pl.BlockSpec(memory_space=pltpu.SMEM)


def params():
    return pltpu.CompilerParams(vmem_limit_bytes=32 * 1024 * 1024)


def plane_weights(planes, rows_y):
    cells = planes * rows_y
    table = np.zeros((3 * cells, cells), np.float64)
    skipped = (planes - WIDTH) * rows_y
    for x in range(planes):
        for y in range(rows_y):
            out = x * rows_y + y
            for k, weight in enumerate(SIDES, 1):
                for step in (k, -k):
                    table[cells + x * rows_y + (y + step) % rows_y, out] += weight
                    row = cells + (x + step) * rows_y + y
                    table[row - skipped if row < cells else row, out] += weight
    table = -0.5 * table
    high = table.astype(BF16)
    return high, (table - high.astype(np.float64)).astype(BF16)


def split(value):
    high = value.astype(BF16)
    return high, (value - high.astype(jnp.float32)).astype(BF16)


def dot3(left, right, contract):
    dot = lambda x, y: lax.dot_general(x, y, (contract, ((), ())), preferred_element_type=jnp.float32)
    return dot(left[0], right[0]) + (dot(left[0], right[1]) + dot(left[1], right[0]))


def pack_kernel(blocks, x_hbm, *refs):
    *t_refs, turned, x_ref, sems = refs
    count, _, rows_z = x_ref.shape
    chunks = sems.shape[0]
    per = count // chunks
    copies = [
        pltpu.make_async_copy(x_hbm.at[pl.ds(i * per, per)], x_ref.at[pl.ds(i * per, per)], sems.at[i])
        for i in range(chunks)
    ]
    for copy in copies:
        copy.start()
    for i, copy in enumerate(copies):
        copy.wait()
        for a in range(i * per, (i + 1) * per):
            turned[pl.ds(a, rows_z, stride=count), :] = x_ref[a].T
    rows = rows_z // blocks * count
    rank = lax.axis_index("orb")
    for m, t_ref in enumerate(t_refs):
        for core in range(2):
            start = pl.multiple_of((rank ^ (2 * m + core)) * rows, rows)
            t_ref[core] = turned[pl.ds(start, rows), :].reshape(t_ref.shape[1:])


def hand_kernel(block_ref, owner_ref, pair_ref, other_ref):
    other_ref[...] = pair_ref[1]


def by_block(refs):
    refs = refs[::-1]
    half = len(refs) // 2 - 1
    return [refs[half + k // 2] if k % 2 else refs[k // 2].at[0] for k in range(2 * half)] + list(refs[2 * half :])


def squeeze(value):
    rows, wide = value.shape
    quarter, free = rows // 4, wide // 4
    lane = lax.broadcasted_iota(jnp.int32, (quarter, wide), 1)
    rest = value[3 * quarter :]
    parts = []
    for j in range(3):
        moved = pltpu.roll(rest, (3 - j) * free, 1)
        parts.append(jnp.where(lane < 3 * free, value[j * quarter : (j + 1) * quarter], moved))
    return jnp.concatenate(parts, axis=0)


def expand(value):
    rows, wide = value.shape
    quarter, free = rows // 3, wide // 4
    lane = lax.broadcasted_iota(jnp.int32, (quarter, wide), 1)
    rest = value[:quarter]
    for j in range(3):
        moved = pltpu.roll(value[j * quarter : (j + 1) * quarter], (j + 1) * free, 1)
        rest = jnp.where((lane >= j * free) & (lane < (j + 1) * free), moved, rest)
    return jnp.concatenate([value, rest], axis=0)


def pick_kernel(block_ref, *refs):
    x_refs, (act_ref, near_ref, far_ref, first_ref, last_ref) = by_block(refs[:-5]), refs[-5:]
    slab, nb, cells = act_ref.shape
    rank = lax.axis_index("orb")
    for k, x_ref in enumerate(x_refs):
        @pl.when((rank ^ block_ref[0]) == k)
        def _(x_ref=x_ref):
            act_ref[...] = x_ref[...]
    odd = rank % 2
    near_ref[...] = act_ref[pl.ds((1 - odd) * (slab - WIDTH), WIDTH)]
    far_ref[...] = act_ref[pl.ds(odd * (slab - WIDTH), WIDTH)]
    flat = act_ref[...].reshape(slab * nb, cells)
    first_ref[...] = squeeze(flat)
    last_ref[...] = squeeze(pltpu.roll(flat, 3 * (cells // 4), 1))


def split_kernel(blocks, act_ref, v_ref, wh_ref, wl_ref, *refs):
    x_refs, (high_ref, low_ref, inner_ref, turned) = by_block(refs[:-4]), refs[-4:]
    slab, nb, cells = act_ref.shape
    rank = lax.axis_index("orb")
    for k, x_ref in enumerate(x_refs):
        rows = pl.ds(pl.multiple_of((rank ^ k) * nb, nb), nb)
        for z in range(slab):
            high, low = split(x_ref[z])
            high_ref[rows, z * cells : (z + 1) * cells] = high
            low_ref[rows, z * cells : (z + 1) * cells] = low
    turned[...] = v_ref[...].T
    mine = pl.ds(pl.multiple_of(rank * slab, slab), slab)
    act = act_ref[...]
    middle = slice(cells, 2 * cells)
    inner = dot3(split(act.reshape(slab * nb, cells)), (wh_ref[middle], wl_ref[middle]), ((1,), (0,)))
    inner = inner.reshape(slab, nb, cells) + (turned[mine, :][:, None, :] - 1.5 * CENTER) * act
    edge = jnp.zeros((WIDTH, nb, cells), jnp.float32)
    tall = jnp.concatenate([edge, act, edge], axis=0)
    for k, weight in enumerate(SIDES, 1):
        upper = tall[WIDTH + k : WIDTH + k + slab]
        lower = tall[WIDTH - k : WIDTH - k + slab]
        inner = inner + (-0.5 * weight) * (upper + lower)
    inner_ref[...] = inner


def project_kernel(
    volume, owner_ref, rot_ref, xh_ref, xl_ref, inner_ref, near_ref, far_ref, xb_ref, xa_ref, wh_ref, wl_ref,
    a_ref, p_ref, around,
):
    slab, nb, cells = inner_ref.shape
    rank = lax.axis_index("orb")
    odd = rank % 2
    around[1 - odd] = near_ref[...]
    around[odd] = far_ref[...]
    before, after = slice(0, cells), slice(2 * cells, 3 * cells)
    applied = dot3(split(expand(xb_ref[...])), (wh_ref[before], wl_ref[before]), ((1,), (0,)))
    applied = applied + dot3(split(expand(xa_ref[...])), (wh_ref[after], wl_ref[after]), ((1,), (0,)))
    a_ref[...] = inner_ref[...] + applied.reshape(slab, nb, cells)
    for z in range(WIDTH):
        below, above = a_ref[z], a_ref[slab - 1 - z]
        for k in range(z + 1, WIDTH + 1):
            below = below + (-0.5 * SIDES[k - 1]) * around[0, WIDTH + z - k]
            above = above + (-0.5 * SIDES[k - 1]) * around[1, k - 1 - z]
        a_ref[z] = below
        a_ref[slab - 1 - z] = above
    flat = jnp.concatenate([a_ref[z] for z in range(slab)], axis=1)
    total = dot3(split(flat), (xh_ref[...], xl_ref[...]), ((1,), (1,)))
    p_ref[:nb] = total * volume
    p_ref[nb:] = jnp.where(rank == owner_ref[0], rot_ref[...], 0.0)


def remove_kernel(xh_ref, xl_ref, a_ref, *refs):
    *p_refs, g_ref = refs
    slab, nb, cells = a_ref.shape
    removed = dot3(split(total(p_refs, 0, nb)), (xh_ref[...], xl_ref[...]), ((1,), (0,)))
    for z in range(slab):
        g_ref[z] = a_ref[z] - removed[:, z * cells : (z + 1) * cells]


def mixing_kernel(nb, *refs):
    *p_refs, high_ref, low_ref = refs
    size, wide = high_ref.shape[0], p_refs[0].shape[1]
    row, col = (lax.broadcasted_iota(jnp.int32, (size, wide), axis) for axis in (0, 1))
    mine = jnp.where(col == lax.axis_index("orb") * nb + row % nb, 1.0, 0.0).astype(BF16)
    orbital, col = (lax.broadcasted_iota(jnp.int32, (nb, size), axis) for axis in (0, 1))
    repeat = jnp.where(orbital == col % nb, 1.0, 0.0).astype(BF16)
    row, col = (lax.broadcasted_iota(jnp.int32, (size, size), axis) for axis in (0, 1))
    same = row // nb == col // nb
    dot = lambda x, y, axes: lax.dot_general(x, y, (axes, ((), ())), preferred_element_type=jnp.float32)
    for part, ref in zip(split(total(p_refs, nb, nb)), (high_ref, low_ref)):
        block = dot(mine, part, ((1,), (1,))).astype(BF16)
        ref[...] = jnp.where(same, dot(block, repeat, ((1,), (0,))), 0.0).astype(BF16)


def update_kernel(blocks, wh_ref, wl_ref, x_ref, *refs):
    g_refs, (grad_hbm, out_hbm, whole, grad, mixed, added, out, sems) = refs[:blocks], refs[blocks:]
    nb, cells, rows_z = x_ref.shape
    rank = lax.axis_index("orb")
    share = rows_z // blocks * nb
    for k in range(blocks):
        at = pl.ds(pl.multiple_of((rank ^ k) * share, share), share)
        whole[at, :] = g_refs[k][...].reshape(share, cells)
    per = nb // CHUNKS
    copies = []
    for i in range(CHUNKS):
        for c in range(i * per, (i + 1) * per):
            plane = whole[pl.ds(c, rows_z, stride=nb), :].T
            grad[c] = plane
            mixed[pl.ds(c, cells, stride=nb), :] = plane
        part = pl.ds(i * per, per)
        copies.append(pltpu.make_async_copy(grad.at[part], grad_hbm.at[part], sems.at[0, i]))
        copies[-1].start()
    size = wh_ref.shape[0]
    mix = (wh_ref[...], wl_ref[...])
    rows = cells // CHUNKS
    tall = rows * nb
    for i in range(CHUNKS):
        parts = split(mixed[i * tall : (i + 1) * tall])
        sides = [jnp.concatenate([p[j : j + size] for j in range(0, tall, size)], axis=1) for p in parts]
        result = dot3(mix, sides, ((1,), (0,)))
        for j in range(tall // size):
            added[i * tall + j * size : i * tall + (j + 1) * size] = result[:, j * rows_z : (j + 1) * rows_z]
        some = pl.ds(i * rows, rows)
        for a in range(nb):
            out[a, some] = x_ref[a, some] + added[pl.ds(i * tall + a, rows, stride=nb), :]
        copies.append(pltpu.make_async_copy(out.at[:, some], out_hbm.at[:, some], sems.at[1, i]))
        copies[-1].start()
    for copy in copies:
        copy.wait()


def swap(value, axis, k):
    count = lax.axis_size(axis)
    return lax.ppermute(value, axis, [(i, i ^ k) for i in range(count)])


def dom_kernel(value_ref, *refs):
    *other_refs, out_ref = refs
    nb = other_refs[0].shape[0]
    out_ref[:nb] = value_ref[:nb] + sum(ref[...] for ref in other_refs)
    out_ref[nb:] = value_ref[nb:]


def total(refs, first, count):
    rows = slice(first, first + count)
    return sum(ref[rows] for ref in refs)


def per_device(orbitals, potential, rotation, block, owner):
    nb, planes, rows_y, rows_z = orbitals.shape
    blocks, doms = lax.axis_size("orb"), lax.axis_size("dom")
    cells = planes * rows_y
    slab = rows_z // blocks
    volume = 1.0 / (cells * doms * rows_z)
    f32 = jnp.float32
    shape = lambda *dims: jax.ShapeDtypeStruct(dims, f32)
    piece, edge = shape(slab, nb, cells), shape(WIDTH, nb, cells)

    flat = orbitals.reshape(nb, cells, rows_z)
    held = pltpu.with_memory_space_constraint(flat, pltpu.HBM)
    chips = blocks // 2
    pieces = pl.pallas_call(
        functools.partial(pack_kernel, blocks),
        out_shape=[shape(2, slab, nb, cells)] * chips,
        in_specs=[HBM],
        out_specs=[VMEM] * chips,
        scratch_shapes=[
            pltpu.VMEM((rows_z * nb, cells), f32),
            pltpu.VMEM((nb, cells, rows_z), f32),
            pltpu.SemaphoreType.DMA((CHUNKS,)),
        ],
        compiler_params=params(),
        name="pack",
    )(held)
    last = 2 * (chips - 1)
    pairs = [swap(value, "orb", 2 * m) if m else value for m, value in enumerate(pieces[:-1])]
    direct = [swap(pieces[-1][core], "orb", last + core) for core in range(2)]
    nearest = pl.pallas_call(
        hand_kernel,
        out_shape=piece,
        in_specs=[SMEM, SMEM, VMEM],
        out_specs=VMEM,
        compiler_params=params(),
        name="hand",
    )(block, owner, pairs[1])
    others = [nearest if m == 1 else value[1] for m, value in enumerate(pairs)]
    spread = (pairs + [swap(value, "orb", 1) for value in others] + direct)[::-1]

    side = shape(3 * slab * nb // 4, cells)
    active, near, far, first, last = pl.pallas_call(
        pick_kernel,
        out_shape=(piece, edge, edge, side, side),
        in_specs=[SMEM] + [VMEM] * len(spread),
        out_specs=[VMEM] * 5,
        compiler_params=params(),
        name="pick",
    )(block, *spread)

    up = lambda count: [(i, (i + 1) % count) for i in range(count)]
    down = lambda count: [(i, (i - 1) % count) for i in range(count)]
    x_before = lax.ppermute(last, "dom", up(doms))
    x_after = lax.ppermute(first, "dom", down(doms))
    z_near = swap(near, "orb", 1)
    z_far = lax.ppermute(far, "orb", [(o, (o + 2 * (o % 2) - 1) % blocks) for o in range(blocks)])

    halves = jax.ShapeDtypeStruct((blocks * nb, slab * cells), BF16)
    weights = [jnp.asarray(w) for w in plane_weights(planes, rows_y)]
    *parts, inner = pl.pallas_call(
        functools.partial(split_kernel, blocks),
        out_shape=(halves, halves, piece),
        in_specs=[VMEM] * (len(spread) + 4),
        out_specs=(VMEM, VMEM, VMEM),
        scratch_shapes=[pltpu.VMEM((rows_z, cells), f32)],
        compiler_params=params(),
        cost_estimate=pl.CostEstimate(flops=3 * blocks * nb * slab * cells, bytes_accessed=0, transcendentals=0),
        name="split",
    )(active, potential.reshape(cells, rows_z), *weights, *spread)

    applied, part = pl.pallas_call(
        functools.partial(project_kernel, volume),
        out_shape=(piece, shape(2 * nb, blocks * nb)),
        in_specs=[SMEM] + [VMEM] * 10,
        out_specs=(VMEM, VMEM),
        scratch_shapes=[pltpu.VMEM((2, WIDTH, nb, cells), f32)],
        compiler_params=params(),
        name="project",
    )(owner, rotation, *parts, inner, z_near, z_far, x_before, x_after, *weights)

    part = part + swap(part, "orb", 1)
    part = pl.pallas_call(
        dom_kernel,
        out_shape=shape(2 * nb, blocks * nb),
        in_specs=[VMEM] * doms,
        out_specs=VMEM,
        compiler_params=params(),
        name="dom",
    )(part, *[swap(part[:nb], "dom", k) for k in range(1, doms)])
    sums = [part] + [swap(part, "orb", k) for k in range(2, blocks, 2)]

    own = pl.pallas_call(
        remove_kernel,
        out_shape=piece,
        in_specs=[VMEM] * (3 + chips),
        out_specs=VMEM,
        compiler_params=params(),
        name="remove",
    )(*parts, applied, *sums)

    gathered = [own] + [None] * (blocks - 1)
    for k in range(2, blocks, 2):
        gathered[k] = swap(own, "orb", k)
    for k in range(0, blocks, 2):
        gathered[k + 1] = swap(gathered[k], "orb", 1)

    square = jax.ShapeDtypeStruct((MIX * nb, MIX * nb), BF16)
    mixing = pl.pallas_call(
        functools.partial(mixing_kernel, nb),
        out_shape=(square, square),
        in_specs=[VMEM] * chips,
        out_specs=(VMEM, VMEM),
        compiler_params=params(),
        name="mixing",
    )(*sums)

    gradient, updated = pl.pallas_call(
        functools.partial(update_kernel, blocks),
        out_shape=(shape(nb, cells, rows_z), shape(nb, cells, rows_z)),
        in_specs=[VMEM] * (3 + blocks),
        out_specs=(HBM, HBM),
        scratch_shapes=[
            pltpu.VMEM((rows_z * nb, cells), f32),
            pltpu.VMEM((nb, cells, rows_z), f32),
            pltpu.VMEM((cells * nb, rows_z), f32),
            pltpu.VMEM((cells * nb, rows_z), f32),
            pltpu.VMEM((nb, cells, rows_z), f32),
            pltpu.SemaphoreType.DMA((2, CHUNKS)),
        ],
        compiler_params=params(),
        name="update",
    )(*mixing, flat, *gathered)
    return gradient.reshape(orbitals.shape), updated.reshape(orbitals.shape)


def solution(mesh):
    in_specs = (P("orb", "dom", None, None), P("dom", None, None), P("orb", None), P(), P())
    out_specs = (P(None, "dom", None, None), P("orb", "dom", None, None))
    return jax.shard_map(
        per_device, mesh=mesh, in_specs=in_specs, out_specs=out_specs, check_vma=False
    )
```

```python
import functools

import jax
import jax.numpy as jnp
import numpy as np
from jax import lax
from jax.experimental import pallas as pl
from jax.experimental.pallas import tpu as pltpu
from jax.sharding import PartitionSpec as P

CENTER = -5369.0 / 1800.0
SIDES = (12.0 / 7.0, -15.0 / 56.0, 10.0 / 189.0, -1.0 / 112.0, 2.0 / 1925.0, -1.0 / 16632.0)
WIDTH = 6
CHUNKS = 4
MIX = 8
BF16 = jnp.bfloat16
VMEM = pl.BlockSpec(memory_space=pltpu.VMEM)
HBM = pl.BlockSpec(memory_space=pltpu.HBM)
SMEM = pl.BlockSpec(memory_space=pltpu.SMEM)


def params():
    return pltpu.CompilerParams(vmem_limit_bytes=32 * 1024 * 1024)


def plane_weights(planes, rows_y):
    cells = planes * rows_y
    table = np.zeros((3 * cells, cells), np.float64)
    skipped = (planes - WIDTH) * rows_y
    for x in range(planes):
        for y in range(rows_y):
            out = x * rows_y + y
            for k, weight in enumerate(SIDES, 1):
                for step in (k, -k):
                    table[cells + x * rows_y + (y + step) % rows_y, out] += weight
                    row = cells + (x + step) * rows_y + y
                    table[row - skipped if row < cells else row, out] += weight
    table = -0.5 * table
    high = table.astype(BF16)
    return high, (table - high.astype(np.float64)).astype(BF16)


def split(value):
    high = value.astype(BF16)
    return high, (value - high.astype(jnp.float32)).astype(BF16)


def dot3(left, right, contract):
    dot = lambda x, y: lax.dot_general(x, y, (contract, ((), ())), preferred_element_type=jnp.float32)
    return dot(left[0], right[0]) + (dot(left[0], right[1]) + dot(left[1], right[0]))


def pack_kernel(blocks, x_hbm, *refs):
    *t_refs, turned, x_ref, sems = refs
    count, _, rows_z = x_ref.shape
    chunks = sems.shape[0]
    per = count // chunks
    copies = [
        pltpu.make_async_copy(x_hbm.at[pl.ds(i * per, per)], x_ref.at[pl.ds(i * per, per)], sems.at[i])
        for i in range(chunks)
    ]
    for copy in copies:
        copy.start()
    for i, copy in enumerate(copies):
        copy.wait()
        for a in range(i * per, (i + 1) * per):
            turned[pl.ds(a, rows_z, stride=count), :] = x_ref[a].T
    rows = rows_z // blocks * count
    rank = lax.axis_index("orb")
    for m, t_ref in enumerate(t_refs):
        for core in range(2):
            start = pl.multiple_of((rank ^ (2 * m + core)) * rows, rows)
            t_ref[core] = turned[pl.ds(start, rows), :].reshape(t_ref.shape[1:])


def hand_kernel(block_ref, owner_ref, pair_ref, other_ref):
    other_ref[...] = pair_ref[1]


def by_block(refs):
    refs = refs[::-1]
    half = len(refs) // 2 - 1
    return [refs[half + k // 2] if k % 2 else refs[k // 2].at[0] for k in range(2 * half)] + list(refs[2 * half :])


def squeeze(value):
    rows, wide = value.shape
    quarter, free = rows // 4, wide // 4
    lane = lax.broadcasted_iota(jnp.int32, (quarter, wide), 1)
    rest = value[3 * quarter :]
    parts = []
    for j in range(3):
        moved = pltpu.roll(rest, (3 - j) * free, 1)
        parts.append(jnp.where(lane < 3 * free, value[j * quarter : (j + 1) * quarter], moved))
    return jnp.concatenate(parts, axis=0)


def expand(value):
    rows, wide = value.shape
    quarter, free = rows // 3, wide // 4
    lane = lax.broadcasted_iota(jnp.int32, (quarter, wide), 1)
    rest = value[:quarter]
    for j in range(3):
        moved = pltpu.roll(value[j * quarter : (j + 1) * quarter], (j + 1) * free, 1)
        rest = jnp.where((lane >= j * free) & (lane < (j + 1) * free), moved, rest)
    return jnp.concatenate([value, rest], axis=0)


def pick_kernel(block_ref, *refs):
    x_refs, (act_ref, near_ref, far_ref, first_ref, last_ref) = by_block(refs[:-5]), refs[-5:]
    slab, nb, cells = act_ref.shape
    rank = lax.axis_index("orb")
    for k, x_ref in enumerate(x_refs):
        @pl.when((rank ^ block_ref[0]) == k)
        def _(x_ref=x_ref):
            act_ref[...] = x_ref[...]
    odd = rank % 2
    near_ref[...] = act_ref[pl.ds((1 - odd) * (slab - WIDTH), WIDTH)]
    far_ref[...] = act_ref[pl.ds(odd * (slab - WIDTH), WIDTH)]
    flat = act_ref[...].reshape(slab * nb, cells)
    first_ref[...] = squeeze(flat)
    last_ref[...] = squeeze(pltpu.roll(flat, 3 * (cells // 4), 1))


def split_kernel(blocks, act_ref, v_ref, wh_ref, wl_ref, *refs):
    x_refs, (high_ref, low_ref, inner_ref, turned) = by_block(refs[:-4]), refs[-4:]
    slab, nb, cells = act_ref.shape
    rank = lax.axis_index("orb")
    for k, x_ref in enumerate(x_refs):
        rows = pl.ds(pl.multiple_of((rank ^ k) * nb, nb), nb)
        for z in range(slab):
            high, low = split(x_ref[z])
            high_ref[rows, z * cells : (z + 1) * cells] = high
            low_ref[rows, z * cells : (z + 1) * cells] = low
    turned[...] = v_ref[...].T
    mine = pl.ds(pl.multiple_of(rank * slab, slab), slab)
    act = act_ref[...]
    middle = slice(cells, 2 * cells)
    inner = dot3(split(act.reshape(slab * nb, cells)), (wh_ref[middle], wl_ref[middle]), ((1,), (0,)))
    inner = inner.reshape(slab, nb, cells) + (turned[mine, :][:, None, :] - 1.5 * CENTER) * act
    edge = jnp.zeros((WIDTH, nb, cells), jnp.float32)
    tall = jnp.concatenate([edge, act, edge], axis=0)
    for k, weight in enumerate(SIDES, 1):
        upper = tall[WIDTH + k : WIDTH + k + slab]
        lower = tall[WIDTH - k : WIDTH - k + slab]
        inner = inner + (-0.5 * weight) * (upper + lower)
    inner_ref[...] = inner


def project_kernel(
    volume, owner_ref, rot_ref, xh_ref, xl_ref, inner_ref, near_ref, far_ref, xb_ref, xa_ref, wh_ref, wl_ref,
    a_ref, p_ref, around,
):
    slab, nb, cells = inner_ref.shape
    rank = lax.axis_index("orb")
    odd = rank % 2
    around[1 - odd] = near_ref[...]
    around[odd] = far_ref[...]
    before, after = slice(0, cells), slice(2 * cells, 3 * cells)
    applied = dot3(split(expand(xb_ref[...])), (wh_ref[before], wl_ref[before]), ((1,), (0,)))
    applied = applied + dot3(split(expand(xa_ref[...])), (wh_ref[after], wl_ref[after]), ((1,), (0,)))
    a_ref[...] = inner_ref[...] + applied.reshape(slab, nb, cells)
    for z in range(WIDTH):
        below, above = a_ref[z], a_ref[slab - 1 - z]
        for k in range(z + 1, WIDTH + 1):
            below = below + (-0.5 * SIDES[k - 1]) * around[0, WIDTH + z - k]
            above = above + (-0.5 * SIDES[k - 1]) * around[1, k - 1 - z]
        a_ref[z] = below
        a_ref[slab - 1 - z] = above
    flat = jnp.concatenate([a_ref[z] for z in range(slab)], axis=1)
    total = dot3(split(flat), (xh_ref[...], xl_ref[...]), ((1,), (1,)))
    p_ref[:nb] = total * volume
    p_ref[nb:] = jnp.where(rank == owner_ref[0], rot_ref[...], 0.0)


def remove_kernel(xh_ref, xl_ref, a_ref, *refs):
    *p_refs, g_ref = refs
    slab, nb, cells = a_ref.shape
    removed = dot3(split(total(p_refs, 0, nb)), (xh_ref[...], xl_ref[...]), ((1,), (0,)))
    for z in range(slab):
        g_ref[z] = a_ref[z] - removed[:, z * cells : (z + 1) * cells]


def mixing_kernel(nb, *refs):
    *p_refs, high_ref, low_ref = refs
    size, wide = high_ref.shape[0], p_refs[0].shape[1]
    row, col = (lax.broadcasted_iota(jnp.int32, (size, wide), axis) for axis in (0, 1))
    mine = jnp.where(col == lax.axis_index("orb") * nb + row % nb, 1.0, 0.0).astype(BF16)
    orbital, col = (lax.broadcasted_iota(jnp.int32, (nb, size), axis) for axis in (0, 1))
    repeat = jnp.where(orbital == col % nb, 1.0, 0.0).astype(BF16)
    row, col = (lax.broadcasted_iota(jnp.int32, (size, size), axis) for axis in (0, 1))
    same = row // nb == col // nb
    dot = lambda x, y, axes: lax.dot_general(x, y, (axes, ((), ())), preferred_element_type=jnp.float32)
    for part, ref in zip(split(total(p_refs, nb, nb)), (high_ref, low_ref)):
        block = dot(mine, part, ((1,), (1,))).astype(BF16)
        ref[...] = jnp.where(same, dot(block, repeat, ((1,), (0,))), 0.0).astype(BF16)


def update_kernel(blocks, sequence, wh_ref, wl_ref, x_ref, *refs):
    g_refs, (grad_hbm, out_hbm, whole, grad, mixed, added, out, sems) = refs[:blocks], refs[blocks:]
    nb, cells, rows_z = x_ref.shape
    rank = lax.axis_index("orb")
    share = rows_z // blocks * nb
    for k, g_ref in zip(sequence, g_refs):
        at = pl.ds(pl.multiple_of((rank ^ k) * share, share), share)
        whole[at, :] = g_ref[...].reshape(share, cells)
    per = nb // CHUNKS
    copies = []
    for i in range(CHUNKS):
        for c in range(i * per, (i + 1) * per):
            plane = whole[pl.ds(c, rows_z, stride=nb), :].T
            grad[c] = plane
            mixed[pl.ds(c, cells, stride=nb), :] = plane
        part = pl.ds(i * per, per)
        copies.append(pltpu.make_async_copy(grad.at[part], grad_hbm.at[part], sems.at[0, i]))
        copies[-1].start()
    size = wh_ref.shape[0]
    mix = (wh_ref[...], wl_ref[...])
    rows = cells // CHUNKS
    tall = rows * nb
    for i in range(CHUNKS):
        parts = split(mixed[i * tall : (i + 1) * tall])
        sides = [jnp.concatenate([p[j : j + size] for j in range(0, tall, size)], axis=1) for p in parts]
        result = dot3(mix, sides, ((1,), (0,)))
        for j in range(tall // size):
            added[i * tall + j * size : i * tall + (j + 1) * size] = result[:, j * rows_z : (j + 1) * rows_z]
        some = pl.ds(i * rows, rows)
        for a in range(nb):
            out[a, some] = x_ref[a, some] + added[pl.ds(i * tall + a, rows, stride=nb), :]
        copies.append(pltpu.make_async_copy(out.at[:, some], out_hbm.at[:, some], sems.at[1, i]))
        copies[-1].start()
    for copy in copies:
        copy.wait()


def swap(value, axis, k):
    count = lax.axis_size(axis)
    return lax.ppermute(value, axis, [(i, i ^ k) for i in range(count)])


def dom_kernel(value_ref, *refs):
    *other_refs, out_ref = refs
    nb = other_refs[0].shape[0]
    out_ref[:nb] = value_ref[:nb] + sum(ref[...] for ref in other_refs)
    out_ref[nb:] = value_ref[nb:]


def total(refs, first, count):
    rows = slice(first, first + count)
    return sum(ref[rows] for ref in refs)


def per_device(orbitals, potential, rotation, block, owner):
    nb, planes, rows_y, rows_z = orbitals.shape
    blocks, doms = lax.axis_size("orb"), lax.axis_size("dom")
    cells = planes * rows_y
    slab = rows_z // blocks
    volume = 1.0 / (cells * doms * rows_z)
    f32 = jnp.float32
    shape = lambda *dims: jax.ShapeDtypeStruct(dims, f32)
    piece, edge = shape(slab, nb, cells), shape(WIDTH, nb, cells)

    flat = orbitals.reshape(nb, cells, rows_z)
    held = pltpu.with_memory_space_constraint(flat, pltpu.HBM)
    chips = half = blocks // 2
    pieces = pl.pallas_call(
        functools.partial(pack_kernel, blocks),
        out_shape=[shape(2, slab, nb, cells)] * chips,
        in_specs=[HBM],
        out_specs=[VMEM] * chips,
        scratch_shapes=[
            pltpu.VMEM((rows_z * nb, cells), f32),
            pltpu.VMEM((nb, cells, rows_z), f32),
            pltpu.SemaphoreType.DMA((CHUNKS,)),
        ],
        compiler_params=params(),
        name="pack",
    )(held)
    last = 2 * (chips - 1)
    pairs = [swap(value, "orb", 2 * m) if m else value for m, value in enumerate(pieces[:-1])]
    direct = [swap(pieces[-1][core], "orb", last + core) for core in range(2)]
    nearest = pl.pallas_call(
        hand_kernel,
        out_shape=piece,
        in_specs=[SMEM, SMEM, VMEM],
        out_specs=VMEM,
        compiler_params=params(),
        name="hand",
    )(block, owner, pairs[1])
    others = [nearest if m == 1 else value[1] for m, value in enumerate(pairs)]
    spread = (pairs + [swap(value, "orb", 1) for value in others] + direct)[::-1]

    side = shape(3 * slab * nb // 4, cells)
    active, near, far, first, last = pl.pallas_call(
        pick_kernel,
        out_shape=(piece, edge, edge, side, side),
        in_specs=[SMEM] + [VMEM] * len(spread),
        out_specs=[VMEM] * 5,
        compiler_params=params(),
        name="pick",
    )(block, *spread)

    up = lambda count: [(i, (i + 1) % count) for i in range(count)]
    down = lambda count: [(i, (i - 1) % count) for i in range(count)]
    x_before = lax.ppermute(last, "dom", up(doms))
    x_after = lax.ppermute(first, "dom", down(doms))
    z_near = swap(near, "orb", 1)
    z_far = lax.ppermute(far, "orb", [(o, (o + 2 * (o % 2) - 1) % blocks) for o in range(blocks)])

    halves = jax.ShapeDtypeStruct((blocks * nb, slab * cells), BF16)
    weights = [jnp.asarray(w) for w in plane_weights(planes, rows_y)]
    *parts, inner = pl.pallas_call(
        functools.partial(split_kernel, blocks),
        out_shape=(halves, halves, piece),
        in_specs=[VMEM] * (len(spread) + 4),
        out_specs=(VMEM, VMEM, VMEM),
        scratch_shapes=[pltpu.VMEM((rows_z, cells), f32)],
        compiler_params=params(),
        cost_estimate=pl.CostEstimate(flops=3 * blocks * nb * slab * cells, bytes_accessed=0, transcendentals=0),
        name="split",
    )(active, potential.reshape(cells, rows_z), *weights, *spread)

    applied, part = pl.pallas_call(
        functools.partial(project_kernel, volume),
        out_shape=(piece, shape(2 * nb, blocks * nb)),
        in_specs=[SMEM] + [VMEM] * 10,
        out_specs=(VMEM, VMEM),
        scratch_shapes=[pltpu.VMEM((2, WIDTH, nb, cells), f32)],
        compiler_params=params(),
        name="project",
    )(owner, rotation, *parts, inner, z_near, z_far, x_before, x_after, *weights)

    part = part + swap(part, "orb", 1)
    part = pl.pallas_call(
        dom_kernel,
        out_shape=shape(2 * nb, blocks * nb),
        in_specs=[VMEM] * doms,
        out_specs=VMEM,
        compiler_params=params(),
        name="dom",
    )(part, *[swap(part[:nb], "dom", k) for k in range(1, doms)])
    sums = [part] + [swap(part, "orb", k) for k in range(2, blocks, 2)]

    own = pl.pallas_call(
        remove_kernel,
        out_shape=piece,
        in_specs=[VMEM] * (3 + chips),
        out_specs=VMEM,
        compiler_params=params(),
        name="remove",
    )(*parts, applied, *sums)

    gathered = [own] + [None] * (blocks - 1)
    for k in range(2, blocks, 2):
        gathered[k] = swap(own, "orb", k)
    for k in range(0, blocks, 2):
        gathered[k + 1] = swap(gathered[k], "orb", 1)

    square = jax.ShapeDtypeStruct((MIX * nb, MIX * nb), BF16)
    mixing = pl.pallas_call(
        functools.partial(mixing_kernel, nb),
        out_shape=(square, square),
        in_specs=[VMEM] * chips,
        out_specs=(VMEM, VMEM),
        compiler_params=params(),
        name="mixing",
    )(*sums)

    sequence = sorted(range(blocks), key=lambda k: (k >= half, -k if k >= half else k))
    gradient, updated = pl.pallas_call(
        functools.partial(update_kernel, blocks, sequence),
        out_shape=(shape(nb, cells, rows_z), shape(nb, cells, rows_z)),
        in_specs=[VMEM] * (3 + blocks),
        out_specs=(HBM, HBM),
        scratch_shapes=[
            pltpu.VMEM((rows_z * nb, cells), f32),
            pltpu.VMEM((nb, cells, rows_z), f32),
            pltpu.VMEM((cells * nb, rows_z), f32),
            pltpu.VMEM((cells * nb, rows_z), f32),
            pltpu.VMEM((nb, cells, rows_z), f32),
            pltpu.SemaphoreType.DMA((2, CHUNKS)),
        ],
        compiler_params=params(),
        name="update",
    )(*mixing, flat, *[gathered[k] for k in sequence])
    return gradient.reshape(orbitals.shape), updated.reshape(orbitals.shape)


def solution(mesh):
    in_specs = (P("orb", "dom", None, None), P("dom", None, None), P("orb", None), P(), P())
    out_specs = (P(None, "dom", None, None), P("orb", "dom", None, None))
    return jax.shard_map(
        per_device, mesh=mesh, in_specs=in_specs, out_specs=out_specs, check_vma=False
    )
```

```python
import functools

import jax
import jax.numpy as jnp
import numpy as np
from jax import lax
from jax.experimental import pallas as pl
from jax.experimental.pallas import tpu as pltpu
from jax.sharding import PartitionSpec as P

CENTER = -5369.0 / 1800.0
SIDES = (12.0 / 7.0, -15.0 / 56.0, 10.0 / 189.0, -1.0 / 112.0, 2.0 / 1925.0, -1.0 / 16632.0)
WIDTH = 6
CHUNKS = 2
MIX = 8
BF16 = jnp.bfloat16
VMEM = pl.BlockSpec(memory_space=pltpu.VMEM)
HBM = pl.BlockSpec(memory_space=pltpu.HBM)
SMEM = pl.BlockSpec(memory_space=pltpu.SMEM)


def params():
    return pltpu.CompilerParams(vmem_limit_bytes=32 * 1024 * 1024)


def plane_weights(planes, rows_y):
    cells = planes * rows_y
    table = np.zeros((3 * cells, cells), np.float64)
    skipped = (planes - WIDTH) * rows_y
    for x in range(planes):
        for y in range(rows_y):
            out = x * rows_y + y
            for k, weight in enumerate(SIDES, 1):
                for step in (k, -k):
                    table[cells + x * rows_y + (y + step) % rows_y, out] += weight
                    row = cells + (x + step) * rows_y + y
                    table[row - skipped if row < cells else row, out] += weight
    table = -0.5 * table
    high = table.astype(BF16)
    return high, (table - high.astype(np.float64)).astype(BF16)


def split(value):
    high = value.astype(BF16)
    return high, (value - high.astype(jnp.float32)).astype(BF16)


def dot3(left, right, contract):
    dot = lambda x, y: lax.dot_general(x, y, (contract, ((), ())), preferred_element_type=jnp.float32)
    return dot(left[0], right[0]) + (dot(left[0], right[1]) + dot(left[1], right[0]))


def pack_kernel(blocks, x_hbm, *refs):
    *t_refs, turned, x_ref, sems = refs
    count, _, rows_z = x_ref.shape
    chunks = sems.shape[0]
    per = count // chunks
    copies = [
        pltpu.make_async_copy(x_hbm.at[pl.ds(i * per, per)], x_ref.at[pl.ds(i * per, per)], sems.at[i])
        for i in range(chunks)
    ]
    for copy in copies:
        copy.start()
    for i, copy in enumerate(copies):
        copy.wait()
        for a in range(i * per, (i + 1) * per):
            turned[pl.ds(a, rows_z, stride=count), :] = x_ref[a].T
    rows = rows_z // blocks * count
    rank = lax.axis_index("orb")
    for m, t_ref in enumerate(t_refs):
        for core in range(2):
            start = pl.multiple_of((rank ^ (2 * m + core)) * rows, rows)
            t_ref[core] = turned[pl.ds(start, rows), :].reshape(t_ref.shape[1:])


def hand_kernel(block_ref, owner_ref, pair_ref, other_ref):
    other_ref[...] = pair_ref[1]


def by_block(refs):
    refs = refs[::-1]
    half = len(refs) // 2 - 1
    return [refs[half + k // 2] if k % 2 else refs[k // 2].at[0] for k in range(2 * half)] + list(refs[2 * half :])


def squeeze(value):
    rows, wide = value.shape
    quarter, free = rows // 4, wide // 4
    lane = lax.broadcasted_iota(jnp.int32, (quarter, wide), 1)
    rest = value[3 * quarter :]
    parts = []
    for j in range(3):
        moved = pltpu.roll(rest, (3 - j) * free, 1)
        parts.append(jnp.where(lane < 3 * free, value[j * quarter : (j + 1) * quarter], moved))
    return jnp.concatenate(parts, axis=0)


def expand(value):
    rows, wide = value.shape
    quarter, free = rows // 3, wide // 4
    lane = lax.broadcasted_iota(jnp.int32, (quarter, wide), 1)
    rest = value[:quarter]
    for j in range(3):
        moved = pltpu.roll(value[j * quarter : (j + 1) * quarter], (j + 1) * free, 1)
        rest = jnp.where((lane >= j * free) & (lane < (j + 1) * free), moved, rest)
    return jnp.concatenate([value, rest], axis=0)


def pick_kernel(block_ref, *refs):
    x_refs, (act_ref, near_ref, far_ref, first_ref, last_ref) = by_block(refs[:-5]), refs[-5:]
    slab, nb, cells = act_ref.shape
    rank = lax.axis_index("orb")
    for k, x_ref in enumerate(x_refs):
        @pl.when((rank ^ block_ref[0]) == k)
        def _(x_ref=x_ref):
            act_ref[...] = x_ref[...]
    odd = rank % 2
    near_ref[...] = act_ref[pl.ds((1 - odd) * (slab - WIDTH), WIDTH)]
    far_ref[...] = act_ref[pl.ds(odd * (slab - WIDTH), WIDTH)]
    flat = act_ref[...].reshape(slab * nb, cells)
    first_ref[...] = squeeze(flat)
    last_ref[...] = squeeze(pltpu.roll(flat, 3 * (cells // 4), 1))


def split_kernel(blocks, act_ref, v_ref, wh_ref, wl_ref, *refs):
    x_refs, (high_ref, low_ref, inner_ref, turned) = by_block(refs[:-4]), refs[-4:]
    slab, nb, cells = act_ref.shape
    rank = lax.axis_index("orb")
    for k, x_ref in enumerate(x_refs):
        rows = pl.ds(pl.multiple_of((rank ^ k) * nb, nb), nb)
        for z in range(slab):
            high, low = split(x_ref[z])
            high_ref[rows, z * cells : (z + 1) * cells] = high
            low_ref[rows, z * cells : (z + 1) * cells] = low
    turned[...] = v_ref[...].T
    mine = pl.ds(pl.multiple_of(rank * slab, slab), slab)
    act = act_ref[...]
    middle = slice(cells, 2 * cells)
    inner = dot3(split(act.reshape(slab * nb, cells)), (wh_ref[middle], wl_ref[middle]), ((1,), (0,)))
    inner = inner.reshape(slab, nb, cells) + (turned[mine, :][:, None, :] - 1.5 * CENTER) * act
    edge = jnp.zeros((WIDTH, nb, cells), jnp.float32)
    tall = jnp.concatenate([edge, act, edge], axis=0)
    for k, weight in enumerate(SIDES, 1):
        upper = tall[WIDTH + k : WIDTH + k + slab]
        lower = tall[WIDTH - k : WIDTH - k + slab]
        inner = inner + (-0.5 * weight) * (upper + lower)
    inner_ref[...] = inner


def project_kernel(
    volume, owner_ref, rot_ref, xh_ref, xl_ref, inner_ref, near_ref, far_ref, xb_ref, xa_ref, wh_ref, wl_ref,
    a_ref, p_ref, around,
):
    slab, nb, cells = inner_ref.shape
    rank = lax.axis_index("orb")
    odd = rank % 2
    around[1 - odd] = near_ref[...]
    around[odd] = far_ref[...]
    before, after = slice(0, cells), slice(2 * cells, 3 * cells)
    applied = dot3(split(expand(xb_ref[...])), (wh_ref[before], wl_ref[before]), ((1,), (0,)))
    applied = applied + dot3(split(expand(xa_ref[...])), (wh_ref[after], wl_ref[after]), ((1,), (0,)))
    a_ref[...] = inner_ref[...] + applied.reshape(slab, nb, cells)
    for z in range(WIDTH):
        below, above = a_ref[z], a_ref[slab - 1 - z]
        for k in range(z + 1, WIDTH + 1):
            below = below + (-0.5 * SIDES[k - 1]) * around[0, WIDTH + z - k]
            above = above + (-0.5 * SIDES[k - 1]) * around[1, k - 1 - z]
        a_ref[z] = below
        a_ref[slab - 1 - z] = above
    flat = jnp.concatenate([a_ref[z] for z in range(slab)], axis=1)
    total = dot3(split(flat), (xh_ref[...], xl_ref[...]), ((1,), (1,)))
    p_ref[:nb] = total * volume
    p_ref[nb:] = jnp.where(rank == owner_ref[0], rot_ref[...], 0.0)


def remove_kernel(xh_ref, xl_ref, a_ref, *refs):
    *p_refs, g_ref = refs
    slab, nb, cells = a_ref.shape
    removed = dot3(split(total(p_refs, 0, nb)), (xh_ref[...], xl_ref[...]), ((1,), (0,)))
    for z in range(slab):
        g_ref[z] = a_ref[z] - removed[:, z * cells : (z + 1) * cells]


def mixing_kernel(nb, *refs):
    *p_refs, high_ref, low_ref = refs
    size, wide = high_ref.shape[0], p_refs[0].shape[1]
    row, col = (lax.broadcasted_iota(jnp.int32, (size, wide), axis) for axis in (0, 1))
    mine = jnp.where(col == lax.axis_index("orb") * nb + row % nb, 1.0, 0.0).astype(BF16)
    orbital, col = (lax.broadcasted_iota(jnp.int32, (nb, size), axis) for axis in (0, 1))
    repeat = jnp.where(orbital == col % nb, 1.0, 0.0).astype(BF16)
    row, col = (lax.broadcasted_iota(jnp.int32, (size, size), axis) for axis in (0, 1))
    same = row // nb == col // nb
    dot = lambda x, y, axes: lax.dot_general(x, y, (axes, ((), ())), preferred_element_type=jnp.float32)
    for part, ref in zip(split(total(p_refs, nb, nb)), (high_ref, low_ref)):
        block = dot(mine, part, ((1,), (1,))).astype(BF16)
        ref[...] = jnp.where(same, dot(block, repeat, ((1,), (0,))), 0.0).astype(BF16)


def update_kernel(blocks, sequence, wh_ref, wl_ref, x_ref, *refs):
    g_refs, (grad_hbm, out_hbm, whole, grad, mixed, added, out, sems) = refs[:blocks], refs[blocks:]
    nb, cells, rows_z = x_ref.shape
    rank = lax.axis_index("orb")
    share = rows_z // blocks * nb
    for k, g_ref in zip(sequence, g_refs):
        at = pl.ds(pl.multiple_of((rank ^ k) * share, share), share)
        whole[at, :] = g_ref[...].reshape(share, cells)
    per = nb // CHUNKS
    copies = []
    for i in range(CHUNKS):
        for c in range(i * per, (i + 1) * per):
            plane = whole[pl.ds(c, rows_z, stride=nb), :].T
            grad[c] = plane
            mixed[pl.ds(c, cells, stride=nb), :] = plane
        part = pl.ds(i * per, per)
        copies.append(pltpu.make_async_copy(grad.at[part], grad_hbm.at[part], sems.at[0, i]))
        copies[-1].start()
    size = wh_ref.shape[0]
    mix = (wh_ref[...], wl_ref[...])
    rows = cells // CHUNKS
    tall = rows * nb
    for i in range(CHUNKS):
        parts = split(mixed[i * tall : (i + 1) * tall])
        sides = [jnp.concatenate([p[j : j + size] for j in range(0, tall, size)], axis=1) for p in parts]
        result = dot3(mix, sides, ((1,), (0,)))
        for j in range(tall // size):
            added[i * tall + j * size : i * tall + (j + 1) * size] = result[:, j * rows_z : (j + 1) * rows_z]
        some = pl.ds(i * rows, rows)
        for a in range(nb):
            out[a, some] = x_ref[a, some] + added[pl.ds(i * tall + a, rows, stride=nb), :]
        copies.append(pltpu.make_async_copy(out.at[:, some], out_hbm.at[:, some], sems.at[1, i]))
        copies[-1].start()
    for copy in copies:
        copy.wait()


def swap(value, axis, k):
    count = lax.axis_size(axis)
    return lax.ppermute(value, axis, [(i, i ^ k) for i in range(count)])


def dom_kernel(value_ref, *refs):
    *other_refs, out_ref = refs
    nb = other_refs[0].shape[0]
    out_ref[:nb] = value_ref[:nb] + sum(ref[...] for ref in other_refs)
    out_ref[nb:] = value_ref[nb:]


def total(refs, first, count):
    rows = slice(first, first + count)
    return sum(ref[rows] for ref in refs)


def per_device(orbitals, potential, rotation, block, owner):
    nb, planes, rows_y, rows_z = orbitals.shape
    blocks, doms = lax.axis_size("orb"), lax.axis_size("dom")
    cells = planes * rows_y
    slab = rows_z // blocks
    volume = 1.0 / (cells * doms * rows_z)
    f32 = jnp.float32
    shape = lambda *dims: jax.ShapeDtypeStruct(dims, f32)
    piece, edge = shape(slab, nb, cells), shape(WIDTH, nb, cells)

    flat = orbitals.reshape(nb, cells, rows_z)
    held = pltpu.with_memory_space_constraint(flat, pltpu.HBM)
    chips = half = blocks // 2
    pieces = pl.pallas_call(
        functools.partial(pack_kernel, blocks),
        out_shape=[shape(2, slab, nb, cells)] * chips,
        in_specs=[HBM],
        out_specs=[VMEM] * chips,
        scratch_shapes=[
            pltpu.VMEM((rows_z * nb, cells), f32),
            pltpu.VMEM((nb, cells, rows_z), f32),
            pltpu.SemaphoreType.DMA((CHUNKS,)),
        ],
        compiler_params=params(),
        name="pack",
    )(held)
    last = 2 * (chips - 1)
    pairs = [swap(value, "orb", 2 * m) if m else value for m, value in enumerate(pieces[:-1])]
    direct = [swap(pieces[-1][core], "orb", last + core) for core in range(2)]
    nearest = pl.pallas_call(
        hand_kernel,
        out_shape=piece,
        in_specs=[SMEM, SMEM, VMEM],
        out_specs=VMEM,
        compiler_params=params(),
        name="hand",
    )(block, owner, pairs[1])
    others = [nearest if m == 1 else value[1] for m, value in enumerate(pairs)]
    spread = (pairs + [swap(value, "orb", 1) for value in others] + direct)[::-1]

    side = shape(3 * slab * nb // 4, cells)
    active, near, far, first, last = pl.pallas_call(
        pick_kernel,
        out_shape=(piece, edge, edge, side, side),
        in_specs=[SMEM] + [VMEM] * len(spread),
        out_specs=[VMEM] * 5,
        compiler_params=params(),
        name="pick",
    )(block, *spread)

    up = lambda count: [(i, (i + 1) % count) for i in range(count)]
    down = lambda count: [(i, (i - 1) % count) for i in range(count)]
    x_before = lax.ppermute(last, "dom", up(doms))
    x_after = lax.ppermute(first, "dom", down(doms))
    z_near = swap(near, "orb", 1)
    z_far = lax.ppermute(far, "orb", [(o, (o + 2 * (o % 2) - 1) % blocks) for o in range(blocks)])

    halves = jax.ShapeDtypeStruct((blocks * nb, slab * cells), BF16)
    weights = [jnp.asarray(w) for w in plane_weights(planes, rows_y)]
    *parts, inner = pl.pallas_call(
        functools.partial(split_kernel, blocks),
        out_shape=(halves, halves, piece),
        in_specs=[VMEM] * (len(spread) + 4),
        out_specs=(VMEM, VMEM, VMEM),
        scratch_shapes=[pltpu.VMEM((rows_z, cells), f32)],
        compiler_params=params(),
        cost_estimate=pl.CostEstimate(flops=3 * blocks * nb * slab * cells, bytes_accessed=0, transcendentals=0),
        name="split",
    )(active, potential.reshape(cells, rows_z), *weights, *spread)

    applied, part = pl.pallas_call(
        functools.partial(project_kernel, volume),
        out_shape=(piece, shape(2 * nb, blocks * nb)),
        in_specs=[SMEM] + [VMEM] * 10,
        out_specs=(VMEM, VMEM),
        scratch_shapes=[pltpu.VMEM((2, WIDTH, nb, cells), f32)],
        compiler_params=params(),
        name="project",
    )(owner, rotation, *parts, inner, z_near, z_far, x_before, x_after, *weights)

    part = part + swap(part, "orb", 1)
    part = pl.pallas_call(
        dom_kernel,
        out_shape=shape(2 * nb, blocks * nb),
        in_specs=[VMEM] * doms,
        out_specs=VMEM,
        compiler_params=params(),
        name="dom",
    )(part, *[swap(part[:nb], "dom", k) for k in range(1, doms)])
    sums = [part] + [swap(part, "orb", k) for k in range(2, blocks, 2)]

    own = pl.pallas_call(
        remove_kernel,
        out_shape=piece,
        in_specs=[VMEM] * (3 + chips),
        out_specs=VMEM,
        compiler_params=params(),
        name="remove",
    )(*parts, applied, *sums)

    gathered = [own] + [None] * (blocks - 1)
    for k in range(2, blocks, 2):
        gathered[k] = swap(own, "orb", k)
    for k in range(0, blocks, 2):
        gathered[k + 1] = swap(gathered[k], "orb", 1)

    square = jax.ShapeDtypeStruct((MIX * nb, MIX * nb), BF16)
    mixing = pl.pallas_call(
        functools.partial(mixing_kernel, nb),
        out_shape=(square, square),
        in_specs=[VMEM] * chips,
        out_specs=(VMEM, VMEM),
        compiler_params=params(),
        name="mixing",
    )(*sums)

    sequence = sorted(range(blocks), key=lambda k: (k >= half, -k if k >= half else k))
    gradient, updated = pl.pallas_call(
        functools.partial(update_kernel, blocks, sequence),
        out_shape=(shape(nb, cells, rows_z), shape(nb, cells, rows_z)),
        in_specs=[VMEM] * (3 + blocks),
        out_specs=(HBM, HBM),
        scratch_shapes=[
            pltpu.VMEM((rows_z * nb, cells), f32),
            pltpu.VMEM((nb, cells, rows_z), f32),
            pltpu.VMEM((cells * nb, rows_z), f32),
            pltpu.VMEM((cells * nb, rows_z), f32),
            pltpu.VMEM((nb, cells, rows_z), f32),
            pltpu.SemaphoreType.DMA((2, CHUNKS)),
        ],
        compiler_params=params(),
        name="update",
    )(*mixing, flat, *[gathered[k] for k in sequence])
    return gradient.reshape(orbitals.shape), updated.reshape(orbitals.shape)


def solution(mesh):
    in_specs = (P("orb", "dom", None, None), P("dom", None, None), P("orb", None), P(), P())
    out_specs = (P(None, "dom", None, None), P("orb", "dom", None, None))
    return jax.shard_map(
        per_device, mesh=mesh, in_specs=in_specs, out_specs=out_specs, check_vma=False
    )
```

```python
import functools

import jax
import jax.numpy as jnp
import numpy as np
from jax import lax
from jax.experimental import pallas as pl
from jax.experimental.pallas import tpu as pltpu
from jax.sharding import PartitionSpec as P

CENTER = -5369.0 / 1800.0
SIDES = (12.0 / 7.0, -15.0 / 56.0, 10.0 / 189.0, -1.0 / 112.0, 2.0 / 1925.0, -1.0 / 16632.0)
WIDTH = 6
CHUNKS = 4
MIX = 8
BF16 = jnp.bfloat16
VMEM = pl.BlockSpec(memory_space=pltpu.VMEM)
HBM = pl.BlockSpec(memory_space=pltpu.HBM)
SMEM = pl.BlockSpec(memory_space=pltpu.SMEM)


def params():
    return pltpu.CompilerParams(vmem_limit_bytes=32 * 1024 * 1024)


def plane_weights(planes, rows_y):
    cells = planes * rows_y
    table = np.zeros((3 * cells, cells), np.float64)
    skipped = (planes - WIDTH) * rows_y
    for x in range(planes):
        for y in range(rows_y):
            out = x * rows_y + y
            for k, weight in enumerate(SIDES, 1):
                for step in (k, -k):
                    table[cells + x * rows_y + (y + step) % rows_y, out] += weight
                    row = cells + (x + step) * rows_y + y
                    table[row - skipped if row < cells else row, out] += weight
    table = -0.5 * table
    high = table.astype(BF16)
    return high, (table - high.astype(np.float64)).astype(BF16)


def split(value):
    high = value.astype(BF16)
    return high, (value - high.astype(jnp.float32)).astype(BF16)


def dot3(left, right, contract):
    dot = lambda x, y: lax.dot_general(x, y, (contract, ((), ())), preferred_element_type=jnp.float32)
    return dot(left[0], right[0]) + (dot(left[0], right[1]) + dot(left[1], right[0]))


def pack_kernel(blocks, x_hbm, *refs):
    *t_refs, turned, x_ref, sems = refs
    count, _, rows_z = x_ref.shape
    chunks = sems.shape[0]
    per = count // chunks
    copies = [
        pltpu.make_async_copy(x_hbm.at[pl.ds(i * per, per)], x_ref.at[pl.ds(i * per, per)], sems.at[i])
        for i in range(chunks)
    ]
    for copy in copies:
        copy.start()
    for i, copy in enumerate(copies):
        copy.wait()
        for a in range(i * per, (i + 1) * per):
            turned[pl.ds(a, rows_z, stride=count), :] = x_ref[a].T
    rows = rows_z // blocks * count
    rank = lax.axis_index("orb")
    for m, t_ref in enumerate(t_refs):
        for core in range(2):
            start = pl.multiple_of((rank ^ (2 * m + core)) * rows, rows)
            t_ref[core] = turned[pl.ds(start, rows), :].reshape(t_ref.shape[1:])


def hand_kernel(block_ref, owner_ref, pair_ref, other_ref):
    other_ref[...] = pair_ref[1]


def by_block(refs):
    refs = refs[::-1]
    half = len(refs) // 2 - 1
    return [refs[half + k // 2] if k % 2 else refs[k // 2].at[0] for k in range(2 * half)] + list(refs[2 * half :])


def squeeze(value):
    rows, wide = value.shape
    quarter, free = rows // 4, wide // 4
    lane = lax.broadcasted_iota(jnp.int32, (quarter, wide), 1)
    rest = value[3 * quarter :]
    parts = []
    for j in range(3):
        moved = pltpu.roll(rest, (3 - j) * free, 1)
        parts.append(jnp.where(lane < 3 * free, value[j * quarter : (j + 1) * quarter], moved))
    return jnp.concatenate(parts, axis=0)


def expand(value):
    rows, wide = value.shape
    quarter, free = rows // 3, wide // 4
    lane = lax.broadcasted_iota(jnp.int32, (quarter, wide), 1)
    rest = value[:quarter]
    for j in range(3):
        moved = pltpu.roll(value[j * quarter : (j + 1) * quarter], (j + 1) * free, 1)
        rest = jnp.where((lane >= j * free) & (lane < (j + 1) * free), moved, rest)
    return jnp.concatenate([value, rest], axis=0)


def pick_kernel(block_ref, *refs):
    x_refs, (act_ref, near_ref, far_ref, first_ref, last_ref) = by_block(refs[:-5]), refs[-5:]
    slab, nb, cells = act_ref.shape
    rank = lax.axis_index("orb")
    for k, x_ref in enumerate(x_refs):
        @pl.when((rank ^ block_ref[0]) == k)
        def _(x_ref=x_ref):
            act_ref[...] = x_ref[...]
    odd = rank % 2
    near_ref[...] = act_ref[pl.ds((1 - odd) * (slab - WIDTH), WIDTH)]
    far_ref[...] = act_ref[pl.ds(odd * (slab - WIDTH), WIDTH)]
    flat = act_ref[...].reshape(slab * nb, cells)
    first_ref[...] = squeeze(flat)
    last_ref[...] = squeeze(pltpu.roll(flat, 3 * (cells // 4), 1))


def split_kernel(blocks, act_ref, v_ref, wh_ref, wl_ref, *refs):
    x_refs, (high_ref, low_ref, inner_ref, turned) = by_block(refs[:-4]), refs[-4:]
    slab, nb, cells = act_ref.shape
    rank = lax.axis_index("orb")
    for k, x_ref in enumerate(x_refs):
        rows = pl.ds(pl.multiple_of((rank ^ k) * nb, nb), nb)
        for z in range(slab):
            high, low = split(x_ref[z])
            high_ref[rows, z * cells : (z + 1) * cells] = high
            low_ref[rows, z * cells : (z + 1) * cells] = low
    turned[...] = v_ref[...].T
    mine = pl.ds(pl.multiple_of(rank * slab, slab), slab)
    act = act_ref[...]
    middle = slice(cells, 2 * cells)
    inner = dot3(split(act.reshape(slab * nb, cells)), (wh_ref[middle], wl_ref[middle]), ((1,), (0,)))
    inner = inner.reshape(slab, nb, cells) + (turned[mine, :][:, None, :] - 1.5 * CENTER) * act
    edge = jnp.zeros((WIDTH, nb, cells), jnp.float32)
    tall = jnp.concatenate([edge, act, edge], axis=0)
    for k, weight in enumerate(SIDES, 1):
        upper = tall[WIDTH + k : WIDTH + k + slab]
        lower = tall[WIDTH - k : WIDTH - k + slab]
        inner = inner + (-0.5 * weight) * (upper + lower)
    inner_ref[...] = inner


def project_kernel(
    volume, owner_ref, rot_ref, xh_ref, xl_ref, inner_ref, near_ref, far_ref, xb_ref, xa_ref, wh_ref, wl_ref,
    a_ref, p_ref, around,
):
    slab, nb, cells = inner_ref.shape
    rank = lax.axis_index("orb")
    odd = rank % 2
    around[1 - odd] = near_ref[...]
    around[odd] = far_ref[...]
    before, after = slice(0, cells), slice(2 * cells, 3 * cells)
    applied = dot3(split(expand(xb_ref[...])), (wh_ref[before], wl_ref[before]), ((1,), (0,)))
    applied = applied + dot3(split(expand(xa_ref[...])), (wh_ref[after], wl_ref[after]), ((1,), (0,)))
    a_ref[...] = inner_ref[...] + applied.reshape(slab, nb, cells)
    for z in range(WIDTH):
        below, above = a_ref[z], a_ref[slab - 1 - z]
        for k in range(z + 1, WIDTH + 1):
            below = below + (-0.5 * SIDES[k - 1]) * around[0, WIDTH + z - k]
            above = above + (-0.5 * SIDES[k - 1]) * around[1, k - 1 - z]
        a_ref[z] = below
        a_ref[slab - 1 - z] = above
    flat = jnp.concatenate([a_ref[z] for z in range(slab)], axis=1)
    total = dot3(split(flat), (xh_ref[...], xl_ref[...]), ((1,), (1,)))
    p_ref[:nb] = total * volume
    p_ref[nb:] = jnp.where(rank == owner_ref[0], rot_ref[...], 0.0)


def remove_kernel(xh_ref, xl_ref, a_ref, *refs):
    *p_refs, g_ref = refs
    slab, nb, cells = a_ref.shape
    removed = dot3(split(total(p_refs, 0, nb)), (xh_ref[...], xl_ref[...]), ((1,), (0,)))
    for z in range(slab):
        g_ref[z] = a_ref[z] - removed[:, z * cells : (z + 1) * cells]


def mixing_kernel(nb, *refs):
    *p_refs, high_ref, low_ref = refs
    size, wide = high_ref.shape[0], p_refs[0].shape[1]
    row, col = (lax.broadcasted_iota(jnp.int32, (size, wide), axis) for axis in (0, 1))
    mine = jnp.where(col == lax.axis_index("orb") * nb + row % nb, 1.0, 0.0).astype(BF16)
    orbital, col = (lax.broadcasted_iota(jnp.int32, (nb, size), axis) for axis in (0, 1))
    repeat = jnp.where(orbital == col % nb, 1.0, 0.0).astype(BF16)
    row, col = (lax.broadcasted_iota(jnp.int32, (size, size), axis) for axis in (0, 1))
    same = row // nb == col // nb
    dot = lambda x, y, axes: lax.dot_general(x, y, (axes, ((), ())), preferred_element_type=jnp.float32)
    for part, ref in zip(split(total(p_refs, nb, nb)), (high_ref, low_ref)):
        block = dot(mine, part, ((1,), (1,))).astype(BF16)
        ref[...] = jnp.where(same, dot(block, repeat, ((1,), (0,))), 0.0).astype(BF16)


def update_kernel(blocks, sequence, wh_ref, wl_ref, x_ref, *refs):
    *g_refs, grad_hbm, out_hbm, whole, grad, mixed, added, out, sems = refs
    nb, cells, rows_z = x_ref.shape
    rank = lax.axis_index("orb")
    share = rows_z // blocks * nb
    for (k, first), g_ref in zip(sequence, g_refs):
        start = (rank ^ k) * share
        count = g_ref.shape[1]
        if count == nb:
            whole[pl.ds(pl.multiple_of(start, share), share), :] = g_ref[...].reshape(share, cells)
        else:
            for z in range(g_ref.shape[0]):
                whole[pl.ds(pl.multiple_of(start + z * nb + first, count), count), :] = g_ref[z]
    per = nb // CHUNKS
    copies = []
    for i in range(CHUNKS):
        for c in range(i * per, (i + 1) * per):
            plane = whole[pl.ds(c, rows_z, stride=nb), :].T
            grad[c] = plane
            mixed[pl.ds(c, cells, stride=nb), :] = plane
        part = pl.ds(i * per, per)
        copies.append(pltpu.make_async_copy(grad.at[part], grad_hbm.at[part], sems.at[0, i]))
        copies[-1].start()
    size = wh_ref.shape[0]
    mix = (wh_ref[...], wl_ref[...])
    rows = cells // CHUNKS
    tall = rows * nb
    for i in range(CHUNKS):
        parts = split(mixed[i * tall : (i + 1) * tall])
        sides = [jnp.concatenate([p[j : j + size] for j in range(0, tall, size)], axis=1) for p in parts]
        result = dot3(mix, sides, ((1,), (0,)))
        for j in range(tall // size):
            added[i * tall + j * size : i * tall + (j + 1) * size] = result[:, j * rows_z : (j + 1) * rows_z]
        some = pl.ds(i * rows, rows)
        for a in range(nb):
            out[a, some] = x_ref[a, some] + added[pl.ds(i * tall + a, rows, stride=nb), :]
        copies.append(pltpu.make_async_copy(out.at[:, some], out_hbm.at[:, some], sems.at[1, i]))
        copies[-1].start()
    for copy in copies:
        copy.wait()


def swap(value, axis, k):
    count = lax.axis_size(axis)
    return lax.ppermute(value, axis, [(i, i ^ k) for i in range(count)])


def dom_kernel(value_ref, *refs):
    *other_refs, out_ref = refs
    nb = other_refs[0].shape[0]
    out_ref[:nb] = value_ref[:nb] + sum(ref[...] for ref in other_refs)
    out_ref[nb:] = value_ref[nb:]


def total(refs, first, count):
    rows = slice(first, first + count)
    return sum(ref[rows] for ref in refs)


def per_device(orbitals, potential, rotation, block, owner):
    nb, planes, rows_y, rows_z = orbitals.shape
    blocks, doms = lax.axis_size("orb"), lax.axis_size("dom")
    cells = planes * rows_y
    slab = rows_z // blocks
    volume = 1.0 / (cells * doms * rows_z)
    f32 = jnp.float32
    shape = lambda *dims: jax.ShapeDtypeStruct(dims, f32)
    piece, edge = shape(slab, nb, cells), shape(WIDTH, nb, cells)

    flat = orbitals.reshape(nb, cells, rows_z)
    held = pltpu.with_memory_space_constraint(flat, pltpu.HBM)
    chips = half = blocks // 2
    pieces = pl.pallas_call(
        functools.partial(pack_kernel, blocks),
        out_shape=[shape(2, slab, nb, cells)] * chips,
        in_specs=[HBM],
        out_specs=[VMEM] * chips,
        scratch_shapes=[
            pltpu.VMEM((rows_z * nb, cells), f32),
            pltpu.VMEM((nb, cells, rows_z), f32),
            pltpu.SemaphoreType.DMA((CHUNKS,)),
        ],
        compiler_params=params(),
        name="pack",
    )(held)
    last = 2 * (chips - 1)
    pairs = [swap(value, "orb", 2 * m) if m else value for m, value in enumerate(pieces[:-1])]
    direct = [swap(pieces[-1][core], "orb", last + core) for core in range(2)]
    nearest = pl.pallas_call(
        hand_kernel,
        out_shape=piece,
        in_specs=[SMEM, SMEM, VMEM],
        out_specs=VMEM,
        compiler_params=params(),
        name="hand",
    )(block, owner, pairs[1])
    others = [nearest if m == 1 else value[1] for m, value in enumerate(pairs)]
    spread = (pairs + [swap(value, "orb", 1) for value in others] + direct)[::-1]

    side = shape(3 * slab * nb // 4, cells)
    active, near, far, first, last = pl.pallas_call(
        pick_kernel,
        out_shape=(piece, edge, edge, side, side),
        in_specs=[SMEM] + [VMEM] * len(spread),
        out_specs=[VMEM] * 5,
        compiler_params=params(),
        name="pick",
    )(block, *spread)

    up = lambda count: [(i, (i + 1) % count) for i in range(count)]
    down = lambda count: [(i, (i - 1) % count) for i in range(count)]
    x_before = lax.ppermute(last, "dom", up(doms))
    x_after = lax.ppermute(first, "dom", down(doms))
    z_near = swap(near, "orb", 1)
    z_far = lax.ppermute(far, "orb", [(o, (o + 2 * (o % 2) - 1) % blocks) for o in range(blocks)])

    halves = jax.ShapeDtypeStruct((blocks * nb, slab * cells), BF16)
    weights = [jnp.asarray(w) for w in plane_weights(planes, rows_y)]
    *parts, inner = pl.pallas_call(
        functools.partial(split_kernel, blocks),
        out_shape=(halves, halves, piece),
        in_specs=[VMEM] * (len(spread) + 4),
        out_specs=(VMEM, VMEM, VMEM),
        scratch_shapes=[pltpu.VMEM((rows_z, cells), f32)],
        compiler_params=params(),
        cost_estimate=pl.CostEstimate(flops=3 * blocks * nb * slab * cells, bytes_accessed=0, transcendentals=0),
        name="split",
    )(active, potential.reshape(cells, rows_z), *weights, *spread)

    applied, part = pl.pallas_call(
        functools.partial(project_kernel, volume),
        out_shape=(piece, shape(2 * nb, blocks * nb)),
        in_specs=[SMEM] + [VMEM] * 10,
        out_specs=(VMEM, VMEM),
        scratch_shapes=[pltpu.VMEM((2, WIDTH, nb, cells), f32)],
        compiler_params=params(),
        name="project",
    )(owner, rotation, *parts, inner, z_near, z_far, x_before, x_after, *weights)

    part = part + swap(part, "orb", 1)
    part = pl.pallas_call(
        dom_kernel,
        out_shape=shape(2 * nb, blocks * nb),
        in_specs=[VMEM] * doms,
        out_specs=VMEM,
        compiler_params=params(),
        name="dom",
    )(part, *[swap(part[:nb], "dom", k) for k in range(1, doms)])
    sums = [part] + [swap(part, "orb", k) for k in range(2, blocks, 2)]

    own = pl.pallas_call(
        remove_kernel,
        out_shape=piece,
        in_specs=[VMEM] * (3 + chips),
        out_specs=VMEM,
        compiler_params=params(),
        name="remove",
    )(*parts, applied, *sums)

    part = nb // 2
    gathered = [[own]] + [None] * (blocks - 1)
    for k in range(2, blocks, 2):
        top = 1 << (k.bit_length() - 1)
        if k == top:
            gathered[k] = [swap(own, "orb", k)]
        else:
            gathered[k] = [swap(own[:, :part], "orb", k), swap(gathered[top][0][:, part:], "orb", k - top)]
    for k in range(0, blocks, 2):
        gathered[k + 1] = [swap(value, "orb", 1) for value in gathered[k]]

    square = jax.ShapeDtypeStruct((MIX * nb, MIX * nb), BF16)
    mixing = pl.pallas_call(
        functools.partial(mixing_kernel, nb),
        out_shape=(square, square),
        in_specs=[VMEM] * chips,
        out_specs=(VMEM, VMEM),
        compiler_params=params(),
        name="mixing",
    )(*sums)

    order = sorted(range(blocks), key=lambda k: (k >= half, -k if k >= half else k))
    sequence = [(k, i * part) for k in order for i in range(len(gathered[k]))]
    gradient, updated = pl.pallas_call(
        functools.partial(update_kernel, blocks, sequence),
        out_shape=(shape(nb, cells, rows_z), shape(nb, cells, rows_z)),
        in_specs=[VMEM] * (3 + len(sequence)),
        out_specs=(HBM, HBM),
        scratch_shapes=[
            pltpu.VMEM((rows_z * nb, cells), f32),
            pltpu.VMEM((nb, cells, rows_z), f32),
            pltpu.VMEM((cells * nb, rows_z), f32),
            pltpu.VMEM((cells * nb, rows_z), f32),
            pltpu.VMEM((nb, cells, rows_z), f32),
            pltpu.SemaphoreType.DMA((2, CHUNKS)),
        ],
        compiler_params=params(),
        name="update",
    )(*mixing, flat, *[value for k in order for value in gathered[k]])
    return gradient.reshape(orbitals.shape), updated.reshape(orbitals.shape)


def solution(mesh):
    in_specs = (P("orb", "dom", None, None), P("dom", None, None), P("orb", None), P(), P())
    out_specs = (P(None, "dom", None, None), P("orb", "dom", None, None))
    return jax.shard_map(
        per_device, mesh=mesh, in_specs=in_specs, out_specs=out_specs, check_vma=False
    )
```

```python
import functools

import jax
import jax.numpy as jnp
import numpy as np
from jax import lax
from jax.experimental import pallas as pl
from jax.experimental.pallas import tpu as pltpu
from jax.sharding import PartitionSpec as P

CENTER = -5369.0 / 1800.0
SIDES = (12.0 / 7.0, -15.0 / 56.0, 10.0 / 189.0, -1.0 / 112.0, 2.0 / 1925.0, -1.0 / 16632.0)
WIDTH = 6
CHUNKS = 4
MIX = 8
BF16 = jnp.bfloat16
VMEM = pl.BlockSpec(memory_space=pltpu.VMEM)
HBM = pl.BlockSpec(memory_space=pltpu.HBM)
SMEM = pl.BlockSpec(memory_space=pltpu.SMEM)


def params():
    return pltpu.CompilerParams(vmem_limit_bytes=32 * 1024 * 1024)


def plane_weights(planes, rows_y):
    cells = planes * rows_y
    table = np.zeros((3 * cells, cells), np.float64)
    skipped = (planes - WIDTH) * rows_y
    for x in range(planes):
        for y in range(rows_y):
            out = x * rows_y + y
            for k, weight in enumerate(SIDES, 1):
                for step in (k, -k):
                    table[cells + x * rows_y + (y + step) % rows_y, out] += weight
                    row = cells + (x + step) * rows_y + y
                    table[row - skipped if row < cells else row, out] += weight
    table = -0.5 * table
    high = table.astype(BF16)
    return high, (table - high.astype(np.float64)).astype(BF16)


def split(value):
    high = value.astype(BF16)
    return high, (value - high.astype(jnp.float32)).astype(BF16)


def dot3(left, right, contract):
    dot = lambda x, y: lax.dot_general(x, y, (contract, ((), ())), preferred_element_type=jnp.float32)
    return dot(left[0], right[0]) + (dot(left[0], right[1]) + dot(left[1], right[0]))


def pack_kernel(blocks, x_hbm, *refs):
    *t_refs, turned, x_ref, sems = refs
    count, _, rows_z = x_ref.shape
    chunks = sems.shape[0]
    per = count // chunks
    copies = [
        pltpu.make_async_copy(x_hbm.at[pl.ds(i * per, per)], x_ref.at[pl.ds(i * per, per)], sems.at[i])
        for i in range(chunks)
    ]
    for copy in copies:
        copy.start()
    for i, copy in enumerate(copies):
        copy.wait()
        for a in range(i * per, (i + 1) * per):
            turned[pl.ds(a, rows_z, stride=count), :] = x_ref[a].T
    rows = rows_z // blocks * count
    rank = lax.axis_index("orb")
    for m, t_ref in enumerate(t_refs):
        for core in range(2):
            start = pl.multiple_of((rank ^ (2 * m + core)) * rows, rows)
            t_ref[core] = turned[pl.ds(start, rows), :].reshape(t_ref.shape[1:])


def hand_kernel(block_ref, owner_ref, pair_ref, other_ref):
    other_ref[...] = pair_ref[1]


def by_block(refs):
    refs = refs[::-1]
    half = len(refs) // 2 - 1
    return [refs[half + k // 2] if k % 2 else refs[k // 2].at[0] for k in range(2 * half)] + list(refs[2 * half :])


def squeeze(value):
    rows, wide = value.shape
    quarter, free = rows // 4, wide // 4
    lane = lax.broadcasted_iota(jnp.int32, (quarter, wide), 1)
    rest = value[3 * quarter :]
    parts = []
    for j in range(3):
        moved = pltpu.roll(rest, (3 - j) * free, 1)
        parts.append(jnp.where(lane < 3 * free, value[j * quarter : (j + 1) * quarter], moved))
    return jnp.concatenate(parts, axis=0)


def expand(value):
    rows, wide = value.shape
    quarter, free = rows // 3, wide // 4
    lane = lax.broadcasted_iota(jnp.int32, (quarter, wide), 1)
    rest = value[:quarter]
    for j in range(3):
        moved = pltpu.roll(value[j * quarter : (j + 1) * quarter], (j + 1) * free, 1)
        rest = jnp.where((lane >= j * free) & (lane < (j + 1) * free), moved, rest)
    return jnp.concatenate([value, rest], axis=0)


def pick_kernel(block_ref, *refs):
    x_refs, (act_ref, near_ref, far_ref, first_ref, last_ref) = by_block(refs[:-5]), refs[-5:]
    slab, nb, cells = act_ref.shape
    rank = lax.axis_index("orb")
    for k, x_ref in enumerate(x_refs):
        @pl.when((rank ^ block_ref[0]) == k)
        def _(x_ref=x_ref):
            act_ref[...] = x_ref[...]
    odd = rank % 2
    near_ref[...] = act_ref[pl.ds((1 - odd) * (slab - WIDTH), WIDTH)]
    far_ref[...] = act_ref[pl.ds(odd * (slab - WIDTH), WIDTH)]
    flat = act_ref[...].reshape(slab * nb, cells)
    first_ref[...] = squeeze(flat)
    last_ref[...] = squeeze(pltpu.roll(flat, 3 * (cells // 4), 1))


def split_kernel(blocks, act_ref, v_ref, wh_ref, wl_ref, *refs):
    x_refs, (high_ref, low_ref, inner_ref, turned) = by_block(refs[:-4]), refs[-4:]
    slab, nb, cells = act_ref.shape
    rank = lax.axis_index("orb")
    for k, x_ref in enumerate(x_refs):
        rows = pl.ds(pl.multiple_of((rank ^ k) * nb, nb), nb)
        for z in range(slab):
            high, low = split(x_ref[z])
            high_ref[rows, z * cells : (z + 1) * cells] = high
            low_ref[rows, z * cells : (z + 1) * cells] = low
    turned[...] = v_ref[...].T
    mine = pl.ds(pl.multiple_of(rank * slab, slab), slab)
    act = act_ref[...]
    middle = slice(cells, 2 * cells)
    inner = dot3(split(act.reshape(slab * nb, cells)), (wh_ref[middle], wl_ref[middle]), ((1,), (0,)))
    inner = inner.reshape(slab, nb, cells) + (turned[mine, :][:, None, :] - 1.5 * CENTER) * act
    edge = jnp.zeros((WIDTH, nb, cells), jnp.float32)
    tall = jnp.concatenate([edge, act, edge], axis=0)
    for k, weight in enumerate(SIDES, 1):
        upper = tall[WIDTH + k : WIDTH + k + slab]
        lower = tall[WIDTH - k : WIDTH - k + slab]
        inner = inner + (-0.5 * weight) * (upper + lower)
    inner_ref[...] = inner


def project_kernel(
    volume, owner_ref, rot_ref, xh_ref, xl_ref, inner_ref, near_ref, far_ref, xb_ref, xa_ref, wh_ref, wl_ref,
    a_ref, p_ref, around,
):
    slab, nb, cells = inner_ref.shape
    rank = lax.axis_index("orb")
    odd = rank % 2
    around[1 - odd] = near_ref[...]
    around[odd] = far_ref[...]
    before, after = slice(0, cells), slice(2 * cells, 3 * cells)
    applied = dot3(split(expand(xb_ref[...])), (wh_ref[before], wl_ref[before]), ((1,), (0,)))
    applied = applied + dot3(split(expand(xa_ref[...])), (wh_ref[after], wl_ref[after]), ((1,), (0,)))
    a_ref[...] = inner_ref[...] + applied.reshape(slab, nb, cells)
    for z in range(WIDTH):
        below, above = a_ref[z], a_ref[slab - 1 - z]
        for k in range(z + 1, WIDTH + 1):
            below = below + (-0.5 * SIDES[k - 1]) * around[0, WIDTH + z - k]
            above = above + (-0.5 * SIDES[k - 1]) * around[1, k - 1 - z]
        a_ref[z] = below
        a_ref[slab - 1 - z] = above
    flat = jnp.concatenate([a_ref[z] for z in range(slab)], axis=1)
    total = dot3(split(flat), (xh_ref[...], xl_ref[...]), ((1,), (1,)))
    p_ref[:nb] = total * volume
    p_ref[nb:] = jnp.where(rank == owner_ref[0], rot_ref[...], 0.0)


def remove_kernel(xh_ref, xl_ref, a_ref, *refs):
    *p_refs, g_ref = refs
    slab, nb, cells = a_ref.shape
    removed = dot3(split(total(p_refs, 0, nb)), (xh_ref[...], xl_ref[...]), ((1,), (0,)))
    for z in range(slab):
        g_ref[z] = a_ref[z] - removed[:, z * cells : (z + 1) * cells]


def mixing_kernel(nb, *refs):
    *p_refs, high_ref, low_ref = refs
    size, wide = high_ref.shape[0], p_refs[0].shape[1]
    row, col = (lax.broadcasted_iota(jnp.int32, (size, wide), axis) for axis in (0, 1))
    mine = jnp.where(col == lax.axis_index("orb") * nb + row % nb, 1.0, 0.0).astype(BF16)
    orbital, col = (lax.broadcasted_iota(jnp.int32, (nb, size), axis) for axis in (0, 1))
    repeat = jnp.where(orbital == col % nb, 1.0, 0.0).astype(BF16)
    row, col = (lax.broadcasted_iota(jnp.int32, (size, size), axis) for axis in (0, 1))
    same = row // nb == col // nb
    dot = lambda x, y, axes: lax.dot_general(x, y, (axes, ((), ())), preferred_element_type=jnp.float32)
    for part, ref in zip(split(total(p_refs, nb, nb)), (high_ref, low_ref)):
        block = dot(mine, part, ((1,), (1,))).astype(BF16)
        ref[...] = jnp.where(same, dot(block, repeat, ((1,), (0,))), 0.0).astype(BF16)


def update_kernel(blocks, sequence, wh_ref, wl_ref, x_ref, *refs):
    g_refs, (grad_hbm, out_hbm, whole, grad, mixed, added, out, sems) = refs[:blocks], refs[blocks:]
    nb, cells, rows_z = x_ref.shape
    rank = lax.axis_index("orb")
    share = rows_z // blocks * nb
    for k, g_ref in zip(sequence, g_refs):
        at = pl.ds(pl.multiple_of((rank ^ k) * share, share), share)
        whole[at, :] = g_ref[...].reshape(share, cells)
    per = nb // CHUNKS
    copies = []
    for i in range(CHUNKS):
        for c in range(i * per, (i + 1) * per):
            plane = whole[pl.ds(c, rows_z, stride=nb), :].T
            grad[c] = plane
            mixed[pl.ds(c, cells, stride=nb), :] = plane
        part = pl.ds(i * per, per)
        copies.append(pltpu.make_async_copy(grad.at[part], grad_hbm.at[part], sems.at[0, i]))
        copies[-1].start()
    size = wh_ref.shape[0]
    mix = (wh_ref[...], wl_ref[...])
    rows = cells // CHUNKS
    tall = rows * nb
    for i in range(CHUNKS):
        parts = split(mixed[i * tall : (i + 1) * tall])
        sides = [jnp.concatenate([p[j : j + size] for j in range(0, tall, size)], axis=1) for p in parts]
        result = dot3(mix, sides, ((1,), (0,)))
        for j in range(tall // size):
            added[i * tall + j * size : i * tall + (j + 1) * size] = result[:, j * rows_z : (j + 1) * rows_z]
        some = pl.ds(i * rows, rows)
        for a in range(nb):
            out[a, some] = x_ref[a, some] + added[pl.ds(i * tall + a, rows, stride=nb), :]
        copies.append(pltpu.make_async_copy(out.at[:, some], out_hbm.at[:, some], sems.at[1, i]))
        copies[-1].start()
    for copy in copies:
        copy.wait()


def swap(value, axis, k):
    count = lax.axis_size(axis)
    return lax.ppermute(value, axis, [(i, i ^ k) for i in range(count)])


def dom_kernel(value_ref, *refs):
    *other_refs, out_ref = refs
    nb = other_refs[0].shape[0]
    out_ref[:nb] = value_ref[:nb] + sum(ref[...] for ref in other_refs)
    out_ref[nb:] = value_ref[nb:]


def total(refs, first, count):
    rows = slice(first, first + count)
    return sum(ref[rows] for ref in refs)


def per_device(orbitals, potential, rotation, block, owner):
    nb, planes, rows_y, rows_z = orbitals.shape
    blocks, doms = lax.axis_size("orb"), lax.axis_size("dom")
    cells = planes * rows_y
    slab = rows_z // blocks
    volume = 1.0 / (cells * doms * rows_z)
    f32 = jnp.float32
    shape = lambda *dims: jax.ShapeDtypeStruct(dims, f32)
    piece, edge = shape(slab, nb, cells), shape(WIDTH, nb, cells)

    flat = orbitals.reshape(nb, cells, rows_z)
    held = pltpu.with_memory_space_constraint(flat, pltpu.HBM)
    chips = half = blocks // 2
    pieces = pl.pallas_call(
        functools.partial(pack_kernel, blocks),
        out_shape=[shape(2, slab, nb, cells)] * chips,
        in_specs=[HBM],
        out_specs=[VMEM] * chips,
        scratch_shapes=[
            pltpu.VMEM((rows_z * nb, cells), f32),
            pltpu.VMEM((nb, cells, rows_z), f32),
            pltpu.SemaphoreType.DMA((CHUNKS,)),
        ],
        compiler_params=params(),
        name="pack",
    )(held)
    last = 2 * (chips - 1)
    pairs = [swap(value, "orb", 2 * m) if m else value for m, value in enumerate(pieces[:-1])]
    direct = [swap(pieces[-1][core], "orb", last + core) for core in range(2)]
    nearest = pl.pallas_call(
        hand_kernel,
        out_shape=piece,
        in_specs=[SMEM, SMEM, VMEM],
        out_specs=VMEM,
        compiler_params=params(),
        name="hand",
    )(block, owner, pairs[1])
    others = [nearest if m == 1 else value[1] for m, value in enumerate(pairs)]
    spread = (pairs + [swap(value, "orb", 1) for value in others] + direct)[::-1]

    side = shape(3 * slab * nb // 4, cells)
    active, near, far, first, last = pl.pallas_call(
        pick_kernel,
        out_shape=(piece, edge, edge, side, side),
        in_specs=[SMEM] + [VMEM] * len(spread),
        out_specs=[VMEM] * 5,
        compiler_params=params(),
        name="pick",
    )(block, *spread)

    up = lambda count: [(i, (i + 1) % count) for i in range(count)]
    down = lambda count: [(i, (i - 1) % count) for i in range(count)]
    x_before = lax.ppermute(last, "dom", up(doms))
    x_after = lax.ppermute(first, "dom", down(doms))
    z_near = swap(near, "orb", 1)
    z_far = lax.ppermute(far, "orb", [(o, (o + 2 * (o % 2) - 1) % blocks) for o in range(blocks)])

    halves = jax.ShapeDtypeStruct((blocks * nb, slab * cells), BF16)
    weights = [jnp.asarray(w) for w in plane_weights(planes, rows_y)]
    *parts, inner = pl.pallas_call(
        functools.partial(split_kernel, blocks),
        out_shape=(halves, halves, piece),
        in_specs=[VMEM] * (len(spread) + 4),
        out_specs=(VMEM, VMEM, VMEM),
        scratch_shapes=[pltpu.VMEM((rows_z, cells), f32)],
        compiler_params=params(),
        cost_estimate=pl.CostEstimate(flops=3 * blocks * nb * slab * cells, bytes_accessed=0, transcendentals=0),
        name="split",
    )(active, potential.reshape(cells, rows_z), *weights, *spread)

    applied, part = pl.pallas_call(
        functools.partial(project_kernel, volume),
        out_shape=(piece, shape(2 * nb, blocks * nb)),
        in_specs=[SMEM] + [VMEM] * 10,
        out_specs=(VMEM, VMEM),
        scratch_shapes=[pltpu.VMEM((2, WIDTH, nb, cells), f32)],
        compiler_params=params(),
        name="project",
    )(owner, rotation, *parts, inner, z_near, z_far, x_before, x_after, *weights)

    part = part + swap(part, "orb", 1)
    part = pl.pallas_call(
        dom_kernel,
        out_shape=shape(2 * nb, blocks * nb),
        in_specs=[VMEM] * doms,
        out_specs=VMEM,
        compiler_params=params(),
        name="dom",
    )(part, *[swap(part[:nb], "dom", k) for k in range(1, doms)])
    sums = [part] + [swap(part, "orb", k) for k in range(2, blocks, 2)]

    own = pl.pallas_call(
        remove_kernel,
        out_shape=piece,
        in_specs=[VMEM] * (3 + chips),
        out_specs=VMEM,
        compiler_params=params(),
        name="remove",
    )(*parts, applied, *sums)

    gathered = [own] + [None] * (blocks - 1)
    for k in range(2, blocks, 2):
        gathered[k] = swap(own, "orb", k)
    gathered[1], gathered[3] = swap(own, "orb", 1), swap(own, "orb", 3)
    for k in range(4, blocks, 2):
        gathered[k + 1] = swap(gathered[k], "orb", 1)

    square = jax.ShapeDtypeStruct((MIX * nb, MIX * nb), BF16)
    mixing = pl.pallas_call(
        functools.partial(mixing_kernel, nb),
        out_shape=(square, square),
        in_specs=[VMEM] * chips,
        out_specs=(VMEM, VMEM),
        compiler_params=params(),
        name="mixing",
    )(*sums)

    sequence = sorted(range(blocks), key=lambda k: (k >= half, -k if k >= half else k))
    gradient, updated = pl.pallas_call(
        functools.partial(update_kernel, blocks, sequence),
        out_shape=(shape(nb, cells, rows_z), shape(nb, cells, rows_z)),
        in_specs=[VMEM] * (3 + blocks),
        out_specs=(HBM, HBM),
        scratch_shapes=[
            pltpu.VMEM((rows_z * nb, cells), f32),
            pltpu.VMEM((nb, cells, rows_z), f32),
            pltpu.VMEM((cells * nb, rows_z), f32),
            pltpu.VMEM((cells * nb, rows_z), f32),
            pltpu.VMEM((nb, cells, rows_z), f32),
            pltpu.SemaphoreType.DMA((2, CHUNKS)),
        ],
        compiler_params=params(),
        name="update",
    )(*mixing, flat, *[gathered[k] for k in sequence])
    return gradient.reshape(orbitals.shape), updated.reshape(orbitals.shape)


def solution(mesh):
    in_specs = (P("orb", "dom", None, None), P("dom", None, None), P("orb", None), P(), P())
    out_specs = (P(None, "dom", None, None), P("orb", "dom", None, None))
    return jax.shard_map(
        per_device, mesh=mesh, in_specs=in_specs, out_specs=out_specs, check_vma=False
    )
```

```python
import functools

import jax
import jax.numpy as jnp
import numpy as np
from jax import lax
from jax.experimental import pallas as pl
from jax.experimental.pallas import tpu as pltpu
from jax.sharding import PartitionSpec as P

CENTER = -5369.0 / 1800.0
SIDES = (12.0 / 7.0, -15.0 / 56.0, 10.0 / 189.0, -1.0 / 112.0, 2.0 / 1925.0, -1.0 / 16632.0)
WIDTH = 6
CHUNKS = 4
MIX = 8
BF16 = jnp.bfloat16
VMEM = pl.BlockSpec(memory_space=pltpu.VMEM)
HBM = pl.BlockSpec(memory_space=pltpu.HBM)
SMEM = pl.BlockSpec(memory_space=pltpu.SMEM)


def params():
    return pltpu.CompilerParams(vmem_limit_bytes=32 * 1024 * 1024)


def plane_weights(planes, rows_y):
    cells = planes * rows_y
    table = np.zeros((3 * cells, cells), np.float64)
    skipped = (planes - WIDTH) * rows_y
    for x in range(planes):
        for y in range(rows_y):
            out = x * rows_y + y
            for k, weight in enumerate(SIDES, 1):
                for step in (k, -k):
                    table[cells + x * rows_y + (y + step) % rows_y, out] += weight
                    row = cells + (x + step) * rows_y + y
                    table[row - skipped if row < cells else row, out] += weight
    table = -0.5 * table
    high = table.astype(BF16)
    return high, (table - high.astype(np.float64)).astype(BF16)


def split(value):
    high = value.astype(BF16)
    return high, (value - high.astype(jnp.float32)).astype(BF16)


def dot3(left, right, contract):
    dot = lambda x, y: lax.dot_general(x, y, (contract, ((), ())), preferred_element_type=jnp.float32)
    return dot(left[0], right[0]) + (dot(left[0], right[1]) + dot(left[1], right[0]))


def pack_kernel(blocks, x_hbm, *refs):
    *t_refs, turned, x_ref, sems = refs
    count, _, rows_z = x_ref.shape
    chunks = sems.shape[0]
    per = count // chunks
    copies = [
        pltpu.make_async_copy(x_hbm.at[pl.ds(i * per, per)], x_ref.at[pl.ds(i * per, per)], sems.at[i])
        for i in range(chunks)
    ]
    for copy in copies:
        copy.start()
    for i, copy in enumerate(copies):
        copy.wait()
        for a in range(i * per, (i + 1) * per):
            turned[pl.ds(a, rows_z, stride=count), :] = x_ref[a].T
    rows = rows_z // blocks * count
    rank = lax.axis_index("orb")
    for m, t_ref in enumerate(t_refs):
        for core in range(2):
            start = pl.multiple_of((rank ^ (2 * m + core)) * rows, rows)
            t_ref[core] = turned[pl.ds(start, rows), :].reshape(t_ref.shape[1:])


def hand_kernel(block_ref, owner_ref, pair_ref, other_ref):
    other_ref[...] = pair_ref[1]


def by_block(refs):
    refs = refs[::-1]
    half = len(refs) // 2 - 1
    return [refs[half + k // 2] if k % 2 else refs[k // 2].at[0] for k in range(2 * half)] + list(refs[2 * half :])


def squeeze(value):
    rows, wide = value.shape
    quarter, free = rows // 4, wide // 4
    lane = lax.broadcasted_iota(jnp.int32, (quarter, wide), 1)
    rest = value[3 * quarter :]
    parts = []
    for j in range(3):
        moved = pltpu.roll(rest, (3 - j) * free, 1)
        parts.append(jnp.where(lane < 3 * free, value[j * quarter : (j + 1) * quarter], moved))
    return jnp.concatenate(parts, axis=0)


def expand(value):
    rows, wide = value.shape
    quarter, free = rows // 3, wide // 4
    lane = lax.broadcasted_iota(jnp.int32, (quarter, wide), 1)
    rest = value[:quarter]
    for j in range(3):
        moved = pltpu.roll(value[j * quarter : (j + 1) * quarter], (j + 1) * free, 1)
        rest = jnp.where((lane >= j * free) & (lane < (j + 1) * free), moved, rest)
    return jnp.concatenate([value, rest], axis=0)


def pick_kernel(block_ref, *refs):
    x_refs, (act_ref, near_ref, far_ref, first_ref, last_ref) = by_block(refs[:-5]), refs[-5:]
    slab, nb, cells = act_ref.shape
    rank = lax.axis_index("orb")
    for k, x_ref in enumerate(x_refs):
        @pl.when((rank ^ block_ref[0]) == k)
        def _(x_ref=x_ref):
            act_ref[...] = x_ref[...]
    odd = rank % 2
    near_ref[...] = act_ref[pl.ds((1 - odd) * (slab - WIDTH), WIDTH)]
    far_ref[...] = act_ref[pl.ds(odd * (slab - WIDTH), WIDTH)]
    flat = act_ref[...].reshape(slab * nb, cells)
    first_ref[...] = squeeze(flat)
    last_ref[...] = squeeze(pltpu.roll(flat, 3 * (cells // 4), 1))


def split_kernel(blocks, act_ref, v_ref, wh_ref, wl_ref, *refs):
    x_refs, (high_ref, low_ref, inner_ref, turned) = by_block(refs[:-4]), refs[-4:]
    slab, nb, cells = act_ref.shape
    rank = lax.axis_index("orb")
    for k, x_ref in enumerate(x_refs):
        rows = pl.ds(pl.multiple_of((rank ^ k) * nb, nb), nb)
        for z in range(slab):
            high, low = split(x_ref[z])
            high_ref[rows, z * cells : (z + 1) * cells] = high
            low_ref[rows, z * cells : (z + 1) * cells] = low
    turned[...] = v_ref[...].T
    mine = pl.ds(pl.multiple_of(rank * slab, slab), slab)
    act = act_ref[...]
    middle = slice(cells, 2 * cells)
    inner = dot3(split(act.reshape(slab * nb, cells)), (wh_ref[middle], wl_ref[middle]), ((1,), (0,)))
    inner = inner.reshape(slab, nb, cells) + (turned[mine, :][:, None, :] - 1.5 * CENTER) * act
    edge = jnp.zeros((WIDTH, nb, cells), jnp.float32)
    tall = jnp.concatenate([edge, act, edge], axis=0)
    for k, weight in enumerate(SIDES, 1):
        upper = tall[WIDTH + k : WIDTH + k + slab]
        lower = tall[WIDTH - k : WIDTH - k + slab]
        inner = inner + (-0.5 * weight) * (upper + lower)
    inner_ref[...] = inner


def project_kernel(
    volume, owner_ref, rot_ref, xh_ref, xl_ref, inner_ref, near_ref, far_ref, xb_ref, xa_ref, wh_ref, wl_ref,
    a_ref, p_ref, around,
):
    slab, nb, cells = inner_ref.shape
    rank = lax.axis_index("orb")
    odd = rank % 2
    around[1 - odd] = near_ref[...]
    around[odd] = far_ref[...]
    before, after = slice(0, cells), slice(2 * cells, 3 * cells)
    applied = dot3(split(expand(xb_ref[...])), (wh_ref[before], wl_ref[before]), ((1,), (0,)))
    applied = applied + dot3(split(expand(xa_ref[...])), (wh_ref[after], wl_ref[after]), ((1,), (0,)))
    a_ref[...] = inner_ref[...] + applied.reshape(slab, nb, cells)
    for z in range(WIDTH):
        below, above = a_ref[z], a_ref[slab - 1 - z]
        for k in range(z + 1, WIDTH + 1):
            below = below + (-0.5 * SIDES[k - 1]) * around[0, WIDTH + z - k]
            above = above + (-0.5 * SIDES[k - 1]) * around[1, k - 1 - z]
        a_ref[z] = below
        a_ref[slab - 1 - z] = above
    flat = jnp.concatenate([a_ref[z] for z in range(slab)], axis=1)
    total = dot3(split(flat), (xh_ref[...], xl_ref[...]), ((1,), (1,)))
    p_ref[:nb] = total * volume
    p_ref[nb:] = jnp.where(rank == owner_ref[0], rot_ref[...], 0.0)


def remove_kernel(xh_ref, xl_ref, a_ref, *refs):
    *p_refs, g_ref = refs
    slab, nb, cells = a_ref.shape
    removed = dot3(split(total(p_refs, 0, nb)), (xh_ref[...], xl_ref[...]), ((1,), (0,)))
    for z in range(slab):
        g_ref[z] = a_ref[z] - removed[:, z * cells : (z + 1) * cells]


def mixing_kernel(nb, *refs):
    *p_refs, high_ref, low_ref = refs
    size, wide = high_ref.shape[0], p_refs[0].shape[1]
    row, col = (lax.broadcasted_iota(jnp.int32, (size, wide), axis) for axis in (0, 1))
    mine = jnp.where(col == lax.axis_index("orb") * nb + row % nb, 1.0, 0.0).astype(BF16)
    orbital, col = (lax.broadcasted_iota(jnp.int32, (nb, size), axis) for axis in (0, 1))
    repeat = jnp.where(orbital == col % nb, 1.0, 0.0).astype(BF16)
    row, col = (lax.broadcasted_iota(jnp.int32, (size, size), axis) for axis in (0, 1))
    same = row // nb == col // nb
    dot = lambda x, y, axes: lax.dot_general(x, y, (axes, ((), ())), preferred_element_type=jnp.float32)
    for part, ref in zip(split(total(p_refs, nb, nb)), (high_ref, low_ref)):
        block = dot(mine, part, ((1,), (1,))).astype(BF16)
        ref[...] = jnp.where(same, dot(block, repeat, ((1,), (0,))), 0.0).astype(BF16)


def update_kernel(blocks, sequence, wh_ref, wl_ref, x_ref, *refs):
    g_refs, (grad_hbm, out_hbm, whole, grad, mixed, added, out, sems) = refs[:blocks], refs[blocks:]
    nb, cells, rows_z = x_ref.shape
    rank = lax.axis_index("orb")
    share = rows_z // blocks * nb
    for k, g_ref in zip(sequence, g_refs):
        at = pl.ds(pl.multiple_of((rank ^ k) * share, share), share)
        whole[at, :] = g_ref[...].reshape(share, cells)
    per = nb // CHUNKS
    copies = []
    for i in range(CHUNKS):
        for c in range(i * per, (i + 1) * per):
            plane = whole[pl.ds(c, rows_z, stride=nb), :].T
            grad[c] = plane
            mixed[pl.ds(c, cells, stride=nb), :] = plane
        part = pl.ds(i * per, per)
        copies.append(pltpu.make_async_copy(grad.at[part], grad_hbm.at[part], sems.at[0, i]))
        copies[-1].start()
    size = wh_ref.shape[0]
    mix = (wh_ref[...], wl_ref[...])
    rows = cells // CHUNKS
    tall = rows * nb
    for i in range(CHUNKS):
        parts = split(mixed[i * tall : (i + 1) * tall])
        sides = [jnp.concatenate([p[j : j + size] for j in range(0, tall, size)], axis=1) for p in parts]
        result = dot3(mix, sides, ((1,), (0,)))
        for j in range(tall // size):
            added[i * tall + j * size : i * tall + (j + 1) * size] = result[:, j * rows_z : (j + 1) * rows_z]
        some = pl.ds(i * rows, rows)
        for a in range(nb):
            out[a, some] = x_ref[a, some] + added[pl.ds(i * tall + a, rows, stride=nb), :]
        copies.append(pltpu.make_async_copy(out.at[:, some], out_hbm.at[:, some], sems.at[1, i]))
        copies[-1].start()
    for copy in copies:
        copy.wait()


def swap(value, axis, k):
    count = lax.axis_size(axis)
    return lax.ppermute(value, axis, [(i, i ^ k) for i in range(count)])


def dom_kernel(value_ref, *refs):
    *other_refs, out_ref = refs
    nb = other_refs[0].shape[0]
    out_ref[:nb] = value_ref[:nb] + sum(ref[...] for ref in other_refs)
    out_ref[nb:] = value_ref[nb:]


def total(refs, first, count):
    rows = slice(first, first + count)
    return sum(ref[rows] for ref in refs)


def per_device(orbitals, potential, rotation, block, owner):
    nb, planes, rows_y, rows_z = orbitals.shape
    blocks, doms = lax.axis_size("orb"), lax.axis_size("dom")
    cells = planes * rows_y
    slab = rows_z // blocks
    volume = 1.0 / (cells * doms * rows_z)
    f32 = jnp.float32
    shape = lambda *dims: jax.ShapeDtypeStruct(dims, f32)
    piece, edge = shape(slab, nb, cells), shape(WIDTH, nb, cells)

    flat = orbitals.reshape(nb, cells, rows_z)
    held = pltpu.with_memory_space_constraint(flat, pltpu.HBM)
    chips = half = blocks // 2
    pieces = pl.pallas_call(
        functools.partial(pack_kernel, blocks),
        out_shape=[shape(2, slab, nb, cells)] * chips,
        in_specs=[HBM],
        out_specs=[VMEM] * chips,
        scratch_shapes=[
            pltpu.VMEM((rows_z * nb, cells), f32),
            pltpu.VMEM((nb, cells, rows_z), f32),
            pltpu.SemaphoreType.DMA((CHUNKS,)),
        ],
        compiler_params=params(),
        name="pack",
    )(held)
    last = 2 * (chips - 1)
    pairs = [swap(value, "orb", 2 * m) if m else value for m, value in enumerate(pieces[:-1])]
    direct = [swap(pieces[-1][core], "orb", last + core) for core in range(2)]
    nearest = pl.pallas_call(
        hand_kernel,
        out_shape=piece,
        in_specs=[SMEM, SMEM, VMEM],
        out_specs=VMEM,
        compiler_params=params(),
        name="hand",
    )(block, owner, pairs[1])
    others = [nearest if m == 1 else value[1] for m, value in enumerate(pairs)]
    spread = (pairs + [swap(value, "orb", 1) for value in others] + direct)[::-1]

    side = shape(3 * slab * nb // 4, cells)
    active, near, far, first, last = pl.pallas_call(
        pick_kernel,
        out_shape=(piece, edge, edge, side, side),
        in_specs=[SMEM] + [VMEM] * len(spread),
        out_specs=[VMEM] * 5,
        compiler_params=params(),
        name="pick",
    )(block, *spread)

    up = lambda count: [(i, (i + 1) % count) for i in range(count)]
    down = lambda count: [(i, (i - 1) % count) for i in range(count)]
    x_before = lax.ppermute(last, "dom", up(doms))
    x_after = lax.ppermute(first, "dom", down(doms))
    z_near = swap(near, "orb", 1)
    z_far = lax.ppermute(far, "orb", [(o, (o + 2 * (o % 2) - 1) % blocks) for o in range(blocks)])

    halves = jax.ShapeDtypeStruct((blocks * nb, slab * cells), BF16)
    weights = [jnp.asarray(w) for w in plane_weights(planes, rows_y)]
    *parts, inner = pl.pallas_call(
        functools.partial(split_kernel, blocks),
        out_shape=(halves, halves, piece),
        in_specs=[VMEM] * (len(spread) + 4),
        out_specs=(VMEM, VMEM, VMEM),
        scratch_shapes=[pltpu.VMEM((rows_z, cells), f32)],
        compiler_params=params(),
        cost_estimate=pl.CostEstimate(flops=3 * blocks * nb * slab * cells, bytes_accessed=0, transcendentals=0),
        name="split",
    )(active, potential.reshape(cells, rows_z), *weights, *spread)

    applied, part = pl.pallas_call(
        functools.partial(project_kernel, volume),
        out_shape=(piece, shape(2 * nb, blocks * nb)),
        in_specs=[SMEM] + [VMEM] * 10,
        out_specs=(VMEM, VMEM),
        scratch_shapes=[pltpu.VMEM((2, WIDTH, nb, cells), f32)],
        compiler_params=params(),
        name="project",
    )(owner, rotation, *parts, inner, z_near, z_far, x_before, x_after, *weights)

    part = part + swap(part, "orb", 1)
    part = pl.pallas_call(
        dom_kernel,
        out_shape=shape(2 * nb, blocks * nb),
        in_specs=[VMEM] * doms,
        out_specs=VMEM,
        compiler_params=params(),
        name="dom",
    )(part, *[swap(part[:nb], "dom", k) for k in range(1, doms)])
    sums = [part] + [swap(part, "orb", k) for k in range(2, blocks, 2)]

    own = pl.pallas_call(
        remove_kernel,
        out_shape=piece,
        in_specs=[VMEM] * (3 + chips),
        out_specs=VMEM,
        compiler_params=params(),
        name="remove",
    )(*parts, applied, *sums)

    gathered = [own] + [None] * (blocks - 1)
    for k in range(2, blocks, 2):
        gathered[k] = swap(own, "orb", k)
    gathered[1], gathered[3] = swap(own, "orb", 1), swap(own, "orb", 3)
    for k in range(4, blocks, 2):
        gathered[k + 1] = swap(gathered[k], "orb", 1)

    square = jax.ShapeDtypeStruct((MIX * nb, MIX * nb), BF16)
    mixing = pl.pallas_call(
        functools.partial(mixing_kernel, nb),
        out_shape=(square, square),
        in_specs=[VMEM] * chips,
        out_specs=(VMEM, VMEM),
        compiler_params=params(),
        name="mixing",
    )(*sums)

    sequence = sorted(range(blocks), key=lambda k: (k >= half, k >= 2, -k))
    gradient, updated = pl.pallas_call(
        functools.partial(update_kernel, blocks, sequence),
        out_shape=(shape(nb, cells, rows_z), shape(nb, cells, rows_z)),
        in_specs=[VMEM] * (3 + blocks),
        out_specs=(HBM, HBM),
        scratch_shapes=[
            pltpu.VMEM((rows_z * nb, cells), f32),
            pltpu.VMEM((nb, cells, rows_z), f32),
            pltpu.VMEM((cells * nb, rows_z), f32),
            pltpu.VMEM((cells * nb, rows_z), f32),
            pltpu.VMEM((nb, cells, rows_z), f32),
            pltpu.SemaphoreType.DMA((2, CHUNKS)),
        ],
        compiler_params=params(),
        name="update",
    )(*mixing, flat, *[gathered[k] for k in sequence])
    return gradient.reshape(orbitals.shape), updated.reshape(orbitals.shape)


def solution(mesh):
    in_specs = (P("orb", "dom", None, None), P("dom", None, None), P("orb", None), P(), P())
    out_specs = (P(None, "dom", None, None), P("orb", "dom", None, None))
    return jax.shard_map(
        per_device, mesh=mesh, in_specs=in_specs, out_specs=out_specs, check_vma=False
    )
```

```python
import functools

import jax
import jax.numpy as jnp
import numpy as np
from jax import lax
from jax.experimental import pallas as pl
from jax.experimental.pallas import tpu as pltpu
from jax.sharding import PartitionSpec as P

CENTER = -5369.0 / 1800.0
SIDES = (12.0 / 7.0, -15.0 / 56.0, 10.0 / 189.0, -1.0 / 112.0, 2.0 / 1925.0, -1.0 / 16632.0)
WIDTH = 6
CHUNKS = 4
MIX = 8
BF16 = jnp.bfloat16
VMEM = pl.BlockSpec(memory_space=pltpu.VMEM)
HBM = pl.BlockSpec(memory_space=pltpu.HBM)
SMEM = pl.BlockSpec(memory_space=pltpu.SMEM)


def params():
    return pltpu.CompilerParams(vmem_limit_bytes=32 * 1024 * 1024)


def plane_weights(planes, rows_y):
    cells = planes * rows_y
    table = np.zeros((3 * cells, cells), np.float64)
    skipped = (planes - WIDTH) * rows_y
    for x in range(planes):
        for y in range(rows_y):
            out = x * rows_y + y
            for k, weight in enumerate(SIDES, 1):
                for step in (k, -k):
                    table[cells + x * rows_y + (y + step) % rows_y, out] += weight
                    row = cells + (x + step) * rows_y + y
                    table[row - skipped if row < cells else row, out] += weight
    table = -0.5 * table
    high = table.astype(BF16)
    return high, (table - high.astype(np.float64)).astype(BF16)


def split(value):
    high = value.astype(BF16)
    return high, (value - high.astype(jnp.float32)).astype(BF16)


def dot3(left, right, contract):
    dot = lambda x, y: lax.dot_general(x, y, (contract, ((), ())), preferred_element_type=jnp.float32)
    return dot(left[0], right[0]) + (dot(left[0], right[1]) + dot(left[1], right[0]))


def pack_kernel(blocks, x_hbm, *refs):
    *t_refs, turned, x_ref, sems = refs
    count, _, rows_z = x_ref.shape
    chunks = sems.shape[0]
    per = count // chunks
    copies = [
        pltpu.make_async_copy(x_hbm.at[pl.ds(i * per, per)], x_ref.at[pl.ds(i * per, per)], sems.at[i])
        for i in range(chunks)
    ]
    for copy in copies:
        copy.start()
    for i, copy in enumerate(copies):
        copy.wait()
        for a in range(i * per, (i + 1) * per):
            turned[pl.ds(a, rows_z, stride=count), :] = x_ref[a].T
    rows = rows_z // blocks * count
    rank = lax.axis_index("orb")
    for m, t_ref in enumerate(t_refs):
        for core in range(2):
            start = pl.multiple_of((rank ^ (2 * m + core)) * rows, rows)
            t_ref[core] = turned[pl.ds(start, rows), :].reshape(t_ref.shape[1:])


def hand_kernel(block_ref, owner_ref, pair_ref, other_ref):
    other_ref[...] = pair_ref[1]


def by_block(refs):
    refs = refs[::-1]
    half = len(refs) // 2 - 1
    return [refs[half + k // 2] if k % 2 else refs[k // 2].at[0] for k in range(2 * half)] + list(refs[2 * half :])


def squeeze(value):
    rows, wide = value.shape
    quarter, free = rows // 4, wide // 4
    lane = lax.broadcasted_iota(jnp.int32, (quarter, wide), 1)
    rest = value[3 * quarter :]
    parts = []
    for j in range(3):
        moved = pltpu.roll(rest, (3 - j) * free, 1)
        parts.append(jnp.where(lane < 3 * free, value[j * quarter : (j + 1) * quarter], moved))
    return jnp.concatenate(parts, axis=0)


def expand(value):
    rows, wide = value.shape
    quarter, free = rows // 3, wide // 4
    lane = lax.broadcasted_iota(jnp.int32, (quarter, wide), 1)
    rest = value[:quarter]
    for j in range(3):
        moved = pltpu.roll(value[j * quarter : (j + 1) * quarter], (j + 1) * free, 1)
        rest = jnp.where((lane >= j * free) & (lane < (j + 1) * free), moved, rest)
    return jnp.concatenate([value, rest], axis=0)


def pick_kernel(block_ref, *refs):
    x_refs, (act_ref, near_ref, far_ref, first_ref, last_ref) = by_block(refs[:-5]), refs[-5:]
    slab, nb, cells = act_ref.shape
    rank = lax.axis_index("orb")
    for k, x_ref in enumerate(x_refs):
        @pl.when((rank ^ block_ref[0]) == k)
        def _(x_ref=x_ref):
            act_ref[...] = x_ref[...]
    odd = rank % 2
    near_ref[...] = act_ref[pl.ds((1 - odd) * (slab - WIDTH), WIDTH)]
    far_ref[...] = act_ref[pl.ds(odd * (slab - WIDTH), WIDTH)]
    flat = act_ref[...].reshape(slab * nb, cells)
    first_ref[...] = squeeze(flat)
    last_ref[...] = squeeze(pltpu.roll(flat, 3 * (cells // 4), 1))


def split_kernel(blocks, act_ref, v_ref, wh_ref, wl_ref, *refs):
    x_refs, (high_ref, low_ref, inner_ref, turned) = by_block(refs[:-4]), refs[-4:]
    slab, nb, cells = act_ref.shape
    rank = lax.axis_index("orb")
    for k, x_ref in enumerate(x_refs):
        rows = pl.ds(pl.multiple_of((rank ^ k) * nb, nb), nb)
        for z in range(slab):
            high, low = split(x_ref[z])
            high_ref[rows, z * cells : (z + 1) * cells] = high
            low_ref[rows, z * cells : (z + 1) * cells] = low
    turned[...] = v_ref[...].T
    mine = pl.ds(pl.multiple_of(rank * slab, slab), slab)
    act = act_ref[...]
    middle = slice(cells, 2 * cells)
    inner = dot3(split(act.reshape(slab * nb, cells)), (wh_ref[middle], wl_ref[middle]), ((1,), (0,)))
    inner = inner.reshape(slab, nb, cells) + (turned[mine, :][:, None, :] - 1.5 * CENTER) * act
    edge = jnp.zeros((WIDTH, nb, cells), jnp.float32)
    tall = jnp.concatenate([edge, act, edge], axis=0)
    for k, weight in enumerate(SIDES, 1):
        upper = tall[WIDTH + k : WIDTH + k + slab]
        lower = tall[WIDTH - k : WIDTH - k + slab]
        inner = inner + (-0.5 * weight) * (upper + lower)
    inner_ref[...] = inner


def project_kernel(
    volume, owner_ref, rot_ref, xh_ref, xl_ref, inner_ref, near_ref, far_ref, xb_ref, xa_ref, wh_ref, wl_ref,
    a_ref, p_ref, around,
):
    slab, nb, cells = inner_ref.shape
    rank = lax.axis_index("orb")
    odd = rank % 2
    around[1 - odd] = near_ref[...]
    around[odd] = far_ref[...]
    before, after = slice(0, cells), slice(2 * cells, 3 * cells)
    applied = dot3(split(expand(xb_ref[...])), (wh_ref[before], wl_ref[before]), ((1,), (0,)))
    applied = applied + dot3(split(expand(xa_ref[...])), (wh_ref[after], wl_ref[after]), ((1,), (0,)))
    a_ref[...] = inner_ref[...] + applied.reshape(slab, nb, cells)
    for z in range(WIDTH):
        below, above = a_ref[z], a_ref[slab - 1 - z]
        for k in range(z + 1, WIDTH + 1):
            below = below + (-0.5 * SIDES[k - 1]) * around[0, WIDTH + z - k]
            above = above + (-0.5 * SIDES[k - 1]) * around[1, k - 1 - z]
        a_ref[z] = below
        a_ref[slab - 1 - z] = above
    flat = jnp.concatenate([a_ref[z] for z in range(slab)], axis=1)
    total = dot3(split(flat), (xh_ref[...], xl_ref[...]), ((1,), (1,)))
    p_ref[:nb] = total * volume
    p_ref[nb:] = jnp.where(rank == owner_ref[0], rot_ref[...], 0.0)


def remove_kernel(xh_ref, xl_ref, a_ref, *refs):
    *p_refs, g_ref = refs
    slab, nb, cells = a_ref.shape
    removed = dot3(split(total(p_refs, 0, nb)), (xh_ref[...], xl_ref[...]), ((1,), (0,)))
    for z in range(slab):
        g_ref[z] = a_ref[z] - removed[:, z * cells : (z + 1) * cells]


def mixing_kernel(nb, *refs):
    *p_refs, high_ref, low_ref = refs
    size, wide = high_ref.shape[0], p_refs[0].shape[1]
    row, col = (lax.broadcasted_iota(jnp.int32, (size, wide), axis) for axis in (0, 1))
    mine = jnp.where(col == lax.axis_index("orb") * nb + row % nb, 1.0, 0.0).astype(BF16)
    orbital, col = (lax.broadcasted_iota(jnp.int32, (nb, size), axis) for axis in (0, 1))
    repeat = jnp.where(orbital == col % nb, 1.0, 0.0).astype(BF16)
    row, col = (lax.broadcasted_iota(jnp.int32, (size, size), axis) for axis in (0, 1))
    same = row // nb == col // nb
    dot = lambda x, y, axes: lax.dot_general(x, y, (axes, ((), ())), preferred_element_type=jnp.float32)
    for part, ref in zip(split(total(p_refs, nb, nb)), (high_ref, low_ref)):
        block = dot(mine, part, ((1,), (1,))).astype(BF16)
        ref[...] = jnp.where(same, dot(block, repeat, ((1,), (0,))), 0.0).astype(BF16)


def collect_kernel(_, *refs):
    *g_refs, out_ref = refs
    for i, g_ref in enumerate(g_refs):
        out_ref[i] = g_ref[...]


def update_kernel(blocks, sequence, wh_ref, wl_ref, x_ref, *refs):
    *g_refs, handed_ref, grad_hbm, out_hbm, whole, grad, mixed, added, out, sems = refs
    nb, cells, rows_z = x_ref.shape
    rank = lax.axis_index("orb")
    share = rows_z // blocks * nb
    pieces = list(zip(sequence, g_refs)) + [(k, handed_ref.at[k // 2 - 1]) for k in range(3, blocks, 2)]
    for k, g_ref in pieces:
        at = pl.ds(pl.multiple_of((rank ^ k) * share, share), share)
        whole[at, :] = g_ref[...].reshape(share, cells)
    per = nb // CHUNKS
    copies = []
    for i in range(CHUNKS):
        for c in range(i * per, (i + 1) * per):
            plane = whole[pl.ds(c, rows_z, stride=nb), :].T
            grad[c] = plane
            mixed[pl.ds(c, cells, stride=nb), :] = plane
        part = pl.ds(i * per, per)
        copies.append(pltpu.make_async_copy(grad.at[part], grad_hbm.at[part], sems.at[0, i]))
        copies[-1].start()
    size = wh_ref.shape[0]
    mix = (wh_ref[...], wl_ref[...])
    rows = cells // CHUNKS
    tall = rows * nb
    for i in range(CHUNKS):
        parts = split(mixed[i * tall : (i + 1) * tall])
        sides = [jnp.concatenate([p[j : j + size] for j in range(0, tall, size)], axis=1) for p in parts]
        result = dot3(mix, sides, ((1,), (0,)))
        for j in range(tall // size):
            added[i * tall + j * size : i * tall + (j + 1) * size] = result[:, j * rows_z : (j + 1) * rows_z]
        some = pl.ds(i * rows, rows)
        for a in range(nb):
            out[a, some] = x_ref[a, some] + added[pl.ds(i * tall + a, rows, stride=nb), :]
        copies.append(pltpu.make_async_copy(out.at[:, some], out_hbm.at[:, some], sems.at[1, i]))
        copies[-1].start()
    for copy in copies:
        copy.wait()


def swap(value, axis, k):
    count = lax.axis_size(axis)
    return lax.ppermute(value, axis, [(i, i ^ k) for i in range(count)])


def dom_kernel(value_ref, *refs):
    *other_refs, out_ref = refs
    nb = other_refs[0].shape[0]
    out_ref[:nb] = value_ref[:nb] + sum(ref[...] for ref in other_refs)
    out_ref[nb:] = value_ref[nb:]


def total(refs, first, count):
    rows = slice(first, first + count)
    return sum(ref[rows] for ref in refs)


def per_device(orbitals, potential, rotation, block, owner):
    nb, planes, rows_y, rows_z = orbitals.shape
    blocks, doms = lax.axis_size("orb"), lax.axis_size("dom")
    cells = planes * rows_y
    slab = rows_z // blocks
    volume = 1.0 / (cells * doms * rows_z)
    f32 = jnp.float32
    shape = lambda *dims: jax.ShapeDtypeStruct(dims, f32)
    piece, edge = shape(slab, nb, cells), shape(WIDTH, nb, cells)

    flat = orbitals.reshape(nb, cells, rows_z)
    held = pltpu.with_memory_space_constraint(flat, pltpu.HBM)
    chips = half = blocks // 2
    pieces = pl.pallas_call(
        functools.partial(pack_kernel, blocks),
        out_shape=[shape(2, slab, nb, cells)] * chips,
        in_specs=[HBM],
        out_specs=[VMEM] * chips,
        scratch_shapes=[
            pltpu.VMEM((rows_z * nb, cells), f32),
            pltpu.VMEM((nb, cells, rows_z), f32),
            pltpu.SemaphoreType.DMA((CHUNKS,)),
        ],
        compiler_params=params(),
        name="pack",
    )(held)
    last = 2 * (chips - 1)
    pairs = [swap(value, "orb", 2 * m) if m else value for m, value in enumerate(pieces[:-1])]
    direct = [swap(pieces[-1][core], "orb", last + core) for core in range(2)]
    nearest = pl.pallas_call(
        hand_kernel,
        out_shape=piece,
        in_specs=[SMEM, SMEM, VMEM],
        out_specs=VMEM,
        compiler_params=params(),
        name="hand",
    )(block, owner, pairs[1])
    others = [nearest if m == 1 else value[1] for m, value in enumerate(pairs)]
    spread = (pairs + [swap(value, "orb", 1) for value in others] + direct)[::-1]

    side = shape(3 * slab * nb // 4, cells)
    active, near, far, first, last = pl.pallas_call(
        pick_kernel,
        out_shape=(piece, edge, edge, side, side),
        in_specs=[SMEM] + [VMEM] * len(spread),
        out_specs=[VMEM] * 5,
        compiler_params=params(),
        name="pick",
    )(block, *spread)

    up = lambda count: [(i, (i + 1) % count) for i in range(count)]
    down = lambda count: [(i, (i - 1) % count) for i in range(count)]
    x_before = lax.ppermute(last, "dom", up(doms))
    x_after = lax.ppermute(first, "dom", down(doms))
    z_near = swap(near, "orb", 1)
    z_far = lax.ppermute(far, "orb", [(o, (o + 2 * (o % 2) - 1) % blocks) for o in range(blocks)])

    halves = jax.ShapeDtypeStruct((blocks * nb, slab * cells), BF16)
    weights = [jnp.asarray(w) for w in plane_weights(planes, rows_y)]
    *parts, inner = pl.pallas_call(
        functools.partial(split_kernel, blocks),
        out_shape=(halves, halves, piece),
        in_specs=[VMEM] * (len(spread) + 4),
        out_specs=(VMEM, VMEM, VMEM),
        scratch_shapes=[pltpu.VMEM((rows_z, cells), f32)],
        compiler_params=params(),
        cost_estimate=pl.CostEstimate(flops=3 * blocks * nb * slab * cells, bytes_accessed=0, transcendentals=0),
        name="split",
    )(active, potential.reshape(cells, rows_z), *weights, *spread)

    applied, part = pl.pallas_call(
        functools.partial(project_kernel, volume),
        out_shape=(piece, shape(2 * nb, blocks * nb)),
        in_specs=[SMEM] + [VMEM] * 10,
        out_specs=(VMEM, VMEM),
        scratch_shapes=[pltpu.VMEM((2, WIDTH, nb, cells), f32)],
        compiler_params=params(),
        name="project",
    )(owner, rotation, *parts, inner, z_near, z_far, x_before, x_after, *weights)

    part = part + swap(part, "orb", 1)
    part = pl.pallas_call(
        dom_kernel,
        out_shape=shape(2 * nb, blocks * nb),
        in_specs=[VMEM] * doms,
        out_specs=VMEM,
        compiler_params=params(),
        name="dom",
    )(part, *[swap(part[:nb], "dom", k) for k in range(1, doms)])
    sums = [part] + [swap(part, "orb", k) for k in range(2, blocks, 2)]

    own = pl.pallas_call(
        remove_kernel,
        out_shape=piece,
        in_specs=[VMEM] * (3 + chips),
        out_specs=VMEM,
        compiler_params=params(),
        name="remove",
    )(*parts, applied, *sums)

    gathered = [own] + [None] * (blocks - 1)
    for k in range(2, blocks, 2):
        gathered[k] = swap(own, "orb", k)
    gathered[1] = swap(own, "orb", 1)
    handed = pl.pallas_call(
        collect_kernel,
        out_shape=shape(chips - 1, slab, nb, cells),
        in_specs=[VMEM] * chips,
        out_specs=VMEM,
        compiler_params=params(),
        name="collect",
    )(*gathered[1:3], *gathered[4::2])

    square = jax.ShapeDtypeStruct((MIX * nb, MIX * nb), BF16)
    mixing = pl.pallas_call(
        functools.partial(mixing_kernel, nb),
        out_shape=(square, square),
        in_specs=[VMEM] * chips,
        out_specs=(VMEM, VMEM),
        compiler_params=params(),
        name="mixing",
    )(*sums)

    sequence = [0, 1, *range(2, half, 2), *range(blocks - 2, half - 1, -2)]
    gradient, updated = pl.pallas_call(
        functools.partial(update_kernel, blocks, sequence),
        out_shape=(shape(nb, cells, rows_z), shape(nb, cells, rows_z)),
        in_specs=[VMEM] * (4 + len(sequence)),
        out_specs=(HBM, HBM),
        scratch_shapes=[
            pltpu.VMEM((rows_z * nb, cells), f32),
            pltpu.VMEM((nb, cells, rows_z), f32),
            pltpu.VMEM((cells * nb, rows_z), f32),
            pltpu.VMEM((cells * nb, rows_z), f32),
            pltpu.VMEM((nb, cells, rows_z), f32),
            pltpu.SemaphoreType.DMA((2, CHUNKS)),
        ],
        compiler_params=params(),
        name="update",
    )(*mixing, flat, *[gathered[k] for k in sequence], swap(handed, "orb", 1))
    return gradient.reshape(orbitals.shape), updated.reshape(orbitals.shape)


def solution(mesh):
    in_specs = (P("orb", "dom", None, None), P("dom", None, None), P("orb", None), P(), P())
    out_specs = (P(None, "dom", None, None), P("orb", "dom", None, None))
    return jax.shard_map(
        per_device, mesh=mesh, in_specs=in_specs, out_specs=out_specs, check_vma=False
    )
```

```python
import functools

import jax
import jax.numpy as jnp
import numpy as np
from jax import lax
from jax.experimental import pallas as pl
from jax.experimental.pallas import tpu as pltpu
from jax.sharding import PartitionSpec as P

CENTER = -5369.0 / 1800.0
SIDES = (12.0 / 7.0, -15.0 / 56.0, 10.0 / 189.0, -1.0 / 112.0, 2.0 / 1925.0, -1.0 / 16632.0)
WIDTH = 6
CHUNKS = 4
MIX = 8
BF16 = jnp.bfloat16
VMEM = pl.BlockSpec(memory_space=pltpu.VMEM)
HBM = pl.BlockSpec(memory_space=pltpu.HBM)
SMEM = pl.BlockSpec(memory_space=pltpu.SMEM)


def params():
    return pltpu.CompilerParams(vmem_limit_bytes=32 * 1024 * 1024)


def plane_weights(planes, rows_y):
    cells = planes * rows_y
    table = np.zeros((3 * cells, cells), np.float64)
    skipped = (planes - WIDTH) * rows_y
    for x in range(planes):
        for y in range(rows_y):
            out = x * rows_y + y
            for k, weight in enumerate(SIDES, 1):
                for step in (k, -k):
                    table[cells + x * rows_y + (y + step) % rows_y, out] += weight
                    row = cells + (x + step) * rows_y + y
                    table[row - skipped if row < cells else row, out] += weight
    table = -0.5 * table
    high = table.astype(BF16)
    return high, (table - high.astype(np.float64)).astype(BF16)


def split(value):
    high = value.astype(BF16)
    return high, (value - high.astype(jnp.float32)).astype(BF16)


def dot3(left, right, contract):
    dot = lambda x, y: lax.dot_general(x, y, (contract, ((), ())), preferred_element_type=jnp.float32)
    return dot(left[0], right[0]) + (dot(left[0], right[1]) + dot(left[1], right[0]))


def pack_kernel(blocks, x_hbm, *refs):
    *t_refs, turned, x_ref, sems = refs
    count, _, rows_z = x_ref.shape
    chunks = sems.shape[0]
    per = count // chunks
    copies = [
        pltpu.make_async_copy(x_hbm.at[pl.ds(i * per, per)], x_ref.at[pl.ds(i * per, per)], sems.at[i])
        for i in range(chunks)
    ]
    for copy in copies:
        copy.start()
    for i, copy in enumerate(copies):
        copy.wait()
        for a in range(i * per, (i + 1) * per):
            turned[pl.ds(a, rows_z, stride=count), :] = x_ref[a].T
    rows = rows_z // blocks * count
    rank = lax.axis_index("orb")
    for m, t_ref in enumerate(t_refs):
        for core in range(2):
            start = pl.multiple_of((rank ^ (2 * m + core)) * rows, rows)
            t_ref[core] = turned[pl.ds(start, rows), :].reshape(t_ref.shape[1:])


def hand_kernel(block_ref, owner_ref, pair_ref, other_ref):
    other_ref[...] = pair_ref[1]


def by_block(refs):
    refs = refs[::-1]
    half = len(refs) // 2 - 1
    return [refs[half + k // 2] if k % 2 else refs[k // 2].at[0] for k in range(2 * half)] + list(refs[2 * half :])


def squeeze(value):
    rows, wide = value.shape
    quarter, free = rows // 4, wide // 4
    lane = lax.broadcasted_iota(jnp.int32, (quarter, wide), 1)
    rest = value[3 * quarter :]
    parts = []
    for j in range(3):
        moved = pltpu.roll(rest, (3 - j) * free, 1)
        parts.append(jnp.where(lane < 3 * free, value[j * quarter : (j + 1) * quarter], moved))
    return jnp.concatenate(parts, axis=0)


def expand(value):
    rows, wide = value.shape
    quarter, free = rows // 3, wide // 4
    lane = lax.broadcasted_iota(jnp.int32, (quarter, wide), 1)
    rest = value[:quarter]
    for j in range(3):
        moved = pltpu.roll(value[j * quarter : (j + 1) * quarter], (j + 1) * free, 1)
        rest = jnp.where((lane >= j * free) & (lane < (j + 1) * free), moved, rest)
    return jnp.concatenate([value, rest], axis=0)


def pick_kernel(block_ref, *refs):
    x_refs, (act_ref, near_ref, far_ref, first_ref, last_ref) = by_block(refs[:-5]), refs[-5:]
    slab, nb, cells = act_ref.shape
    rank = lax.axis_index("orb")
    for k, x_ref in enumerate(x_refs):
        @pl.when((rank ^ block_ref[0]) == k)
        def _(x_ref=x_ref):
            act_ref[...] = x_ref[...]
    odd = rank % 2
    near_ref[...] = act_ref[pl.ds((1 - odd) * (slab - WIDTH), WIDTH)]
    far_ref[...] = act_ref[pl.ds(odd * (slab - WIDTH), WIDTH)]
    flat = act_ref[...].reshape(slab * nb, cells)
    first_ref[...] = squeeze(flat)
    last_ref[...] = squeeze(pltpu.roll(flat, 3 * (cells // 4), 1))


def split_kernel(blocks, act_ref, v_ref, wh_ref, wl_ref, *refs):
    x_refs, (high_ref, low_ref, inner_ref, turned) = by_block(refs[:-4]), refs[-4:]
    slab, nb, cells = act_ref.shape
    rank = lax.axis_index("orb")
    for k, x_ref in enumerate(x_refs):
        rows = pl.ds(pl.multiple_of((rank ^ k) * nb, nb), nb)
        for z in range(slab):
            high, low = split(x_ref[z])
            high_ref[rows, z * cells : (z + 1) * cells] = high
            low_ref[rows, z * cells : (z + 1) * cells] = low
    turned[...] = v_ref[...].T
    mine = pl.ds(pl.multiple_of(rank * slab, slab), slab)
    act = act_ref[...]
    middle = slice(cells, 2 * cells)
    inner = dot3(split(act.reshape(slab * nb, cells)), (wh_ref[middle], wl_ref[middle]), ((1,), (0,)))
    inner = inner.reshape(slab, nb, cells) + (turned[mine, :][:, None, :] - 1.5 * CENTER) * act
    edge = jnp.zeros((WIDTH, nb, cells), jnp.float32)
    tall = jnp.concatenate([edge, act, edge], axis=0)
    for k, weight in enumerate(SIDES, 1):
        upper = tall[WIDTH + k : WIDTH + k + slab]
        lower = tall[WIDTH - k : WIDTH - k + slab]
        inner = inner + (-0.5 * weight) * (upper + lower)
    inner_ref[...] = inner


def project_kernel(
    volume, owner_ref, rot_ref, xh_ref, xl_ref, inner_ref, near_ref, far_ref, xb_ref, xa_ref, wh_ref, wl_ref,
    a_ref, p_ref, around,
):
    slab, nb, cells = inner_ref.shape
    rank = lax.axis_index("orb")
    odd = rank % 2
    around[1 - odd] = near_ref[...]
    around[odd] = far_ref[...]
    before, after = slice(0, cells), slice(2 * cells, 3 * cells)
    applied = dot3(split(expand(xb_ref[...])), (wh_ref[before], wl_ref[before]), ((1,), (0,)))
    applied = applied + dot3(split(expand(xa_ref[...])), (wh_ref[after], wl_ref[after]), ((1,), (0,)))
    a_ref[...] = inner_ref[...] + applied.reshape(slab, nb, cells)
    for z in range(WIDTH):
        below, above = a_ref[z], a_ref[slab - 1 - z]
        for k in range(z + 1, WIDTH + 1):
            below = below + (-0.5 * SIDES[k - 1]) * around[0, WIDTH + z - k]
            above = above + (-0.5 * SIDES[k - 1]) * around[1, k - 1 - z]
        a_ref[z] = below
        a_ref[slab - 1 - z] = above
    flat = jnp.concatenate([a_ref[z] for z in range(slab)], axis=1)
    total = dot3(split(flat), (xh_ref[...], xl_ref[...]), ((1,), (1,)))
    p_ref[:nb] = total * volume
    p_ref[nb:] = jnp.where(rank == owner_ref[0], rot_ref[...], 0.0)


def remove_kernel(xh_ref, xl_ref, a_ref, *refs):
    *p_refs, g_ref = refs
    slab, nb, cells = a_ref.shape
    removed = dot3(split(total(p_refs, 0, nb)), (xh_ref[...], xl_ref[...]), ((1,), (0,)))
    for z in range(slab):
        g_ref[z] = a_ref[z] - removed[:, z * cells : (z + 1) * cells]


def mixing_kernel(nb, *refs):
    *p_refs, high_ref, low_ref = refs
    size, wide = high_ref.shape[0], p_refs[0].shape[1]
    row, col = (lax.broadcasted_iota(jnp.int32, (size, wide), axis) for axis in (0, 1))
    mine = jnp.where(col == lax.axis_index("orb") * nb + row % nb, 1.0, 0.0).astype(BF16)
    orbital, col = (lax.broadcasted_iota(jnp.int32, (nb, size), axis) for axis in (0, 1))
    repeat = jnp.where(orbital == col % nb, 1.0, 0.0).astype(BF16)
    row, col = (lax.broadcasted_iota(jnp.int32, (size, size), axis) for axis in (0, 1))
    same = row // nb == col // nb
    dot = lambda x, y, axes: lax.dot_general(x, y, (axes, ((), ())), preferred_element_type=jnp.float32)
    for part, ref in zip(split(total(p_refs, nb, nb)), (high_ref, low_ref)):
        block = dot(mine, part, ((1,), (1,))).astype(BF16)
        ref[...] = jnp.where(same, dot(block, repeat, ((1,), (0,))), 0.0).astype(BF16)


def update_kernel(blocks, sequence, wh_ref, wl_ref, x_ref, *refs):
    g_refs, (grad_hbm, out_hbm, whole, grad, mixed, added, out, sems) = refs[:blocks], refs[blocks:]
    nb, cells, rows_z = x_ref.shape
    rank = lax.axis_index("orb")
    share = rows_z // blocks * nb
    for k, g_ref in zip(sequence, g_refs):
        at = pl.ds(pl.multiple_of((rank ^ k) * share, share), share)
        whole[at, :] = g_ref[...].reshape(share, cells)
    per = nb // CHUNKS
    copies = []
    for i in range(CHUNKS):
        for c in range(i * per, (i + 1) * per):
            plane = whole[pl.ds(c, rows_z, stride=nb), :].T
            grad[c] = plane
            mixed[pl.ds(c, cells, stride=nb), :] = plane
        part = pl.ds(i * per, per)
        copies.append(pltpu.make_async_copy(grad.at[part], grad_hbm.at[part], sems.at[0, i]))
        copies[-1].start()
    size = wh_ref.shape[0]
    mix = (wh_ref[...], wl_ref[...])
    rows = cells // CHUNKS
    tall = rows * nb
    for i in range(CHUNKS):
        parts = split(mixed[i * tall : (i + 1) * tall])
        sides = [jnp.concatenate([p[j : j + size] for j in range(0, tall, size)], axis=1) for p in parts]
        result = dot3(mix, sides, ((1,), (0,)))
        for j in range(tall // size):
            added[i * tall + j * size : i * tall + (j + 1) * size] = result[:, j * rows_z : (j + 1) * rows_z]
        some = pl.ds(i * rows, rows)
        for a in range(nb):
            out[a, some] = x_ref[a, some] + added[pl.ds(i * tall + a, rows, stride=nb), :]
        copies.append(pltpu.make_async_copy(out.at[:, some], out_hbm.at[:, some], sems.at[1, i]))
        copies[-1].start()
    for copy in copies:
        copy.wait()


def swap(value, axis, k):
    count = lax.axis_size(axis)
    return lax.ppermute(value, axis, [(i, i ^ k) for i in range(count)])


def dom_kernel(value_ref, *refs):
    *other_refs, out_ref = refs
    nb = other_refs[0].shape[0]
    out_ref[:nb] = value_ref[:nb] + sum(ref[...] for ref in other_refs)
    out_ref[nb:] = value_ref[nb:]


def total(refs, first, count):
    rows = slice(first, first + count)
    return sum(ref[rows] for ref in refs)


def per_device(orbitals, potential, rotation, block, owner):
    nb, planes, rows_y, rows_z = orbitals.shape
    blocks, doms = lax.axis_size("orb"), lax.axis_size("dom")
    cells = planes * rows_y
    slab = rows_z // blocks
    volume = 1.0 / (cells * doms * rows_z)
    f32 = jnp.float32
    shape = lambda *dims: jax.ShapeDtypeStruct(dims, f32)
    piece, edge = shape(slab, nb, cells), shape(WIDTH, nb, cells)

    flat = orbitals.reshape(nb, cells, rows_z)
    held = pltpu.with_memory_space_constraint(flat, pltpu.HBM)
    chips = half = blocks // 2
    pieces = pl.pallas_call(
        functools.partial(pack_kernel, blocks),
        out_shape=[shape(2, slab, nb, cells)] * chips,
        in_specs=[HBM],
        out_specs=[VMEM] * chips,
        scratch_shapes=[
            pltpu.VMEM(((rows_z + 1) * nb, cells), f32),
            pltpu.VMEM((nb, cells, rows_z), f32),
            pltpu.SemaphoreType.DMA((CHUNKS,)),
        ],
        compiler_params=params(),
        name="pack",
    )(held)
    last = 2 * (chips - 1)
    pairs = [swap(value, "orb", 2 * m) if m else value for m, value in enumerate(pieces[:-1])]
    direct = [swap(pieces[-1][core], "orb", last + core) for core in range(2)]
    nearest = pl.pallas_call(
        hand_kernel,
        out_shape=piece,
        in_specs=[SMEM, SMEM, VMEM],
        out_specs=VMEM,
        compiler_params=params(),
        name="hand",
    )(block, owner, pairs[1])
    others = [nearest if m == 1 else value[1] for m, value in enumerate(pairs)]
    spread = (pairs + [swap(value, "orb", 1) for value in others] + direct)[::-1]

    side = shape(3 * slab * nb // 4, cells)
    active, near, far, first, last = pl.pallas_call(
        pick_kernel,
        out_shape=(piece, edge, edge, side, side),
        in_specs=[SMEM] + [VMEM] * len(spread),
        out_specs=[VMEM] * 5,
        compiler_params=params(),
        name="pick",
    )(block, *spread)

    up = lambda count: [(i, (i + 1) % count) for i in range(count)]
    down = lambda count: [(i, (i - 1) % count) for i in range(count)]
    x_before = lax.ppermute(last, "dom", up(doms))
    x_after = lax.ppermute(first, "dom", down(doms))
    z_near = swap(near, "orb", 1)
    z_far = lax.ppermute(far, "orb", [(o, (o + 2 * (o % 2) - 1) % blocks) for o in range(blocks)])

    halves = jax.ShapeDtypeStruct((blocks * nb, slab * cells), BF16)
    weights = [jnp.asarray(w) for w in plane_weights(planes, rows_y)]
    *parts, inner = pl.pallas_call(
        functools.partial(split_kernel, blocks),
        out_shape=(halves, halves, piece),
        in_specs=[VMEM] * (len(spread) + 4),
        out_specs=(VMEM, VMEM, VMEM),
        scratch_shapes=[pltpu.VMEM((rows_z, cells), f32)],
        compiler_params=params(),
        cost_estimate=pl.CostEstimate(flops=3 * blocks * nb * slab * cells, bytes_accessed=0, transcendentals=0),
        name="split",
    )(active, potential.reshape(cells, rows_z), *weights, *spread)

    applied, part = pl.pallas_call(
        functools.partial(project_kernel, volume),
        out_shape=(piece, shape(2 * nb, blocks * nb)),
        in_specs=[SMEM] + [VMEM] * 10,
        out_specs=(VMEM, VMEM),
        scratch_shapes=[pltpu.VMEM((2, WIDTH, nb, cells), f32)],
        compiler_params=params(),
        name="project",
    )(owner, rotation, *parts, inner, z_near, z_far, x_before, x_after, *weights)

    part = part + swap(part, "orb", 1)
    part = pl.pallas_call(
        dom_kernel,
        out_shape=shape(2 * nb, blocks * nb),
        in_specs=[VMEM] * doms,
        out_specs=VMEM,
        compiler_params=params(),
        name="dom",
    )(part, *[swap(part[:nb], "dom", k) for k in range(1, doms)])
    sums = [part] + [swap(part, "orb", k) for k in range(2, blocks, 2)]

    own = pl.pallas_call(
        remove_kernel,
        out_shape=piece,
        in_specs=[VMEM] * (3 + chips),
        out_specs=VMEM,
        compiler_params=params(),
        name="remove",
    )(*parts, applied, *sums)

    gathered = [own] + [None] * (blocks - 1)
    for k in range(2, blocks, 2):
        gathered[k] = swap(own, "orb", k)
    for k in range(0, blocks, 2):
        gathered[k + 1] = swap(gathered[k], "orb", 1)

    square = jax.ShapeDtypeStruct((MIX * nb, MIX * nb), BF16)
    mixing = pl.pallas_call(
        functools.partial(mixing_kernel, nb),
        out_shape=(square, square),
        in_specs=[VMEM] * chips,
        out_specs=(VMEM, VMEM),
        compiler_params=params(),
        name="mixing",
    )(*sums)

    sequence = sorted(range(blocks), key=lambda k: (k >= half, -k if k >= half else k))
    gradient, updated = pl.pallas_call(
        functools.partial(update_kernel, blocks, sequence),
        out_shape=(shape(nb, cells, rows_z), shape(nb, cells, rows_z)),
        in_specs=[VMEM] * (3 + blocks),
        out_specs=(HBM, HBM),
        scratch_shapes=[
            pltpu.VMEM(((rows_z + 1) * nb, cells), f32),
            pltpu.VMEM((nb, cells, rows_z), f32),
            pltpu.VMEM(((cells + 1) * nb, rows_z), f32),
            pltpu.VMEM(((cells + 1) * nb, rows_z), f32),
            pltpu.VMEM((nb, cells, rows_z), f32),
            pltpu.SemaphoreType.DMA((2, CHUNKS)),
        ],
        compiler_params=params(),
        name="update",
    )(*mixing, flat, *[gathered[k] for k in sequence])
    return gradient.reshape(orbitals.shape), updated.reshape(orbitals.shape)


def solution(mesh):
    in_specs = (P("orb", "dom", None, None), P("dom", None, None), P("orb", None), P(), P())
    out_specs = (P(None, "dom", None, None), P("orb", "dom", None, None))
    return jax.shard_map(
        per_device, mesh=mesh, in_specs=in_specs, out_specs=out_specs, check_vma=False
    )
```

```python
import functools

import jax
import jax.numpy as jnp
import numpy as np
from jax import lax
from jax.experimental import pallas as pl
from jax.experimental.pallas import tpu as pltpu
from jax.sharding import PartitionSpec as P

CENTER = -5369.0 / 1800.0
SIDES = (12.0 / 7.0, -15.0 / 56.0, 10.0 / 189.0, -1.0 / 112.0, 2.0 / 1925.0, -1.0 / 16632.0)
WIDTH = 6
CHUNKS = 4
MIX = 8
BF16 = jnp.bfloat16
VMEM = pl.BlockSpec(memory_space=pltpu.VMEM)
HBM = pl.BlockSpec(memory_space=pltpu.HBM)
SMEM = pl.BlockSpec(memory_space=pltpu.SMEM)


def params():
    return pltpu.CompilerParams(vmem_limit_bytes=32 * 1024 * 1024)


def plane_weights(planes, rows_y):
    cells = planes * rows_y
    table = np.zeros((3 * cells, cells), np.float64)
    skipped = (planes - WIDTH) * rows_y
    for x in range(planes):
        for y in range(rows_y):
            out = x * rows_y + y
            for k, weight in enumerate(SIDES, 1):
                for step in (k, -k):
                    table[2 * cells + x * rows_y + (y + step) % rows_y, out] += weight
                    row = (x + step) * rows_y + y
                    if row < 0:
                        table[cells + row - skipped, out] += weight
                    elif row >= cells:
                        table[row, out] += weight
                    else:
                        table[2 * cells + row, out] += weight
    table = -0.5 * table
    high = table.astype(BF16)
    return high, (table - high.astype(np.float64)).astype(BF16)


def split(value):
    high = value.astype(BF16)
    return high, (value - high.astype(jnp.float32)).astype(BF16)


def dot3(left, right, contract):
    dot = lambda x, y: lax.dot_general(x, y, (contract, ((), ())), preferred_element_type=jnp.float32)
    rows = left[0].shape[0]
    both = dot(jnp.concatenate(left, axis=0), right[0])
    return both[:rows] + (both[rows:] + dot(left[0], right[1]))


def pack_kernel(blocks, x_hbm, *refs):
    *t_refs, turned, x_ref, sems = refs
    count, _, rows_z = x_ref.shape
    chunks = sems.shape[0]
    per = count // chunks
    copies = [
        pltpu.make_async_copy(x_hbm.at[pl.ds(i * per, per)], x_ref.at[pl.ds(i * per, per)], sems.at[i])
        for i in range(chunks)
    ]
    for copy in copies:
        copy.start()
    for i, copy in enumerate(copies):
        copy.wait()
        for a in range(i * per, (i + 1) * per):
            turned[pl.ds(a, rows_z, stride=count), :] = x_ref[a].T
    rows = rows_z // blocks * count
    rank = lax.axis_index("orb")
    for m, t_ref in enumerate(t_refs):
        for core in range(2):
            start = pl.multiple_of((rank ^ (2 * m + core)) * rows, rows)
            t_ref[core] = turned[pl.ds(start, rows), :].reshape(t_ref.shape[1:])


def hand_kernel(block_ref, owner_ref, pair_ref, other_ref):
    other_ref[...] = pair_ref[1]


def by_block(refs):
    refs = refs[::-1]
    half = len(refs) // 2 - 1
    return [refs[half + k // 2] if k % 2 else refs[k // 2].at[0] for k in range(2 * half)] + list(refs[2 * half :])


def squeeze(value):
    rows, wide = value.shape
    quarter, free = rows // 4, wide // 4
    lane = lax.broadcasted_iota(jnp.int32, (quarter, wide), 1)
    rest = value[3 * quarter :]
    parts = []
    for j in range(3):
        moved = pltpu.roll(rest, (3 - j) * free, 1)
        parts.append(jnp.where(lane < 3 * free, value[j * quarter : (j + 1) * quarter], moved))
    return jnp.concatenate(parts, axis=0)


def expand(value):
    rows, wide = value.shape
    quarter, free = rows // 3, wide // 4
    lane = lax.broadcasted_iota(jnp.int32, (quarter, wide), 1)
    rest = value[:quarter]
    for j in range(3):
        moved = pltpu.roll(value[j * quarter : (j + 1) * quarter], (j + 1) * free, 1)
        rest = jnp.where((lane >= j * free) & (lane < (j + 1) * free), moved, rest)
    return jnp.concatenate([value, rest], axis=0)


def pick_kernel(block_ref, *refs):
    x_refs, (act_ref, near_ref, far_ref, first_ref, last_ref) = by_block(refs[:-5]), refs[-5:]
    slab, nb, cells = act_ref.shape
    rank = lax.axis_index("orb")
    for k, x_ref in enumerate(x_refs):
        @pl.when((rank ^ block_ref[0]) == k)
        def _(x_ref=x_ref):
            act_ref[...] = x_ref[...]
    odd = rank % 2
    near_ref[...] = act_ref[pl.ds((1 - odd) * (slab - WIDTH), WIDTH)]
    far_ref[...] = act_ref[pl.ds(odd * (slab - WIDTH), WIDTH)]
    flat = act_ref[...].reshape(slab * nb, cells)
    first_ref[...] = squeeze(flat)
    last_ref[...] = squeeze(pltpu.roll(flat, 3 * (cells // 4), 1))


def split_kernel(blocks, act_ref, v_ref, wh_ref, wl_ref, *refs):
    x_refs, (high_ref, low_ref, inner_ref, turned) = by_block(refs[:-4]), refs[-4:]
    slab, nb, cells = act_ref.shape
    rank = lax.axis_index("orb")
    for k, x_ref in enumerate(x_refs):
        rows = pl.ds(pl.multiple_of((rank ^ k) * nb, nb), nb)
        for z in range(slab):
            high, low = split(x_ref[z])
            high_ref[rows, z * cells : (z + 1) * cells] = high
            low_ref[rows, z * cells : (z + 1) * cells] = low
    turned[...] = v_ref[...].T
    mine = pl.ds(pl.multiple_of(rank * slab, slab), slab)
    act = act_ref[...]
    middle = slice(2 * cells, 3 * cells)
    inner = dot3(split(act.reshape(slab * nb, cells)), (wh_ref[middle], wl_ref[middle]), ((1,), (0,)))
    inner = inner.reshape(slab, nb, cells) + (turned[mine, :][:, None, :] - 1.5 * CENTER) * act
    edge = jnp.zeros((WIDTH, nb, cells), jnp.float32)
    tall = jnp.concatenate([edge, act, edge], axis=0)
    for k, weight in enumerate(SIDES, 1):
        upper = tall[WIDTH + k : WIDTH + k + slab]
        lower = tall[WIDTH - k : WIDTH - k + slab]
        inner = inner + (-0.5 * weight) * (upper + lower)
    inner_ref[...] = inner


def project_kernel(
    volume, owner_ref, rot_ref, xh_ref, xl_ref, inner_ref, near_ref, far_ref, xb_ref, xa_ref, wh_ref, wl_ref,
    a_ref, p_ref, around,
):
    slab, nb, cells = inner_ref.shape
    rank = lax.axis_index("orb")
    odd = rank % 2
    around[1 - odd] = near_ref[...]
    around[odd] = far_ref[...]
    beside = slice(0, 2 * cells)
    wide = jnp.concatenate([expand(xb_ref[...]), expand(xa_ref[...])], axis=1)
    applied = dot3(split(wide), (wh_ref[beside], wl_ref[beside]), ((1,), (0,)))
    a_ref[...] = inner_ref[...] + applied.reshape(slab, nb, cells)
    for z in range(WIDTH):
        below, above = a_ref[z], a_ref[slab - 1 - z]
        for k in range(z + 1, WIDTH + 1):
            below = below + (-0.5 * SIDES[k - 1]) * around[0, WIDTH + z - k]
            above = above + (-0.5 * SIDES[k - 1]) * around[1, k - 1 - z]
        a_ref[z] = below
        a_ref[slab - 1 - z] = above
    flat = jnp.concatenate([a_ref[z] for z in range(slab)], axis=1)
    total = dot3(split(flat), (xh_ref[...], xl_ref[...]), ((1,), (1,)))
    p_ref[:nb] = total * volume
    p_ref[nb:] = jnp.where(rank == owner_ref[0], rot_ref[...], 0.0)


def remove_kernel(xh_ref, xl_ref, a_ref, *refs):
    *p_refs, g_ref = refs
    slab, nb, cells = a_ref.shape
    removed = dot3(split(total(p_refs, 0, nb)), (xh_ref[...], xl_ref[...]), ((1,), (0,)))
    for z in range(slab):
        g_ref[z] = a_ref[z] - removed[:, z * cells : (z + 1) * cells]


def mixing_kernel(nb, *refs):
    *p_refs, high_ref, low_ref = refs
    size, wide = high_ref.shape[0], p_refs[0].shape[1]
    row, col = (lax.broadcasted_iota(jnp.int32, (size, wide), axis) for axis in (0, 1))
    mine = jnp.where(col == lax.axis_index("orb") * nb + row % nb, 1.0, 0.0).astype(BF16)
    orbital, col = (lax.broadcasted_iota(jnp.int32, (nb, size), axis) for axis in (0, 1))
    repeat = jnp.where(orbital == col % nb, 1.0, 0.0).astype(BF16)
    row, col = (lax.broadcasted_iota(jnp.int32, (size, size), axis) for axis in (0, 1))
    same = row // nb == col // nb
    dot = lambda x, y, axes: lax.dot_general(x, y, (axes, ((), ())), preferred_element_type=jnp.float32)
    for part, ref in zip(split(total(p_refs, nb, nb)), (high_ref, low_ref)):
        block = dot(mine, part, ((1,), (1,))).astype(BF16)
        ref[...] = jnp.where(same, dot(block, repeat, ((1,), (0,))), 0.0).astype(BF16)


def update_kernel(blocks, sequence, wh_ref, wl_ref, x_ref, *refs):
    g_refs, (grad_hbm, out_hbm, whole, grad, mixed, added, out, sems) = refs[:blocks], refs[blocks:]
    nb, cells, rows_z = x_ref.shape
    rank = lax.axis_index("orb")
    share = rows_z // blocks * nb
    for k, g_ref in zip(sequence, g_refs):
        at = pl.ds(pl.multiple_of((rank ^ k) * share, share), share)
        whole[at, :] = g_ref[...].reshape(share, cells)
    per = nb // CHUNKS
    copies = []
    for i in range(CHUNKS):
        for c in range(i * per, (i + 1) * per):
            plane = whole[pl.ds(c, rows_z, stride=nb), :].T
            grad[c] = plane
            mixed[pl.ds(c, cells, stride=nb), :] = plane
        part = pl.ds(i * per, per)
        copies.append(pltpu.make_async_copy(grad.at[part], grad_hbm.at[part], sems.at[0, i]))
        copies[-1].start()
    size = wh_ref.shape[0]
    mix = (wh_ref[...], wl_ref[...])
    rows = cells // CHUNKS
    tall = rows * nb
    for i in range(CHUNKS):
        parts = split(mixed[i * tall : (i + 1) * tall])
        sides = [jnp.concatenate([p[j : j + size] for j in range(0, tall, size)], axis=1) for p in parts]
        result = dot3(mix, sides, ((1,), (0,)))
        for j in range(tall // size):
            added[i * tall + j * size : i * tall + (j + 1) * size] = result[:, j * rows_z : (j + 1) * rows_z]
        some = pl.ds(i * rows, rows)
        for a in range(nb):
            out[a, some] = x_ref[a, some] + added[pl.ds(i * tall + a, rows, stride=nb), :]
        copies.append(pltpu.make_async_copy(out.at[:, some], out_hbm.at[:, some], sems.at[1, i]))
        copies[-1].start()
    for copy in copies:
        copy.wait()


def swap(value, axis, k):
    count = lax.axis_size(axis)
    return lax.ppermute(value, axis, [(i, i ^ k) for i in range(count)])


def dom_kernel(value_ref, *refs):
    *other_refs, out_ref = refs
    nb = other_refs[0].shape[0]
    out_ref[:nb] = value_ref[:nb] + sum(ref[...] for ref in other_refs)
    out_ref[nb:] = value_ref[nb:]


def total(refs, first, count):
    rows = slice(first, first + count)
    return sum(ref[rows] for ref in refs)


def per_device(orbitals, potential, rotation, block, owner):
    nb, planes, rows_y, rows_z = orbitals.shape
    blocks, doms = lax.axis_size("orb"), lax.axis_size("dom")
    cells = planes * rows_y
    slab = rows_z // blocks
    volume = 1.0 / (cells * doms * rows_z)
    f32 = jnp.float32
    shape = lambda *dims: jax.ShapeDtypeStruct(dims, f32)
    piece, edge = shape(slab, nb, cells), shape(WIDTH, nb, cells)

    flat = orbitals.reshape(nb, cells, rows_z)
    held = pltpu.with_memory_space_constraint(flat, pltpu.HBM)
    chips = half = blocks // 2
    pieces = pl.pallas_call(
        functools.partial(pack_kernel, blocks),
        out_shape=[shape(2, slab, nb, cells)] * chips,
        in_specs=[HBM],
        out_specs=[VMEM] * chips,
        scratch_shapes=[
            pltpu.VMEM(((rows_z + 1) * nb, cells), f32),
            pltpu.VMEM((nb, cells, rows_z), f32),
            pltpu.SemaphoreType.DMA((CHUNKS,)),
        ],
        compiler_params=params(),
        name="pack",
    )(held)
    last = 2 * (chips - 1)
    pairs = [swap(value, "orb", 2 * m) if m else value for m, value in enumerate(pieces[:-1])]
    direct = [swap(pieces[-1][core], "orb", last + core) for core in range(2)]
    nearest = pl.pallas_call(
        hand_kernel,
        out_shape=piece,
        in_specs=[SMEM, SMEM, VMEM],
        out_specs=VMEM,
        compiler_params=params(),
        name="hand",
    )(block, owner, pairs[1])
    others = [nearest if m == 1 else value[1] for m, value in enumerate(pairs)]
    spread = (pairs + [swap(value, "orb", 1) for value in others] + direct)[::-1]

    side = shape(3 * slab * nb // 4, cells)
    active, near, far, first, last = pl.pallas_call(
        pick_kernel,
        out_shape=(piece, edge, edge, side, side),
        in_specs=[SMEM] + [VMEM] * len(spread),
        out_specs=[VMEM] * 5,
        compiler_params=params(),
        name="pick",
    )(block, *spread)

    up = lambda count: [(i, (i + 1) % count) for i in range(count)]
    down = lambda count: [(i, (i - 1) % count) for i in range(count)]
    x_before = lax.ppermute(last, "dom", up(doms))
    x_after = lax.ppermute(first, "dom", down(doms))
    z_near = swap(near, "orb", 1)
    z_far = lax.ppermute(far, "orb", [(o, (o + 2 * (o % 2) - 1) % blocks) for o in range(blocks)])

    halves = jax.ShapeDtypeStruct((blocks * nb, slab * cells), BF16)
    weights = [jnp.asarray(w) for w in plane_weights(planes, rows_y)]
    *parts, inner = pl.pallas_call(
        functools.partial(split_kernel, blocks),
        out_shape=(halves, halves, piece),
        in_specs=[VMEM] * (len(spread) + 4),
        out_specs=(VMEM, VMEM, VMEM),
        scratch_shapes=[pltpu.VMEM((rows_z, cells), f32)],
        compiler_params=params(),
        cost_estimate=pl.CostEstimate(flops=3 * blocks * nb * slab * cells, bytes_accessed=0, transcendentals=0),
        name="split",
    )(active, potential.reshape(cells, rows_z), *weights, *spread)

    applied, part = pl.pallas_call(
        functools.partial(project_kernel, volume),
        out_shape=(piece, shape(2 * nb, blocks * nb)),
        in_specs=[SMEM] + [VMEM] * 10,
        out_specs=(VMEM, VMEM),
        scratch_shapes=[pltpu.VMEM((2, WIDTH, nb, cells), f32)],
        compiler_params=params(),
        name="project",
    )(owner, rotation, *parts, inner, z_near, z_far, x_before, x_after, *weights)

    part = part + swap(part, "orb", 1)
    part = pl.pallas_call(
        dom_kernel,
        out_shape=shape(2 * nb, blocks * nb),
        in_specs=[VMEM] * doms,
        out_specs=VMEM,
        compiler_params=params(),
        name="dom",
    )(part, *[swap(part[:nb], "dom", k) for k in range(1, doms)])
    sums = [part] + [swap(part, "orb", k) for k in range(2, blocks, 2)]

    own = pl.pallas_call(
        remove_kernel,
        out_shape=piece,
        in_specs=[VMEM] * (3 + chips),
        out_specs=VMEM,
        compiler_params=params(),
        name="remove",
    )(*parts, applied, *sums)

    gathered = [own] + [None] * (blocks - 1)
    for k in range(2, blocks, 2):
        gathered[k] = swap(own, "orb", k)
    for k in range(0, blocks, 2):
        gathered[k + 1] = swap(gathered[k], "orb", 1)

    square = jax.ShapeDtypeStruct((MIX * nb, MIX * nb), BF16)
    mixing = pl.pallas_call(
        functools.partial(mixing_kernel, nb),
        out_shape=(square, square),
        in_specs=[VMEM] * chips,
        out_specs=(VMEM, VMEM),
        compiler_params=params(),
        name="mixing",
    )(*sums)

    sequence = sorted(range(blocks), key=lambda k: (k >= half, -k if k >= half else k))
    gradient, updated = pl.pallas_call(
        functools.partial(update_kernel, blocks, sequence),
        out_shape=(shape(nb, cells, rows_z), shape(nb, cells, rows_z)),
        in_specs=[VMEM] * (3 + blocks),
        out_specs=(HBM, HBM),
        scratch_shapes=[
            pltpu.VMEM(((rows_z + 1) * nb, cells), f32),
            pltpu.VMEM((nb, cells, rows_z), f32),
            pltpu.VMEM(((cells + 1) * nb, rows_z), f32),
            pltpu.VMEM(((cells + 1) * nb, rows_z), f32),
            pltpu.VMEM((nb, cells, rows_z), f32),
            pltpu.SemaphoreType.DMA((2, CHUNKS)),
        ],
        compiler_params=params(),
        name="update",
    )(*mixing, flat, *[gathered[k] for k in sequence])
    return gradient.reshape(orbitals.shape), updated.reshape(orbitals.shape)


def solution(mesh):
    in_specs = (P("orb", "dom", None, None), P("dom", None, None), P("orb", None), P(), P())
    out_specs = (P(None, "dom", None, None), P("orb", "dom", None, None))
    return jax.shard_map(
        per_device, mesh=mesh, in_specs=in_specs, out_specs=out_specs, check_vma=False
    )
```

```python
import functools

import jax
import jax.numpy as jnp
import numpy as np
from jax import lax
from jax.experimental import pallas as pl
from jax.experimental.pallas import tpu as pltpu
from jax.sharding import PartitionSpec as P

CENTER = -5369.0 / 1800.0
SIDES = (12.0 / 7.0, -15.0 / 56.0, 10.0 / 189.0, -1.0 / 112.0, 2.0 / 1925.0, -1.0 / 16632.0)
WIDTH = 6
CHUNKS = 4
MIX = 8
BF16 = jnp.bfloat16
VMEM = pl.BlockSpec(memory_space=pltpu.VMEM)
HBM = pl.BlockSpec(memory_space=pltpu.HBM)
SMEM = pl.BlockSpec(memory_space=pltpu.SMEM)


def params():
    return pltpu.CompilerParams(vmem_limit_bytes=32 * 1024 * 1024)


def plane_weights(planes, rows_y):
    cells = planes * rows_y
    table = np.zeros((3 * cells, cells), np.float64)
    skipped = (planes - WIDTH) * rows_y
    for x in range(planes):
        for y in range(rows_y):
            out = x * rows_y + y
            for k, weight in enumerate(SIDES, 1):
                for step in (k, -k):
                    table[2 * cells + x * rows_y + (y + step) % rows_y, out] += weight
                    row = (x + step) * rows_y + y
                    if row < 0:
                        table[cells + row - skipped, out] += weight
                    elif row >= cells:
                        table[row, out] += weight
                    else:
                        table[2 * cells + row, out] += weight
    table = -0.5 * table
    high = table.astype(BF16)
    return high, (table - high.astype(np.float64)).astype(BF16)


def split(value):
    high = value.astype(BF16)
    return high, (value - high.astype(jnp.float32)).astype(BF16)


def dot3(left, right, contract):
    dot = lambda x, y: lax.dot_general(x, y, (contract, ((), ())), preferred_element_type=jnp.float32)
    rows = left[0].shape[0]
    both = dot(jnp.concatenate(left, axis=0), right[0])
    return both[:rows] + (both[rows:] + dot(left[0], right[1]))


def pack_kernel(blocks, x_hbm, *refs):
    *t_refs, turned, x_ref, sems = refs
    count, _, rows_z = x_ref.shape
    chunks = sems.shape[0]
    per = count // chunks
    copies = [
        pltpu.make_async_copy(x_hbm.at[pl.ds(i * per, per)], x_ref.at[pl.ds(i * per, per)], sems.at[i])
        for i in range(chunks)
    ]
    for copy in copies:
        copy.start()
    for i, copy in enumerate(copies):
        copy.wait()
        for a in range(i * per, (i + 1) * per):
            turned[pl.ds(a, rows_z, stride=count), :] = x_ref[a].T
    rows = rows_z // blocks * count
    rank = lax.axis_index("orb")
    for m, t_ref in enumerate(t_refs):
        for core in range(2):
            start = pl.multiple_of((rank ^ (2 * m + core)) * rows, rows)
            t_ref[core] = turned[pl.ds(start, rows), :].reshape(t_ref.shape[1:])


def hand_kernel(block_ref, owner_ref, pair_ref, other_ref):
    other_ref[...] = pair_ref[1]


def by_block(refs):
    refs = refs[::-1]
    half = len(refs) // 2 - 1
    return [refs[half + k // 2] if k % 2 else refs[k // 2].at[0] for k in range(2 * half)] + list(refs[2 * half :])


def squeeze(value):
    rows, wide = value.shape
    quarter, free = rows // 4, wide // 4
    lane = lax.broadcasted_iota(jnp.int32, (quarter, wide), 1)
    rest = value[3 * quarter :]
    parts = []
    for j in range(3):
        moved = pltpu.roll(rest, (3 - j) * free, 1)
        parts.append(jnp.where(lane < 3 * free, value[j * quarter : (j + 1) * quarter], moved))
    return jnp.concatenate(parts, axis=0)


def expand(value):
    rows, wide = value.shape
    quarter, free = rows // 3, wide // 4
    lane = lax.broadcasted_iota(jnp.int32, (quarter, wide), 1)
    rest = value[:quarter]
    for j in range(3):
        moved = pltpu.roll(value[j * quarter : (j + 1) * quarter], (j + 1) * free, 1)
        rest = jnp.where((lane >= j * free) & (lane < (j + 1) * free), moved, rest)
    return jnp.concatenate([value, rest], axis=0)


def pick_kernel(block_ref, *refs):
    x_refs, (act_ref, near_ref, far_ref, first_ref, last_ref) = by_block(refs[:-5]), refs[-5:]
    slab, nb, cells = act_ref.shape
    rank = lax.axis_index("orb")
    for k, x_ref in enumerate(x_refs):
        @pl.when((rank ^ block_ref[0]) == k)
        def _(x_ref=x_ref):
            act_ref[...] = x_ref[...]
    odd = rank % 2
    near_ref[...] = act_ref[pl.ds((1 - odd) * (slab - WIDTH), WIDTH)]
    far_ref[...] = act_ref[pl.ds(odd * (slab - WIDTH), WIDTH)]
    flat = act_ref[...].reshape(slab * nb, cells)
    first_ref[...] = squeeze(flat)
    last_ref[...] = squeeze(pltpu.roll(flat, 3 * (cells // 4), 1))


def split_kernel(blocks, act_ref, v_ref, wh_ref, wl_ref, *refs):
    x_refs, (high_ref, low_ref, inner_ref, turned) = by_block(refs[:-4]), refs[-4:]
    slab, nb, cells = act_ref.shape
    rank = lax.axis_index("orb")
    for k, x_ref in enumerate(x_refs):
        rows = pl.ds(pl.multiple_of((rank ^ k) * nb, nb), nb)
        for z in range(slab):
            high, low = split(x_ref[z])
            high_ref[rows, z * cells : (z + 1) * cells] = high
            low_ref[rows, z * cells : (z + 1) * cells] = low
    turned[...] = v_ref[...].T
    mine = pl.ds(pl.multiple_of(rank * slab, slab), slab)
    act = act_ref[...]
    middle = slice(2 * cells, 3 * cells)
    inner = dot3(split(act.reshape(slab * nb, cells)), (wh_ref[middle], wl_ref[middle]), ((1,), (0,)))
    inner = inner.reshape(slab, nb, cells) + (turned[mine, :][:, None, :] - 1.5 * CENTER) * act
    edge = jnp.zeros((WIDTH, nb, cells), jnp.float32)
    tall = jnp.concatenate([edge, act, edge], axis=0)
    for k, weight in enumerate(SIDES, 1):
        upper = tall[WIDTH + k : WIDTH + k + slab]
        lower = tall[WIDTH - k : WIDTH - k + slab]
        inner = inner + (-0.5 * weight) * (upper + lower)
    inner_ref[...] = inner


def project_kernel(
    volume, owner_ref, rot_ref, xh_ref, xl_ref, inner_ref, far_ref, near_ref, xb_ref, xa_ref, wh_ref, wl_ref,
    a_ref, p_ref, around,
):
    slab, nb, cells = inner_ref.shape
    rank = lax.axis_index("orb")
    odd = rank % 2
    around[1 - odd] = near_ref[...]
    around[odd] = far_ref[...]
    beside = slice(0, 2 * cells)
    wide = jnp.concatenate([expand(xb_ref[...]), expand(xa_ref[...])], axis=1)
    applied = dot3(split(wide), (wh_ref[beside], wl_ref[beside]), ((1,), (0,)))
    a_ref[...] = inner_ref[...] + applied.reshape(slab, nb, cells)
    for z in range(WIDTH):
        below, above = a_ref[z], a_ref[slab - 1 - z]
        for k in range(z + 1, WIDTH + 1):
            below = below + (-0.5 * SIDES[k - 1]) * around[0, WIDTH + z - k]
            above = above + (-0.5 * SIDES[k - 1]) * around[1, k - 1 - z]
        a_ref[z] = below
        a_ref[slab - 1 - z] = above
    flat = jnp.concatenate([a_ref[z] for z in range(slab)], axis=1)
    total = dot3(split(flat), (xh_ref[...], xl_ref[...]), ((1,), (1,)))
    p_ref[:nb] = total * volume
    p_ref[nb:] = jnp.where(rank == owner_ref[0], rot_ref[...], 0.0)


def remove_kernel(xh_ref, xl_ref, a_ref, *refs):
    *p_refs, g_ref = refs
    slab, nb, cells = a_ref.shape
    removed = dot3(split(total(p_refs, 0, nb)), (xh_ref[...], xl_ref[...]), ((1,), (0,)))
    for z in range(slab):
        g_ref[z] = a_ref[z] - removed[:, z * cells : (z + 1) * cells]


def mixing_kernel(nb, *refs):
    *p_refs, high_ref, low_ref = refs
    size, wide = high_ref.shape[0], p_refs[0].shape[1]
    row, col = (lax.broadcasted_iota(jnp.int32, (size, wide), axis) for axis in (0, 1))
    mine = jnp.where(col == lax.axis_index("orb") * nb + row // MIX, 1.0, 0.0).astype(BF16)
    orbital, col = (lax.broadcasted_iota(jnp.int32, (nb, size), axis) for axis in (0, 1))
    repeat = jnp.where(orbital == col // MIX, 1.0, 0.0).astype(BF16)
    row, col = (lax.broadcasted_iota(jnp.int32, (size, size), axis) for axis in (0, 1))
    same = row % MIX == col % MIX
    dot = lambda x, y, axes: lax.dot_general(x, y, (axes, ((), ())), preferred_element_type=jnp.float32)
    for part, ref in zip(split(total(p_refs, nb, nb)), (high_ref, low_ref)):
        block = dot(mine, part, ((1,), (1,))).astype(BF16)
        ref[...] = jnp.where(same, dot(block, repeat, ((1,), (0,))), 0.0).astype(BF16)


def update_kernel(blocks, sequence, wh_ref, wl_ref, x_ref, *refs):
    g_refs, (grad_hbm, out_hbm, whole, grad, out, sems) = refs[:blocks], refs[blocks:]
    nb, cells, rows_z = x_ref.shape
    rank = lax.axis_index("orb")
    share = rows_z // blocks * nb
    for k, g_ref in zip(sequence, g_refs):
        at = pl.ds(pl.multiple_of((rank ^ k) * share, share), share)
        whole[at, :] = g_ref[...].reshape(share, cells)
    per = nb // CHUNKS
    copies = []
    for i in range(CHUNKS):
        for c in range(i * per, (i + 1) * per):
            grad[c] = whole[pl.ds(c, rows_z, stride=nb), :].T
        part = pl.ds(i * per, per)
        copies.append(pltpu.make_async_copy(grad.at[part], grad_hbm.at[part], sems.at[0, i]))
        copies[-1].start()
    mix = (wh_ref[...], wl_ref[...])
    rows = cells // CHUNKS
    for i in range(CHUNKS):
        some = pl.ds(i * rows, rows)
        places = [pl.ds(start, MIX) for start in range(i * rows, (i + 1) * rows, MIX)]
        sides = [jnp.concatenate([grad[c, at] for c in range(nb)], axis=0) for at in places]
        result = dot3(mix, split(jnp.concatenate(sides, axis=1)), ((1,), (0,)))
        for j, at in enumerate(places):
            for a in range(nb):
                out[a, at] = x_ref[a, at] + result[a * MIX : (a + 1) * MIX, j * rows_z : (j + 1) * rows_z]
        copies.append(pltpu.make_async_copy(out.at[:, some], out_hbm.at[:, some], sems.at[1, i]))
        copies[-1].start()
    for copy in copies:
        copy.wait()


def swap(value, axis, k):
    count = lax.axis_size(axis)
    return lax.ppermute(value, axis, [(i, i ^ k) for i in range(count)])


def dom_kernel(value_ref, *refs):
    *other_refs, out_ref = refs
    nb = other_refs[0].shape[0]
    out_ref[:nb] = value_ref[:nb] + sum(ref[...] for ref in other_refs)
    out_ref[nb:] = value_ref[nb:]


def total(refs, first, count):
    rows = slice(first, first + count)
    return sum(ref[rows] for ref in refs)


def per_device(orbitals, potential, rotation, block, owner):
    nb, planes, rows_y, rows_z = orbitals.shape
    blocks, doms = lax.axis_size("orb"), lax.axis_size("dom")
    cells = planes * rows_y
    slab = rows_z // blocks
    volume = 1.0 / (cells * doms * rows_z)
    f32 = jnp.float32
    shape = lambda *dims: jax.ShapeDtypeStruct(dims, f32)
    piece, edge = shape(slab, nb, cells), shape(WIDTH, nb, cells)

    flat = orbitals.reshape(nb, cells, rows_z)
    held = pltpu.with_memory_space_constraint(flat, pltpu.HBM)
    chips = half = blocks // 2
    pieces = pl.pallas_call(
        functools.partial(pack_kernel, blocks),
        out_shape=[shape(2, slab, nb, cells)] * chips,
        in_specs=[HBM],
        out_specs=[VMEM] * chips,
        scratch_shapes=[
            pltpu.VMEM(((rows_z + 1) * nb, cells), f32),
            pltpu.VMEM((nb, cells, rows_z), f32),
            pltpu.SemaphoreType.DMA((CHUNKS,)),
        ],
        compiler_params=params(),
        name="pack",
    )(held)
    last = 2 * (chips - 1)
    pairs = [swap(value, "orb", 2 * m) if m else value for m, value in enumerate(pieces[:-1])]
    direct = [swap(pieces[-1][core], "orb", last + core) for core in range(2)]
    nearest = pl.pallas_call(
        hand_kernel,
        out_shape=piece,
        in_specs=[SMEM, SMEM, VMEM],
        out_specs=VMEM,
        compiler_params=params(),
        name="hand",
    )(block, owner, pairs[1])
    others = [nearest if m == 1 else value[1] for m, value in enumerate(pairs)]
    spread = (pairs + [swap(value, "orb", 1) for value in others] + direct)[::-1]

    side = shape(3 * slab * nb // 4, cells)
    active, near, far, first, last = pl.pallas_call(
        pick_kernel,
        out_shape=(piece, edge, edge, side, side),
        in_specs=[SMEM] + [VMEM] * len(spread),
        out_specs=[VMEM] * 5,
        compiler_params=params(),
        name="pick",
    )(block, *spread)

    up = lambda count: [(i, (i + 1) % count) for i in range(count)]
    down = lambda count: [(i, (i - 1) % count) for i in range(count)]
    x_before = lax.ppermute(last, "dom", up(doms))
    x_after = lax.ppermute(first, "dom", down(doms))
    z_near = swap(near, "orb", 1)
    z_far = lax.ppermute(far, "orb", [(o, (o + 2 * (o % 2) - 1) % blocks) for o in range(blocks)])

    halves = jax.ShapeDtypeStruct((blocks * nb, slab * cells), BF16)
    weights = [jnp.asarray(w) for w in plane_weights(planes, rows_y)]
    *parts, inner = pl.pallas_call(
        functools.partial(split_kernel, blocks),
        out_shape=(halves, halves, piece),
        in_specs=[VMEM] * (len(spread) + 4),
        out_specs=(VMEM, VMEM, VMEM),
        scratch_shapes=[pltpu.VMEM((rows_z, cells), f32)],
        compiler_params=params(),
        cost_estimate=pl.CostEstimate(flops=3 * blocks * nb * slab * cells, bytes_accessed=0, transcendentals=0),
        name="split",
    )(active, potential.reshape(cells, rows_z), *weights, *spread)

    applied, part = pl.pallas_call(
        functools.partial(project_kernel, volume),
        out_shape=(piece, shape(2 * nb, blocks * nb)),
        in_specs=[SMEM] + [VMEM] * 10,
        out_specs=(VMEM, VMEM),
        scratch_shapes=[pltpu.VMEM((2, WIDTH, nb, cells), f32)],
        compiler_params=params(),
        name="project",
    )(owner, rotation, *parts, inner, z_far, z_near, x_before, x_after, *weights)

    part = part + swap(part, "orb", 1)
    part = pl.pallas_call(
        dom_kernel,
        out_shape=shape(2 * nb, blocks * nb),
        in_specs=[VMEM] * doms,
        out_specs=VMEM,
        compiler_params=params(),
        name="dom",
    )(part, *[swap(part[:nb], "dom", k) for k in range(1, doms)])
    sums = [part] + [swap(part, "orb", k) for k in range(2, blocks, 2)]

    own = pl.pallas_call(
        remove_kernel,
        out_shape=piece,
        in_specs=[VMEM] * (3 + chips),
        out_specs=VMEM,
        compiler_params=params(),
        name="remove",
    )(*parts, applied, *sums)

    gathered = [own] + [None] * (blocks - 1)
    for k in range(2, blocks, 2):
        gathered[k] = swap(own, "orb", k)
    for k in range(0, blocks, 2):
        gathered[k + 1] = swap(gathered[k], "orb", 1)

    square = jax.ShapeDtypeStruct((MIX * nb, MIX * nb), BF16)
    mixing = pl.pallas_call(
        functools.partial(mixing_kernel, nb),
        out_shape=(square, square),
        in_specs=[VMEM] * chips,
        out_specs=(VMEM, VMEM),
        compiler_params=params(),
        name="mixing",
    )(*sums)

    sequence = sorted(range(blocks), key=lambda k: (k >= half, -k if k >= half else k))
    gradient, updated = pl.pallas_call(
        functools.partial(update_kernel, blocks, sequence),
        out_shape=(shape(nb, cells, rows_z), shape(nb, cells, rows_z)),
        in_specs=[VMEM] * (3 + blocks),
        out_specs=(HBM, HBM),
        scratch_shapes=[
            pltpu.VMEM(((rows_z + 1) * nb, cells), f32),
            pltpu.VMEM((nb, cells, rows_z), f32),
            pltpu.VMEM((nb, cells, rows_z), f32),
            pltpu.SemaphoreType.DMA((2, CHUNKS)),
        ],
        compiler_params=params(),
        name="update",
    )(*mixing, flat, *[gathered[k] for k in sequence])
    return gradient.reshape(orbitals.shape), updated.reshape(orbitals.shape)


def solution(mesh):
    in_specs = (P("orb", "dom", None, None), P("dom", None, None), P("orb", None), P(), P())
    out_specs = (P(None, "dom", None, None), P("orb", "dom", None, None))
    return jax.shard_map(
        per_device, mesh=mesh, in_specs=in_specs, out_specs=out_specs, check_vma=False
    )
```

```python
import functools

import jax
import jax.numpy as jnp
import numpy as np
from jax import lax
from jax.experimental import pallas as pl
from jax.experimental.pallas import tpu as pltpu
from jax.sharding import PartitionSpec as P

CENTER = -5369.0 / 1800.0
SIDES = (12.0 / 7.0, -15.0 / 56.0, 10.0 / 189.0, -1.0 / 112.0, 2.0 / 1925.0, -1.0 / 16632.0)
WIDTH = 6
CHUNKS = 4
MIX = 8
BF16 = jnp.bfloat16
VMEM = pl.BlockSpec(memory_space=pltpu.VMEM)
HBM = pl.BlockSpec(memory_space=pltpu.HBM)
SMEM = pl.BlockSpec(memory_space=pltpu.SMEM)


def params():
    return pltpu.CompilerParams(vmem_limit_bytes=32 * 1024 * 1024)


def plane_weights(planes, rows_y):
    cells = planes * rows_y
    table = np.zeros((3 * cells, cells), np.float64)
    skipped = (planes - WIDTH) * rows_y
    for x in range(planes):
        for y in range(rows_y):
            out = x * rows_y + y
            for k, weight in enumerate(SIDES, 1):
                for step in (k, -k):
                    table[2 * cells + x * rows_y + (y + step) % rows_y, out] += weight
                    row = (x + step) * rows_y + y
                    if row < 0:
                        table[cells + row - skipped, out] += weight
                    elif row >= cells:
                        table[row, out] += weight
                    else:
                        table[2 * cells + row, out] += weight
    table = -0.5 * table
    high = table.astype(BF16)
    return high, (table - high.astype(np.float64)).astype(BF16)


def split(value):
    high = value.astype(BF16)
    return high, (value - high.astype(jnp.float32)).astype(BF16)


def dot3(left, right, contract):
    dot = lambda x, y: lax.dot_general(x, y, (contract, ((), ())), preferred_element_type=jnp.float32)
    rows = left[0].shape[0]
    both = dot(jnp.concatenate(left, axis=0), right[0])
    return both[:rows] + (both[rows:] + dot(left[0], right[1]))


def pack_kernel(blocks, x_hbm, *refs):
    *t_refs, turned, x_ref, sems = refs
    count, _, rows_z = x_ref.shape
    chunks = sems.shape[0]
    per = count // chunks
    copies = [
        pltpu.make_async_copy(x_hbm.at[pl.ds(i * per, per)], x_ref.at[pl.ds(i * per, per)], sems.at[i])
        for i in range(chunks)
    ]
    for copy in copies:
        copy.start()
    for i, copy in enumerate(copies):
        copy.wait()
        for a in range(i * per, (i + 1) * per):
            turned[pl.ds(a, rows_z, stride=count), :] = x_ref[a].T
    rows = rows_z // blocks * count
    rank = lax.axis_index("orb")
    for m, t_ref in enumerate(t_refs):
        for core in range(2):
            start = pl.multiple_of((rank ^ (2 * m + core)) * rows, rows)
            t_ref[core] = turned[pl.ds(start, rows), :].reshape(t_ref.shape[1:])


def hand_kernel(block_ref, owner_ref, pair_ref, other_ref):
    other_ref[...] = pair_ref[1]


def by_block(refs):
    refs = refs[::-1]
    half = len(refs) // 2 - 1
    return [refs[half + k // 2] if k % 2 else refs[k // 2].at[0] for k in range(2 * half)] + list(refs[2 * half :])


def squeeze(value):
    rows, wide = value.shape
    quarter, free = rows // 4, wide // 4
    lane = lax.broadcasted_iota(jnp.int32, (quarter, wide), 1)
    rest = value[3 * quarter :]
    parts = []
    for j in range(3):
        moved = pltpu.roll(rest, (3 - j) * free, 1)
        parts.append(jnp.where(lane < 3 * free, value[j * quarter : (j + 1) * quarter], moved))
    return jnp.concatenate(parts, axis=0)


def expand(value):
    rows, wide = value.shape
    quarter, free = rows // 3, wide // 4
    lane = lax.broadcasted_iota(jnp.int32, (quarter, wide), 1)
    rest = value[:quarter]
    for j in range(3):
        moved = pltpu.roll(value[j * quarter : (j + 1) * quarter], (j + 1) * free, 1)
        rest = jnp.where((lane >= j * free) & (lane < (j + 1) * free), moved, rest)
    return jnp.concatenate([value, rest], axis=0)


def pick_kernel(block_ref, *refs):
    x_refs, (act_ref, near_ref, far_ref, first_ref, last_ref) = by_block(refs[:-5]), refs[-5:]
    slab, nb, cells = act_ref.shape
    rank = lax.axis_index("orb")
    for k, x_ref in enumerate(x_refs):
        @pl.when((rank ^ block_ref[0]) == k)
        def _(x_ref=x_ref):
            act_ref[...] = x_ref[...]
    odd = rank % 2
    near_ref[...] = act_ref[pl.ds((1 - odd) * (slab - WIDTH), WIDTH)]
    far_ref[...] = act_ref[pl.ds(odd * (slab - WIDTH), WIDTH)]
    flat = act_ref[...].reshape(slab * nb, cells)
    first_ref[...] = squeeze(flat)
    last_ref[...] = squeeze(pltpu.roll(flat, 3 * (cells // 4), 1))


def split_kernel(blocks, act_ref, v_ref, wh_ref, wl_ref, *refs):
    x_refs, (high_ref, low_ref, inner_ref, turned) = by_block(refs[:-4]), refs[-4:]
    slab, nb, cells = act_ref.shape
    rank = lax.axis_index("orb")
    for k, x_ref in enumerate(x_refs):
        rows = pl.ds(pl.multiple_of((rank ^ k) * nb, nb), nb)
        for z in range(slab):
            high, low = split(x_ref[z])
            high_ref[rows, z * cells : (z + 1) * cells] = high
            low_ref[rows, z * cells : (z + 1) * cells] = low
    turned[...] = v_ref[...].T
    mine = pl.ds(pl.multiple_of(rank * slab, slab), slab)
    act = act_ref[...]
    middle = slice(2 * cells, 3 * cells)
    inner = dot3(split(act.reshape(slab * nb, cells)), (wh_ref[middle], wl_ref[middle]), ((1,), (0,)))
    inner = inner.reshape(slab, nb, cells) + (turned[mine, :][:, None, :] - 1.5 * CENTER) * act
    edge = jnp.zeros((WIDTH, nb, cells), jnp.float32)
    tall = jnp.concatenate([edge, act, edge], axis=0)
    for k, weight in enumerate(SIDES, 1):
        upper = tall[WIDTH + k : WIDTH + k + slab]
        lower = tall[WIDTH - k : WIDTH - k + slab]
        inner = inner + (-0.5 * weight) * (upper + lower)
    inner_ref[...] = inner


def project_kernel(
    volume, owner_ref, rot_ref, xh_ref, xl_ref, inner_ref, far_ref, near_ref, xb_ref, xa_ref, wh_ref, wl_ref,
    a_ref, p_ref, around,
):
    slab, nb, cells = inner_ref.shape
    rank = lax.axis_index("orb")
    odd = rank % 2
    around[1 - odd] = near_ref[...]
    around[odd] = far_ref[...]
    beside = slice(0, 2 * cells)
    wide = jnp.concatenate([expand(xb_ref[...]), expand(xa_ref[...])], axis=1)
    applied = dot3(split(wide), (wh_ref[beside], wl_ref[beside]), ((1,), (0,)))
    a_ref[...] = inner_ref[...] + applied.reshape(slab, nb, cells)
    for z in range(WIDTH):
        below, above = a_ref[z], a_ref[slab - 1 - z]
        for k in range(z + 1, WIDTH + 1):
            below = below + (-0.5 * SIDES[k - 1]) * around[0, WIDTH + z - k]
            above = above + (-0.5 * SIDES[k - 1]) * around[1, k - 1 - z]
        a_ref[z] = below
        a_ref[slab - 1 - z] = above
    flat = jnp.concatenate([a_ref[z] for z in range(slab)], axis=1)
    total = dot3(split(flat), (xh_ref[...], xl_ref[...]), ((1,), (1,)))
    p_ref[:nb] = total * volume
    p_ref[nb:] = jnp.where(rank == owner_ref[0], rot_ref[...], 0.0)


def remove_kernel(xh_ref, xl_ref, a_ref, *refs):
    *p_refs, g_ref = refs
    slab, nb, cells = a_ref.shape
    removed = dot3(split(total(p_refs, 0, nb)), (xh_ref[...], xl_ref[...]), ((1,), (0,)))
    for z in range(slab):
        g_ref[z] = a_ref[z] - removed[:, z * cells : (z + 1) * cells]


def mixing_kernel(nb, *refs):
    *p_refs, high_ref, low_ref = refs
    size, wide = high_ref.shape[0], p_refs[0].shape[1]
    row, col = (lax.broadcasted_iota(jnp.int32, (size, wide), axis) for axis in (0, 1))
    mine = jnp.where(col == lax.axis_index("orb") * nb + row // MIX, 1.0, 0.0).astype(BF16)
    orbital, col = (lax.broadcasted_iota(jnp.int32, (nb, size), axis) for axis in (0, 1))
    repeat = jnp.where(orbital == col // MIX, 1.0, 0.0).astype(BF16)
    row, col = (lax.broadcasted_iota(jnp.int32, (size, size), axis) for axis in (0, 1))
    same = row % MIX == col % MIX
    dot = lambda x, y, axes: lax.dot_general(x, y, (axes, ((), ())), preferred_element_type=jnp.float32)
    for part, ref in zip(split(total(p_refs, nb, nb)), (high_ref, low_ref)):
        block = dot(mine, part, ((1,), (1,))).astype(BF16)
        ref[...] = jnp.where(same, dot(block, repeat, ((1,), (0,))), 0.0).astype(BF16)


def update_kernel(blocks, sequence, wh_ref, wl_ref, x_ref, *refs):
    g_refs, (grad_hbm, out_hbm, whole, grad, out, sems) = refs[:blocks], refs[blocks:]
    nb, cells, rows_z = x_ref.shape
    rank = lax.axis_index("orb")
    share = rows_z // blocks * nb
    for k, g_ref in zip(sequence, g_refs):
        at = pl.ds(pl.multiple_of((rank ^ k) * share, share), share)
        whole[at, :] = g_ref[...].reshape(share, cells)
    per = nb // CHUNKS
    copies = []
    for i in range(CHUNKS):
        for c in range(i * per, (i + 1) * per):
            grad[c] = whole[pl.ds(c, rows_z, stride=nb), :].T
        part = pl.ds(i * per, per)
        copies.append(pltpu.make_async_copy(grad.at[part], grad_hbm.at[part], sems.at[0, i]))
        copies[-1].start()
    mix = (wh_ref[...], wl_ref[...])
    rows = cells // CHUNKS
    for i in range(CHUNKS):
        some = pl.ds(i * rows, rows)
        places = [pl.ds(start, MIX) for start in range(i * rows, (i + 1) * rows, MIX)]
        sides = [jnp.concatenate([grad[c, at] for c in range(nb)], axis=0) for at in places]
        result = dot3(mix, split(jnp.concatenate(sides, axis=1)), ((1,), (0,)))
        for j, at in enumerate(places):
            for a in range(nb):
                out[a, at] = x_ref[a, at] + result[a * MIX : (a + 1) * MIX, j * rows_z : (j + 1) * rows_z]
        copies.append(pltpu.make_async_copy(out.at[:, some], out_hbm.at[:, some], sems.at[1, i]))
        copies[-1].start()
    for copy in copies:
        copy.wait()


def swap(value, axis, k):
    count = lax.axis_size(axis)
    return lax.ppermute(value, axis, [(i, i ^ k) for i in range(count)])


def dom_kernel(value_ref, *refs):
    *other_refs, out_ref = refs
    nb = other_refs[0].shape[0]
    out_ref[:nb] = value_ref[:nb] + sum(ref[...] for ref in other_refs)
    out_ref[nb:] = value_ref[nb:]


def total(refs, first, count):
    rows = slice(first, first + count)
    return sum(ref[rows] for ref in refs)


def per_device(orbitals, potential, rotation, block, owner):
    nb, planes, rows_y, rows_z = orbitals.shape
    blocks, doms = lax.axis_size("orb"), lax.axis_size("dom")
    cells = planes * rows_y
    slab = rows_z // blocks
    volume = 1.0 / (cells * doms * rows_z)
    f32 = jnp.float32
    shape = lambda *dims: jax.ShapeDtypeStruct(dims, f32)
    piece, edge = shape(slab, nb, cells), shape(WIDTH, nb, cells)

    flat = orbitals.reshape(nb, cells, rows_z)
    held = pltpu.with_memory_space_constraint(flat, pltpu.HBM)
    chips = half = blocks // 2
    pieces = pl.pallas_call(
        functools.partial(pack_kernel, blocks),
        out_shape=[shape(2, slab, nb, cells)] * chips,
        in_specs=[HBM],
        out_specs=[VMEM] * chips,
        scratch_shapes=[
            pltpu.VMEM(((rows_z + 1) * nb, cells), f32),
            pltpu.VMEM((nb, cells, rows_z), f32),
            pltpu.SemaphoreType.DMA((CHUNKS,)),
        ],
        compiler_params=params(),
        name="pack",
    )(held)
    last = 2 * (chips - 1)
    pairs = [swap(value, "orb", 2 * m) if m else value for m, value in enumerate(pieces[:-1])]
    direct = [swap(pieces[-1][core], "orb", last + core) for core in range(2)]
    nearest = pl.pallas_call(
        hand_kernel,
        out_shape=piece,
        in_specs=[SMEM, SMEM, VMEM],
        out_specs=VMEM,
        compiler_params=params(),
        name="hand",
    )(block, owner, pairs[1])
    others = [nearest if m == 1 else value[1] for m, value in enumerate(pairs)]
    spread = (pairs + [swap(value, "orb", 1) for value in others] + direct)[::-1]

    side = shape(3 * slab * nb // 4, cells)
    active, near, far, first, last = pl.pallas_call(
        pick_kernel,
        out_shape=(piece, edge, edge, side, side),
        in_specs=[SMEM] + [VMEM] * len(spread),
        out_specs=[VMEM] * 5,
        compiler_params=params(),
        name="pick",
    )(block, *spread)

    up = lambda count: [(i, (i + 1) % count) for i in range(count)]
    down = lambda count: [(i, (i - 1) % count) for i in range(count)]
    x_before = lax.ppermute(last, "dom", up(doms))
    x_after = lax.ppermute(first, "dom", down(doms))
    z_near = swap(near, "orb", 1)
    z_far = lax.ppermute(far, "orb", [(o, (o + 2 * (o % 2) - 1) % blocks) for o in range(blocks)])

    halves = jax.ShapeDtypeStruct((blocks * nb, slab * cells), BF16)
    weights = [jnp.asarray(w) for w in plane_weights(planes, rows_y)]
    *parts, inner = pl.pallas_call(
        functools.partial(split_kernel, blocks),
        out_shape=(halves, halves, piece),
        in_specs=[VMEM] * (len(spread) + 4),
        out_specs=(VMEM, VMEM, VMEM),
        scratch_shapes=[pltpu.VMEM((rows_z, cells), f32)],
        compiler_params=params(),
        cost_estimate=pl.CostEstimate(flops=3 * blocks * nb * slab * cells, bytes_accessed=0, transcendentals=0),
        name="split",
    )(active, potential.reshape(cells, rows_z), *weights, *spread)

    applied, part = pl.pallas_call(
        functools.partial(project_kernel, volume),
        out_shape=(piece, shape(2 * nb, blocks * nb)),
        in_specs=[SMEM] + [VMEM] * 10,
        out_specs=(VMEM, VMEM),
        scratch_shapes=[pltpu.VMEM((2, WIDTH, nb, cells), f32)],
        compiler_params=params(),
        name="project",
    )(owner, rotation, *parts, inner, z_far, z_near, x_before, x_after, *weights)

    part = part + swap(part, "orb", 1)
    part = pl.pallas_call(
        dom_kernel,
        out_shape=shape(2 * nb, blocks * nb),
        in_specs=[VMEM] * doms,
        out_specs=VMEM,
        compiler_params=params(),
        name="dom",
    )(part, *[swap(part[:nb], "dom", k) for k in range(1, doms)])
    sums = [part] + [swap(part, "orb", k) for k in sorted(range(2, blocks, 2), key=lambda k: (k != half, k))]

    own = pl.pallas_call(
        remove_kernel,
        out_shape=piece,
        in_specs=[VMEM] * (3 + chips),
        out_specs=VMEM,
        compiler_params=params(),
        name="remove",
    )(*parts, applied, *sums)

    gathered = [own] + [None] * (blocks - 1)
    for k in range(2, blocks, 2):
        gathered[k] = swap(own, "orb", k)
    for k in range(0, blocks, 2):
        gathered[k + 1] = swap(gathered[k], "orb", 1)

    square = jax.ShapeDtypeStruct((MIX * nb, MIX * nb), BF16)
    mixing = pl.pallas_call(
        functools.partial(mixing_kernel, nb),
        out_shape=(square, square),
        in_specs=[VMEM] * chips,
        out_specs=(VMEM, VMEM),
        compiler_params=params(),
        name="mixing",
    )(*sums)

    sequence = sorted(range(blocks), key=lambda k: (k >= half, -k if k >= half else k))
    gradient, updated = pl.pallas_call(
        functools.partial(update_kernel, blocks, sequence),
        out_shape=(shape(nb, cells, rows_z), shape(nb, cells, rows_z)),
        in_specs=[VMEM] * (3 + blocks),
        out_specs=(HBM, HBM),
        scratch_shapes=[
            pltpu.VMEM(((rows_z + 1) * nb, cells), f32),
            pltpu.VMEM((nb, cells, rows_z), f32),
            pltpu.VMEM((nb, cells, rows_z), f32),
            pltpu.SemaphoreType.DMA((2, CHUNKS)),
        ],
        compiler_params=params(),
        name="update",
    )(*mixing, flat, *[gathered[k] for k in sequence])
    return gradient.reshape(orbitals.shape), updated.reshape(orbitals.shape)


def solution(mesh):
    in_specs = (P("orb", "dom", None, None), P("dom", None, None), P("orb", None), P(), P())
    out_specs = (P(None, "dom", None, None), P("orb", "dom", None, None))
    return jax.shard_map(
        per_device, mesh=mesh, in_specs=in_specs, out_specs=out_specs, check_vma=False
    )
```

```python
import functools

import jax
import jax.numpy as jnp
import numpy as np
from jax import lax
from jax.experimental import pallas as pl
from jax.experimental.pallas import tpu as pltpu
from jax.sharding import PartitionSpec as P

CENTER = -5369.0 / 1800.0
SIDES = (12.0 / 7.0, -15.0 / 56.0, 10.0 / 189.0, -1.0 / 112.0, 2.0 / 1925.0, -1.0 / 16632.0)
WIDTH = 6
CHUNKS = 4
MIX = 8
BF16 = jnp.bfloat16
VMEM = pl.BlockSpec(memory_space=pltpu.VMEM)
HBM = pl.BlockSpec(memory_space=pltpu.HBM)
SMEM = pl.BlockSpec(memory_space=pltpu.SMEM)


def params():
    return pltpu.CompilerParams(vmem_limit_bytes=32 * 1024 * 1024)


def plane_weights(planes, rows_y):
    cells = planes * rows_y
    table = np.zeros((3 * cells, cells), np.float64)
    skipped = (planes - WIDTH) * rows_y
    for x in range(planes):
        for y in range(rows_y):
            out = x * rows_y + y
            for k, weight in enumerate(SIDES, 1):
                for step in (k, -k):
                    table[2 * cells + x * rows_y + (y + step) % rows_y, out] += weight
                    row = (x + step) * rows_y + y
                    if row < 0:
                        table[cells + row - skipped, out] += weight
                    elif row >= cells:
                        table[row, out] += weight
                    else:
                        table[2 * cells + row, out] += weight
    table = -0.5 * table
    high = table.astype(BF16)
    return high, (table - high.astype(np.float64)).astype(BF16)


def split(value):
    high = value.astype(BF16)
    return high, (value - high.astype(jnp.float32)).astype(BF16)


def dot3(left, right, contract):
    dot = lambda x, y: lax.dot_general(x, y, (contract, ((), ())), preferred_element_type=jnp.float32)
    rows = left[0].shape[0]
    both = dot(jnp.concatenate(left, axis=0), right[0])
    return both[:rows] + (both[rows:] + dot(left[0], right[1]))


def pack_kernel(blocks, x_hbm, *refs):
    *t_refs, turned, x_ref, sems = refs
    count, _, rows_z = x_ref.shape
    chunks = sems.shape[0]
    per = count // chunks
    copies = [
        pltpu.make_async_copy(x_hbm.at[pl.ds(i * per, per)], x_ref.at[pl.ds(i * per, per)], sems.at[i])
        for i in range(chunks)
    ]
    for copy in copies:
        copy.start()
    for i, copy in enumerate(copies):
        copy.wait()
        for a in range(i * per, (i + 1) * per):
            turned[pl.ds(a, rows_z, stride=count), :] = x_ref[a].T
    rows = rows_z // blocks * count
    rank = lax.axis_index("orb")
    for m, t_ref in enumerate(t_refs):
        for core in range(2):
            start = pl.multiple_of((rank ^ (2 * m + core)) * rows, rows)
            t_ref[core] = turned[pl.ds(start, rows), :].reshape(t_ref.shape[1:])


def hand_kernel(block_ref, owner_ref, pair_ref, other_ref):
    other_ref[...] = pair_ref[1]


def by_block(refs):
    refs = refs[::-1]
    half = len(refs) // 2 - 1
    return [refs[half + k // 2] if k % 2 else refs[k // 2].at[0] for k in range(2 * half)] + list(refs[2 * half :])


def squeeze(value):
    rows, wide = value.shape
    quarter, free = rows // 4, wide // 4
    lane = lax.broadcasted_iota(jnp.int32, (quarter, wide), 1)
    rest = value[3 * quarter :]
    parts = []
    for j in range(3):
        moved = pltpu.roll(rest, (3 - j) * free, 1)
        parts.append(jnp.where(lane < 3 * free, value[j * quarter : (j + 1) * quarter], moved))
    return jnp.concatenate(parts, axis=0)


def expand(value):
    rows, wide = value.shape
    quarter, free = rows // 3, wide // 4
    lane = lax.broadcasted_iota(jnp.int32, (quarter, wide), 1)
    rest = value[:quarter]
    for j in range(3):
        moved = pltpu.roll(value[j * quarter : (j + 1) * quarter], (j + 1) * free, 1)
        rest = jnp.where((lane >= j * free) & (lane < (j + 1) * free), moved, rest)
    return jnp.concatenate([value, rest], axis=0)


def pick_kernel(block_ref, *refs):
    x_refs, (act_ref, near_ref, far_ref, first_ref, last_ref) = by_block(refs[:-5]), refs[-5:]
    slab, nb, cells = act_ref.shape
    rank = lax.axis_index("orb")
    for k, x_ref in enumerate(x_refs):
        @pl.when((rank ^ block_ref[0]) == k)
        def _(x_ref=x_ref):
            act_ref[...] = x_ref[...]
    odd = rank % 2
    near_ref[...] = act_ref[pl.ds((1 - odd) * (slab - WIDTH), WIDTH)]
    far_ref[...] = act_ref[pl.ds(odd * (slab - WIDTH), WIDTH)]
    flat = act_ref[...].reshape(slab * nb, cells)
    first_ref[...] = squeeze(flat)
    last_ref[...] = squeeze(pltpu.roll(flat, 3 * (cells // 4), 1))


def split_kernel(blocks, act_ref, v_ref, wh_ref, wl_ref, *refs):
    x_refs, (high_ref, low_ref, inner_ref, turned) = by_block(refs[:-4]), refs[-4:]
    slab, nb, cells = act_ref.shape
    rank = lax.axis_index("orb")
    for k, x_ref in enumerate(x_refs):
        rows = pl.ds(pl.multiple_of((rank ^ k) * nb, nb), nb)
        for z in range(slab):
            high, low = split(x_ref[z])
            high_ref[rows, z * cells : (z + 1) * cells] = high
            low_ref[rows, z * cells : (z + 1) * cells] = low
    turned[...] = v_ref[...].T
    mine = pl.ds(pl.multiple_of(rank * slab, slab), slab)
    act = act_ref[...]
    middle = slice(2 * cells, 3 * cells)
    inner = dot3(split(act.reshape(slab * nb, cells)), (wh_ref[middle], wl_ref[middle]), ((1,), (0,)))
    inner = inner.reshape(slab, nb, cells) + (turned[mine, :][:, None, :] - 1.5 * CENTER) * act
    edge = jnp.zeros((WIDTH, nb, cells), jnp.float32)
    tall = jnp.concatenate([edge, act, edge], axis=0)
    for k, weight in enumerate(SIDES, 1):
        upper = tall[WIDTH + k : WIDTH + k + slab]
        lower = tall[WIDTH - k : WIDTH - k + slab]
        inner = inner + (-0.5 * weight) * (upper + lower)
    inner_ref[...] = inner


def project_kernel(
    volume, owner_ref, rot_ref, xh_ref, xl_ref, inner_ref, far_ref, near_ref, xb_ref, xa_ref, wh_ref, wl_ref,
    a_ref, p_ref, around,
):
    slab, nb, cells = inner_ref.shape
    rank = lax.axis_index("orb")
    odd = rank % 2
    around[1 - odd] = near_ref[...]
    around[odd] = far_ref[...]
    beside = slice(0, 2 * cells)
    wide = jnp.concatenate([expand(xb_ref[...]), expand(xa_ref[...])], axis=1)
    applied = dot3(split(wide), (wh_ref[beside], wl_ref[beside]), ((1,), (0,)))
    a_ref[...] = inner_ref[...] + applied.reshape(slab, nb, cells)
    for z in range(WIDTH):
        below, above = a_ref[z], a_ref[slab - 1 - z]
        for k in range(z + 1, WIDTH + 1):
            below = below + (-0.5 * SIDES[k - 1]) * around[0, WIDTH + z - k]
            above = above + (-0.5 * SIDES[k - 1]) * around[1, k - 1 - z]
        a_ref[z] = below
        a_ref[slab - 1 - z] = above
    flat = jnp.concatenate([a_ref[z] for z in range(slab)], axis=1)
    total = dot3(split(flat), (xh_ref[...], xl_ref[...]), ((1,), (1,)))
    p_ref[:nb] = total * volume
    p_ref[nb:] = jnp.where(rank == owner_ref[0], rot_ref[...], 0.0)


def remove_kernel(xh_ref, xl_ref, a_ref, *refs):
    *p_refs, g_ref = refs
    slab, nb, cells = a_ref.shape
    removed = dot3(split(total(p_refs, 0, nb)), (xh_ref[...], xl_ref[...]), ((1,), (0,)))
    for z in range(slab):
        g_ref[z] = a_ref[z] - removed[:, z * cells : (z + 1) * cells]


def mixing_kernel(nb, *refs):
    *p_refs, high_ref, low_ref = refs
    size, wide = high_ref.shape[0], p_refs[0].shape[1]
    row, col = (lax.broadcasted_iota(jnp.int32, (size, wide), axis) for axis in (0, 1))
    mine = jnp.where(col == lax.axis_index("orb") * nb + row // MIX, 1.0, 0.0).astype(BF16)
    orbital, col = (lax.broadcasted_iota(jnp.int32, (nb, size), axis) for axis in (0, 1))
    repeat = jnp.where(orbital == col // MIX, 1.0, 0.0).astype(BF16)
    row, col = (lax.broadcasted_iota(jnp.int32, (size, size), axis) for axis in (0, 1))
    same = row % MIX == col % MIX
    dot = lambda x, y, axes: lax.dot_general(x, y, (axes, ((), ())), preferred_element_type=jnp.float32)
    for part, ref in zip(split(total(p_refs, nb, nb)), (high_ref, low_ref)):
        block = dot(mine, part, ((1,), (1,))).astype(BF16)
        ref[...] = jnp.where(same, dot(block, repeat, ((1,), (0,))), 0.0).astype(BF16)


def update_kernel(blocks, sequence, wh_ref, wl_ref, x_ref, *refs):
    g_refs, (grad_hbm, out_hbm, whole, grad, out, sems) = refs[:blocks], refs[blocks:]
    nb, cells, rows_z = x_ref.shape
    rank = lax.axis_index("orb")
    share = rows_z // blocks * nb
    for k, g_ref in zip(sequence, g_refs):
        at = pl.ds(pl.multiple_of((rank ^ k) * share, share), share)
        whole[at, :] = g_ref[...].reshape(share, cells)
    per = nb // CHUNKS
    copies = []
    for i in range(CHUNKS):
        for c in range(i * per, (i + 1) * per):
            grad[c] = whole[pl.ds(c, rows_z, stride=nb), :].T
        part = pl.ds(i * per, per)
        copies.append(pltpu.make_async_copy(grad.at[part], grad_hbm.at[part], sems.at[0, i]))
        copies[-1].start()
    mix = (wh_ref[...], wl_ref[...])
    rows = cells // CHUNKS
    for i in range(CHUNKS):
        some = pl.ds(i * rows, rows)
        places = [pl.ds(start, MIX) for start in range(i * rows, (i + 1) * rows, MIX)]
        sides = [jnp.concatenate([grad[c, at] for c in range(nb)], axis=0) for at in places]
        result = dot3(mix, split(jnp.concatenate(sides, axis=1)), ((1,), (0,)))
        for j, at in enumerate(places):
            for a in range(nb):
                out[a, at] = x_ref[a, at] + result[a * MIX : (a + 1) * MIX, j * rows_z : (j + 1) * rows_z]
        copies.append(pltpu.make_async_copy(out.at[:, some], out_hbm.at[:, some], sems.at[1, i]))
        copies[-1].start()
    for copy in copies:
        copy.wait()


def swap(value, axis, k):
    count = lax.axis_size(axis)
    return lax.ppermute(value, axis, [(i, i ^ k) for i in range(count)])


def dom_kernel(value_ref, *refs):
    *other_refs, out_ref = refs
    nb = other_refs[0].shape[0]
    out_ref[:nb] = value_ref[:nb] + sum(ref[...] for ref in other_refs)
    out_ref[nb:] = value_ref[nb:]


def total(refs, first, count):
    rows = slice(first, first + count)
    return sum(ref[rows] for ref in refs)


def per_device(orbitals, potential, rotation, block, owner):
    nb, planes, rows_y, rows_z = orbitals.shape
    blocks, doms = lax.axis_size("orb"), lax.axis_size("dom")
    cells = planes * rows_y
    slab = rows_z // blocks
    volume = 1.0 / (cells * doms * rows_z)
    f32 = jnp.float32
    shape = lambda *dims: jax.ShapeDtypeStruct(dims, f32)
    piece, edge = shape(slab, nb, cells), shape(WIDTH, nb, cells)

    flat = orbitals.reshape(nb, cells, rows_z)
    held = pltpu.with_memory_space_constraint(flat, pltpu.HBM)
    chips = half = blocks // 2
    pieces = pl.pallas_call(
        functools.partial(pack_kernel, blocks),
        out_shape=[shape(2, slab, nb, cells)] * chips,
        in_specs=[HBM],
        out_specs=[VMEM] * chips,
        scratch_shapes=[
            pltpu.VMEM(((rows_z + 1) * nb, cells), f32),
            pltpu.VMEM((nb, cells, rows_z), f32),
            pltpu.SemaphoreType.DMA((CHUNKS,)),
        ],
        compiler_params=params(),
        name="pack",
    )(held)
    last = 2 * (chips - 1)
    pairs = [swap(value, "orb", 2 * m) if m else value for m, value in enumerate(pieces[:-1])]
    direct = [swap(pieces[-1][core], "orb", last + core) for core in range(2)]
    nearest = pl.pallas_call(
        hand_kernel,
        out_shape=piece,
        in_specs=[SMEM, SMEM, VMEM],
        out_specs=VMEM,
        compiler_params=params(),
        name="hand",
    )(block, owner, pairs[1])
    others = [nearest if m == 1 else value[1] for m, value in enumerate(pairs)]
    spread = (pairs + [swap(value, "orb", 1) for value in others] + direct)[::-1]

    side = shape(3 * slab * nb // 4, cells)
    active, near, far, first, last = pl.pallas_call(
        pick_kernel,
        out_shape=(piece, edge, edge, side, side),
        in_specs=[SMEM] + [VMEM] * len(spread),
        out_specs=[VMEM] * 5,
        compiler_params=params(),
        name="pick",
    )(block, *spread)

    up = lambda count: [(i, (i + 1) % count) for i in range(count)]
    down = lambda count: [(i, (i - 1) % count) for i in range(count)]
    x_before = lax.ppermute(last, "dom", up(doms))
    x_after = lax.ppermute(first, "dom", down(doms))
    z_near = swap(near, "orb", 1)
    z_far = lax.ppermute(far, "orb", [(o, (o + 2 * (o % 2) - 1) % blocks) for o in range(blocks)])

    halves = jax.ShapeDtypeStruct((blocks * nb, slab * cells), BF16)
    weights = [jnp.asarray(w) for w in plane_weights(planes, rows_y)]
    *parts, inner = pl.pallas_call(
        functools.partial(split_kernel, blocks),
        out_shape=(halves, halves, piece),
        in_specs=[VMEM] * (len(spread) + 4),
        out_specs=(VMEM, VMEM, VMEM),
        scratch_shapes=[pltpu.VMEM((rows_z, cells), f32)],
        compiler_params=params(),
        cost_estimate=pl.CostEstimate(flops=3 * blocks * nb * slab * cells, bytes_accessed=0, transcendentals=0),
        name="split",
    )(active, potential.reshape(cells, rows_z), *weights, *spread)

    applied, part = pl.pallas_call(
        functools.partial(project_kernel, volume),
        out_shape=(piece, shape(2 * nb, blocks * nb)),
        in_specs=[SMEM] + [VMEM] * 10,
        out_specs=(VMEM, VMEM),
        scratch_shapes=[pltpu.VMEM((2, WIDTH, nb, cells), f32)],
        compiler_params=params(),
        name="project",
    )(owner, rotation, *parts, inner, z_far, z_near, x_before, x_after, *weights)

    part = part + swap(part, "orb", 1)
    part = pl.pallas_call(
        dom_kernel,
        out_shape=shape(2 * nb, blocks * nb),
        in_specs=[VMEM] * doms,
        out_specs=VMEM,
        compiler_params=params(),
        name="dom",
    )(part, *[swap(part[:nb], "dom", k) for k in sorted(range(1, doms), key=lambda k: (k.bit_count() > 1, -k))])
    sums = [part] + [swap(part, "orb", k) for k in range(2, blocks, 2)]

    own = pl.pallas_call(
        remove_kernel,
        out_shape=piece,
        in_specs=[VMEM] * (3 + chips),
        out_specs=VMEM,
        compiler_params=params(),
        name="remove",
    )(*parts, applied, *sums)

    gathered = [own] + [None] * (blocks - 1)
    for k in range(2, blocks, 2):
        gathered[k] = swap(own, "orb", k)
    for k in range(0, blocks, 2):
        gathered[k + 1] = swap(gathered[k], "orb", 1)

    square = jax.ShapeDtypeStruct((MIX * nb, MIX * nb), BF16)
    mixing = pl.pallas_call(
        functools.partial(mixing_kernel, nb),
        out_shape=(square, square),
        in_specs=[VMEM] * chips,
        out_specs=(VMEM, VMEM),
        compiler_params=params(),
        name="mixing",
    )(*sums)

    sequence = sorted(range(blocks), key=lambda k: (k >= half, -k if k >= half else k))
    gradient, updated = pl.pallas_call(
        functools.partial(update_kernel, blocks, sequence),
        out_shape=(shape(nb, cells, rows_z), shape(nb, cells, rows_z)),
        in_specs=[VMEM] * (3 + blocks),
        out_specs=(HBM, HBM),
        scratch_shapes=[
            pltpu.VMEM(((rows_z + 1) * nb, cells), f32),
            pltpu.VMEM((nb, cells, rows_z), f32),
            pltpu.VMEM((nb, cells, rows_z), f32),
            pltpu.SemaphoreType.DMA((2, CHUNKS)),
        ],
        compiler_params=params(),
        name="update",
    )(*mixing, flat, *[gathered[k] for k in sequence])
    return gradient.reshape(orbitals.shape), updated.reshape(orbitals.shape)


def solution(mesh):
    in_specs = (P("orb", "dom", None, None), P("dom", None, None), P("orb", None), P(), P())
    out_specs = (P(None, "dom", None, None), P("orb", "dom", None, None))
    return jax.shard_map(
        per_device, mesh=mesh, in_specs=in_specs, out_specs=out_specs, check_vma=False
    )
```

```python
import functools

import jax
import jax.numpy as jnp
import numpy as np
from jax import lax
from jax.experimental import pallas as pl
from jax.experimental.pallas import tpu as pltpu
from jax.sharding import PartitionSpec as P

CENTER = -5369.0 / 1800.0
SIDES = (12.0 / 7.0, -15.0 / 56.0, 10.0 / 189.0, -1.0 / 112.0, 2.0 / 1925.0, -1.0 / 16632.0)
WIDTH = 6
CHUNKS = 4
MIX = 8
BF16 = jnp.bfloat16
VMEM = pl.BlockSpec(memory_space=pltpu.VMEM)
HBM = pl.BlockSpec(memory_space=pltpu.HBM)
SMEM = pl.BlockSpec(memory_space=pltpu.SMEM)


def params():
    return pltpu.CompilerParams(vmem_limit_bytes=32 * 1024 * 1024)


def plane_weights(planes, rows_y):
    cells = planes * rows_y
    table = np.zeros((3 * cells, cells), np.float64)
    skipped = (planes - WIDTH) * rows_y
    for x in range(planes):
        for y in range(rows_y):
            out = x * rows_y + y
            for k, weight in enumerate(SIDES, 1):
                for step in (k, -k):
                    table[2 * cells + x * rows_y + (y + step) % rows_y, out] += weight
                    row = (x + step) * rows_y + y
                    if row < 0:
                        table[cells + row - skipped, out] += weight
                    elif row >= cells:
                        table[row, out] += weight
                    else:
                        table[2 * cells + row, out] += weight
    table = -0.5 * table
    high = table.astype(BF16)
    return high, (table - high.astype(np.float64)).astype(BF16)


def split(value):
    high = value.astype(BF16)
    return high, (value - high.astype(jnp.float32)).astype(BF16)


def dot3(left, right, contract):
    dot = lambda x, y: lax.dot_general(x, y, (contract, ((), ())), preferred_element_type=jnp.float32)
    rows = left[0].shape[0]
    both = dot(jnp.concatenate(left, axis=0), right[0])
    return both[:rows] + (both[rows:] + dot(left[0], right[1]))


def pack_kernel(blocks, x_hbm, *refs):
    *t_refs, turned, x_ref, sems = refs
    count, _, rows_z = x_ref.shape
    chunks = sems.shape[0]
    per = count // chunks
    copies = [
        pltpu.make_async_copy(x_hbm.at[pl.ds(i * per, per)], x_ref.at[pl.ds(i * per, per)], sems.at[i])
        for i in range(chunks)
    ]
    for copy in copies:
        copy.start()
    for i, copy in enumerate(copies):
        copy.wait()
        for a in range(i * per, (i + 1) * per):
            turned[pl.ds(a, rows_z, stride=count), :] = x_ref[a].T
    rows = rows_z // blocks * count
    rank = lax.axis_index("orb")
    for m, t_ref in enumerate(t_refs):
        for core in range(2):
            start = pl.multiple_of((rank ^ (2 * m + core)) * rows, rows)
            t_ref[core] = turned[pl.ds(start, rows), :].reshape(t_ref.shape[1:])


def hand_kernel(block_ref, owner_ref, pair_ref, other_ref):
    other_ref[...] = pair_ref[1]


def by_block(refs):
    refs = refs[::-1]
    half = len(refs) // 2 - 1
    return [refs[half + k // 2] if k % 2 else refs[k // 2].at[0] for k in range(2 * half)] + list(refs[2 * half :])


def squeeze(value):
    rows, wide = value.shape
    quarter, free = rows // 4, wide // 4
    lane = lax.broadcasted_iota(jnp.int32, (quarter, wide), 1)
    rest = value[3 * quarter :]
    parts = []
    for j in range(3):
        moved = pltpu.roll(rest, (3 - j) * free, 1)
        parts.append(jnp.where(lane < 3 * free, value[j * quarter : (j + 1) * quarter], moved))
    return jnp.concatenate(parts, axis=0)


def expand(value):
    rows, wide = value.shape
    quarter, free = rows // 3, wide // 4
    lane = lax.broadcasted_iota(jnp.int32, (quarter, wide), 1)
    rest = value[:quarter]
    for j in range(3):
        moved = pltpu.roll(value[j * quarter : (j + 1) * quarter], (j + 1) * free, 1)
        rest = jnp.where((lane >= j * free) & (lane < (j + 1) * free), moved, rest)
    return jnp.concatenate([value, rest], axis=0)


def pick_kernel(block_ref, *refs):
    x_refs, (act_ref, near_ref, far_ref, first_ref, last_ref) = by_block(refs[:-5]), refs[-5:]
    slab, nb, cells = act_ref.shape
    rank = lax.axis_index("orb")
    for k, x_ref in enumerate(x_refs):
        @pl.when((rank ^ block_ref[0]) == k)
        def _(x_ref=x_ref):
            act_ref[...] = x_ref[...]
    odd = rank % 2
    near_ref[...] = act_ref[pl.ds((1 - odd) * (slab - WIDTH), WIDTH)]
    far_ref[...] = act_ref[pl.ds(odd * (slab - WIDTH), WIDTH)]
    flat = act_ref[...].reshape(slab * nb, cells)
    first_ref[...] = squeeze(flat)
    last_ref[...] = squeeze(pltpu.roll(flat, 3 * (cells // 4), 1))


def split_kernel(blocks, act_ref, v_ref, wh_ref, wl_ref, *refs):
    x_refs, (high_ref, low_ref, inner_ref, turned) = by_block(refs[:-4]), refs[-4:]
    slab, nb, cells = act_ref.shape
    rank = lax.axis_index("orb")
    for k, x_ref in enumerate(x_refs):
        rows = pl.ds(pl.multiple_of((rank ^ k) * nb, nb), nb)
        for z in range(slab):
            high, low = split(x_ref[z])
            high_ref[rows, z * cells : (z + 1) * cells] = high
            low_ref[rows, z * cells : (z + 1) * cells] = low
    turned[...] = v_ref[...].T
    mine = pl.ds(pl.multiple_of(rank * slab, slab), slab)
    act = act_ref[...]
    middle = slice(2 * cells, 3 * cells)
    inner = dot3(split(act.reshape(slab * nb, cells)), (wh_ref[middle], wl_ref[middle]), ((1,), (0,)))
    inner = inner.reshape(slab, nb, cells) + (turned[mine, :][:, None, :] - 1.5 * CENTER) * act
    edge = jnp.zeros((WIDTH, nb, cells), jnp.float32)
    tall = jnp.concatenate([edge, act, edge], axis=0)
    for k, weight in enumerate(SIDES, 1):
        upper = tall[WIDTH + k : WIDTH + k + slab]
        lower = tall[WIDTH - k : WIDTH - k + slab]
        inner = inner + (-0.5 * weight) * (upper + lower)
    inner_ref[...] = inner


def project_kernel(
    volume, owner_ref, rot_ref, xh_ref, xl_ref, inner_ref, far_ref, near_ref, xb_ref, xa_ref, wh_ref, wl_ref,
    a_ref, p_ref, around,
):
    slab, nb, cells = inner_ref.shape
    rank = lax.axis_index("orb")
    odd = rank % 2
    around[1 - odd] = near_ref[...]
    around[odd] = far_ref[...]
    beside = slice(0, 2 * cells)
    wide = jnp.concatenate([expand(xb_ref[...]), expand(xa_ref[...])], axis=1)
    applied = dot3(split(wide), (wh_ref[beside], wl_ref[beside]), ((1,), (0,)))
    a_ref[...] = inner_ref[...] + applied.reshape(slab, nb, cells)
    for z in range(WIDTH):
        below, above = a_ref[z], a_ref[slab - 1 - z]
        for k in range(z + 1, WIDTH + 1):
            below = below + (-0.5 * SIDES[k - 1]) * around[0, WIDTH + z - k]
            above = above + (-0.5 * SIDES[k - 1]) * around[1, k - 1 - z]
        a_ref[z] = below
        a_ref[slab - 1 - z] = above
    flat = jnp.concatenate([a_ref[z] for z in range(slab)], axis=1)
    total = dot3(split(flat), (xh_ref[...], xl_ref[...]), ((1,), (1,)))
    p_ref[:nb] = total * volume
    p_ref[nb:] = jnp.where(rank == owner_ref[0], rot_ref[...], 0.0)


def remove_kernel(xh_ref, xl_ref, a_ref, *refs):
    *p_refs, g_ref = refs
    slab, nb, cells = a_ref.shape
    removed = dot3(split(total(p_refs, 0, nb)), (xh_ref[...], xl_ref[...]), ((1,), (0,)))
    for z in range(slab):
        g_ref[z] = a_ref[z] - removed[:, z * cells : (z + 1) * cells]


def mixing_kernel(nb, *refs):
    *p_refs, high_ref, low_ref = refs
    size, wide = high_ref.shape[0], p_refs[0].shape[1]
    row, col = (lax.broadcasted_iota(jnp.int32, (size, wide), axis) for axis in (0, 1))
    mine = jnp.where(col == lax.axis_index("orb") * nb + row // MIX, 1.0, 0.0).astype(BF16)
    orbital, col = (lax.broadcasted_iota(jnp.int32, (nb, size), axis) for axis in (0, 1))
    repeat = jnp.where(orbital == col // MIX, 1.0, 0.0).astype(BF16)
    row, col = (lax.broadcasted_iota(jnp.int32, (size, size), axis) for axis in (0, 1))
    same = row % MIX == col % MIX
    dot = lambda x, y, axes: lax.dot_general(x, y, (axes, ((), ())), preferred_element_type=jnp.float32)
    for part, ref in zip(split(total(p_refs, nb, nb)), (high_ref, low_ref)):
        block = dot(mine, part, ((1,), (1,))).astype(BF16)
        ref[...] = jnp.where(same, dot(block, repeat, ((1,), (0,))), 0.0).astype(BF16)


def update_kernel(blocks, sequence, wh_ref, wl_ref, x_ref, *refs):
    g_refs, (grad_hbm, out_hbm, whole, grad, out, sems) = refs[:blocks], refs[blocks:]
    nb, cells, rows_z = x_ref.shape
    rank = lax.axis_index("orb")
    share = rows_z // blocks * nb
    for k, g_ref in zip(sequence, g_refs):
        at = pl.ds(pl.multiple_of((rank ^ k) * share, share), share)
        whole[at, :] = g_ref[...].reshape(share, cells)
    per = nb // CHUNKS
    copies = []
    for i in range(CHUNKS):
        for c in range(i * per, (i + 1) * per):
            grad[c] = whole[pl.ds(c, rows_z, stride=nb), :].T
        part = pl.ds(i * per, per)
        copies.append(pltpu.make_async_copy(grad.at[part], grad_hbm.at[part], sems.at[0, i]))
        copies[-1].start()
    mix = (wh_ref[...], wl_ref[...])
    rows = cells // CHUNKS
    for i in range(CHUNKS):
        some = pl.ds(i * rows, rows)
        places = [pl.ds(start, MIX) for start in range(i * rows, (i + 1) * rows, MIX)]
        sides = [jnp.concatenate([grad[c, at] for c in range(nb)], axis=0) for at in places]
        result = dot3(mix, split(jnp.concatenate(sides, axis=1)), ((1,), (0,)))
        for j, at in enumerate(places):
            for a in range(nb):
                out[a, at] = x_ref[a, at] + result[a * MIX : (a + 1) * MIX, j * rows_z : (j + 1) * rows_z]
        copies.append(pltpu.make_async_copy(out.at[:, some], out_hbm.at[:, some], sems.at[1, i]))
        copies[-1].start()
    for copy in copies:
        copy.wait()


def swap(value, axis, k):
    count = lax.axis_size(axis)
    return lax.ppermute(value, axis, [(i, i ^ k) for i in range(count)])


def dom_kernel(value_ref, *refs):
    *other_refs, out_ref = refs
    nb = other_refs[0].shape[0]
    out_ref[:nb] = value_ref[:nb] + sum(ref[...] for ref in other_refs)
    out_ref[nb:] = value_ref[nb:]


def total(refs, first, count):
    rows = slice(first, first + count)
    return sum(ref[rows] for ref in refs)


def per_device(orbitals, potential, rotation, block, owner):
    nb, planes, rows_y, rows_z = orbitals.shape
    blocks, doms = lax.axis_size("orb"), lax.axis_size("dom")
    cells = planes * rows_y
    slab = rows_z // blocks
    volume = 1.0 / (cells * doms * rows_z)
    f32 = jnp.float32
    shape = lambda *dims: jax.ShapeDtypeStruct(dims, f32)
    piece, edge = shape(slab, nb, cells), shape(WIDTH, nb, cells)

    flat = orbitals.reshape(nb, cells, rows_z)
    held = pltpu.with_memory_space_constraint(flat, pltpu.HBM)
    chips = half = blocks // 2
    pieces = pl.pallas_call(
        functools.partial(pack_kernel, blocks),
        out_shape=[shape(2, slab, nb, cells)] * chips,
        in_specs=[HBM],
        out_specs=[VMEM] * chips,
        scratch_shapes=[
            pltpu.VMEM(((rows_z + 1) * nb, cells), f32),
            pltpu.VMEM((nb, cells, rows_z), f32),
            pltpu.SemaphoreType.DMA((CHUNKS,)),
        ],
        compiler_params=params(),
        name="pack",
    )(held)
    last = 2 * (chips - 1)
    pairs = [swap(value, "orb", 2 * m) if m else value for m, value in enumerate(pieces[:-1])]
    direct = [swap(pieces[-1][core], "orb", last + core) for core in range(2)]
    nearest = pl.pallas_call(
        hand_kernel,
        out_shape=piece,
        in_specs=[SMEM, SMEM, VMEM],
        out_specs=VMEM,
        compiler_params=params(),
        name="hand",
    )(block, owner, pairs[1])
    others = [nearest if m == 1 else value[1] for m, value in enumerate(pairs)]
    spread = (pairs + [swap(value, "orb", 1) for value in others] + direct)[::-1]

    side = shape(3 * slab * nb // 4, cells)
    active, near, far, first, last = pl.pallas_call(
        pick_kernel,
        out_shape=(piece, edge, edge, side, side),
        in_specs=[SMEM] + [VMEM] * len(spread),
        out_specs=[VMEM] * 5,
        compiler_params=params(),
        name="pick",
    )(block, *spread)

    up = lambda count: [(i, (i + 1) % count) for i in range(count)]
    down = lambda count: [(i, (i - 1) % count) for i in range(count)]
    x_before = lax.ppermute(last, "dom", up(doms))
    x_after = lax.ppermute(first, "dom", down(doms))
    z_near = swap(near, "orb", 1)
    z_far = lax.ppermute(far, "orb", [(o, (o + 2 * (o % 2) - 1) % blocks) for o in range(blocks)])

    halves = jax.ShapeDtypeStruct((blocks * nb, slab * cells), BF16)
    weights = [jnp.asarray(w) for w in plane_weights(planes, rows_y)]
    *parts, inner = pl.pallas_call(
        functools.partial(split_kernel, blocks),
        out_shape=(halves, halves, piece),
        in_specs=[VMEM] * (len(spread) + 4),
        out_specs=(VMEM, VMEM, VMEM),
        scratch_shapes=[pltpu.VMEM((rows_z, cells), f32)],
        compiler_params=params(),
        cost_estimate=pl.CostEstimate(flops=3 * blocks * nb * slab * cells, bytes_accessed=0, transcendentals=0),
        name="split",
    )(active, potential.reshape(cells, rows_z), *weights, *spread)

    applied, part = pl.pallas_call(
        functools.partial(project_kernel, volume),
        out_shape=(piece, shape(2 * nb, blocks * nb)),
        in_specs=[SMEM] + [VMEM] * 10,
        out_specs=(VMEM, VMEM),
        scratch_shapes=[pltpu.VMEM((2, WIDTH, nb, cells), f32)],
        compiler_params=params(),
        name="project",
    )(owner, rotation, *parts, inner, z_far, z_near, x_before, x_after, *weights)

    part = part + swap(part, "orb", 1)
    part = pl.pallas_call(
        dom_kernel,
        out_shape=shape(2 * nb, blocks * nb),
        in_specs=[VMEM] * doms,
        out_specs=VMEM,
        compiler_params=params(),
        name="dom",
    )(part, *[swap(part[:nb], "dom", k) for k in sorted(range(1, doms), key=lambda k: (k == 1, k))])
    sums = [part] + [swap(part, "orb", k) for k in range(2, blocks, 2)]

    own = pl.pallas_call(
        remove_kernel,
        out_shape=piece,
        in_specs=[VMEM] * (3 + chips),
        out_specs=VMEM,
        compiler_params=params(),
        name="remove",
    )(*parts, applied, *sums)

    gathered = [own] + [None] * (blocks - 1)
    for k in range(2, blocks, 2):
        gathered[k] = swap(own, "orb", k)
    for k in range(0, blocks, 2):
        gathered[k + 1] = swap(gathered[k], "orb", 1)

    square = jax.ShapeDtypeStruct((MIX * nb, MIX * nb), BF16)
    mixing = pl.pallas_call(
        functools.partial(mixing_kernel, nb),
        out_shape=(square, square),
        in_specs=[VMEM] * chips,
        out_specs=(VMEM, VMEM),
        compiler_params=params(),
        name="mixing",
    )(*sums)

    sequence = sorted(range(blocks), key=lambda k: (k >= half, -k if k >= half else k))
    gradient, updated = pl.pallas_call(
        functools.partial(update_kernel, blocks, sequence),
        out_shape=(shape(nb, cells, rows_z), shape(nb, cells, rows_z)),
        in_specs=[VMEM] * (3 + blocks),
        out_specs=(HBM, HBM),
        scratch_shapes=[
            pltpu.VMEM(((rows_z + 1) * nb, cells), f32),
            pltpu.VMEM((nb, cells, rows_z), f32),
            pltpu.VMEM((nb, cells, rows_z), f32),
            pltpu.SemaphoreType.DMA((2, CHUNKS)),
        ],
        compiler_params=params(),
        name="update",
    )(*mixing, flat, *[gathered[k] for k in sequence])
    return gradient.reshape(orbitals.shape), updated.reshape(orbitals.shape)


def solution(mesh):
    in_specs = (P("orb", "dom", None, None), P("dom", None, None), P("orb", None), P(), P())
    out_specs = (P(None, "dom", None, None), P("orb", "dom", None, None))
    return jax.shard_map(
        per_device, mesh=mesh, in_specs=in_specs, out_specs=out_specs, check_vma=False
    )
```

```python
import functools

import jax
import jax.numpy as jnp
import numpy as np
from jax import lax
from jax.experimental import pallas as pl
from jax.experimental.pallas import tpu as pltpu
from jax.sharding import PartitionSpec as P

CENTER = -5369.0 / 1800.0
SIDES = (12.0 / 7.0, -15.0 / 56.0, 10.0 / 189.0, -1.0 / 112.0, 2.0 / 1925.0, -1.0 / 16632.0)
WIDTH = 6
CHUNKS = 4
MIX = 8
BF16 = jnp.bfloat16
VMEM = pl.BlockSpec(memory_space=pltpu.VMEM)
HBM = pl.BlockSpec(memory_space=pltpu.HBM)
SMEM = pl.BlockSpec(memory_space=pltpu.SMEM)


def params():
    return pltpu.CompilerParams(vmem_limit_bytes=32 * 1024 * 1024)


def plane_weights(planes, rows_y):
    cells = planes * rows_y
    table = np.zeros((3 * cells, cells), np.float64)
    skipped = (planes - WIDTH) * rows_y
    for x in range(planes):
        for y in range(rows_y):
            out = x * rows_y + y
            for k, weight in enumerate(SIDES, 1):
                for step in (k, -k):
                    table[2 * cells + x * rows_y + (y + step) % rows_y, out] += weight
                    row = (x + step) * rows_y + y
                    if row < 0:
                        table[cells + row - skipped, out] += weight
                    elif row >= cells:
                        table[row, out] += weight
                    else:
                        table[2 * cells + row, out] += weight
    table = -0.5 * table
    high = table.astype(BF16)
    return high, (table - high.astype(np.float64)).astype(BF16)


def split(value):
    high = value.astype(BF16)
    return high, (value - high.astype(jnp.float32)).astype(BF16)


def dot3(left, right, contract):
    dot = lambda x, y: lax.dot_general(x, y, (contract, ((), ())), preferred_element_type=jnp.float32)
    rows = left[0].shape[0]
    both = dot(jnp.concatenate(left, axis=0), right[0])
    return both[:rows] + (both[rows:] + dot(left[0], right[1]))


def pack_kernel(blocks, x_hbm, *refs):
    *t_refs, turned, x_ref, sems = refs
    count, _, rows_z = x_ref.shape
    chunks = sems.shape[0]
    per = count // chunks
    copies = [
        pltpu.make_async_copy(x_hbm.at[pl.ds(i * per, per)], x_ref.at[pl.ds(i * per, per)], sems.at[i])
        for i in range(chunks)
    ]
    for copy in copies:
        copy.start()
    for i, copy in enumerate(copies):
        copy.wait()
        for a in range(i * per, (i + 1) * per):
            turned[pl.ds(a, rows_z, stride=count), :] = x_ref[a].T
    rows = rows_z // blocks * count
    rank = lax.axis_index("orb")
    for m, t_ref in enumerate(t_refs):
        for core in range(2):
            start = pl.multiple_of((rank ^ (2 * m + core)) * rows, rows)
            t_ref[core] = turned[pl.ds(start, rows), :].reshape(t_ref.shape[1:])


def hand_kernel(block_ref, owner_ref, pair_ref, other_ref):
    other_ref[...] = pair_ref[1]


def by_block(refs):
    refs = refs[::-1]
    half = len(refs) // 2 - 1
    return [refs[half + k // 2] if k % 2 else refs[k // 2].at[0] for k in range(2 * half)] + list(refs[2 * half :])


def squeeze(value):
    rows, wide = value.shape
    quarter, free = rows // 4, wide // 4
    lane = lax.broadcasted_iota(jnp.int32, (quarter, wide), 1)
    rest = value[3 * quarter :]
    parts = []
    for j in range(3):
        moved = pltpu.roll(rest, (3 - j) * free, 1)
        parts.append(jnp.where(lane < 3 * free, value[j * quarter : (j + 1) * quarter], moved))
    return jnp.concatenate(parts, axis=0)


def expand(value):
    rows, wide = value.shape
    quarter, free = rows // 3, wide // 4
    lane = lax.broadcasted_iota(jnp.int32, (quarter, wide), 1)
    rest = value[:quarter]
    for j in range(3):
        moved = pltpu.roll(value[j * quarter : (j + 1) * quarter], (j + 1) * free, 1)
        rest = jnp.where((lane >= j * free) & (lane < (j + 1) * free), moved, rest)
    return jnp.concatenate([value, rest], axis=0)


def pick_kernel(block_ref, *refs):
    x_refs, (act_ref, near_ref, far_ref, first_ref, last_ref) = by_block(refs[:-5]), refs[-5:]
    slab, nb, cells = act_ref.shape
    rank = lax.axis_index("orb")
    for k, x_ref in enumerate(x_refs):
        @pl.when((rank ^ block_ref[0]) == k)
        def _(x_ref=x_ref):
            act_ref[...] = x_ref[...]
    odd = rank % 2
    near_ref[...] = act_ref[pl.ds((1 - odd) * (slab - WIDTH), WIDTH)]
    far_ref[...] = act_ref[pl.ds(odd * (slab - WIDTH), WIDTH)]
    flat = act_ref[...].reshape(slab * nb, cells)
    first_ref[...] = squeeze(flat)
    last_ref[...] = squeeze(pltpu.roll(flat, 3 * (cells // 4), 1))


def split_kernel(blocks, act_ref, v_ref, wh_ref, wl_ref, *refs):
    x_refs, (high_ref, low_ref, inner_ref, turned) = by_block(refs[:-4]), refs[-4:]
    slab, nb, cells = act_ref.shape
    rank = lax.axis_index("orb")
    for k, x_ref in enumerate(x_refs):
        rows = pl.ds(pl.multiple_of((rank ^ k) * nb, nb), nb)
        for z in range(slab):
            high, low = split(x_ref[z])
            high_ref[rows, z * cells : (z + 1) * cells] = high
            low_ref[rows, z * cells : (z + 1) * cells] = low
    turned[...] = v_ref[...].T
    mine = pl.ds(pl.multiple_of(rank * slab, slab), slab)
    act = act_ref[...]
    middle = slice(2 * cells, 3 * cells)
    inner = dot3(split(act.reshape(slab * nb, cells)), (wh_ref[middle], wl_ref[middle]), ((1,), (0,)))
    inner = inner.reshape(slab, nb, cells) + (turned[mine, :][:, None, :] - 1.5 * CENTER) * act
    edge = jnp.zeros((WIDTH, nb, cells), jnp.float32)
    tall = jnp.concatenate([edge, act, edge], axis=0)
    for k, weight in enumerate(SIDES, 1):
        upper = tall[WIDTH + k : WIDTH + k + slab]
        lower = tall[WIDTH - k : WIDTH - k + slab]
        inner = inner + (-0.5 * weight) * (upper + lower)
    inner_ref[...] = inner


def project_kernel(
    volume, owner_ref, rot_ref, xh_ref, xl_ref, inner_ref, far_ref, near_ref, xb_ref, xa_ref, wh_ref, wl_ref,
    a_ref, p_ref, around,
):
    slab, nb, cells = inner_ref.shape
    rank = lax.axis_index("orb")
    odd = rank % 2
    around[1 - odd] = near_ref[...]
    around[odd] = far_ref[...]
    beside = slice(0, 2 * cells)
    wide = jnp.concatenate([expand(xb_ref[...]), expand(xa_ref[...])], axis=1)
    applied = dot3(split(wide), (wh_ref[beside], wl_ref[beside]), ((1,), (0,)))
    a_ref[...] = inner_ref[...] + applied.reshape(slab, nb, cells)
    for z in range(WIDTH):
        below, above = a_ref[z], a_ref[slab - 1 - z]
        for k in range(z + 1, WIDTH + 1):
            below = below + (-0.5 * SIDES[k - 1]) * around[0, WIDTH + z - k]
            above = above + (-0.5 * SIDES[k - 1]) * around[1, k - 1 - z]
        a_ref[z] = below
        a_ref[slab - 1 - z] = above
    flat = jnp.concatenate([a_ref[z] for z in range(slab)], axis=1)
    total = dot3(split(flat), (xh_ref[...], xl_ref[...]), ((1,), (1,)))
    p_ref[:nb] = total * volume
    p_ref[nb:] = jnp.where(rank == owner_ref[0], rot_ref[...], 0.0)


def remove_kernel(xh_ref, xl_ref, a_ref, *refs):
    *p_refs, g_ref = refs
    slab, nb, cells = a_ref.shape
    removed = dot3(split(total(p_refs, 0, nb)), (xh_ref[...], xl_ref[...]), ((1,), (0,)))
    for z in range(slab):
        g_ref[z] = a_ref[z] - removed[:, z * cells : (z + 1) * cells]


def mixing_kernel(nb, *refs):
    *p_refs, high_ref, low_ref = refs
    size, wide = high_ref.shape[0], p_refs[0].shape[1]
    row, col = (lax.broadcasted_iota(jnp.int32, (size, wide), axis) for axis in (0, 1))
    mine = jnp.where(col == lax.axis_index("orb") * nb + row // MIX, 1.0, 0.0).astype(BF16)
    orbital, col = (lax.broadcasted_iota(jnp.int32, (nb, size), axis) for axis in (0, 1))
    repeat = jnp.where(orbital == col // MIX, 1.0, 0.0).astype(BF16)
    row, col = (lax.broadcasted_iota(jnp.int32, (size, size), axis) for axis in (0, 1))
    same = row % MIX == col % MIX
    dot = lambda x, y, axes: lax.dot_general(x, y, (axes, ((), ())), preferred_element_type=jnp.float32)
    for part, ref in zip(split(total(p_refs, nb, nb)), (high_ref, low_ref)):
        block = dot(mine, part, ((1,), (1,))).astype(BF16)
        ref[...] = jnp.where(same, dot(block, repeat, ((1,), (0,))), 0.0).astype(BF16)


def update_kernel(blocks, sequence, wh_ref, wl_ref, x_ref, *refs):
    g_refs, (grad_hbm, out_hbm, whole, grad, out, sems) = refs[:blocks], refs[blocks:]
    nb, cells, rows_z = x_ref.shape
    rank = lax.axis_index("orb")
    share = rows_z // blocks * nb
    for k, g_ref in zip(sequence, g_refs):
        at = pl.ds(pl.multiple_of((rank ^ k) * share, share), share)
        whole[at, :] = g_ref[...].reshape(share, cells)
    per = nb // CHUNKS
    copies = []
    for i in range(CHUNKS):
        for c in range(i * per, (i + 1) * per):
            grad[c] = whole[pl.ds(c, rows_z, stride=nb), :].T
        part = pl.ds(i * per, per)
        copies.append(pltpu.make_async_copy(grad.at[part], grad_hbm.at[part], sems.at[0, i]))
        copies[-1].start()
    mix = (wh_ref[...], wl_ref[...])
    rows = cells // CHUNKS
    for i in range(CHUNKS):
        some = pl.ds(i * rows, rows)
        places = [pl.ds(start, MIX) for start in range(i * rows, (i + 1) * rows, MIX)]
        sides = [jnp.concatenate([grad[c, at] for c in range(nb)], axis=0) for at in places]
        result = dot3(mix, split(jnp.concatenate(sides, axis=1)), ((1,), (0,)))
        for j, at in enumerate(places):
            for a in range(nb):
                out[a, at] = x_ref[a, at] + result[a * MIX : (a + 1) * MIX, j * rows_z : (j + 1) * rows_z]
        copies.append(pltpu.make_async_copy(out.at[:, some], out_hbm.at[:, some], sems.at[1, i]))
        copies[-1].start()
    for copy in copies:
        copy.wait()


def swap(value, axis, k):
    count = lax.axis_size(axis)
    return lax.ppermute(value, axis, [(i, i ^ k) for i in range(count)])


def dom_kernel(value_ref, *refs):
    *other_refs, out_ref = refs
    nb = other_refs[0].shape[0]
    out_ref[:nb] = value_ref[:nb] + sum(ref[...] for ref in other_refs)
    out_ref[nb:] = value_ref[nb:]


def total(refs, first, count):
    rows = slice(first, first + count)
    return sum(ref[rows] for ref in refs)


def per_device(orbitals, potential, rotation, block, owner):
    nb, planes, rows_y, rows_z = orbitals.shape
    blocks, doms = lax.axis_size("orb"), lax.axis_size("dom")
    cells = planes * rows_y
    slab = rows_z // blocks
    volume = 1.0 / (cells * doms * rows_z)
    f32 = jnp.float32
    shape = lambda *dims: jax.ShapeDtypeStruct(dims, f32)
    piece, edge = shape(slab, nb, cells), shape(WIDTH, nb, cells)

    flat = orbitals.reshape(nb, cells, rows_z)
    held = pltpu.with_memory_space_constraint(flat, pltpu.HBM)
    chips = half = blocks // 2
    pieces = pl.pallas_call(
        functools.partial(pack_kernel, blocks),
        out_shape=[shape(2, slab, nb, cells)] * chips,
        in_specs=[HBM],
        out_specs=[VMEM] * chips,
        scratch_shapes=[
            pltpu.VMEM(((rows_z + 1) * nb, cells), f32),
            pltpu.VMEM((nb, cells, rows_z), f32),
            pltpu.SemaphoreType.DMA((CHUNKS,)),
        ],
        compiler_params=params(),
        name="pack",
    )(held)
    last = 2 * (chips - 1)
    pairs = [swap(value, "orb", 2 * m) if m else value for m, value in enumerate(pieces[:-1])]
    direct = [swap(pieces[-1][core], "orb", last + core) for core in range(2)]
    nearest = pl.pallas_call(
        hand_kernel,
        out_shape=piece,
        in_specs=[SMEM, SMEM, VMEM],
        out_specs=VMEM,
        compiler_params=params(),
        name="hand",
    )(block, owner, pairs[1])
    others = [nearest if m == 1 else value[1] for m, value in enumerate(pairs)]
    spread = (pairs + [swap(value, "orb", 1) for value in others] + direct)[::-1]

    side = shape(3 * slab * nb // 4, cells)
    active, near, far, first, last = pl.pallas_call(
        pick_kernel,
        out_shape=(piece, edge, edge, side, side),
        in_specs=[SMEM] + [VMEM] * len(spread),
        out_specs=[VMEM] * 5,
        compiler_params=params(),
        name="pick",
    )(block, *spread)

    up = lambda count: [(i, (i + 1) % count) for i in range(count)]
    down = lambda count: [(i, (i - 1) % count) for i in range(count)]
    x_before = lax.ppermute(last, "dom", up(doms))
    x_after = lax.ppermute(first, "dom", down(doms))
    z_near = swap(near, "orb", 1)
    z_far = lax.ppermute(far, "orb", [(o, (o + 2 * (o % 2) - 1) % blocks) for o in range(blocks)])

    halves = jax.ShapeDtypeStruct((blocks * nb, slab * cells), BF16)
    weights = [jnp.asarray(w) for w in plane_weights(planes, rows_y)]
    *parts, inner = pl.pallas_call(
        functools.partial(split_kernel, blocks),
        out_shape=(halves, halves, piece),
        in_specs=[VMEM] * (len(spread) + 4),
        out_specs=(VMEM, VMEM, VMEM),
        scratch_shapes=[pltpu.VMEM((rows_z, cells), f32)],
        compiler_params=params(),
        cost_estimate=pl.CostEstimate(flops=3 * blocks * nb * slab * cells, bytes_accessed=0, transcendentals=0),
        name="split",
    )(active, potential.reshape(cells, rows_z), *weights, *spread)

    applied, part = pl.pallas_call(
        functools.partial(project_kernel, volume),
        out_shape=(piece, shape(2 * nb, blocks * nb)),
        in_specs=[SMEM] + [VMEM] * 10,
        out_specs=(VMEM, VMEM),
        scratch_shapes=[pltpu.VMEM((2, WIDTH, nb, cells), f32)],
        compiler_params=params(),
        name="project",
    )(owner, rotation, *parts, inner, z_far, z_near, x_before, x_after, *weights)

    part = part + swap(part, "orb", 1)
    part = pl.pallas_call(
        dom_kernel,
        out_shape=shape(2 * nb, blocks * nb),
        in_specs=[VMEM] * doms,
        out_specs=VMEM,
        compiler_params=params(),
        name="dom",
    )(part, *[swap(part[:nb], "dom", k) for k in sorted(range(1, doms), key=lambda k: (k.bit_count() > 1, -k))])
    sums = [part] + [swap(part, "orb", k) for k in range(2, blocks, 2)]

    own = pl.pallas_call(
        remove_kernel,
        out_shape=piece,
        in_specs=[VMEM] * (3 + chips),
        out_specs=VMEM,
        compiler_params=params(),
        name="remove",
    )(*parts, applied, *sums)

    gathered = [own] + [None] * (blocks - 1)
    for k in range(2, blocks, 2):
        gathered[k] = swap(own, "orb", k)
    for k in range(0, blocks, 2):
        gathered[k + 1] = swap(gathered[k], "orb", 1)

    square = jax.ShapeDtypeStruct((MIX * nb, MIX * nb), BF16)
    mixing = pl.pallas_call(
        functools.partial(mixing_kernel, nb),
        out_shape=(square, square),
        in_specs=[VMEM] * chips,
        out_specs=(VMEM, VMEM),
        compiler_params=params(),
        name="mixing",
    )(*sums)

    sequence = sorted(range(blocks), key=lambda k: (k > 1, k < half + 2, k >= half, -k if k >= half else k))
    gradient, updated = pl.pallas_call(
        functools.partial(update_kernel, blocks, sequence),
        out_shape=(shape(nb, cells, rows_z), shape(nb, cells, rows_z)),
        in_specs=[VMEM] * (3 + blocks),
        out_specs=(HBM, HBM),
        scratch_shapes=[
            pltpu.VMEM(((rows_z + 1) * nb, cells), f32),
            pltpu.VMEM((nb, cells, rows_z), f32),
            pltpu.VMEM((nb, cells, rows_z), f32),
            pltpu.SemaphoreType.DMA((2, CHUNKS)),
        ],
        compiler_params=params(),
        name="update",
    )(*mixing, flat, *[gathered[k] for k in sequence])
    return gradient.reshape(orbitals.shape), updated.reshape(orbitals.shape)


def solution(mesh):
    in_specs = (P("orb", "dom", None, None), P("dom", None, None), P("orb", None), P(), P())
    out_specs = (P(None, "dom", None, None), P("orb", "dom", None, None))
    return jax.shard_map(
        per_device, mesh=mesh, in_specs=in_specs, out_specs=out_specs, check_vma=False
    )
```
